32 devices in a mesh: grp: 2 (over x), row: 16 (over z, y, core), feat: 1.
Axes of the slice: x: 2, y: 2, z: 4, core: 2. Of those that a mesh axis runs over, the one named last changes fastest.
Arguments:
- tokens_in: bfloat16 [192, 64, 1024], P(('grp', 'row'), None, 'feat'), parts along dimension 0, may hold values from -40 to 40
- upstream: bfloat16 [192, 64, 1024], P(('grp', 'row'), None, 'feat'), parts along dimension 0, may hold values from -6 to 6
- member_pick: int32 [192, 1], P(('grp', 'row')), parts along dimension 0, may hold values from 0 to 1
- norm_gain: float32 [2, 1024], replicated, may hold values from 0.1 to 1.9
- up_proj: bfloat16 [2, 1024, 4096], P(None, 'row', 'feat'), may hold values from -0.1875 to 0.1875
- down_proj: bfloat16 [2, 1024, 4096], P(None, 'row', 'feat'), may hold values from -0.09375 to 0.09375
Outputs:
- value_out: bfloat16 [192, 64, 1024], P(('grp', 'row'), None, 'feat'), parts along dimension 0
- grad_in: bfloat16 [192, 64, 1024], P(('grp', 'row'), None, 'feat'), parts along dimension 0
- norm_coupling: float32 [192, 64], P(('grp', 'row')), parts along dimension 0
The draws below stay inside these ranges and needn't reach their ends.
There are 2 independent parts, one for each index of `grp`. The reference program is written for one: setup_inputs(seed, part) draws one part's arguments, and reference() takes and returns one part's arrays. A program takes and returns all parts, laid end to end along the dimension named above; an argument that names none is the same for every part. Nothing has to cross between parts.
Inputs may be any that keep to these rules, and one draw needn't show every extreme that they name: `member_pick`: each row names exactly one member, and every member is named by at least one row.
All inputs are finite; a program needn't handle non-finite values.
Results may differ from the reference program's by a relative error of at most 0.0095.
Values may be sent and summed in bfloat16 or wider, within the bound.
No kernel may reach another device: no remote copies, remote signals or barrier semaphores. Data moves between devices by JAX's collectives and lax.ppermute only.
A program may use at most 128 MiB of HBM per device.

```python
import math
import jax
import jax.numpy as jnp
from jax import lax

D = 1024
FF = 4096
MEMBERS = 2
PICK = 1
SEQ = 64
ROWS = 96


def draw_tokens_in(key, part):
    key = jax.random.fold_in(key, 11)
    key_col, key_tok, key_base = jax.random.split(key, 3)
    column = jnp.exp(jax.random.uniform(key_col, (1, 1, D), jnp.float32, math.log(0.3), math.log(3.0)))
    token = jnp.exp(jax.random.uniform(key_tok, (ROWS, SEQ, 1), jnp.float32, math.log(0.5), math.log(2.0)))
    base = jnp.clip(jax.random.normal(key_base, (ROWS, SEQ, D), jnp.float32), -4.0, 4.0)
    return (base * column * token).astype(jnp.bfloat16)


def block_levels(own_key, shape, cuts, low, largest):
    gain = 1.0
    for axis_at, blocks in cuts:
        heights = jax.random.uniform(jax.random.fold_in(jax.random.fold_in(own_key, 6), axis_at), (blocks,), jnp.float32, low / len(cuts), largest / len(cuts))
        gain = gain * jnp.repeat(jnp.exp(heights), shape[axis_at] // blocks).reshape((-1,) + (1,) * (len(shape) - 1 - axis_at))
    return gain


def different_ones(own_key, rows, amount, top, lift):
    ranking = jax.random.permutation(jax.random.fold_in(own_key, 1), amount)
    boost = ranking
    for power in range(3):
        boost = boost * boost // amount
    boost = boost * lift // amount
    chance = jax.random.randint(jax.random.fold_in(own_key, 2), (rows, amount), 0, 4096) + boost
    holders = jax.random.permutation(jax.random.fold_in(own_key, 3), rows)[jnp.arange(amount) % rows]
    chance = jnp.where(jnp.arange(rows)[:, None] == holders[None, :], 1 << 14, chance)
    priority = chance * amount + jnp.arange(amount)
    return lax.top_k(priority.astype(jnp.int32), top)[1].astype(jnp.int32)


def centred(own_key, shape, spread, most, cuts=(), kind=jnp.bfloat16):
    values = jax.random.normal(own_key, shape, jnp.float32) * spread
    if len(cuts) > 0:
        values = block_levels(own_key, shape, cuts, -0.22, 0.18) * values
    return jnp.clip(values, min=-most, max=most).astype(kind)


def setup_inputs(seed: int = 0, part: int = 0) -> dict:
    keys = jax.random.split(jax.random.key(seed), 7)
    part_splits = jax.random.split(jax.random.fold_in(keys[6], part), 7)
    tokens_in = draw_tokens_in(jax.random.fold_in(jax.random.fold_in(keys[6], part), 71), part)
    upstream = centred(part_splits[1], (ROWS, SEQ, D), 1.0, 6.0, ((0, 16),))
    member_pick = different_ones(part_splits[2], ROWS, MEMBERS, PICK, 0)
    norm_gain = jnp.clip(1.0 + 0.18 * jax.random.normal(keys[3], (MEMBERS, D), jnp.float32), 0.1, 1.9)
    up_proj = centred(keys[4], (MEMBERS, D, FF), D ** -0.5, 0.1875, ((1, 16),))
    down_proj = centred(keys[5], (MEMBERS, D, FF), FF ** -0.5, 0.09375, ((1, 16),))
    return dict(tokens_in=tokens_in, upstream=upstream, member_pick=member_pick, norm_gain=norm_gain, up_proj=up_proj, down_proj=down_proj)


coef_c = math.sqrt(2.0 / math.pi)

def gelu_tanh(v):
    return 0.5 * v * (1.0 + jnp.tanh(coef_c * (v + 0.044715 * v * v * v)))

def gelu_slope(v):
    inner = jnp.tanh(coef_c * (v + 0.044715 * v * v * v))
    return 0.5 * (1.0 + inner) + 0.5 * v * (1.0 - inner * inner) * coef_c * (1.0 + 3.0 * 0.044715 * v * v)

def reference(tokens_in, upstream, member_pick, norm_gain, up_proj, down_proj):
    count = ROWS * SEQ
    flat_x = tokens_in.reshape(count, D).astype(jnp.float32)
    flat_g = upstream.reshape(count, D)
    inv_rms = 1.0 / jnp.sqrt(lax.optimization_barrier(jnp.mean(flat_x * flat_x, axis=1, keepdims=True)) + 1e-06)
    normed = flat_x * inv_rms
    labels = jnp.arange(MEMBERS, dtype=jnp.int32)
    chosen = lax.optimization_barrier(jnp.sum((member_pick[:, :, None] == labels[None, None, :]).astype(jnp.float32), axis=1)) / PICK
    chosen_tok = jnp.repeat(chosen, SEQ, axis=0)
    out_total = jnp.zeros((count, D), jnp.float32)
    back = jnp.zeros((count, D), jnp.float32)
    for member in range(MEMBERS):
        lifted = (normed * norm_gain[member][None, :]).astype(jnp.bfloat16)
        hidden = jnp.dot(lifted, up_proj[member], preferred_element_type=jnp.float32)
        act = gelu_tanh(hidden).astype(jnp.bfloat16)
        branch = jnp.dot(act, down_proj[member].T, preferred_element_type=jnp.float32)
        act_grad = jnp.dot(flat_g, down_proj[member], preferred_element_type=jnp.float32)
        pre_grad = (act_grad * gelu_slope(hidden)).astype(jnp.bfloat16)
        in_grad = jnp.dot(pre_grad, up_proj[member].T, preferred_element_type=jnp.float32)
        weight_col = chosen_tok[:, member:member + 1]
        out_total = out_total + weight_col * branch
        back = back + weight_col * norm_gain[member][None, :] * in_grad
    value_out = (flat_x + out_total).astype(jnp.bfloat16)
    stat = lax.optimization_barrier(jnp.mean(normed * back, axis=1, keepdims=True))
    coupling = stat * math.sqrt(D)
    grad_in = (flat_g.astype(jnp.float32) + (back - normed * stat) * inv_rms).astype(jnp.bfloat16)
    return (value_out.reshape(ROWS, SEQ, D), grad_in.reshape(ROWS, SEQ, D), coupling.reshape(ROWS, SEQ))
```

```python
import functools
import math

import jax
import jax.numpy as jnp
from jax import lax
from jax.experimental import pallas as pl
from jax.experimental.pallas import tpu as pltpu
from jax.sharding import PartitionSpec as P

coef_c = math.sqrt(2.0 / math.pi)


def gelu_tanh(v):
    return 0.5 * v * (1.0 + jnp.tanh(coef_c * (v + 0.044715 * v * v * v)))


def gelu_slope(v):
    inner = jnp.tanh(coef_c * (v + 0.044715 * v * v * v))
    return 0.5 * (1.0 + inner) + 0.5 * v * (1.0 - inner * inner) * coef_c * (
        1.0 + 3.0 * 0.044715 * v * v
    )


def on_device_general(tokens_in, upstream, member_pick, norm_gain, up_proj, down_proj):
    rows, seq, half = tokens_in.shape
    count = rows * seq
    members = up_proj.shape[0]
    pick = member_pick.shape[1]
    whole_x, whole_g = (
        lax.all_gather(tokens_in, "feat", axis=2, tiled=True),
        lax.all_gather(upstream, "feat", axis=2, tiled=True),
    )
    width = whole_x.shape[2]
    flat_x = whole_x.reshape(count, width).astype(jnp.float32)
    flat_g = whole_g.reshape(count, width)
    inv_rms = 1.0 / jnp.sqrt(jnp.mean(flat_x * flat_x, axis=1, keepdims=True) + 1e-06)
    normed = flat_x * inv_rms
    labels = jnp.arange(members, dtype=jnp.int32)
    chosen = (
        jnp.sum((member_pick[:, :, None] == labels[None, None, :]).astype(jnp.float32), axis=1)
        / pick
    )
    chosen_tok = jnp.repeat(chosen, seq, axis=0)
    out_half = jnp.zeros((count, half), jnp.float32)
    back_half = jnp.zeros((count, half), jnp.float32)
    for member in range(members):
        lifted = (normed * norm_gain[member][None, :]).astype(jnp.bfloat16)
        up_full = lax.all_gather(up_proj[member], "row", axis=0, tiled=True)
        hidden = jnp.dot(lifted, up_full, preferred_element_type=jnp.float32)
        act = gelu_tanh(hidden).astype(jnp.bfloat16)
        piece = lax.all_gather(down_proj[member], "row", axis=0, tiled=True)
        block = lax.dot_general(
            act, piece, (((1,), (1,)), ((), ())), preferred_element_type=jnp.float32
        )
        grads = jnp.dot(flat_g, piece, preferred_element_type=jnp.float32)
        pre_grad = (grads * gelu_slope(hidden)).astype(jnp.bfloat16)
        in_grad = lax.dot_general(
            pre_grad, up_full, (((1,), (1,)), ((), ())), preferred_element_type=jnp.float32
        )
        weight_col = chosen_tok[:, member : member + 1]
        out_term = weight_col * block
        back_term = weight_col * norm_gain[member][None, :] * in_grad
        out_part, back_part = (
            lax.psum_scatter(
                out_term.astype(jnp.bfloat16), "feat", scatter_dimension=1, tiled=True
            ).astype(jnp.float32),
            lax.psum_scatter(
                back_term.astype(jnp.bfloat16), "feat", scatter_dimension=1, tiled=True
            ).astype(jnp.float32),
        )
        out_half = out_half + out_part
        back_half = back_half + back_part
    own_x = tokens_in.reshape(count, half).astype(jnp.float32)
    normed_half = own_x * inv_rms
    stat = lax.psum(jnp.sum(normed_half * back_half, axis=1, keepdims=True), "feat") / width
    coupling = stat * math.sqrt(width)
    own_g = upstream.reshape(count, half).astype(jnp.float32)
    value_out = (own_x + out_half).astype(jnp.bfloat16)
    grad_in = (own_g + (back_half - normed_half * stat) * inv_rms).astype(jnp.bfloat16)
    return (
        value_out.reshape(rows, seq, half),
        grad_in.reshape(rows, seq, half),
        coupling.reshape(rows, seq),
    )


VMEM_LIMIT = 56 * 1024 * 1024
BF16 = jnp.bfloat16
F32 = jnp.float32


def prep_kernel(perm_ref, sorted_ref, x_ref, g_ref, gain_ref, lifted_ref, gs_ref):
    p = pl.program_id(0)
    x = x_ref[0].astype(F32)
    inv = 1.0 / jnp.sqrt(jnp.mean(x * x, axis=1, keepdims=True) + 1e-06)
    gain = gain_ref[pl.ds(sorted_ref[p], 1), :]
    lifted_ref[0] = ((x * inv) * gain).astype(BF16)
    gs_ref[0] = g_ref[0]


def prep(perm, member_sorted, x_pair, g_pair, gain):
    rows, seq, width = x_pair.shape
    block = pl.BlockSpec((1, seq, width), lambda p, perm, ms: (perm[p], 0, 0))
    out = pl.BlockSpec((1, seq, width), lambda p, perm, ms: (p, 0, 0))
    return pl.pallas_call(
        prep_kernel,
        grid_spec=pltpu.PrefetchScalarGridSpec(
            num_scalar_prefetch=2,
            grid=(rows,),
            in_specs=[block, block, pl.BlockSpec(gain.shape, lambda p, perm, ms: (0, 0))],
            out_specs=[out, out],
        ),
        out_shape=[jax.ShapeDtypeStruct((rows, seq, width), BF16)] * 2,
        name="prep",
    )(perm, member_sorted, x_pair, g_pair, gain)


def chunk_kernel(member, per_block, seq, sub, first, flag_ref, sorted_ref, *refs):
    if first:
        lifted_ref, g_ref, up_ref, down_ref, out_ref, back_ref = refs
    else:
        lifted_ref, g_ref, up_ref, down_ref, out_in, back_in, out_ref, back_ref = refs
    j = pl.program_id(0)
    used = flag_ref[member * pl.num_programs(0) + j] > 0

    @pl.when(used)
    def _():
        width = lifted_ref.shape[1]
        lifted = lifted_ref[...]
        g = g_ref[...]
        weight = jnp.concatenate(
            [
                jnp.full((seq, 1), (sorted_ref[j * per_block + i] == member).astype(F32), F32)
                for i in range(per_block)
            ],
            axis=0,
        )
        hidden_units = up_ref.shape[-1]
        out_sum = jnp.zeros(out_ref.shape, F32)
        back_sum = jnp.zeros(back_ref.shape, F32)
        for s in range(hidden_units // sub):
            cols = slice(s * sub, (s + 1) * sub)
            up = up_ref[:, 0, :, cols].reshape(width, sub)
            down = down_ref[:, 0, :, cols].reshape(width, sub)
            v = jnp.dot(lifted, up, preferred_element_type=F32)
            grads = jnp.dot(g, down, preferred_element_type=F32)
            square = v * v
            t = jnp.tanh(coef_c * (v + 0.044715 * square * v))
            act = (0.5 * v * (1.0 + t)).astype(BF16)
            slope = 0.5 * (1.0 + t) + 0.5 * v * (1.0 - t * t) * coef_c * (
                1.0 + 3.0 * 0.044715 * square
            )
            pre = (grads * slope).astype(BF16)
            dims = (((1,), (1,)), ((), ()))
            out_sum += lax.dot_general(act, down, dims, preferred_element_type=F32)
            back_sum += lax.dot_general(pre, up, dims, preferred_element_type=F32)
        if first:
            out_ref[...] = weight * out_sum
            back_ref[...] = weight * back_sum
        else:
            out_ref[...] = out_in[...] + weight * out_sum
            back_ref[...] = back_in[...] + weight * back_sum

    @pl.when(jnp.logical_not(used))
    def _():
        if first:
            out_ref[...] = jnp.zeros_like(out_ref)
            back_ref[...] = jnp.zeros_like(back_ref)
        else:
            out_ref[...] = out_in[...]
            back_ref[...] = back_in[...]


def chunk(member, per_block, seq, flags, member_sorted, lifted, g, weights, sums):
    tokens, width = lifted.shape
    blocks, _, depth, hidden = weights.shape
    size = per_block * seq
    first = sums is None
    tok = pl.BlockSpec((size, width), lambda j, f, s: (j, 0))
    up = pl.BlockSpec((blocks, 1, depth, hidden), lambda j, f, s: (0, 0, 0, 0))
    down = pl.BlockSpec((blocks, 1, depth, hidden), lambda j, f, s: (0, 1, 0, 0))
    sub = math.gcd(hidden, 512)
    args = [flags, member_sorted, lifted, g, weights, weights]
    specs = [tok, tok, up, down]
    alias = {}
    if not first:
        args += list(sums)
        specs += [tok, tok]
        alias = {6: 0, 7: 1}
    return pl.pallas_call(
        functools.partial(chunk_kernel, member, per_block, seq, sub, first),
        grid_spec=pltpu.PrefetchScalarGridSpec(
            num_scalar_prefetch=2, grid=(tokens // size,), in_specs=specs, out_specs=[tok, tok]
        ),
        out_shape=[jax.ShapeDtypeStruct((tokens, width), F32)] * 2,
        input_output_aliases=alias,
        compiler_params=pltpu.CompilerParams(vmem_limit_bytes=VMEM_LIMIT),
        cost_estimate=pl.CostEstimate(
            flops=8 * tokens * width * hidden * 2 // 3,
            bytes_accessed=2 * weights.size + 20 * lifted.size,
            transcendentals=tokens * hidden,
        ),
        name="chunk",
    )(*args)


def pack_kernel(pos_ref, out_ref, back_ref, packed_ref):
    packed_ref[0, 0] = out_ref[...].astype(BF16)
    packed_ref[1, 0] = back_ref[...].astype(BF16)


def pack(pos_partner, out_sum, back_sum, rows, seq):
    width = out_sum.shape[1]
    tok = pl.BlockSpec((seq, width), lambda r, pos: (pos[r], 0))
    return pl.pallas_call(
        pack_kernel,
        grid_spec=pltpu.PrefetchScalarGridSpec(
            num_scalar_prefetch=1,
            grid=(rows,),
            in_specs=[tok, tok],
            out_specs=pl.BlockSpec((2, 1, seq, width), lambda r, pos: (0, r, 0, 0)),
        ),
        out_shape=jax.ShapeDtypeStruct((2, rows, seq, width), BF16),
        name="pack",
    )(pos_partner, out_sum, back_sum)


def finish_kernel(
    pos_ref, member_ref, x_ref, g_ref, gain_ref, out_ref, back_ref, other_ref,
    value_ref, grad_ref, coupling_ref,
):
    r = pl.program_id(0)
    width = x_ref.shape[2]
    x = x_ref[0].astype(F32)
    inv = 1.0 / jnp.sqrt(jnp.mean(x * x, axis=1, keepdims=True) + 1e-06)
    normed = x * inv
    gain = gain_ref[pl.ds(member_ref[r], 1), :]
    back = gain * (back_ref[...] + other_ref[1, 0].astype(F32))
    stat = jnp.sum(normed * back, axis=1, keepdims=True) / width
    value_ref[0] = (x + (out_ref[...] + other_ref[0, 0].astype(F32))).astype(BF16)
    grad_ref[0] = (g_ref[0].astype(F32) + (back - normed * stat) * inv).astype(BF16)
    coupling_ref[0] = stat * math.sqrt(width)


def finish(pos_own, member_own, x, g, gain, out_sum, back_sum, other):
    rows, seq, width = x.shape
    row = pl.BlockSpec((1, seq, width), lambda r, pos, mem: (r, 0, 0))
    tok = pl.BlockSpec((seq, width), lambda r, pos, mem: (pos[r], 0))
    return pl.pallas_call(
        finish_kernel,
        grid_spec=pltpu.PrefetchScalarGridSpec(
            num_scalar_prefetch=2,
            grid=(rows,),
            in_specs=[
                row,
                row,
                pl.BlockSpec(gain.shape, lambda r, pos, mem: (0, 0)),
                tok,
                tok,
                pl.BlockSpec((2, 1, seq, width), lambda r, pos, mem: (0, r, 0, 0)),
            ],
            out_specs=[row, row, pl.BlockSpec((1, seq, 1), lambda r, pos, mem: (r, 0, 0))],
        ),
        out_shape=[
            jax.ShapeDtypeStruct((rows, seq, width), BF16),
            jax.ShapeDtypeStruct((rows, seq, width), BF16),
            jax.ShapeDtypeStruct((rows, seq, 1), F32),
        ],
        name="finish",
    )(pos_own, member_own, x, g, gain, out_sum, back_sum, other)


def on_device_pairs(ranks, tokens_in, upstream, member_pick, norm_gain, up_proj, down_proj):
    rows, seq, width = tokens_in.shape
    members, depth, hidden = up_proj.shape
    half = hidden // 2
    core = lax.rem(lax.axis_index("row"), 2)
    swap = [(i, i ^ 1) for i in range(ranks)]

    def partner(a):
        return lax.ppermute(a, "row", swap)

    both = jnp.stack([up_proj, down_proj])
    mine = lax.dynamic_slice_in_dim(both, core * half, half, 3)
    theirs = partner(lax.dynamic_slice_in_dim(both, (1 - core) * half, half, 3))
    even = core == 0
    shard = jnp.concatenate(
        [jnp.where(even, mine, theirs), jnp.where(even, theirs, mine)], axis=2
    )
    same_core = [list(range(c, ranks, 2)) for c in range(2)]
    parts = 2
    size = half // parts

    pick_own = member_pick[:, 0]
    pick_pair = jnp.concatenate([pick_own, partner(pick_own)])
    x_pair = jnp.concatenate([tokens_in, partner(tokens_in)])
    g_pair = jnp.concatenate([upstream, partner(upstream)])
    index = jnp.arange(2 * rows, dtype=jnp.int32)
    before = (pick_pair[None, :] < pick_pair[:, None]) | (
        (pick_pair[None, :] == pick_pair[:, None]) & (index[None, :] < index[:, None])
    )
    pos = jnp.sum(before.astype(jnp.int32), axis=1)
    at = pos[None, :] == index[:, None]
    perm = jnp.sum(jnp.where(at, index[None, :], 0), axis=1)
    member_sorted = jnp.sum(jnp.where(at, pick_pair[None, :], 0), axis=1)
    per_block = math.gcd(2 * rows, 4)
    labels = jnp.arange(members, dtype=jnp.int32)
    flags = jnp.any(
        member_sorted.reshape(1, -1, per_block) == labels[:, None, None], axis=2
    ).astype(jnp.int32).reshape(-1)

    lifted, g_sorted = prep(perm, member_sorted, x_pair, g_pair, norm_gain)
    lifted = lifted.reshape(2 * rows * seq, width)
    g_sorted = g_sorted.reshape(2 * rows * seq, width)

    sums = None
    for member in range(members):
        for part in range(parts):
            piece = shard[:, member, :, part * size : (part + 1) * size]
            weights = lax.all_gather(piece, "row", axis_index_groups=same_core)
            sums = chunk(
                member, per_block, seq, flags, member_sorted, lifted, g_sorted, weights, sums
            )
    other = partner(pack(pos[rows:], sums[0], sums[1], rows, seq))
    value_out, grad_in, coupling = finish(
        pos[:rows], pick_own, tokens_in, upstream, norm_gain, sums[0], sums[1], other
    )
    return value_out, grad_in, coupling.reshape(rows, seq)


def solution(mesh):
    ranks = mesh.shape["row"]
    paired = mesh.shape["feat"] == 1 and ranks % 2 == 0

    def on_device(tokens_in, upstream, member_pick, norm_gain, up_proj, down_proj):
        args = (tokens_in, upstream, member_pick, norm_gain, up_proj, down_proj)
        if paired and member_pick.shape[1] == 1:
            return on_device_pairs(ranks, *args)
        return on_device_general(*args)

    in_specs = (
        P(("grp", "row"), None, "feat"),
        P(("grp", "row"), None, "feat"),
        P(("grp", "row"), None),
        P(),
        P(None, "row", "feat"),
        P(None, "row", "feat"),
    )
    out_specs = (
        P(("grp", "row"), None, "feat"),
        P(("grp", "row"), None, "feat"),
        P(("grp", "row"), None),
    )
    return jax.shard_map(
        on_device, mesh=mesh, in_specs=in_specs, out_specs=out_specs, check_vma=False
    )
```

```python
import functools
import math

import jax
import jax.numpy as jnp
from jax import lax
from jax.experimental import pallas as pl
from jax.experimental.pallas import tpu as pltpu
from jax.sharding import PartitionSpec as P

coef_c = math.sqrt(2.0 / math.pi)


def gelu_tanh(v):
    return 0.5 * v * (1.0 + jnp.tanh(coef_c * (v + 0.044715 * v * v * v)))


def gelu_slope(v):
    inner = jnp.tanh(coef_c * (v + 0.044715 * v * v * v))
    return 0.5 * (1.0 + inner) + 0.5 * v * (1.0 - inner * inner) * coef_c * (
        1.0 + 3.0 * 0.044715 * v * v
    )


def on_device_general(tokens_in, upstream, member_pick, norm_gain, up_proj, down_proj):
    rows, seq, half = tokens_in.shape
    count = rows * seq
    members = up_proj.shape[0]
    pick = member_pick.shape[1]
    whole_x, whole_g = (
        lax.all_gather(tokens_in, "feat", axis=2, tiled=True),
        lax.all_gather(upstream, "feat", axis=2, tiled=True),
    )
    width = whole_x.shape[2]
    flat_x = whole_x.reshape(count, width).astype(jnp.float32)
    flat_g = whole_g.reshape(count, width)
    inv_rms = 1.0 / jnp.sqrt(jnp.mean(flat_x * flat_x, axis=1, keepdims=True) + 1e-06)
    normed = flat_x * inv_rms
    labels = jnp.arange(members, dtype=jnp.int32)
    chosen = (
        jnp.sum((member_pick[:, :, None] == labels[None, None, :]).astype(jnp.float32), axis=1)
        / pick
    )
    chosen_tok = jnp.repeat(chosen, seq, axis=0)
    out_half = jnp.zeros((count, half), jnp.float32)
    back_half = jnp.zeros((count, half), jnp.float32)
    for member in range(members):
        lifted = (normed * norm_gain[member][None, :]).astype(jnp.bfloat16)
        up_full = lax.all_gather(up_proj[member], "row", axis=0, tiled=True)
        hidden = jnp.dot(lifted, up_full, preferred_element_type=jnp.float32)
        act = gelu_tanh(hidden).astype(jnp.bfloat16)
        piece = lax.all_gather(down_proj[member], "row", axis=0, tiled=True)
        block = lax.dot_general(
            act, piece, (((1,), (1,)), ((), ())), preferred_element_type=jnp.float32
        )
        grads = jnp.dot(flat_g, piece, preferred_element_type=jnp.float32)
        pre_grad = (grads * gelu_slope(hidden)).astype(jnp.bfloat16)
        in_grad = lax.dot_general(
            pre_grad, up_full, (((1,), (1,)), ((), ())), preferred_element_type=jnp.float32
        )
        weight_col = chosen_tok[:, member : member + 1]
        out_term = weight_col * block
        back_term = weight_col * norm_gain[member][None, :] * in_grad
        out_part, back_part = (
            lax.psum_scatter(
                out_term.astype(jnp.bfloat16), "feat", scatter_dimension=1, tiled=True
            ).astype(jnp.float32),
            lax.psum_scatter(
                back_term.astype(jnp.bfloat16), "feat", scatter_dimension=1, tiled=True
            ).astype(jnp.float32),
        )
        out_half = out_half + out_part
        back_half = back_half + back_part
    own_x = tokens_in.reshape(count, half).astype(jnp.float32)
    normed_half = own_x * inv_rms
    stat = lax.psum(jnp.sum(normed_half * back_half, axis=1, keepdims=True), "feat") / width
    coupling = stat * math.sqrt(width)
    own_g = upstream.reshape(count, half).astype(jnp.float32)
    value_out = (own_x + out_half).astype(jnp.bfloat16)
    grad_in = (own_g + (back_half - normed_half * stat) * inv_rms).astype(jnp.bfloat16)
    return (
        value_out.reshape(rows, seq, half),
        grad_in.reshape(rows, seq, half),
        coupling.reshape(rows, seq),
    )


VMEM_LIMIT = 56 * 1024 * 1024
BF16 = jnp.bfloat16
F32 = jnp.float32


def prep_kernel(perm_ref, sorted_ref, x_ref, g_ref, gain_ref, lifted_ref, gs_ref):
    def row(p, carry):
        x = x_ref[perm_ref[p]].astype(F32)
        inv = 1.0 / jnp.sqrt(jnp.mean(x * x, axis=1, keepdims=True) + 1e-06)
        gain = gain_ref[pl.ds(sorted_ref[p], 1), :]
        lifted_ref[p] = ((x * inv) * gain).astype(BF16)
        gs_ref[p] = g_ref[perm_ref[p]]
        return carry

    lax.fori_loop(0, x_ref.shape[0], row, 0)


def prep(perm, member_sorted, x_pair, g_pair, gain):
    smem = pl.BlockSpec(memory_space=pltpu.SMEM)
    vmem = pl.BlockSpec(memory_space=pltpu.VMEM)
    return pl.pallas_call(
        prep_kernel,
        in_specs=[smem, smem, vmem, vmem, vmem],
        out_specs=[vmem, vmem],
        out_shape=[jax.ShapeDtypeStruct(x_pair.shape, BF16)] * 2,
        compiler_params=pltpu.CompilerParams(vmem_limit_bytes=VMEM_LIMIT),
        name="prep",
    )(perm, member_sorted, x_pair, g_pair, gain)


def chunk_kernel(
    member, per_block, seq, sub, own, first, opens,
    low_ref, high_ref, sorted_ref, place_ref, lifted_ref, g_ref, here_ref, there_ref,
    here_x_ref, there_x_ref, *refs,
):
    if first:
        out_ref, back_ref, weights_ref, sems = refs
    else:
        out_in, back_in, out_ref, back_ref, weights_ref, sems = refs
    j = pl.program_id(0)
    _, _, depth2, hidden_units = weights_ref.shape
    lines = weights_ref.shape[0]
    depth = depth2 // 2
    common = here_ref.shape[1] - own

    @pl.when(j == 0)
    def _():
        x, y = place_ref[0], place_ref[1]
        mine = pl.multiple_of(x * (depth2 - own), 16)
        others = pl.multiple_of((1 - x) * (depth2 - own), 16)
        copies = []
        for line, ref, x_ref in ((y, here_ref, here_x_ref), (1 - y, there_ref, there_x_ref)):
            for src, at, size in (
                (ref.at[:, pl.ds(0, own)], mine, own),
                (ref.at[:, pl.ds(own, common)], own, common),
                (x_ref, others, own),
            ):
                copies.append(
                    pltpu.make_async_copy(
                        src, weights_ref.at[:, line, pl.ds(at, size)], sems.at[len(copies)]
                    )
                )
        for copy in copies:
            copy.start()
        for copy in copies:
            copy.wait()

    if not first:

        @pl.when(jnp.logical_and(j == 0, high_ref[member] < low_ref[member]))
        def _():
            out_ref[...] = out_in[...]
            back_ref[...] = back_in[...]

    @pl.when(low_ref[member] + j <= high_ref[member])
    def _():
        at = low_ref[member] + j
        width = lifted_ref.shape[1]
        lifted = lifted_ref[...]
        g = g_ref[...]
        weight = jnp.concatenate(
            [
                jnp.full((seq, 1), (sorted_ref[at * per_block + i] == member).astype(F32), F32)
                for i in range(per_block)
            ],
            axis=0,
        )
        out_sum = jnp.zeros(out_ref.shape, F32)
        back_sum = jnp.zeros(back_ref.shape, F32)
        for s in range(hidden_units // sub):
            cols = slice(s * sub, (s + 1) * sub)
            up = weights_ref[:, :, :depth, cols].reshape(width, sub)
            down = weights_ref[:, :, depth:, cols].reshape(width, sub)
            v = jnp.dot(lifted, up, preferred_element_type=F32)
            grads = jnp.dot(g, down, preferred_element_type=F32)
            square = v * v
            t = jnp.tanh(coef_c * (v + 0.044715 * square * v))
            act = (0.5 * v * (1.0 + t)).astype(BF16)
            slope = 0.5 * (1.0 + t) + 0.5 * v * (1.0 - t * t) * coef_c * (
                1.0 + 3.0 * 0.044715 * square
            )
            pre = (grads * slope).astype(BF16)
            dims = (((1,), (1,)), ((), ()))
            out_sum += lax.dot_general(act, down, dims, preferred_element_type=F32)
            back_sum += lax.dot_general(pre, up, dims, preferred_element_type=F32)
        if first:
            out_ref[...] = weight * out_sum
            back_ref[...] = weight * back_sum
        elif opens:
            old = (sorted_ref[at * per_block] < member)
            out_ref[...] = jnp.where(old, out_in[...], 0.0) + weight * out_sum
            back_ref[...] = jnp.where(old, back_in[...], 0.0) + weight * back_sum
        else:
            out_ref[...] = out_in[...] + weight * out_sum
            back_ref[...] = back_in[...] + weight * back_sum


def chunk(member, opens, per_block, seq, scalars, lifted, g, pieces, sums):
    tokens, width = lifted.shape
    lines, rows, hidden = pieces[0].shape
    own = pieces[2].shape[1]
    depth2 = 2 * own + (rows - own)
    size = per_block * seq
    first = sums is None
    tok = pl.BlockSpec(
        (size, width),
        lambda j, low, high, s, p: (
            jnp.maximum(jnp.minimum(low[member] + j, high[member]), 0), 0
        ),
    )
    hbm = pl.BlockSpec(memory_space=pl.ANY)
    sub = math.gcd(hidden, 512)
    args = [*scalars, lifted, g, *pieces]
    specs = [tok, tok, hbm, hbm, hbm, hbm]
    alias = {}
    if not first:
        alias = {len(args): 0, len(args) + 1: 1}
        args += list(sums)
        specs += [tok, tok]
    return pl.pallas_call(
        functools.partial(chunk_kernel, member, per_block, seq, sub, own, first, opens),
        grid_spec=pltpu.PrefetchScalarGridSpec(
            num_scalar_prefetch=4,
            grid=(tokens // size,),
            in_specs=specs,
            out_specs=[tok, tok],
            scratch_shapes=[
                pltpu.VMEM((lines, 2, depth2, hidden), BF16),
                pltpu.SemaphoreType.DMA((6,)),
            ],
        ),
        out_shape=[jax.ShapeDtypeStruct((tokens, width), F32)] * 2,
        input_output_aliases=alias,
        compiler_params=pltpu.CompilerParams(vmem_limit_bytes=VMEM_LIMIT),
        cost_estimate=pl.CostEstimate(
            flops=8 * tokens * width * hidden * 2 // 3,
            bytes_accessed=4 * width * hidden + 20 * lifted.size,
            transcendentals=tokens * hidden,
        ),
        name="chunk",
    )(*args)


def pack_kernel(pos_ref, out_ref, back_ref, packed_ref, buffer, sems):
    rows = packed_ref.shape[1]
    seq = packed_ref.shape[2]
    copies = []
    for r in range(rows):
        at = pl.ds(pl.multiple_of(pos_ref[r] * seq, seq), seq)
        for i, ref in enumerate((out_ref, back_ref)):
            copy = pltpu.make_async_copy(ref.at[at], buffer.at[i, r], sems.at[i, r])
            copy.start()
            copies.append((copy, i, r))
    for copy, i, r in copies:
        copy.wait()
        packed_ref[i, r] = buffer[i, r].astype(BF16)


def pack(pos_partner, out_sum, back_sum, rows, seq):
    width = out_sum.shape[1]
    hbm = pl.BlockSpec(memory_space=pl.ANY)
    return pl.pallas_call(
        pack_kernel,
        in_specs=[pl.BlockSpec(memory_space=pltpu.SMEM), hbm, hbm],
        out_specs=pl.BlockSpec(memory_space=pltpu.VMEM),
        out_shape=jax.ShapeDtypeStruct((2, rows, seq, width), BF16),
        scratch_shapes=[
            pltpu.VMEM((2, rows, seq, width), F32),
            pltpu.SemaphoreType.DMA((2, rows)),
        ],
        compiler_params=pltpu.CompilerParams(vmem_limit_bytes=VMEM_LIMIT),
        name="pack",
    )(pos_partner, out_sum, back_sum)


def finish_kernel(
    pos_ref, member_ref, x_ref, g_ref, gain_ref, out_ref, back_ref, other_ref,
    value_ref, grad_ref, coupling_ref, buffer, sems,
):
    rows, seq, width = x_ref.shape
    copies = []
    for r in range(rows):
        at = pl.ds(pl.multiple_of(pos_ref[r] * seq, seq), seq)
        for i, ref in enumerate((out_ref, back_ref)):
            copy = pltpu.make_async_copy(ref.at[at], buffer.at[i, r], sems.at[i, r])
            copy.start()
            copies.append(copy)
    diagonal = lax.broadcasted_iota(jnp.int32, (seq, seq), 0) == lax.broadcasted_iota(
        jnp.int32, (seq, seq), 1
    )
    for r in range(rows):
        copies[2 * r].wait()
        copies[2 * r + 1].wait()
        x = x_ref[r].astype(F32)
        inv = 1.0 / jnp.sqrt(jnp.mean(x * x, axis=1, keepdims=True) + 1e-06)
        normed = x * inv
        gain = gain_ref[pl.ds(member_ref[r], 1), :]
        back = gain * (buffer[1, r] + other_ref[1, r].astype(F32))
        stat = jnp.sum(normed * back, axis=1, keepdims=True) / width
        value_ref[r] = (x + (buffer[0, r] + other_ref[0, r].astype(F32))).astype(BF16)
        grad_ref[r] = (g_ref[r].astype(F32) + (back - normed * stat) * inv).astype(BF16)
        line = jnp.sum(jnp.where(diagonal, stat, 0.0), axis=0, keepdims=True)
        coupling_ref[pl.ds(r, 1), :] = line * math.sqrt(width)


def finish(pos_own, member_own, x, g, gain, out_sum, back_sum, other):
    rows, seq, width = x.shape
    smem = pl.BlockSpec(memory_space=pltpu.SMEM)
    vmem = pl.BlockSpec(memory_space=pltpu.VMEM)
    hbm = pl.BlockSpec(memory_space=pl.ANY)
    return pl.pallas_call(
        finish_kernel,
        in_specs=[smem, smem, vmem, vmem, vmem, hbm, hbm, vmem],
        out_specs=[vmem, vmem, vmem],
        out_shape=[
            jax.ShapeDtypeStruct((rows, seq, width), BF16),
            jax.ShapeDtypeStruct((rows, seq, width), BF16),
            jax.ShapeDtypeStruct((rows, seq), F32),
        ],
        scratch_shapes=[
            pltpu.VMEM((2, rows, seq, width), F32),
            pltpu.SemaphoreType.DMA((2, rows)),
        ],
        compiler_params=pltpu.CompilerParams(vmem_limit_bytes=VMEM_LIMIT),
        name="finish",
    )(pos_own, member_own, x, g, gain, out_sum, back_sum, other)


def chunk_sizes(half, members):
    unit = half // 8
    if unit % 128:
        return [[half]] * members
    small = [unit, unit, 2 * unit, 2 * unit, 2 * unit]
    plan = [[2 * unit] * 4 for _ in range(members)]
    plan[0] = small
    plan[-1] = small[::-1]
    return plan


def on_device_pairs(ranks, tokens_in, upstream, member_pick, norm_gain, up_proj, down_proj):
    rows, seq, width = tokens_in.shape
    members, depth, hidden = up_proj.shape
    half = hidden // 2
    rank = lax.axis_index("row")
    core = lax.rem(rank, 2)
    x_at = lax.axis_index("grp")
    y_at = lax.rem(rank // 2, 2)

    def partner(a):
        return lax.ppermute(a, "row", [(i, i ^ 1) for i in range(ranks)])

    def over_y(a):
        return lax.ppermute(a, "row", [(i, i ^ 2) for i in range(ranks)])

    def over_x(a):
        return lax.ppermute(a, "grp", [(0, 1), (1, 0)])

    lines = [list(range(i, ranks, 4)) for i in range(4)]

    both = jnp.stack([up_proj, down_proj], axis=1)
    mine = lax.dynamic_slice_in_dim(both, core * half, half, 3)
    theirs = partner(lax.dynamic_slice_in_dim(both, (1 - core) * half, half, 3))
    even = core == 0
    shard = jnp.concatenate(
        [jnp.where(even, mine, theirs), jnp.where(even, theirs, mine)], axis=2
    ).reshape(members, 4 * depth, half)
    own = 5 * depth // 4
    piece_all = jnp.concatenate(
        [
            jnp.where(x_at == 0, shard[:, :own], shard[:, 4 * depth - own :]),
            shard[:, own : 4 * depth - own],
        ],
        axis=1,
    )

    pick_own = member_pick[:, 0]
    pick_pair = jnp.concatenate([pick_own, partner(pick_own)])
    x_pair = jnp.concatenate([tokens_in, partner(tokens_in)])
    g_pair = jnp.concatenate([upstream, partner(upstream)])
    index = jnp.arange(2 * rows, dtype=jnp.int32)
    before = (pick_pair[None, :] < pick_pair[:, None]) | (
        (pick_pair[None, :] == pick_pair[:, None]) & (index[None, :] < index[:, None])
    )
    pos = jnp.sum(before.astype(jnp.int32), axis=1)
    at = pos[None, :] == index[:, None]
    perm = jnp.sum(jnp.where(at, index[None, :], 0), axis=1)
    member_sorted = jnp.sum(jnp.where(at, pick_pair[None, :], 0), axis=1)
    per_block = math.gcd(2 * rows, 4)
    labels = jnp.arange(members, dtype=jnp.int32)[:, None]
    start = jnp.sum((pick_pair[None, :] < labels).astype(jnp.int32), axis=1)
    count = jnp.sum((pick_pair[None, :] == labels).astype(jnp.int32), axis=1)
    low = jnp.minimum(start, 2 * rows - 1) // per_block
    high = jnp.where(count > 0, (start + count - 1) // per_block, low - 1)

    lifted, g_sorted = prep(perm, member_sorted, x_pair, g_pair, norm_gain)
    lifted = lifted.reshape(2 * rows * seq, width)
    g_sorted = g_sorted.reshape(2 * rows * seq, width)
    scalars = (low, high, member_sorted, jnp.stack([x_at, y_at]))

    sums = None
    for member, sizes in enumerate(chunk_sizes(half, members)):
        for part, size in enumerate(sizes):
            first_unit = sum(sizes[:part])
            piece = piece_all[member, :, first_unit : first_unit + size]
            here = lax.all_gather(piece, "row", axis_index_groups=lines)
            there = over_y(here)
            here_x = over_x(here[:, :own])
            there_x = over_x(there[:, :own])
            pieces = (here, there, here_x, there_x)
            sums = chunk(
                member, part == 0, per_block, seq, scalars, lifted, g_sorted, pieces, sums
            )
    other = partner(pack(pos[rows:], sums[0], sums[1], rows, seq))
    return tuple(
        finish(pos[:rows], pick_own, tokens_in, upstream, norm_gain, sums[0], sums[1], other)
    )


def solution(mesh):
    ranks = mesh.shape["row"]
    paired = mesh.shape["feat"] == 1 and ranks % 4 == 0 and mesh.shape["grp"] == 2

    def on_device(tokens_in, upstream, member_pick, norm_gain, up_proj, down_proj):
        args = (tokens_in, upstream, member_pick, norm_gain, up_proj, down_proj)
        if paired and member_pick.shape[1] == 1:
            return on_device_pairs(ranks, *args)
        return on_device_general(*args)

    in_specs = (
        P(("grp", "row"), None, "feat"),
        P(("grp", "row"), None, "feat"),
        P(("grp", "row"), None),
        P(),
        P(None, "row", "feat"),
        P(None, "row", "feat"),
    )
    out_specs = (
        P(("grp", "row"), None, "feat"),
        P(("grp", "row"), None, "feat"),
        P(("grp", "row"), None),
    )
    return jax.shard_map(
        on_device, mesh=mesh, in_specs=in_specs, out_specs=out_specs, check_vma=False
    )
```

```python
import functools
import math

import jax
import jax.numpy as jnp
from jax import lax
from jax.experimental import pallas as pl
from jax.experimental.pallas import tpu as pltpu
from jax.sharding import PartitionSpec as P

coef_c = math.sqrt(2.0 / math.pi)


def gelu_tanh(v):
    return 0.5 * v * (1.0 + jnp.tanh(coef_c * (v + 0.044715 * v * v * v)))


def gelu_slope(v):
    inner = jnp.tanh(coef_c * (v + 0.044715 * v * v * v))
    return 0.5 * (1.0 + inner) + 0.5 * v * (1.0 - inner * inner) * coef_c * (
        1.0 + 3.0 * 0.044715 * v * v
    )


def on_device_general(tokens_in, upstream, member_pick, norm_gain, up_proj, down_proj):
    rows, seq, half = tokens_in.shape
    count = rows * seq
    members = up_proj.shape[0]
    pick = member_pick.shape[1]
    whole_x, whole_g = (
        lax.all_gather(tokens_in, "feat", axis=2, tiled=True),
        lax.all_gather(upstream, "feat", axis=2, tiled=True),
    )
    width = whole_x.shape[2]
    flat_x = whole_x.reshape(count, width).astype(jnp.float32)
    flat_g = whole_g.reshape(count, width)
    inv_rms = 1.0 / jnp.sqrt(jnp.mean(flat_x * flat_x, axis=1, keepdims=True) + 1e-06)
    normed = flat_x * inv_rms
    labels = jnp.arange(members, dtype=jnp.int32)
    chosen = (
        jnp.sum((member_pick[:, :, None] == labels[None, None, :]).astype(jnp.float32), axis=1)
        / pick
    )
    chosen_tok = jnp.repeat(chosen, seq, axis=0)
    out_half = jnp.zeros((count, half), jnp.float32)
    back_half = jnp.zeros((count, half), jnp.float32)
    for member in range(members):
        lifted = (normed * norm_gain[member][None, :]).astype(jnp.bfloat16)
        up_full = lax.all_gather(up_proj[member], "row", axis=0, tiled=True)
        hidden = jnp.dot(lifted, up_full, preferred_element_type=jnp.float32)
        act = gelu_tanh(hidden).astype(jnp.bfloat16)
        piece = lax.all_gather(down_proj[member], "row", axis=0, tiled=True)
        block = lax.dot_general(
            act, piece, (((1,), (1,)), ((), ())), preferred_element_type=jnp.float32
        )
        grads = jnp.dot(flat_g, piece, preferred_element_type=jnp.float32)
        pre_grad = (grads * gelu_slope(hidden)).astype(jnp.bfloat16)
        in_grad = lax.dot_general(
            pre_grad, up_full, (((1,), (1,)), ((), ())), preferred_element_type=jnp.float32
        )
        weight_col = chosen_tok[:, member : member + 1]
        out_term = weight_col * block
        back_term = weight_col * norm_gain[member][None, :] * in_grad
        out_part, back_part = (
            lax.psum_scatter(
                out_term.astype(jnp.bfloat16), "feat", scatter_dimension=1, tiled=True
            ).astype(jnp.float32),
            lax.psum_scatter(
                back_term.astype(jnp.bfloat16), "feat", scatter_dimension=1, tiled=True
            ).astype(jnp.float32),
        )
        out_half = out_half + out_part
        back_half = back_half + back_part
    own_x = tokens_in.reshape(count, half).astype(jnp.float32)
    normed_half = own_x * inv_rms
    stat = lax.psum(jnp.sum(normed_half * back_half, axis=1, keepdims=True), "feat") / width
    coupling = stat * math.sqrt(width)
    own_g = upstream.reshape(count, half).astype(jnp.float32)
    value_out = (own_x + out_half).astype(jnp.bfloat16)
    grad_in = (own_g + (back_half - normed_half * stat) * inv_rms).astype(jnp.bfloat16)
    return (
        value_out.reshape(rows, seq, half),
        grad_in.reshape(rows, seq, half),
        coupling.reshape(rows, seq),
    )


VMEM_LIMIT = 56 * 1024 * 1024
BF16 = jnp.bfloat16
F32 = jnp.float32


def prep_kernel(perm_ref, sorted_ref, x_ref, g_ref, gain_ref, lifted_ref, gs_ref):
    def row(p, carry):
        x = x_ref[perm_ref[p]].astype(F32)
        inv = 1.0 / jnp.sqrt(jnp.mean(x * x, axis=1, keepdims=True) + 1e-06)
        gain = gain_ref[pl.ds(sorted_ref[p], 1), :]
        lifted_ref[p] = ((x * inv) * gain).astype(BF16)
        gs_ref[p] = g_ref[perm_ref[p]]
        return carry

    lax.fori_loop(0, x_ref.shape[0], row, 0)


def prep(perm, member_sorted, x_pair, g_pair, gain):
    smem = pl.BlockSpec(memory_space=pltpu.SMEM)
    vmem = pl.BlockSpec(memory_space=pltpu.VMEM)
    return pl.pallas_call(
        prep_kernel,
        in_specs=[smem, smem, vmem, vmem, vmem],
        out_specs=[vmem, vmem],
        out_shape=[jax.ShapeDtypeStruct(x_pair.shape, BF16)] * 2,
        compiler_params=pltpu.CompilerParams(vmem_limit_bytes=VMEM_LIMIT),
        name="prep",
    )(perm, member_sorted, x_pair, g_pair, gain)


def chunk_kernel(
    member, per_block, seq, sub, first, opens, parts,
    low_ref, high_ref, sorted_ref, place_ref, lifted_ref, g_ref, *refs,
):
    pieces, refs = refs[: 6 * parts], refs[6 * parts :]
    if first:
        out_ref, back_ref, weights_ref, sems = refs
    else:
        out_in, back_in, out_ref, back_ref, weights_ref, sems = refs
    j = pl.program_id(0)
    lines, _, depth2, hidden_units = weights_ref.shape
    depth = depth2 // 2

    @pl.when(j == 0)
    def _():
        x, y, z = place_ref[0], place_ref[1], place_ref[2]
        mine = pl.multiple_of(x * depth, depth)
        others = pl.multiple_of((1 - x) * depth, depth)
        copies = []

        def put(src, to_z, to_y, at, size, cols):
            copies.append(
                pltpu.make_async_copy(
                    src, weights_ref.at[to_z, to_y, pl.ds(at, size), cols], sems.at[len(copies)]
                )
            )

        for part in range(parts):
            own, own_y, here, there, here_x, there_x = pieces[6 * part : 6 * part + 6]
            units = hidden_units // parts
            cols = pl.ds(part * units, units)
            put(own, z, y, 0, depth2, cols)
            put(own_y, z, 1 - y, 0, depth2, cols)
            for d in range(1, lines):
                from_z = lax.rem(z + lines - d, lines)
                put(here.at[d - 1], from_z, y, mine, depth, cols)
                put(there.at[d - 1], from_z, 1 - y, mine, depth, cols)
                put(here_x.at[d - 1], from_z, y, others, depth, cols)
                put(there_x.at[d - 1], from_z, 1 - y, others, depth, cols)
        for copy in copies:
            copy.start()
        for copy in copies:
            copy.wait()

    if not first:

        @pl.when(jnp.logical_and(j == 0, high_ref[member] < low_ref[member]))
        def _():
            out_ref[...] = out_in[...]
            back_ref[...] = back_in[...]

    @pl.when(low_ref[member] + j <= high_ref[member])
    def _():
        at = low_ref[member] + j
        width = lifted_ref.shape[1]
        lifted = lifted_ref[...]
        g = g_ref[...]
        weight = jnp.concatenate(
            [
                jnp.full((seq, 1), (sorted_ref[at * per_block + i] == member).astype(F32), F32)
                for i in range(per_block)
            ],
            axis=0,
        )
        out_sum = jnp.zeros(out_ref.shape, F32)
        back_sum = jnp.zeros(back_ref.shape, F32)
        for s in range(hidden_units // sub):
            cols = slice(s * sub, (s + 1) * sub)
            up = weights_ref[:, :, :depth, cols].reshape(width, sub)
            down = weights_ref[:, :, depth:, cols].reshape(width, sub)
            v = jnp.dot(lifted, up, preferred_element_type=F32)
            grads = jnp.dot(g, down, preferred_element_type=F32)
            square = v * v
            t = jnp.tanh(coef_c * (v + 0.044715 * square * v))
            act = (0.5 * v * (1.0 + t)).astype(BF16)
            slope = 0.5 * (1.0 + t) + 0.5 * v * (1.0 - t * t) * coef_c * (
                1.0 + 3.0 * 0.044715 * square
            )
            pre = (grads * slope).astype(BF16)
            dims = (((1,), (1,)), ((), ()))
            out_sum += lax.dot_general(act, down, dims, preferred_element_type=F32)
            back_sum += lax.dot_general(pre, up, dims, preferred_element_type=F32)
        if first:
            out_ref[...] = weight * out_sum
            back_ref[...] = weight * back_sum
        elif opens:
            old = sorted_ref[at * per_block] < member
            out_ref[...] = jnp.where(old, out_in[...], 0.0) + weight * out_sum
            back_ref[...] = jnp.where(old, back_in[...], 0.0) + weight * back_sum
        else:
            out_ref[...] = out_in[...] + weight * out_sum
            back_ref[...] = back_in[...] + weight * back_sum


def chunk(member, opens, per_block, seq, scalars, lifted, g, pieces, sums):
    tokens, width = lifted.shape
    parts = len(pieces)
    depth2, units = pieces[0][0].shape
    lines = pieces[0][2].shape[0] + 1
    hidden = parts * units
    size = per_block * seq
    first = sums is None
    tok = pl.BlockSpec(
        (size, width),
        lambda j, low, high, s, p: (
            jnp.maximum(jnp.minimum(low[member] + j, high[member]), 0), 0
        ),
    )
    hbm = pl.BlockSpec(memory_space=pl.ANY)
    sub = math.gcd(hidden, 512)
    args = [*scalars, lifted, g]
    for part in pieces:
        args += part
    specs = [tok, tok] + [hbm] * (6 * parts)
    alias = {}
    if not first:
        alias = {len(args): 0, len(args) + 1: 1}
        args += list(sums)
        specs += [tok, tok]
    return pl.pallas_call(
        functools.partial(chunk_kernel, member, per_block, seq, sub, first, opens, parts),
        grid_spec=pltpu.PrefetchScalarGridSpec(
            num_scalar_prefetch=4,
            grid=(tokens // size,),
            in_specs=specs,
            out_specs=[tok, tok],
            scratch_shapes=[
                pltpu.VMEM((lines, 2, depth2, hidden), BF16),
                pltpu.SemaphoreType.DMA((parts * (4 * lines - 2),)),
            ],
        ),
        out_shape=[jax.ShapeDtypeStruct((tokens, width), F32)] * 2,
        input_output_aliases=alias,
        compiler_params=pltpu.CompilerParams(vmem_limit_bytes=VMEM_LIMIT),
        cost_estimate=pl.CostEstimate(
            flops=8 * tokens * width * hidden * 2 // 3,
            bytes_accessed=4 * width * hidden + 20 * lifted.size,
            transcendentals=tokens * hidden,
        ),
        name="chunk",
    )(*args)


def pack_kernel(pos_ref, out_ref, back_ref, packed_ref, buffer, sems):
    rows = packed_ref.shape[1]
    seq = packed_ref.shape[2]
    copies = []
    for r in range(rows):
        at = pl.ds(pl.multiple_of(pos_ref[r] * seq, seq), seq)
        for i, ref in enumerate((out_ref, back_ref)):
            copy = pltpu.make_async_copy(ref.at[at], buffer.at[i, r], sems.at[i, r])
            copy.start()
            copies.append((copy, i, r))
    for copy, i, r in copies:
        copy.wait()
        packed_ref[i, r] = buffer[i, r].astype(BF16)


def pack(pos_partner, out_sum, back_sum, rows, seq):
    width = out_sum.shape[1]
    hbm = pl.BlockSpec(memory_space=pl.ANY)
    return pl.pallas_call(
        pack_kernel,
        in_specs=[pl.BlockSpec(memory_space=pltpu.SMEM), hbm, hbm],
        out_specs=pl.BlockSpec(memory_space=pltpu.VMEM),
        out_shape=jax.ShapeDtypeStruct((2, rows, seq, width), BF16),
        scratch_shapes=[
            pltpu.VMEM((2, rows, seq, width), F32),
            pltpu.SemaphoreType.DMA((2, rows)),
        ],
        compiler_params=pltpu.CompilerParams(vmem_limit_bytes=VMEM_LIMIT),
        name="pack",
    )(pos_partner, out_sum, back_sum)


def finish_kernel(
    pos_ref, member_ref, x_ref, g_ref, gain_ref, out_ref, back_ref, other_ref,
    value_ref, grad_ref, coupling_ref, buffer, sems,
):
    rows, seq, width = x_ref.shape
    copies = []
    for r in range(rows):
        at = pl.ds(pl.multiple_of(pos_ref[r] * seq, seq), seq)
        for i, ref in enumerate((out_ref, back_ref)):
            copy = pltpu.make_async_copy(ref.at[at], buffer.at[i, r], sems.at[i, r])
            copy.start()
            copies.append(copy)
    diagonal = lax.broadcasted_iota(jnp.int32, (seq, seq), 0) == lax.broadcasted_iota(
        jnp.int32, (seq, seq), 1
    )
    for r in range(rows):
        copies[2 * r].wait()
        copies[2 * r + 1].wait()
        x = x_ref[r].astype(F32)
        inv = 1.0 / jnp.sqrt(jnp.mean(x * x, axis=1, keepdims=True) + 1e-06)
        normed = x * inv
        gain = gain_ref[pl.ds(member_ref[r], 1), :]
        back = gain * (buffer[1, r] + other_ref[1, r].astype(F32))
        stat = jnp.sum(normed * back, axis=1, keepdims=True) / width
        value_ref[r] = (x + (buffer[0, r] + other_ref[0, r].astype(F32))).astype(BF16)
        grad_ref[r] = (g_ref[r].astype(F32) + (back - normed * stat) * inv).astype(BF16)
        line = jnp.sum(jnp.where(diagonal, stat, 0.0), axis=0, keepdims=True)
        coupling_ref[pl.ds(r, 1), :] = line * math.sqrt(width)


def finish(pos_own, member_own, x, g, gain, out_sum, back_sum, other):
    rows, seq, width = x.shape
    smem = pl.BlockSpec(memory_space=pltpu.SMEM)
    vmem = pl.BlockSpec(memory_space=pltpu.VMEM)
    hbm = pl.BlockSpec(memory_space=pl.ANY)
    return pl.pallas_call(
        finish_kernel,
        in_specs=[smem, smem, vmem, vmem, vmem, hbm, hbm, vmem],
        out_specs=[vmem, vmem, vmem],
        out_shape=[
            jax.ShapeDtypeStruct((rows, seq, width), BF16),
            jax.ShapeDtypeStruct((rows, seq, width), BF16),
            jax.ShapeDtypeStruct((rows, seq), F32),
        ],
        scratch_shapes=[
            pltpu.VMEM((2, rows, seq, width), F32),
            pltpu.SemaphoreType.DMA((2, rows)),
        ],
        compiler_params=pltpu.CompilerParams(vmem_limit_bytes=VMEM_LIMIT),
        name="finish",
    )(pos_own, member_own, x, g, gain, out_sum, back_sum, other)


def on_device_pairs(ranks, tokens_in, upstream, member_pick, norm_gain, up_proj, down_proj):
    rows, seq, width = tokens_in.shape
    members, depth, hidden = up_proj.shape
    half = hidden // 2
    rank = lax.axis_index("row")
    core = lax.rem(rank, 2)
    x_at = lax.axis_index("grp")
    y_at = lax.rem(rank // 2, 2)

    def partner(a):
        return lax.ppermute(a, "row", [(i, i ^ 1) for i in range(ranks)])

    def over_y(a):
        return lax.ppermute(a, "row", [(i, i ^ 2) for i in range(ranks)])

    def over_x(a):
        return lax.ppermute(a, "grp", [(0, 1), (1, 0)])

    def shift_z(a, d):
        return lax.ppermute(a, "row", [(i, (i + 4 * d) % ranks) for i in range(ranks)])

    def after(a, *others):
        return lax.optimization_barrier((a, *others))[0]

    both = jnp.stack([up_proj, down_proj], axis=1)
    mine = lax.dynamic_slice_in_dim(both, core * half, half, 3)
    theirs = partner(lax.dynamic_slice_in_dim(both, (1 - core) * half, half, 3))
    even = core == 0
    shard = jnp.concatenate(
        [jnp.where(even, mine, theirs), jnp.where(even, theirs, mine)], axis=2
    ).reshape(members, 4 * depth, half)
    along = jnp.where(x_at == 0, shard[:, : 2 * depth], shard[:, 2 * depth :])
    pick_own = member_pick[:, 0]
    pick_pair = jnp.concatenate([pick_own, partner(pick_own)])
    x_pair = jnp.concatenate([tokens_in, partner(tokens_in)])
    g_pair = jnp.concatenate([upstream, partner(upstream)])
    index = jnp.arange(2 * rows, dtype=jnp.int32)
    before = (pick_pair[None, :] < pick_pair[:, None]) | (
        (pick_pair[None, :] == pick_pair[:, None]) & (index[None, :] < index[:, None])
    )
    pos = jnp.sum(before.astype(jnp.int32), axis=1)
    at = pos[None, :] == index[:, None]
    perm = jnp.sum(jnp.where(at, index[None, :], 0), axis=1)
    member_sorted = jnp.sum(jnp.where(at, pick_pair[None, :], 0), axis=1)
    per_block = math.gcd(2 * rows, 4)
    labels = jnp.arange(members, dtype=jnp.int32)[:, None]
    start = jnp.sum((pick_pair[None, :] < labels).astype(jnp.int32), axis=1)
    end = jnp.sum((pick_pair[None, :] <= labels).astype(jnp.int32), axis=1)
    low = jnp.minimum(start, 2 * rows - 1) // per_block
    high = jnp.where(end > start, (end - 1) // per_block, low - 1)

    lifted, g_sorted = prep(perm, member_sorted, x_pair, g_pair, norm_gain)
    lifted = lifted.reshape(2 * rows * seq, width)
    g_sorted = g_sorted.reshape(2 * rows * seq, width)
    scalars = (low, high, member_sorted, jnp.stack([x_at, y_at, rank // 4]))

    count = 4
    size = half // count
    sums = None
    pieces, y_done = [], []
    for member in range(members):
        for part in range(count):
            cols = slice(part * size, (part + 1) * size)
            own, mine = shard[member, :, cols], along[member, :, cols]
            at = len(pieces)
            if at >= 2:
                mine = after(mine, pieces[at - 2][2])
            if at >= 3:
                mine = after(mine, y_done[at - 3])
            own_y = over_y(own)
            here = jnp.stack([shift_z(mine, d) for d in range(1, ranks // 4)])
            here_x = over_x(here)
            there = over_y(here)
            if at == members * count - 3:
                there_x = over_y(here_x)
            else:
                there_x = over_x(there)
            y_done.append(there)
            pieces.append((own, own_y, here, there, here_x, there_x))
    for member in range(members):
        for part in range(0, count, 2):
            at = member * count + part
            sums = chunk(
                member, part == 0, per_block, seq, scalars, lifted, g_sorted,
                pieces[at : at + 2], sums,
            )
    other = partner(pack(pos[rows:], sums[0], sums[1], rows, seq))
    return tuple(
        finish(pos[:rows], pick_own, tokens_in, upstream, norm_gain, sums[0], sums[1], other)
    )


def solution(mesh):
    ranks = mesh.shape["row"]
    paired = mesh.shape["feat"] == 1 and ranks % 4 == 0 and mesh.shape["grp"] == 2

    def on_device(tokens_in, upstream, member_pick, norm_gain, up_proj, down_proj):
        args = (tokens_in, upstream, member_pick, norm_gain, up_proj, down_proj)
        if paired and member_pick.shape[1] == 1:
            return on_device_pairs(ranks, *args)
        return on_device_general(*args)

    in_specs = (
        P(("grp", "row"), None, "feat"),
        P(("grp", "row"), None, "feat"),
        P(("grp", "row"), None),
        P(),
        P(None, "row", "feat"),
        P(None, "row", "feat"),
    )
    out_specs = (
        P(("grp", "row"), None, "feat"),
        P(("grp", "row"), None, "feat"),
        P(("grp", "row"), None),
    )
    return jax.shard_map(
        on_device, mesh=mesh, in_specs=in_specs, out_specs=out_specs, check_vma=False
    )
```

```python
import functools
import math

import jax
import jax.numpy as jnp
from jax import lax
from jax.experimental import pallas as pl
from jax.experimental.pallas import tpu as pltpu
from jax.sharding import PartitionSpec as P

coef_c = math.sqrt(2.0 / math.pi)


def gelu_tanh(v):
    return 0.5 * v * (1.0 + jnp.tanh(coef_c * (v + 0.044715 * v * v * v)))


def gelu_slope(v):
    inner = jnp.tanh(coef_c * (v + 0.044715 * v * v * v))
    return 0.5 * (1.0 + inner) + 0.5 * v * (1.0 - inner * inner) * coef_c * (
        1.0 + 3.0 * 0.044715 * v * v
    )


def on_device_general(tokens_in, upstream, member_pick, norm_gain, up_proj, down_proj):
    rows, seq, half = tokens_in.shape
    count = rows * seq
    members = up_proj.shape[0]
    pick = member_pick.shape[1]
    whole_x, whole_g = (
        lax.all_gather(tokens_in, "feat", axis=2, tiled=True),
        lax.all_gather(upstream, "feat", axis=2, tiled=True),
    )
    width = whole_x.shape[2]
    flat_x = whole_x.reshape(count, width).astype(jnp.float32)
    flat_g = whole_g.reshape(count, width)
    inv_rms = 1.0 / jnp.sqrt(jnp.mean(flat_x * flat_x, axis=1, keepdims=True) + 1e-06)
    normed = flat_x * inv_rms
    labels = jnp.arange(members, dtype=jnp.int32)
    chosen = (
        jnp.sum((member_pick[:, :, None] == labels[None, None, :]).astype(jnp.float32), axis=1)
        / pick
    )
    chosen_tok = jnp.repeat(chosen, seq, axis=0)
    out_half = jnp.zeros((count, half), jnp.float32)
    back_half = jnp.zeros((count, half), jnp.float32)
    for member in range(members):
        lifted = (normed * norm_gain[member][None, :]).astype(jnp.bfloat16)
        up_full = lax.all_gather(up_proj[member], "row", axis=0, tiled=True)
        hidden = jnp.dot(lifted, up_full, preferred_element_type=jnp.float32)
        act = gelu_tanh(hidden).astype(jnp.bfloat16)
        piece = lax.all_gather(down_proj[member], "row", axis=0, tiled=True)
        block = lax.dot_general(
            act, piece, (((1,), (1,)), ((), ())), preferred_element_type=jnp.float32
        )
        grads = jnp.dot(flat_g, piece, preferred_element_type=jnp.float32)
        pre_grad = (grads * gelu_slope(hidden)).astype(jnp.bfloat16)
        in_grad = lax.dot_general(
            pre_grad, up_full, (((1,), (1,)), ((), ())), preferred_element_type=jnp.float32
        )
        weight_col = chosen_tok[:, member : member + 1]
        out_term = weight_col * block
        back_term = weight_col * norm_gain[member][None, :] * in_grad
        out_part, back_part = (
            lax.psum_scatter(
                out_term.astype(jnp.bfloat16), "feat", scatter_dimension=1, tiled=True
            ).astype(jnp.float32),
            lax.psum_scatter(
                back_term.astype(jnp.bfloat16), "feat", scatter_dimension=1, tiled=True
            ).astype(jnp.float32),
        )
        out_half = out_half + out_part
        back_half = back_half + back_part
    own_x = tokens_in.reshape(count, half).astype(jnp.float32)
    normed_half = own_x * inv_rms
    stat = lax.psum(jnp.sum(normed_half * back_half, axis=1, keepdims=True), "feat") / width
    coupling = stat * math.sqrt(width)
    own_g = upstream.reshape(count, half).astype(jnp.float32)
    value_out = (own_x + out_half).astype(jnp.bfloat16)
    grad_in = (own_g + (back_half - normed_half * stat) * inv_rms).astype(jnp.bfloat16)
    return (
        value_out.reshape(rows, seq, half),
        grad_in.reshape(rows, seq, half),
        coupling.reshape(rows, seq),
    )


VMEM_LIMIT = 56 * 1024 * 1024
BF16 = jnp.bfloat16
F32 = jnp.float32


def prep_kernel(perm_ref, sorted_ref, x_ref, g_ref, gain_ref, lifted_ref, gs_ref):
    def row(p, carry):
        x = x_ref[perm_ref[p]].astype(F32)
        inv = 1.0 / jnp.sqrt(jnp.mean(x * x, axis=1, keepdims=True) + 1e-06)
        gain = gain_ref[pl.ds(sorted_ref[p], 1), :]
        lifted_ref[p] = ((x * inv) * gain).astype(BF16)
        gs_ref[p] = g_ref[perm_ref[p]]
        return carry

    lax.fori_loop(0, x_ref.shape[0], row, 0)


def prep(perm, member_sorted, x_pair, g_pair, gain):
    smem = pl.BlockSpec(memory_space=pltpu.SMEM)
    vmem = pl.BlockSpec(memory_space=pltpu.VMEM)
    return pl.pallas_call(
        prep_kernel,
        in_specs=[smem, smem, vmem, vmem, vmem],
        out_specs=[vmem, vmem],
        out_shape=[jax.ShapeDtypeStruct(x_pair.shape, BF16)] * 2,
        compiler_params=pltpu.CompilerParams(vmem_limit_bytes=VMEM_LIMIT),
        name="prep",
    )(perm, member_sorted, x_pair, g_pair, gain)


def chunk_kernel(
    member, per_block, seq, kind, units,
    low_ref, high_ref, sorted_ref, place_ref, perm_ref, lifted_ref, g_ref, *refs,
):
    first, opens, last = kind
    parts = len(units)
    pieces, refs = refs[: 6 * parts], refs[6 * parts :]
    if first:
        out_ref, back_ref, weights_ref, sems = refs
    else:
        out_in, back_in, out_ref, back_ref, weights_ref, sems = refs
    j = pl.program_id(0)
    lines, _, depth2, hidden_units = weights_ref.shape
    depth = depth2 // 2
    at = j if last else low_ref[member] + j
    inside = jnp.logical_and(at >= low_ref[member], at <= high_ref[member])

    @pl.when(j == 0)
    def _():
        x, y, z = place_ref[0], place_ref[1], place_ref[2]
        mine = pl.multiple_of(x * depth, depth)
        others = pl.multiple_of((1 - x) * depth, depth)
        copies = []

        def put(src, to_z, to_y, at, size, cols):
            copies.append(
                pltpu.make_async_copy(
                    src, weights_ref.at[to_z, to_y, pl.ds(at, size), cols], sems.at[len(copies)]
                )
            )

        for part in range(parts):
            own, own_y, here, there, here_x, there_x = pieces[6 * part : 6 * part + 6]
            cols = pl.ds(sum(units[:part]), units[part])
            own, own_y = (
                ref.at[min(member, ref.shape[0] - 1), :, pl.ds(start, units[part])]
                for ref, start in (own, own_y)
            )
            put(own, z, y, 0, depth2, cols)
            put(own_y, z, 1 - y, 0, depth2, cols)
            for d in range(1, lines):
                from_z = lax.rem(z + lines - d, lines)
                put(here.at[d - 1], from_z, y, mine, depth, cols)
                put(there.at[d - 1], from_z, 1 - y, mine, depth, cols)
                put(here_x.at[d - 1], from_z, y, others, depth, cols)
                put(there_x.at[d - 1], from_z, 1 - y, others, depth, cols)
        for copy in copies:
            copy.start()
        for copy in copies:
            copy.wait()

    def sums():
        width = lifted_ref.shape[1]
        lifted = lifted_ref[...]
        g = g_ref[...]
        weight = jnp.concatenate(
            [
                jnp.full((seq, 1), (sorted_ref[at * per_block + i] == member).astype(F32), F32)
                for i in range(per_block)
            ],
            axis=0,
        )
        out_sum = jnp.zeros(lifted.shape, F32)
        back_sum = jnp.zeros(lifted.shape, F32)
        bounds = list(range(0, hidden_units, 512)) + [hidden_units]
        for s, e in zip(bounds[:-1], bounds[1:]):
            up = weights_ref[:, :, :depth, s:e].reshape(width, e - s)
            down = weights_ref[:, :, depth:, s:e].reshape(width, e - s)
            v = jnp.dot(lifted, up, preferred_element_type=F32)
            grads = jnp.dot(g, down, preferred_element_type=F32)
            square = v * v
            t = jnp.tanh(coef_c * (v + 0.044715 * square * v))
            act = (0.5 * v * (1.0 + t)).astype(BF16)
            slope = 0.5 * (1.0 + t) + 0.5 * v * (1.0 - t * t) * coef_c * (
                1.0 + 3.0 * 0.044715 * square
            )
            pre = (grads * slope).astype(BF16)
            dims = (((1,), (1,)), ((), ()))
            out_sum += lax.dot_general(act, down, dims, preferred_element_type=F32)
            back_sum += lax.dot_general(pre, up, dims, preferred_element_type=F32)
        return weight * out_sum, weight * back_sum

    if last:
        rows = out_ref.shape[1]

        def store(i, value):
            for p in range(per_block):
                row = perm_ref[at * per_block + p]
                tokens = value[p * seq : (p + 1) * seq]

                @pl.when(row < rows)
                def _():
                    out_ref[i, jnp.minimum(row, rows - 1)] = tokens

                @pl.when(row >= rows)
                def _():
                    back_ref[i, jnp.maximum(row - rows, 0)] = tokens.astype(BF16)

        @pl.when(inside)
        def _():
            out_sum, back_sum = sums()
            store(0, out_in[...] + out_sum)
            store(1, back_in[...] + back_sum)

        @pl.when(jnp.logical_not(inside))
        def _():
            store(0, out_in[...])
            store(1, back_in[...])

        return

    if not first:

        @pl.when(jnp.logical_and(j == 0, high_ref[member] < low_ref[member]))
        def _():
            out_ref[...] = out_in[...]
            back_ref[...] = back_in[...]

    @pl.when(inside)
    def _():
        out_sum, back_sum = sums()
        if first:
            out_ref[...] = out_sum
            back_ref[...] = back_sum
        elif opens:
            old = sorted_ref[at * per_block] < member
            out_ref[...] = jnp.where(old, out_in[...], 0.0) + out_sum
            back_ref[...] = jnp.where(old, back_in[...], 0.0) + back_sum
        else:
            out_ref[...] = out_in[...] + out_sum
            back_ref[...] = back_in[...] + back_sum


def chunk(member, kind, per_block, seq, scalars, lifted, g, pieces, sums):
    first, _, last = kind
    tokens, width = lifted.shape
    units = [part[2].shape[2] for part in pieces]
    depth2 = pieces[0][0][0].shape[1]
    lines = pieces[0][2].shape[0] + 1
    hidden = sum(units)
    size = per_block * seq

    def block(j, low, high, *_):
        if last:
            return j, 0
        return jnp.maximum(jnp.minimum(low[member] + j, high[member]), 0), 0

    tok = pl.BlockSpec((size, width), block)
    hbm = pl.BlockSpec(memory_space=pl.ANY)
    args = [*scalars, lifted, g]
    starts = []
    for own, own_y, *rest in pieces:
        args += [own[0], own_y[0], *rest]
        starts.append((own[1], own_y[1]))
    specs = [tok, tok] + [hbm] * (6 * len(pieces))
    alias = {}
    out_specs = [tok, tok]
    out_shape = [jax.ShapeDtypeStruct((tokens, width), F32)] * 2
    if not first:
        alias = {len(args): 0, len(args) + 1: 1}
        args += list(sums)
        specs += [tok, tok]
    if last:
        alias = {}
        shape = (2, tokens // (2 * seq), seq, width)
        out_specs = [pl.BlockSpec(shape, lambda *_: (0, 0, 0, 0))] * 2
        out_shape = [jax.ShapeDtypeStruct(shape, F32), jax.ShapeDtypeStruct(shape, BF16)]

    def kernel(*refs):
        refs = list(refs)
        base = len(scalars) + 2
        for part, (own, own_y) in enumerate(starts):
            refs[base + 6 * part] = (refs[base + 6 * part], own)
            refs[base + 6 * part + 1] = (refs[base + 6 * part + 1], own_y)
        chunk_kernel(member, per_block, seq, kind, units, *refs)

    return pl.pallas_call(
        kernel,
        grid_spec=pltpu.PrefetchScalarGridSpec(
            num_scalar_prefetch=len(scalars),
            grid=(tokens // size,),
            in_specs=specs,
            out_specs=out_specs,
            scratch_shapes=[
                pltpu.VMEM((lines, 2, depth2, hidden), BF16),
                pltpu.SemaphoreType.DMA((len(pieces) * (4 * lines - 2),)),
            ],
        ),
        out_shape=out_shape,
        input_output_aliases=alias,
        compiler_params=pltpu.CompilerParams(vmem_limit_bytes=VMEM_LIMIT),
        cost_estimate=pl.CostEstimate(
            flops=8 * tokens * width * hidden * 2 // 3,
            bytes_accessed=4 * width * hidden + 20 * lifted.size,
            transcendentals=tokens * hidden,
        ),
        name="chunk",
    )(*args)


def finish_kernel(
    member_ref, x_ref, g_ref, gain_ref, own_ref, other_ref, value_ref, grad_ref, coupling_ref
):
    rows, seq, width = x_ref.shape
    diagonal = lax.broadcasted_iota(jnp.int32, (seq, seq), 0) == lax.broadcasted_iota(
        jnp.int32, (seq, seq), 1
    )
    for r in range(rows):
        x = x_ref[r].astype(F32)
        inv = 1.0 / jnp.sqrt(jnp.mean(x * x, axis=1, keepdims=True) + 1e-06)
        normed = x * inv
        gain = gain_ref[pl.ds(member_ref[pl.program_id(0) * rows + r], 1), :]
        back = gain * (own_ref[1, r] + other_ref[1, r].astype(F32))
        stat = jnp.sum(normed * back, axis=1, keepdims=True) / width
        value_ref[r] = (x + (own_ref[0, r] + other_ref[0, r].astype(F32))).astype(BF16)
        grad_ref[r] = (g_ref[r].astype(F32) + (back - normed * stat) * inv).astype(BF16)
        line = jnp.sum(jnp.where(diagonal, stat, 0.0), axis=0, keepdims=True)
        coupling_ref[r] = line * math.sqrt(width)


def finish(member_own, x, g, gain, own, other):
    rows, seq, width = x.shape
    step = math.gcd(rows, 2)
    row = pl.BlockSpec((step, seq, width), lambda r, mem: (r, 0, 0))
    two = pl.BlockSpec((2, step, seq, width), lambda r, mem: (0, r, 0, 0))
    return pl.pallas_call(
        finish_kernel,
        grid_spec=pltpu.PrefetchScalarGridSpec(
            num_scalar_prefetch=1,
            grid=(rows // step,),
            in_specs=[row, row, pl.BlockSpec(gain.shape, lambda r, mem: (0, 0)), two, two],
            out_specs=[row, row, pl.BlockSpec((step, 1, seq), lambda r, mem: (r, 0, 0))],
        ),
        out_shape=[
            jax.ShapeDtypeStruct((rows, seq, width), BF16),
            jax.ShapeDtypeStruct((rows, seq, width), BF16),
            jax.ShapeDtypeStruct((rows, 1, seq), F32),
        ],
        compiler_params=pltpu.CompilerParams(vmem_limit_bytes=VMEM_LIMIT),
        name="finish",
    )(member_own, x, g, gain, own, other)


def plan_chunks(half, members):
    unit = half // 8
    if unit % 128 or members != 2:
        return [(m, [half // 2, half - half // 2], False) for m in range(members)]
    return [
        (0, [unit, 2 * unit], False),
        (0, [3 * unit, 2 * unit], False),
        (1, [2 * unit, 3 * unit], True),
        (1, [2 * unit, unit], False),
    ]


def on_device_pairs(ranks, tokens_in, upstream, member_pick, norm_gain, up_proj, down_proj):
    rows, seq, width = tokens_in.shape
    members, depth, hidden = up_proj.shape
    half = hidden // 2
    rank = lax.axis_index("row")
    core = lax.rem(rank, 2)
    x_at = lax.axis_index("grp")
    y_at = lax.rem(rank // 2, 2)

    def partner(a):
        return lax.ppermute(a, "row", [(i, i ^ 1) for i in range(ranks)])

    def over_y(a):
        return lax.ppermute(a, "row", [(i, i ^ 2) for i in range(ranks)])

    def over_x(a):
        return lax.ppermute(a, "grp", [(0, 1), (1, 0)])

    def shift_z(a, d):
        return lax.ppermute(a, "row", [(i, (i + 4 * d) % ranks) for i in range(ranks)])

    def after(a, *others):
        return lax.optimization_barrier((a, *others))[0]

    both = jnp.stack([up_proj, down_proj], axis=1)
    mine = lax.dynamic_slice_in_dim(both, core * half, half, 3)
    theirs = partner(lax.dynamic_slice_in_dim(both, (1 - core) * half, half, 3))
    even = core == 0
    shard = jnp.concatenate(
        [jnp.where(even, mine, theirs), jnp.where(even, theirs, mine)], axis=2
    ).reshape(members, 4 * depth, half)
    along = jnp.where(x_at == 0, shard[:, : 2 * depth], shard[:, 2 * depth :])
    pick_own = member_pick[:, 0]
    pick_pair = jnp.concatenate([pick_own, partner(pick_own)])
    x_pair = jnp.concatenate([tokens_in, partner(tokens_in)])
    g_pair = jnp.concatenate([upstream, partner(upstream)])
    index = jnp.arange(2 * rows, dtype=jnp.int32)
    before = (pick_pair[None, :] < pick_pair[:, None]) | (
        (pick_pair[None, :] == pick_pair[:, None]) & (index[None, :] < index[:, None])
    )
    pos = jnp.sum(before.astype(jnp.int32), axis=1)
    at = pos[None, :] == index[:, None]
    perm = jnp.sum(jnp.where(at, index[None, :], 0), axis=1)
    member_sorted = jnp.sum(jnp.where(at, pick_pair[None, :], 0), axis=1)
    per_block = math.gcd(2 * rows, 4)
    labels = jnp.arange(members, dtype=jnp.int32)[:, None]
    start = jnp.sum((pick_pair[None, :] < labels).astype(jnp.int32), axis=1)
    end = jnp.sum((pick_pair[None, :] <= labels).astype(jnp.int32), axis=1)
    low = jnp.minimum(start, 2 * rows - 1) // per_block
    high = jnp.where(end > start, (end - 1) // per_block, low - 1)

    lifted, g_sorted = prep(perm, member_sorted, x_pair, g_pair, norm_gain)
    lifted = lifted.reshape(2 * rows * seq, width)
    g_sorted = g_sorted.reshape(2 * rows * seq, width)
    scalars = (low, high, member_sorted, jnp.stack([x_at, y_at, rank // 4]), perm)

    own_y = [over_y(shard[member]) for member in range(members)]
    steps = plan_chunks(half, members)
    sums = None
    z_done, y_done, x_done, yx_done, all_sums = [], [], [], [], []
    start = [0] * members
    for i, (member, sizes, x_first) in enumerate(steps):
        pieces = []
        for part, size in enumerate(sizes):
            first_unit = start[member]
            start[member] += size
            at = len(z_done)
            mine = along[member, :, first_unit : first_unit + size]
            waits = []
            for done, behind in ((z_done, 2), (y_done, 3), (x_done, 3), (yx_done, 4)):
                if at >= behind:
                    waits.append(done[at - behind])
            if i >= 3 and part == 0:
                waits.append(all_sums[i - 3][0])
            if waits:
                mine = after(mine, *waits)
            here = jnp.stack([shift_z(mine, d) for d in range(1, ranks // 4)])
            here_x = over_x(here)
            there = over_y(here)
            there_x = over_y(here_x) if x_first and part else over_x(there)
            z_done.append(here)
            y_done.append(there)
            x_done.append(here_x)
            yx_done.append(there_x)
            pieces.append(
                ((shard, first_unit), (own_y[member][None], first_unit), here, there, here_x, there_x)
            )
        first, last = i == 0, i == len(steps) - 1
        opens = not any(m == member for m, _, _ in steps[:i])
        sums = chunk(
            member, (first, opens, last), per_block, seq, scalars, lifted, g_sorted, pieces, sums
        )
        all_sums.append(sums)
    own, packed = sums
    value_out, grad_in, coupling = finish(
        pick_own, tokens_in, upstream, norm_gain, own, partner(packed)
    )
    return value_out, grad_in, coupling.reshape(rows, seq)


def solution(mesh):
    ranks = mesh.shape["row"]
    paired = mesh.shape["feat"] == 1 and ranks % 4 == 0 and mesh.shape["grp"] == 2

    def on_device(tokens_in, upstream, member_pick, norm_gain, up_proj, down_proj):
        args = (tokens_in, upstream, member_pick, norm_gain, up_proj, down_proj)
        if paired and member_pick.shape[1] == 1:
            return on_device_pairs(ranks, *args)
        return on_device_general(*args)

    in_specs = (
        P(("grp", "row"), None, "feat"),
        P(("grp", "row"), None, "feat"),
        P(("grp", "row"), None),
        P(),
        P(None, "row", "feat"),
        P(None, "row", "feat"),
    )
    out_specs = (
        P(("grp", "row"), None, "feat"),
        P(("grp", "row"), None, "feat"),
        P(("grp", "row"), None),
    )
    return jax.shard_map(
        on_device, mesh=mesh, in_specs=in_specs, out_specs=out_specs, check_vma=False
    )
```

```python
import functools
import math

import jax
import jax.numpy as jnp
from jax import lax
from jax.experimental import pallas as pl
from jax.experimental.pallas import tpu as pltpu
from jax.sharding import PartitionSpec as P

coef_c = math.sqrt(2.0 / math.pi)


def gelu_tanh(v):
    return 0.5 * v * (1.0 + jnp.tanh(coef_c * (v + 0.044715 * v * v * v)))


def gelu_slope(v):
    inner = jnp.tanh(coef_c * (v + 0.044715 * v * v * v))
    return 0.5 * (1.0 + inner) + 0.5 * v * (1.0 - inner * inner) * coef_c * (
        1.0 + 3.0 * 0.044715 * v * v
    )


def on_device_general(tokens_in, upstream, member_pick, norm_gain, up_proj, down_proj):
    rows, seq, half = tokens_in.shape
    count = rows * seq
    members = up_proj.shape[0]
    pick = member_pick.shape[1]
    whole_x, whole_g = (
        lax.all_gather(tokens_in, "feat", axis=2, tiled=True),
        lax.all_gather(upstream, "feat", axis=2, tiled=True),
    )
    width = whole_x.shape[2]
    flat_x = whole_x.reshape(count, width).astype(jnp.float32)
    flat_g = whole_g.reshape(count, width)
    inv_rms = 1.0 / jnp.sqrt(jnp.mean(flat_x * flat_x, axis=1, keepdims=True) + 1e-06)
    normed = flat_x * inv_rms
    labels = jnp.arange(members, dtype=jnp.int32)
    chosen = (
        jnp.sum((member_pick[:, :, None] == labels[None, None, :]).astype(jnp.float32), axis=1)
        / pick
    )
    chosen_tok = jnp.repeat(chosen, seq, axis=0)
    out_half = jnp.zeros((count, half), jnp.float32)
    back_half = jnp.zeros((count, half), jnp.float32)
    for member in range(members):
        lifted = (normed * norm_gain[member][None, :]).astype(jnp.bfloat16)
        up_full = lax.all_gather(up_proj[member], "row", axis=0, tiled=True)
        hidden = jnp.dot(lifted, up_full, preferred_element_type=jnp.float32)
        act = gelu_tanh(hidden).astype(jnp.bfloat16)
        piece = lax.all_gather(down_proj[member], "row", axis=0, tiled=True)
        block = lax.dot_general(
            act, piece, (((1,), (1,)), ((), ())), preferred_element_type=jnp.float32
        )
        grads = jnp.dot(flat_g, piece, preferred_element_type=jnp.float32)
        pre_grad = (grads * gelu_slope(hidden)).astype(jnp.bfloat16)
        in_grad = lax.dot_general(
            pre_grad, up_full, (((1,), (1,)), ((), ())), preferred_element_type=jnp.float32
        )
        weight_col = chosen_tok[:, member : member + 1]
        out_term = weight_col * block
        back_term = weight_col * norm_gain[member][None, :] * in_grad
        out_part, back_part = (
            lax.psum_scatter(
                out_term.astype(jnp.bfloat16), "feat", scatter_dimension=1, tiled=True
            ).astype(jnp.float32),
            lax.psum_scatter(
                back_term.astype(jnp.bfloat16), "feat", scatter_dimension=1, tiled=True
            ).astype(jnp.float32),
        )
        out_half = out_half + out_part
        back_half = back_half + back_part
    own_x = tokens_in.reshape(count, half).astype(jnp.float32)
    normed_half = own_x * inv_rms
    stat = lax.psum(jnp.sum(normed_half * back_half, axis=1, keepdims=True), "feat") / width
    coupling = stat * math.sqrt(width)
    own_g = upstream.reshape(count, half).astype(jnp.float32)
    value_out = (own_x + out_half).astype(jnp.bfloat16)
    grad_in = (own_g + (back_half - normed_half * stat) * inv_rms).astype(jnp.bfloat16)
    return (
        value_out.reshape(rows, seq, half),
        grad_in.reshape(rows, seq, half),
        coupling.reshape(rows, seq),
    )


VMEM_LIMIT = 56 * 1024 * 1024
BF16 = jnp.bfloat16
F32 = jnp.float32


def prep_kernel(perm_ref, sorted_ref, x_ref, g_ref, gain_ref, lifted_ref, gs_ref):
    def row(p, carry):
        x = x_ref[perm_ref[p]].astype(F32)
        inv = 1.0 / jnp.sqrt(jnp.mean(x * x, axis=1, keepdims=True) + 1e-06)
        gain = gain_ref[pl.ds(sorted_ref[p], 1), :]
        lifted_ref[p] = ((x * inv) * gain).astype(BF16)
        gs_ref[p] = g_ref[perm_ref[p]]
        return carry

    lax.fori_loop(0, x_ref.shape[0], row, 0)


def prep(perm, member_sorted, x_pair, g_pair, gain):
    smem = pl.BlockSpec(memory_space=pltpu.SMEM)
    vmem = pl.BlockSpec(memory_space=pltpu.VMEM)
    return pl.pallas_call(
        prep_kernel,
        in_specs=[smem, smem, vmem, vmem, vmem],
        out_specs=[vmem, vmem],
        out_shape=[jax.ShapeDtypeStruct(x_pair.shape, BF16)] * 2,
        compiler_params=pltpu.CompilerParams(vmem_limit_bytes=VMEM_LIMIT),
        name="prep",
    )(perm, member_sorted, x_pair, g_pair, gain)


def chunk_kernel(
    member, per_block, seq, kind, units,
    low_ref, high_ref, sorted_ref, place_ref, perm_ref, dest_ref, lifted_ref, g_ref, *refs,
):
    first, opens, last = kind
    parts = len(units)
    pieces, refs = refs[: 4 * parts], refs[4 * parts :]
    if first:
        *outs, weights_ref, sems = refs
    else:
        out_in, back_in, *outs, weights_ref, sems = refs
    out_ref, back_ref = outs[:2]
    j = pl.program_id(0)
    lines, _, depth2, hidden_units = weights_ref.shape
    depth = depth2 // 2
    at = j if last else low_ref[member] + j
    inside = jnp.logical_and(at >= low_ref[member], at <= high_ref[member])

    @pl.when(j == 0)
    def _():
        y, z = place_ref[0], place_ref[1]
        copies = []

        def put(src, to_z, to_y, cols):
            copies.append(
                pltpu.make_async_copy(
                    src, weights_ref.at[to_z, to_y, :, cols], sems.at[len(copies)]
                )
            )

        for part in range(parts):
            cols = pl.ds(sum(units[:part]), units[part])
            (own, start), (own_y, start_y), here, there = pieces[4 * part : 4 * part + 4]
            put(own.at[member, :, pl.ds(start, units[part])], z, y, cols)
            put(own_y.at[:, pl.ds(start_y, units[part])], z, 1 - y, cols)
            for d in range(1, lines):
                from_z = lax.rem(z + lines - d, lines)
                put(here.at[d - 1], from_z, y, cols)
                put(there.at[d - 1], from_z, 1 - y, cols)
        for copy in copies:
            copy.start()
        for copy in copies:
            copy.wait()

    def sums():
        width = lifted_ref.shape[1]
        lifted = lifted_ref[...]
        g = g_ref[...]
        weight = jnp.concatenate(
            [
                jnp.full((seq, 1), (sorted_ref[at * per_block + i] == member).astype(F32), F32)
                for i in range(per_block)
            ],
            axis=0,
        )
        out_sum = jnp.zeros(lifted.shape, F32)
        back_sum = jnp.zeros(lifted.shape, F32)
        bounds = list(range(0, hidden_units, 512)) + [hidden_units]
        for s, e in zip(bounds[:-1], bounds[1:]):
            up = weights_ref[:, :, :depth, s:e].reshape(width, e - s)
            down = weights_ref[:, :, depth:, s:e].reshape(width, e - s)
            v = jnp.dot(lifted, up, preferred_element_type=F32)
            grads = jnp.dot(g, down, preferred_element_type=F32)
            square = v * v
            t = jnp.tanh(coef_c * (v + 0.044715 * square * v))
            act = (0.5 * v * (1.0 + t)).astype(BF16)
            slope = 0.5 * (1.0 + t) + 0.5 * v * (1.0 - t * t) * coef_c * (
                1.0 + 3.0 * 0.044715 * square
            )
            pre = (grads * slope).astype(BF16)
            dims = (((1,), (1,)), ((), ()))
            out_sum += lax.dot_general(act, down, dims, preferred_element_type=F32)
            back_sum += lax.dot_general(pre, up, dims, preferred_element_type=F32)
        return weight * out_sum, weight * back_sum

    def old_sums():
        if first:
            return 0.0, 0.0
        if opens:
            old = sorted_ref[at * per_block] < member
            return jnp.where(old, out_in[...], 0.0), jnp.where(old, back_in[...], 0.0)
        return out_in[...], back_in[...]

    if last:
        rows = out_ref.shape[0]

        def store(i, value):
            for p in range(per_block):
                row = perm_ref[at * per_block + p]
                to = dest_ref[row]
                tokens = value[p * seq : (p + 1) * seq]

                @pl.when(row < rows)
                def _():
                    outs[i][to] = tokens

                low_row = rows
                for packed_ref in outs[2:]:
                    high_row = low_row + packed_ref.shape[1]

                    @pl.when(jnp.logical_and(row >= low_row, row < high_row))
                    def _():
                        packed_ref[i, to] = tokens.astype(BF16)

                    low_row = high_row

        @pl.when(inside)
        def _():
            out_sum, back_sum = sums()
            out_old, back_old = old_sums()
            store(0, out_old + out_sum)
            store(1, back_old + back_sum)

        @pl.when(jnp.logical_not(inside))
        def _():
            store(0, out_in[...])
            store(1, back_in[...])

        return

    if not first:

        @pl.when(jnp.logical_and(j == 0, high_ref[member] < low_ref[member]))
        def _():
            out_ref[...] = out_in[...]
            back_ref[...] = back_in[...]

    @pl.when(inside)
    def _():
        out_sum, back_sum = sums()
        out_old, back_old = old_sums()
        out_ref[...] = out_old + out_sum
        back_ref[...] = back_old + back_sum


def chunk(member, kind, per_block, scalars, lifted, g, pieces, sums, splits=None):
    first, _, last = kind
    rows, seq, width = lifted.shape
    tokens = rows * seq
    units = [part[2].shape[2] for part in pieces]
    lines = pieces[0][2].shape[0] + 1
    depth2 = pieces[0][2].shape[1]
    hidden = sum(units)
    size = per_block * seq

    def block(j, low, high, *_):
        if last:
            return j, 0
        return jnp.maximum(jnp.minimum(low[member] + j, high[member]), 0), 0

    tok = pl.BlockSpec((size, width), block)
    hbm = pl.BlockSpec(memory_space=pl.ANY)
    args = [*scalars, lifted.reshape(tokens, width), g.reshape(tokens, width)]
    starts = []
    for own, own_y, here, there in pieces:
        args += [own[0], own_y[0], here, there]
        starts.append((own[1], own_y[1]))
    specs = [tok, tok] + [hbm] * (4 * len(pieces))
    alias = {}
    out_specs = [tok, tok]
    out_shape = [jax.ShapeDtypeStruct((tokens, width), F32)] * 2
    if not first:
        alias = {len(args): 0, len(args) + 1: 1}
        args += [a.reshape(tokens, width) for a in sums]
        specs += [tok, tok]
    if last:
        alias = {}
        out_shape = [jax.ShapeDtypeStruct((splits[0], seq, width), F32)] * 2
        out_shape += [jax.ShapeDtypeStruct((2, n, seq, width), BF16) for n in splits[1:]]
        out_specs = [
            pl.BlockSpec(a.shape, lambda *_, n=len(a.shape): (0,) * n) for a in out_shape
        ]

    def kernel(*refs):
        refs = list(refs)
        base = len(scalars) + 2
        for part, (own, own_y) in enumerate(starts):
            refs[base + 4 * part] = (refs[base + 4 * part], own)
            refs[base + 4 * part + 1] = (refs[base + 4 * part + 1], own_y)
        chunk_kernel(member, per_block, seq, kind, units, *refs)

    return pl.pallas_call(
        kernel,
        grid_spec=pltpu.PrefetchScalarGridSpec(
            num_scalar_prefetch=len(scalars),
            grid=(tokens // size,),
            in_specs=specs,
            out_specs=out_specs,
            scratch_shapes=[
                pltpu.VMEM((lines, 2, depth2, hidden), BF16),
                pltpu.SemaphoreType.DMA((len(pieces) * 2 * lines,)),
            ],
        ),
        out_shape=out_shape,
        input_output_aliases=alias,
        compiler_params=pltpu.CompilerParams(vmem_limit_bytes=VMEM_LIMIT),
        cost_estimate=pl.CostEstimate(
            flops=8 * tokens * width * hidden * 2 // 3,
            bytes_accessed=4 * width * hidden + 20 * lifted.size,
            transcendentals=tokens * hidden,
        ),
        name="chunk",
    )(*args)


def finish_kernel(
    member_ref, x_ref, g_ref, gain_ref, out_ref, back_ref, other_ref, across_ref,
    value_ref, grad_ref, coupling_ref,
):
    rows, seq, width = x_ref.shape
    diagonal = lax.broadcasted_iota(jnp.int32, (seq, seq), 0) == lax.broadcasted_iota(
        jnp.int32, (seq, seq), 1
    )
    for r in range(rows):
        x = x_ref[r].astype(F32)
        inv = 1.0 / jnp.sqrt(jnp.mean(x * x, axis=1, keepdims=True) + 1e-06)
        normed = x * inv
        gain = gain_ref[pl.ds(member_ref[pl.program_id(0) * rows + r], 1), :]
        back = gain * (
            back_ref[r] + other_ref[1, r].astype(F32) + across_ref[1, r].astype(F32)
        )
        stat = jnp.sum(normed * back, axis=1, keepdims=True) / width
        out = out_ref[r] + other_ref[0, r].astype(F32) + across_ref[0, r].astype(F32)
        value_ref[r] = (x + out).astype(BF16)
        grad_ref[r] = (g_ref[r].astype(F32) + (back - normed * stat) * inv).astype(BF16)
        line = jnp.sum(jnp.where(diagonal, stat, 0.0), axis=0, keepdims=True)
        coupling_ref[r] = line * math.sqrt(width)


def finish(member_own, x, g, gain, out, back, other, across):
    rows, seq, width = x.shape
    step = math.gcd(rows, 2)
    row = pl.BlockSpec((step, seq, width), lambda r, mem: (r, 0, 0))
    two = pl.BlockSpec((2, step, seq, width), lambda r, mem: (0, r, 0, 0))
    return pl.pallas_call(
        finish_kernel,
        grid_spec=pltpu.PrefetchScalarGridSpec(
            num_scalar_prefetch=1,
            grid=(rows // step,),
            in_specs=[
                row, row, pl.BlockSpec(gain.shape, lambda r, mem: (0, 0)), row, row, two, two
            ],
            out_specs=[row, row, pl.BlockSpec((step, 1, seq), lambda r, mem: (r, 0, 0))],
        ),
        out_shape=[
            jax.ShapeDtypeStruct((rows, seq, width), BF16),
            jax.ShapeDtypeStruct((rows, seq, width), BF16),
            jax.ShapeDtypeStruct((rows, 1, seq), F32),
        ],
        compiler_params=pltpu.CompilerParams(vmem_limit_bytes=VMEM_LIMIT),
        name="finish",
    )(member_own, x, g, gain, out, back, other, across)


def sort_rows(picks, members, per_block):
    n = picks.shape[0]
    index = jnp.arange(n, dtype=jnp.int32)
    before = (picks[None, :] < picks[:, None]) | (
        (picks[None, :] == picks[:, None]) & (index[None, :] < index[:, None])
    )
    pos = jnp.sum(before.astype(jnp.int32), axis=1)
    at = pos[None, :] == index[:, None]
    perm = jnp.sum(jnp.where(at, index[None, :], 0), axis=1)
    member_sorted = jnp.sum(jnp.where(at, picks[None, :], 0), axis=1)
    labels = jnp.arange(members, dtype=jnp.int32)[:, None]
    start = jnp.sum((picks[None, :] < labels).astype(jnp.int32), axis=1)
    end = jnp.sum((picks[None, :] <= labels).astype(jnp.int32), axis=1)
    low = jnp.minimum(start, n - 1) // per_block
    high = jnp.where(end > start, (end - 1) // per_block, low - 1)
    return pos, perm, member_sorted, low, high


def on_device_shared(ranks, tokens_in, upstream, member_pick, norm_gain, up_proj, down_proj):
    rows, seq, width = tokens_in.shape
    members, depth, hidden = up_proj.shape
    rank = lax.axis_index("row")
    core = lax.rem(rank, 2)
    x_at = lax.axis_index("grp")
    y_at = lax.rem(rank // 2, 2)
    lines = ranks // 4

    def partner(a):
        return lax.ppermute(a, "row", [(i, i ^ 1) for i in range(ranks)])

    def over_y(a):
        return lax.ppermute(a, "row", [(i, i ^ 2) for i in range(ranks)])

    def over_x(a):
        return lax.ppermute(a, "grp", [(0, 1), (1, 0)])

    def shift_z(a, d):
        return lax.ppermute(a, "row", [(i, (i + 4 * d) % ranks) for i in range(ranks)])

    def after(a, *others):
        return lax.optimization_barrier((a, *others))[0]

    quarter = 3 * hidden // 16
    half = hidden // 8
    both = jnp.stack([up_proj, down_proj], axis=1)

    def units_of(c):
        return jnp.concatenate(
            [
                lax.dynamic_slice_in_dim(both, (2 * x_at + c) * quarter, quarter, 3),
                lax.dynamic_slice_in_dim(both, 4 * quarter + c * half, half, 3),
            ],
            axis=3,
        )

    mine = units_of(core)
    theirs = partner(units_of(1 - core))
    even = core == 0
    shard = jnp.concatenate(
        [jnp.where(even, mine, theirs), jnp.where(even, theirs, mine)], axis=2
    ).reshape(members, 4 * depth, quarter + half)

    pick_own = member_pick[:, 0]
    x_over, g_over, pick_over = over_x(tokens_in), over_x(upstream), over_x(pick_own)
    pick_pair = jnp.concatenate([pick_own, partner(pick_own)])
    pick_all = jnp.concatenate([pick_pair, pick_over, partner(pick_over)])
    x_pair = jnp.concatenate([tokens_in, partner(tokens_in)])
    g_pair = jnp.concatenate([upstream, partner(upstream)])
    x_all = jnp.concatenate([x_pair, x_over, partner(x_over)])
    g_all = jnp.concatenate([g_pair, g_over, partner(g_over)])
    per_block = math.gcd(2 * rows, 4)
    place = jnp.stack([y_at, rank // 4])
    pos, perm, member_sorted, low, high = sort_rows(pick_pair, members, per_block)
    index = jnp.arange(4 * rows, dtype=jnp.int32)
    scalars_alone = (low, high, member_sorted, place, perm, lax.rem(index[: 2 * rows], rows))
    lifted_alone, g_alone = prep(perm, member_sorted, x_pair, g_pair, norm_gain)
    _, perm, member_sorted, low, high = sort_rows(pick_all, members, per_block)
    dest = jnp.concatenate([pos, lax.rem(index[2 * rows :], rows)])
    scalars_shared = (low, high, member_sorted, place, perm, dest)
    lifted_shared, g_shared = prep(perm, member_sorted, x_all, g_all, norm_gain)

    third = quarter // 3
    transfers = [
        (0, 0, third),
        (0, third, 2 * third),
        (1, 0, 2 * third),
        (1, 2 * third, third),
        (0, quarter, half),
        (1, quarter, half),
    ]
    z_done, y_done, own_y, pieces = [], [], {}, []
    for at, (member, start, size) in enumerate(transfers):
        mine = shard[member, :, start : start + size]
        waits = []
        if at >= 2:
            waits += [z_done[at - 2], y_done[at - 2 if at < 4 else at - 3]]
        if at == 2:
            waits.append(own_y[0])
        if at == 4:
            waits.append(own_y[1])
        if waits:
            mine = after(mine, *waits)
        if at in (0, 1):
            own_y[at] = over_y(after(shard[at], *z_done[:at]))
        here = jnp.stack([shift_z(mine, d) for d in range(1, lines)])
        z_done.append(here)
        if at == 4:
            sums = chunk(
                0, (True, False, False), per_block, scalars_shared, lifted_shared, g_shared,
                pieces[0:2], None,
            )
            out, back, over_same, over_other = chunk(
                1, (False, True, True), per_block, scalars_shared, lifted_shared, g_shared,
                pieces[2:4], sums, (2 * rows, rows, rows),
            )
            across = (over_same.astype(F32) + partner(over_other).astype(F32)).astype(BF16)
        if at == 5:
            here = after(here, across)
            across = over_x(across)
        there = over_y(here)
        y_done.append(there)
        pieces.append(((shard, start), (own_y[member], start), here, there))

    sums = chunk(
        0, (False, False, False), per_block, scalars_alone, lifted_alone, g_alone, pieces[4:5],
        (out, back),
    )
    sums = (after(sums[0], across), sums[1])
    out, back, packed = chunk(
        1, (False, False, True), per_block, scalars_alone, lifted_alone, g_alone, pieces[5:6], sums,
        (rows, rows),
    )
    value_out, grad_in, coupling = finish(
        pick_own, tokens_in, upstream, norm_gain, out, back, partner(packed), across
    )
    return value_out, grad_in, coupling.reshape(rows, seq)


def solution(mesh):
    ranks = mesh.shape["row"]
    four = mesh.shape["feat"] == 1 and ranks % 4 == 0 and mesh.shape["grp"] == 2

    def on_device(tokens_in, upstream, member_pick, norm_gain, up_proj, down_proj):
        args = (tokens_in, upstream, member_pick, norm_gain, up_proj, down_proj)
        if four and member_pick.shape[1] == 1 and up_proj.shape[0] == 2:
            return on_device_shared(ranks, *args)
        return on_device_general(*args)

    in_specs = (
        P(("grp", "row"), None, "feat"),
        P(("grp", "row"), None, "feat"),
        P(("grp", "row"), None),
        P(),
        P(None, "row", "feat"),
        P(None, "row", "feat"),
    )
    out_specs = (
        P(("grp", "row"), None, "feat"),
        P(("grp", "row"), None, "feat"),
        P(("grp", "row"), None),
    )
    return jax.shard_map(
        on_device, mesh=mesh, in_specs=in_specs, out_specs=out_specs, check_vma=False
    )
```

```python
import functools
import math

import jax
import jax.numpy as jnp
from jax import lax
from jax.experimental import pallas as pl
from jax.experimental.pallas import tpu as pltpu
from jax.sharding import PartitionSpec as P

coef_c = math.sqrt(2.0 / math.pi)


def gelu_tanh(v):
    return 0.5 * v * (1.0 + jnp.tanh(coef_c * (v + 0.044715 * v * v * v)))


def gelu_slope(v):
    inner = jnp.tanh(coef_c * (v + 0.044715 * v * v * v))
    return 0.5 * (1.0 + inner) + 0.5 * v * (1.0 - inner * inner) * coef_c * (
        1.0 + 3.0 * 0.044715 * v * v
    )


def on_device_general(tokens_in, upstream, member_pick, norm_gain, up_proj, down_proj):
    rows, seq, half = tokens_in.shape
    count = rows * seq
    members = up_proj.shape[0]
    pick = member_pick.shape[1]
    whole_x, whole_g = (
        lax.all_gather(tokens_in, "feat", axis=2, tiled=True),
        lax.all_gather(upstream, "feat", axis=2, tiled=True),
    )
    width = whole_x.shape[2]
    flat_x = whole_x.reshape(count, width).astype(jnp.float32)
    flat_g = whole_g.reshape(count, width)
    inv_rms = 1.0 / jnp.sqrt(jnp.mean(flat_x * flat_x, axis=1, keepdims=True) + 1e-06)
    normed = flat_x * inv_rms
    labels = jnp.arange(members, dtype=jnp.int32)
    chosen = (
        jnp.sum((member_pick[:, :, None] == labels[None, None, :]).astype(jnp.float32), axis=1)
        / pick
    )
    chosen_tok = jnp.repeat(chosen, seq, axis=0)
    out_half = jnp.zeros((count, half), jnp.float32)
    back_half = jnp.zeros((count, half), jnp.float32)
    for member in range(members):
        lifted = (normed * norm_gain[member][None, :]).astype(jnp.bfloat16)
        up_full = lax.all_gather(up_proj[member], "row", axis=0, tiled=True)
        hidden = jnp.dot(lifted, up_full, preferred_element_type=jnp.float32)
        act = gelu_tanh(hidden).astype(jnp.bfloat16)
        piece = lax.all_gather(down_proj[member], "row", axis=0, tiled=True)
        block = lax.dot_general(
            act, piece, (((1,), (1,)), ((), ())), preferred_element_type=jnp.float32
        )
        grads = jnp.dot(flat_g, piece, preferred_element_type=jnp.float32)
        pre_grad = (grads * gelu_slope(hidden)).astype(jnp.bfloat16)
        in_grad = lax.dot_general(
            pre_grad, up_full, (((1,), (1,)), ((), ())), preferred_element_type=jnp.float32
        )
        weight_col = chosen_tok[:, member : member + 1]
        out_term = weight_col * block
        back_term = weight_col * norm_gain[member][None, :] * in_grad
        out_part, back_part = (
            lax.psum_scatter(
                out_term.astype(jnp.bfloat16), "feat", scatter_dimension=1, tiled=True
            ).astype(jnp.float32),
            lax.psum_scatter(
                back_term.astype(jnp.bfloat16), "feat", scatter_dimension=1, tiled=True
            ).astype(jnp.float32),
        )
        out_half = out_half + out_part
        back_half = back_half + back_part
    own_x = tokens_in.reshape(count, half).astype(jnp.float32)
    normed_half = own_x * inv_rms
    stat = lax.psum(jnp.sum(normed_half * back_half, axis=1, keepdims=True), "feat") / width
    coupling = stat * math.sqrt(width)
    own_g = upstream.reshape(count, half).astype(jnp.float32)
    value_out = (own_x + out_half).astype(jnp.bfloat16)
    grad_in = (own_g + (back_half - normed_half * stat) * inv_rms).astype(jnp.bfloat16)
    return (
        value_out.reshape(rows, seq, half),
        grad_in.reshape(rows, seq, half),
        coupling.reshape(rows, seq),
    )


VMEM_LIMIT = 56 * 1024 * 1024
BF16 = jnp.bfloat16
F32 = jnp.float32


def prep_kernel(perm_ref, sorted_ref, x_ref, g_ref, gain_ref, lifted_ref, gs_ref):
    def row(p, carry):
        x = x_ref[perm_ref[p]].astype(F32)
        inv = 1.0 / jnp.sqrt(jnp.mean(x * x, axis=1, keepdims=True) + 1e-06)
        gain = gain_ref[pl.ds(sorted_ref[p], 1), :]
        lifted_ref[p] = ((x * inv) * gain).astype(BF16)
        gs_ref[p] = g_ref[perm_ref[p]]
        return carry

    lax.fori_loop(0, x_ref.shape[0], row, 0)


def prep(perm, member_sorted, x_pair, g_pair, gain):
    smem = pl.BlockSpec(memory_space=pltpu.SMEM)
    vmem = pl.BlockSpec(memory_space=pltpu.VMEM)
    return pl.pallas_call(
        prep_kernel,
        in_specs=[smem, smem, vmem, vmem, vmem],
        out_specs=[vmem, vmem],
        out_shape=[jax.ShapeDtypeStruct(x_pair.shape, BF16)] * 2,
        compiler_params=pltpu.CompilerParams(vmem_limit_bytes=VMEM_LIMIT),
        name="prep",
    )(perm, member_sorted, x_pair, g_pair, gain)


def chunk_kernel(
    member, per_block, seq, kind, units,
    low_ref, high_ref, sorted_ref, place_ref, perm_ref, dest_ref, lifted_ref, g_ref, *refs,
):
    first, opens, last = kind
    parts = len(units)
    pieces, refs = refs[: 4 * parts], refs[4 * parts :]
    if first:
        *outs, weights_ref, sems = refs
    else:
        out_in, back_in, *outs, weights_ref, sems = refs
    out_ref, back_ref = outs[:2]
    j = pl.program_id(0)
    lines, _, depth2, hidden_units = weights_ref.shape
    depth = depth2 // 2
    at = j if last else low_ref[member] + j
    inside = jnp.logical_and(at >= low_ref[member], at <= high_ref[member])

    @pl.when(j == 0)
    def _():
        y, z = place_ref[0], place_ref[1]
        copies = []

        def put(src, to_z, to_y, cols):
            copies.append(
                pltpu.make_async_copy(
                    src, weights_ref.at[to_z, to_y, :, cols], sems.at[len(copies)]
                )
            )

        for part in range(parts):
            cols = pl.ds(sum(units[:part]), units[part])
            own, own_y, here, there = (
                (ref, pl.ds(start, units[part])) for ref, start in pieces[4 * part : 4 * part + 4]
            )
            put(own[0].at[member, :, own[1]], z, y, cols)
            put(own_y[0].at[:, own_y[1]], z, 1 - y, cols)
            for d in range(1, lines):
                from_z = lax.rem(z + lines - d, lines)
                put(here[0].at[d - 1, :, here[1]], from_z, y, cols)
                put(there[0].at[d - 1, :, there[1]], from_z, 1 - y, cols)
        for copy in copies:
            copy.start()
        for copy in copies:
            copy.wait()

    def sums():
        width = lifted_ref.shape[1]
        lifted = lifted_ref[...]
        g = g_ref[...]
        weight = jnp.concatenate(
            [
                jnp.full((seq, 1), (sorted_ref[at * per_block + i] == member).astype(F32), F32)
                for i in range(per_block)
            ],
            axis=0,
        )
        out_sum = jnp.zeros(lifted.shape, F32)
        back_sum = jnp.zeros(lifted.shape, F32)
        bounds = list(range(0, hidden_units, 512)) + [hidden_units]
        for s, e in zip(bounds[:-1], bounds[1:]):
            up = weights_ref[:, :, :depth, s:e].reshape(width, e - s)
            down = weights_ref[:, :, depth:, s:e].reshape(width, e - s)
            v = jnp.dot(lifted, up, preferred_element_type=F32)
            grads = jnp.dot(g, down, preferred_element_type=F32)
            square = v * v
            t = jnp.tanh(coef_c * (v + 0.044715 * square * v))
            act = (0.5 * v * (1.0 + t)).astype(BF16)
            slope = 0.5 * (1.0 + t) + 0.5 * v * (1.0 - t * t) * coef_c * (
                1.0 + 3.0 * 0.044715 * square
            )
            pre = (grads * slope).astype(BF16)
            dims = (((1,), (1,)), ((), ()))
            out_sum += lax.dot_general(act, down, dims, preferred_element_type=F32)
            back_sum += lax.dot_general(pre, up, dims, preferred_element_type=F32)
        return weight * out_sum, weight * back_sum

    def old_sums():
        if first:
            return 0.0, 0.0
        if opens:
            old = sorted_ref[at * per_block] < member
            return jnp.where(old, out_in[...], 0.0), jnp.where(old, back_in[...], 0.0)
        return out_in[...], back_in[...]

    if last:
        rows = out_ref.shape[0]

        def store(i, value):
            for p in range(per_block):
                row = perm_ref[at * per_block + p]
                to = dest_ref[row]
                tokens = value[p * seq : (p + 1) * seq]

                @pl.when(row < rows)
                def _():
                    outs[i][to] = tokens

                low_row = rows
                for packed_ref in outs[2:]:
                    high_row = low_row + packed_ref.shape[1]

                    @pl.when(jnp.logical_and(row >= low_row, row < high_row))
                    def _():
                        packed_ref[i, to] = tokens.astype(BF16)

                    low_row = high_row

        @pl.when(inside)
        def _():
            out_sum, back_sum = sums()
            out_old, back_old = old_sums()
            store(0, out_old + out_sum)
            store(1, back_old + back_sum)

        @pl.when(jnp.logical_not(inside))
        def _():
            store(0, out_in[...])
            store(1, back_in[...])

        return

    if not first:

        @pl.when(jnp.logical_and(j == 0, high_ref[member] < low_ref[member]))
        def _():
            out_ref[...] = out_in[...]
            back_ref[...] = back_in[...]

    @pl.when(inside)
    def _():
        out_sum, back_sum = sums()
        out_old, back_old = old_sums()
        out_ref[...] = out_old + out_sum
        back_ref[...] = back_old + back_sum


def chunk(member, kind, per_block, scalars, lifted, g, pieces, sums, splits=None):
    first, _, last = kind
    rows, seq, width = lifted.shape
    tokens = rows * seq
    units = [part[0] for part in pieces]
    lines = pieces[0][3][0].shape[0] + 1
    depth2 = pieces[0][3][0].shape[1]
    hidden = sum(units)
    size = per_block * seq

    def block(j, low, high, *_):
        if last:
            return j, 0
        return jnp.maximum(jnp.minimum(low[member] + j, high[member]), 0), 0

    tok = pl.BlockSpec((size, width), block)
    hbm = pl.BlockSpec(memory_space=pl.ANY)
    args = [*scalars, lifted.reshape(tokens, width), g.reshape(tokens, width)]
    starts = []
    for _, *four in pieces:
        args += [array for array, _ in four]
        starts += [start for _, start in four]
    specs = [tok, tok] + [hbm] * (4 * len(pieces))
    alias = {}
    out_specs = [tok, tok]
    out_shape = [jax.ShapeDtypeStruct((tokens, width), F32)] * 2
    if not first:
        alias = {len(args): 0, len(args) + 1: 1}
        args += [a.reshape(tokens, width) for a in sums]
        specs += [tok, tok]
    if last:
        alias = {}
        out_shape = [jax.ShapeDtypeStruct((splits[0], seq, width), F32)] * 2
        out_shape += [jax.ShapeDtypeStruct((2, n, seq, width), BF16) for n in splits[1:]]
        out_specs = [
            pl.BlockSpec(a.shape, lambda *_, n=len(a.shape): (0,) * n) for a in out_shape
        ]

    def kernel(*refs):
        refs = list(refs)
        base = len(scalars) + 2
        for i, start in enumerate(starts):
            refs[base + i] = (refs[base + i], start)
        chunk_kernel(member, per_block, seq, kind, units, *refs)

    return pl.pallas_call(
        kernel,
        grid_spec=pltpu.PrefetchScalarGridSpec(
            num_scalar_prefetch=len(scalars),
            grid=(tokens // size,),
            in_specs=specs,
            out_specs=out_specs,
            scratch_shapes=[
                pltpu.VMEM((lines, 2, depth2, hidden), BF16),
                pltpu.SemaphoreType.DMA((len(pieces) * 2 * lines,)),
            ],
        ),
        out_shape=out_shape,
        input_output_aliases=alias,
        compiler_params=pltpu.CompilerParams(vmem_limit_bytes=VMEM_LIMIT),
        cost_estimate=pl.CostEstimate(
            flops=8 * tokens * width * hidden * 2 // 3,
            bytes_accessed=4 * width * hidden + 20 * lifted.size,
            transcendentals=tokens * hidden,
        ),
        name="chunk",
    )(*args)


def finish_kernel(
    member_ref, x_ref, g_ref, gain_ref, out_ref, back_ref, other_ref, across_out_ref,
    across_back_ref, value_ref, grad_ref, coupling_ref,
):
    rows, seq, width = x_ref.shape
    diagonal = lax.broadcasted_iota(jnp.int32, (seq, seq), 0) == lax.broadcasted_iota(
        jnp.int32, (seq, seq), 1
    )
    for r in range(rows):
        x = x_ref[r].astype(F32)
        inv = 1.0 / jnp.sqrt(jnp.mean(x * x, axis=1, keepdims=True) + 1e-06)
        normed = x * inv
        gain = gain_ref[pl.ds(member_ref[pl.program_id(0) * rows + r], 1), :]
        back = gain * (
            back_ref[r] + other_ref[1, r].astype(F32) + across_back_ref[r].astype(F32)
        )
        stat = jnp.sum(normed * back, axis=1, keepdims=True) / width
        out = out_ref[r] + other_ref[0, r].astype(F32) + across_out_ref[r].astype(F32)
        value_ref[r] = (x + out).astype(BF16)
        grad_ref[r] = (g_ref[r].astype(F32) + (back - normed * stat) * inv).astype(BF16)
        line = jnp.sum(jnp.where(diagonal, stat, 0.0), axis=0, keepdims=True)
        coupling_ref[pl.ds(pl.program_id(0) * rows + r, 1), :] = line * math.sqrt(width)


def finish(member_own, x, g, gain, out, back, other, across_out, across_back):
    rows, seq, width = x.shape
    step = math.gcd(rows, 2)
    row = pl.BlockSpec((step, seq, width), lambda r, mem: (r, 0, 0))
    two = pl.BlockSpec((2, step, seq, width), lambda r, mem: (0, r, 0, 0))
    return pl.pallas_call(
        finish_kernel,
        grid_spec=pltpu.PrefetchScalarGridSpec(
            num_scalar_prefetch=1,
            grid=(rows // step,),
            in_specs=[
                row, row, pl.BlockSpec(gain.shape, lambda r, mem: (0, 0)), row, row, two, row, row
            ],
            out_specs=[row, row, pl.BlockSpec((rows, seq), lambda r, mem: (0, 0))],
        ),
        out_shape=[
            jax.ShapeDtypeStruct((rows, seq, width), BF16),
            jax.ShapeDtypeStruct((rows, seq, width), BF16),
            jax.ShapeDtypeStruct((rows, seq), F32),
        ],
        compiler_params=pltpu.CompilerParams(vmem_limit_bytes=VMEM_LIMIT),
        name="finish",
    )(member_own, x, g, gain, out, back, other, across_out, across_back)


def sort_rows(picks, members, per_block):
    n = picks.shape[0]
    index = jnp.arange(n, dtype=jnp.int32)
    before = (picks[None, :] < picks[:, None]) | (
        (picks[None, :] == picks[:, None]) & (index[None, :] < index[:, None])
    )
    pos = jnp.sum(before.astype(jnp.int32), axis=1)
    at = pos[None, :] == index[:, None]
    perm = jnp.sum(jnp.where(at, index[None, :], 0), axis=1)
    member_sorted = jnp.sum(jnp.where(at, picks[None, :], 0), axis=1)
    labels = jnp.arange(members, dtype=jnp.int32)[:, None]
    start = jnp.sum((picks[None, :] < labels).astype(jnp.int32), axis=1)
    end = jnp.sum((picks[None, :] <= labels).astype(jnp.int32), axis=1)
    low = jnp.minimum(start, n - 1) // per_block
    high = jnp.where(end > start, (end - 1) // per_block, low - 1)
    return pos, perm, member_sorted, low, high


def on_device_shared(ranks, tokens_in, upstream, member_pick, norm_gain, up_proj, down_proj):
    rows, seq, width = tokens_in.shape
    members, depth, hidden = up_proj.shape
    rank = lax.axis_index("row")
    core = lax.rem(rank, 2)
    x_at = lax.axis_index("grp")
    y_at = lax.rem(rank // 2, 2)
    lines = ranks // 4

    def partner(a):
        return lax.ppermute(a, "row", [(i, i ^ 1) for i in range(ranks)])

    def over_y(a):
        return lax.ppermute(a, "row", [(i, i ^ 2) for i in range(ranks)])

    def over_x(a):
        return lax.ppermute(a, "grp", [(0, 1), (1, 0)])

    def shift_z(a, d):
        return lax.ppermute(a, "row", [(i, (i + 4 * d) % ranks) for i in range(ranks)])

    def after(a, *others):
        return lax.optimization_barrier((a, *others))[0]

    quarter = 3 * hidden // 16
    half = hidden // 8
    both = jnp.stack([up_proj, down_proj], axis=1)

    def units_of(c):
        return jnp.concatenate(
            [
                lax.dynamic_slice_in_dim(both, (2 * x_at + c) * quarter, quarter, 3),
                lax.dynamic_slice_in_dim(both, 4 * quarter + c * half, half, 3),
            ],
            axis=3,
        )

    mine = units_of(core)
    theirs = partner(units_of(1 - core))
    even = core == 0
    shard = jnp.concatenate(
        [jnp.where(even, mine, theirs), jnp.where(even, theirs, mine)], axis=2
    ).reshape(members, 4 * depth, quarter + half)

    third = quarter // 3
    groups = [
        [(0, 0, third)],
        [(0, third, 2 * third)],
        [(1, 0, 2 * third)],
        [(1, 2 * third, third), (0, quarter, half // 2)],
        [(0, quarter + half // 2, half // 2), (1, quarter, half // 2)],
        [(1, quarter + half // 2, half // 2)],
    ]
    send = [
        jnp.concatenate([shard[m, :, at : at + n] for m, at, n in group], axis=1)
        for group in groups
    ]
    here, there, own_y = [], [], []

    def exchange(step, arrived):
        results = []
        if step < len(groups):
            mine = after(send[step], *arrived)
            results += [shift_z(mine, d) for d in range(1, lines)]
        if step > 0:
            there.append(over_y(after(here[step - 1], *arrived)))
            results.append(there[-1])
        if step < len(groups):
            here.append(jnp.stack(results[: lines - 1]))
        return results

    def piece(group, i):
        member, start, units = groups[group][i]
        at = sum(n for _, _, n in groups[group][:i])
        return (
            units, (shard, start), (own_y[member], start), (here[group], at), (there[group], at)
        )

    pick_own = member_pick[:, 0]
    pick_over = over_x(pick_own)
    pick_pair = jnp.concatenate([pick_own, partner(pick_own)])
    pick_all = jnp.concatenate([pick_pair, pick_over, partner(pick_over)])
    per_block = math.gcd(2 * rows, 4)
    place = jnp.stack([y_at, rank // 4])
    index = jnp.arange(4 * rows, dtype=jnp.int32)
    pos, perm, member_sorted, low, high = sort_rows(pick_pair, members, per_block)
    scalars_alone = (low, high, member_sorted, place, perm, lax.rem(index[: 2 * rows], rows))
    _, perm_all, member_sorted_all, low, high = sort_rows(pick_all, members, per_block)
    dest = jnp.concatenate([pos, lax.rem(index[2 * rows :], rows)])
    scalars_shared = (low, high, member_sorted_all, place, perm_all, dest)

    arrived = exchange(0, [])
    own_y.append(over_y(shard[0]))
    x_over, x_partner, g_partner = over_x(tokens_in), partner(tokens_in), partner(upstream)
    arrived += [own_y[0], x_over, x_partner, g_partner]

    set_0, arrived = arrived, exchange(1, arrived)
    g_over, x_other = over_x(after(upstream, *set_0)), partner(after(x_over, *set_0))
    arrived += [g_over, x_other]

    set_1, arrived = arrived, exchange(2, arrived)
    own_y.append(over_y(after(shard[1], *set_1)))
    g_other = partner(after(g_over, *set_1))
    arrived += [own_y[1], g_other]

    set_2, arrived = arrived, exchange(3, arrived)
    x_all = jnp.concatenate([tokens_in, x_partner, x_over, after(x_other, *set_2)])
    g_all = jnp.concatenate([upstream, g_partner, g_over, g_other])
    lifted_shared, g_shared = prep(perm_all, member_sorted_all, x_all, g_all, norm_gain)
    sums = chunk(
        0, (True, False, False), per_block, scalars_shared, lifted_shared, g_shared,
        [piece(0, 0), piece(1, 0)], None,
    )
    arrived += [sums[0]]

    set_3, arrived = arrived, exchange(4, arrived)
    x_pair = jnp.concatenate([tokens_in, after(x_partner, *set_3)])
    g_pair = jnp.concatenate([upstream, g_partner])
    lifted_alone, g_alone = prep(perm, member_sorted, x_pair, g_pair, norm_gain)
    arrived += [lifted_alone]

    set_4, arrived = arrived, exchange(5, arrived)
    out, back, over_same, over_other = chunk(
        1, (False, True, True), per_block, scalars_shared, lifted_shared, g_shared,
        [piece(2, 0), piece(3, 0)], (after(sums[0], *set_4), sums[1]), (2 * rows, rows, rows),
    )

    exchange(6, arrived)
    across = (over_same.astype(F32) + partner(over_other).astype(F32)).astype(BF16)
    across_out = over_x(across[0])
    across_back = over_x(after(across[1], across_out))
    sums = chunk(
        0, (False, False, False), per_block, scalars_alone, lifted_alone, g_alone,
        [piece(3, 1), piece(4, 0)], (after(out, across), back),
    )
    out, back, packed = chunk(
        1, (False, False, True), per_block, scalars_alone, lifted_alone, g_alone,
        [piece(4, 1), piece(5, 0)], (after(sums[0], across_out, across_back), sums[1]),
        (rows, rows),
    )
    return tuple(
        finish(
            pick_own, tokens_in, upstream, norm_gain, out, back, partner(packed),
            across_out, across_back,
        )
    )


def solution(mesh):
    ranks = mesh.shape["row"]
    four = mesh.shape["feat"] == 1 and ranks % 4 == 0 and mesh.shape["grp"] == 2

    def on_device(tokens_in, upstream, member_pick, norm_gain, up_proj, down_proj):
        args = (tokens_in, upstream, member_pick, norm_gain, up_proj, down_proj)
        if four and member_pick.shape[1] == 1 and up_proj.shape[0] == 2:
            return on_device_shared(ranks, *args)
        return on_device_general(*args)

    in_specs = (
        P(("grp", "row"), None, "feat"),
        P(("grp", "row"), None, "feat"),
        P(("grp", "row"), None),
        P(),
        P(None, "row", "feat"),
        P(None, "row", "feat"),
    )
    out_specs = (
        P(("grp", "row"), None, "feat"),
        P(("grp", "row"), None, "feat"),
        P(("grp", "row"), None),
    )
    return jax.shard_map(
        on_device, mesh=mesh, in_specs=in_specs, out_specs=out_specs, check_vma=False
    )
```

```python
import functools
import math

import jax
import jax.numpy as jnp
from jax import lax
from jax.experimental import pallas as pl
from jax.experimental.pallas import tpu as pltpu
from jax.sharding import PartitionSpec as P

coef_c = math.sqrt(2.0 / math.pi)


def gelu_tanh(v):
    return 0.5 * v * (1.0 + jnp.tanh(coef_c * (v + 0.044715 * v * v * v)))


def gelu_slope(v):
    inner = jnp.tanh(coef_c * (v + 0.044715 * v * v * v))
    return 0.5 * (1.0 + inner) + 0.5 * v * (1.0 - inner * inner) * coef_c * (
        1.0 + 3.0 * 0.044715 * v * v
    )


def on_device_general(tokens_in, upstream, member_pick, norm_gain, up_proj, down_proj):
    rows, seq, half = tokens_in.shape
    count = rows * seq
    members = up_proj.shape[0]
    pick = member_pick.shape[1]
    whole_x, whole_g = (
        lax.all_gather(tokens_in, "feat", axis=2, tiled=True),
        lax.all_gather(upstream, "feat", axis=2, tiled=True),
    )
    width = whole_x.shape[2]
    flat_x = whole_x.reshape(count, width).astype(jnp.float32)
    flat_g = whole_g.reshape(count, width)
    inv_rms = 1.0 / jnp.sqrt(jnp.mean(flat_x * flat_x, axis=1, keepdims=True) + 1e-06)
    normed = flat_x * inv_rms
    labels = jnp.arange(members, dtype=jnp.int32)
    chosen = (
        jnp.sum((member_pick[:, :, None] == labels[None, None, :]).astype(jnp.float32), axis=1)
        / pick
    )
    chosen_tok = jnp.repeat(chosen, seq, axis=0)
    out_half = jnp.zeros((count, half), jnp.float32)
    back_half = jnp.zeros((count, half), jnp.float32)
    for member in range(members):
        lifted = (normed * norm_gain[member][None, :]).astype(jnp.bfloat16)
        up_full = lax.all_gather(up_proj[member], "row", axis=0, tiled=True)
        hidden = jnp.dot(lifted, up_full, preferred_element_type=jnp.float32)
        act = gelu_tanh(hidden).astype(jnp.bfloat16)
        piece = lax.all_gather(down_proj[member], "row", axis=0, tiled=True)
        block = lax.dot_general(
            act, piece, (((1,), (1,)), ((), ())), preferred_element_type=jnp.float32
        )
        grads = jnp.dot(flat_g, piece, preferred_element_type=jnp.float32)
        pre_grad = (grads * gelu_slope(hidden)).astype(jnp.bfloat16)
        in_grad = lax.dot_general(
            pre_grad, up_full, (((1,), (1,)), ((), ())), preferred_element_type=jnp.float32
        )
        weight_col = chosen_tok[:, member : member + 1]
        out_term = weight_col * block
        back_term = weight_col * norm_gain[member][None, :] * in_grad
        out_part, back_part = (
            lax.psum_scatter(
                out_term.astype(jnp.bfloat16), "feat", scatter_dimension=1, tiled=True
            ).astype(jnp.float32),
            lax.psum_scatter(
                back_term.astype(jnp.bfloat16), "feat", scatter_dimension=1, tiled=True
            ).astype(jnp.float32),
        )
        out_half = out_half + out_part
        back_half = back_half + back_part
    own_x = tokens_in.reshape(count, half).astype(jnp.float32)
    normed_half = own_x * inv_rms
    stat = lax.psum(jnp.sum(normed_half * back_half, axis=1, keepdims=True), "feat") / width
    coupling = stat * math.sqrt(width)
    own_g = upstream.reshape(count, half).astype(jnp.float32)
    value_out = (own_x + out_half).astype(jnp.bfloat16)
    grad_in = (own_g + (back_half - normed_half * stat) * inv_rms).astype(jnp.bfloat16)
    return (
        value_out.reshape(rows, seq, half),
        grad_in.reshape(rows, seq, half),
        coupling.reshape(rows, seq),
    )


VMEM_LIMIT = 56 * 1024 * 1024
BF16 = jnp.bfloat16
F32 = jnp.float32


def prep_kernel(
    perm_ref, sorted_ref, near_ref, over_ref, far_ref, gain_ref, lifted_ref, g_out_ref
):
    rows = near_ref.shape[1]

    def row(p, carry):
        at = perm_ref[p]
        i = lax.rem(at, rows)

        def emit(x, g):
            x = x.astype(F32)
            inv = 1.0 / jnp.sqrt(jnp.mean(x * x, axis=1, keepdims=True) + 1e-06)
            gain = gain_ref[pl.ds(sorted_ref[p], 1), :]
            lifted_ref[p] = ((x * inv) * gain).astype(BF16)
            g_out_ref[p] = g

        for source in range(4):

            @pl.when(at // rows == source)
            def _():
                if source % 2:
                    emit(far_ref[source // 2, 0, i], far_ref[source // 2, 1, i])
                else:
                    ref = over_ref if source else near_ref
                    emit(ref[0, i], ref[1, i])

        return carry

    lax.fori_loop(0, lifted_ref.shape[0], row, 0)


def prep(perm, member_sorted, near, over, far, gain):
    smem = pl.BlockSpec(memory_space=pltpu.SMEM)
    vmem = pl.BlockSpec(memory_space=pltpu.VMEM)
    shape = (perm.shape[0], *near.shape[2:])
    return pl.pallas_call(
        prep_kernel,
        in_specs=[smem, smem, vmem, vmem, vmem, vmem],
        out_specs=[vmem, vmem],
        out_shape=[jax.ShapeDtypeStruct(shape, BF16)] * 2,
        compiler_params=pltpu.CompilerParams(vmem_limit_bytes=VMEM_LIMIT),
        cost_estimate=pl.CostEstimate(
            flops=8 * perm.shape[0] * near.shape[2] * near.shape[3],
            bytes_accessed=16 * perm.shape[0] * near.shape[2] * near.shape[3],
            transcendentals=0,
        ),
        name="prep",
    )(perm, member_sorted, near, over, far, gain)


def chunk_kernel(
    member, per_block, seq, kind, units,
    low_ref, high_ref, sorted_ref, place_ref, perm_ref, dest_ref, lifted_ref, g_ref, *refs,
):
    first, opens, last = kind
    parts = len(units)
    pieces, refs = refs[: 2 * parts], refs[2 * parts :]
    if first:
        *outs, weights_ref, sems = refs
    else:
        out_in, back_in, *outs, weights_ref, sems = refs
    out_ref, back_ref = outs[:2]
    j = pl.program_id(0)
    lines, _, depth2, hidden_units = weights_ref.shape
    depth = depth2 // 2
    at = j if last else low_ref[member] + j
    inside = jnp.logical_and(at >= low_ref[member], at <= high_ref[member])

    @pl.when(j == 0)
    def _():
        y, z = place_ref[0], place_ref[1]
        copies = []

        def put(src, to_z, to_y, cols):
            copies.append(
                pltpu.make_async_copy(
                    src, weights_ref.at[to_z, to_y, :, cols], sems.at[len(copies)]
                )
            )

        for part in range(parts):
            cols = pl.ds(sum(units[:part]), units[part])
            for to_y, (ref, start) in zip((y, 1 - y), pieces[2 * part : 2 * part + 2]):
                for d in range(lines):
                    from_z = lax.rem(z + lines - d, lines)
                    put(ref.at[d, :, pl.ds(start, units[part])], from_z, to_y, cols)
        for copy in copies:
            copy.start()
        for copy in copies:
            copy.wait()

    def sums():
        width = lifted_ref.shape[1]
        lifted = lifted_ref[...]
        g = g_ref[...]
        weight = jnp.concatenate(
            [
                jnp.full((seq, 1), (sorted_ref[at * per_block + i] == member).astype(F32), F32)
                for i in range(per_block)
            ],
            axis=0,
        )
        out_sum = jnp.zeros(lifted.shape, F32)
        back_sum = jnp.zeros(lifted.shape, F32)
        bounds = list(range(0, hidden_units, 512)) + [hidden_units]
        for s, e in zip(bounds[:-1], bounds[1:]):
            up = weights_ref[:, :, :depth, s:e].reshape(width, e - s)
            down = weights_ref[:, :, depth:, s:e].reshape(width, e - s)
            v = jnp.dot(lifted, up, preferred_element_type=F32)
            grads = jnp.dot(g, down, preferred_element_type=F32)
            square = v * v
            t = jnp.tanh(coef_c * (v + 0.044715 * square * v))
            act = (0.5 * v * (1.0 + t)).astype(BF16)
            slope = 0.5 * (1.0 + t) + 0.5 * v * (1.0 - t * t) * coef_c * (
                1.0 + 3.0 * 0.044715 * square
            )
            pre = (grads * slope).astype(BF16)
            dims = (((1,), (1,)), ((), ()))
            out_sum += lax.dot_general(act, down, dims, preferred_element_type=F32)
            back_sum += lax.dot_general(pre, up, dims, preferred_element_type=F32)
        return weight * out_sum, weight * back_sum

    def old_sums():
        if first:
            return 0.0, 0.0
        if opens:
            old = sorted_ref[at * per_block] < member
            return jnp.where(old, out_in[...], 0.0), jnp.where(old, back_in[...], 0.0)
        return out_in[...], back_in[...]

    if last:
        rows = out_ref.shape[0]

        def store(i, value):
            for p in range(per_block):
                row = perm_ref[at * per_block + p]
                to = dest_ref[row]
                tokens = value[p * seq : (p + 1) * seq]

                @pl.when(row < rows)
                def _():
                    outs[i][to] = tokens

                low_row = rows
                for packed_ref in outs[2:]:
                    high_row = low_row + packed_ref.shape[1]

                    @pl.when(jnp.logical_and(row >= low_row, row < high_row))
                    def _():
                        packed_ref[i, to] = tokens.astype(BF16)

                    low_row = high_row

        @pl.when(inside)
        def _():
            out_sum, back_sum = sums()
            out_old, back_old = old_sums()
            store(0, out_old + out_sum)
            store(1, back_old + back_sum)

        @pl.when(jnp.logical_not(inside))
        def _():
            store(0, out_in[...])
            store(1, back_in[...])

        return

    if not first:

        @pl.when(jnp.logical_and(j == 0, high_ref[member] < low_ref[member]))
        def _():
            out_ref[...] = out_in[...]
            back_ref[...] = back_in[...]

    @pl.when(inside)
    def _():
        out_sum, back_sum = sums()
        out_old, back_old = old_sums()
        out_ref[...] = out_old + out_sum
        back_ref[...] = back_old + back_sum


def chunk(member, kind, per_block, scalars, lifted, g, pieces, sums, splits=None):
    first, _, last = kind
    rows, seq, width = lifted.shape
    tokens = rows * seq
    units = [part[0] for part in pieces]
    lines, depth2, _ = pieces[0][1][0].shape
    hidden = sum(units)
    size = per_block * seq

    def block(j, low, high, *_):
        if last:
            return j, 0
        return jnp.maximum(jnp.minimum(low[member] + j, high[member]), 0), 0

    tok = pl.BlockSpec((size, width), block)
    hbm = pl.BlockSpec(memory_space=pl.ANY)
    args = [*scalars, lifted.reshape(tokens, width), g.reshape(tokens, width)]
    starts = []
    for _, *both in pieces:
        args += [array for array, _ in both]
        starts += [start for _, start in both]
    specs = [tok, tok] + [hbm] * len(starts)
    alias = {}
    out_specs = [tok, tok]
    out_shape = [jax.ShapeDtypeStruct((tokens, width), F32)] * 2
    if not first:
        alias = {len(args): 0, len(args) + 1: 1}
        args += [a.reshape(tokens, width) for a in sums]
        specs += [tok, tok]
    if last:
        alias = {}
        out_shape = [jax.ShapeDtypeStruct((splits[0], seq, width), F32)] * 2
        out_shape += [jax.ShapeDtypeStruct((2, n, seq, width), BF16) for n in splits[1:]]
        out_specs = [
            pl.BlockSpec(a.shape, lambda *_, n=len(a.shape): (0,) * n) for a in out_shape
        ]

    def kernel(*refs):
        refs = list(refs)
        base = len(scalars) + 2
        for i, start in enumerate(starts):
            refs[base + i] = (refs[base + i], start)
        chunk_kernel(member, per_block, seq, kind, units, *refs)

    return pl.pallas_call(
        kernel,
        grid_spec=pltpu.PrefetchScalarGridSpec(
            num_scalar_prefetch=len(scalars),
            grid=(tokens // size,),
            in_specs=specs,
            out_specs=out_specs,
            scratch_shapes=[
                pltpu.VMEM((lines, 2, depth2, hidden), BF16),
                pltpu.SemaphoreType.DMA((len(pieces) * 2 * lines,)),
            ],
        ),
        out_shape=out_shape,
        input_output_aliases=alias,
        compiler_params=pltpu.CompilerParams(vmem_limit_bytes=VMEM_LIMIT),
        cost_estimate=pl.CostEstimate(
            flops=8 * tokens * width * hidden * 2 // 3,
            bytes_accessed=4 * width * hidden + 20 * lifted.size,
            transcendentals=tokens * hidden,
        ),
        name="chunk",
    )(*args)


def finish_kernel(
    member_ref, x_ref, g_ref, gain_ref, out_ref, back_ref, other_ref, across_ref,
    value_ref, grad_ref, coupling_ref,
):
    rows, seq, width = x_ref.shape
    diagonal = lax.broadcasted_iota(jnp.int32, (seq, seq), 0) == lax.broadcasted_iota(
        jnp.int32, (seq, seq), 1
    )
    for r in range(rows):
        x = x_ref[r].astype(F32)
        inv = 1.0 / jnp.sqrt(jnp.mean(x * x, axis=1, keepdims=True) + 1e-06)
        normed = x * inv
        gain = gain_ref[pl.ds(member_ref[pl.program_id(0) * rows + r], 1), :]
        back = gain * (
            back_ref[r] + other_ref[1, r].astype(F32) + across_ref[1, r].astype(F32)
        )
        stat = jnp.sum(normed * back, axis=1, keepdims=True) / width
        out = out_ref[r] + other_ref[0, r].astype(F32) + across_ref[0, r].astype(F32)
        value_ref[r] = (x + out).astype(BF16)
        grad_ref[r] = (g_ref[r].astype(F32) + (back - normed * stat) * inv).astype(BF16)
        line = jnp.sum(jnp.where(diagonal, stat, 0.0), axis=0, keepdims=True)
        coupling_ref[pl.ds(pl.program_id(0) * rows + r, 1), :] = line * math.sqrt(width)


def finish(member_own, x, g, gain, out, back, other, across):
    rows, seq, width = x.shape
    step = math.gcd(rows, 2)
    row = pl.BlockSpec((step, seq, width), lambda r, mem: (r, 0, 0))
    two = pl.BlockSpec((2, step, seq, width), lambda r, mem: (0, r, 0, 0))
    return pl.pallas_call(
        finish_kernel,
        grid_spec=pltpu.PrefetchScalarGridSpec(
            num_scalar_prefetch=1,
            grid=(rows // step,),
            in_specs=[
                row, row, pl.BlockSpec(gain.shape, lambda r, mem: (0, 0)), row, row, two, two
            ],
            out_specs=[row, row, pl.BlockSpec((rows, seq), lambda r, mem: (0, 0))],
        ),
        out_shape=[
            jax.ShapeDtypeStruct((rows, seq, width), BF16),
            jax.ShapeDtypeStruct((rows, seq, width), BF16),
            jax.ShapeDtypeStruct((rows, seq), F32),
        ],
        compiler_params=pltpu.CompilerParams(vmem_limit_bytes=VMEM_LIMIT),
        name="finish",
    )(member_own, x, g, gain, out, back, other, across)


def sort_rows(picks, members, per_block):
    n = picks.shape[0]
    index = jnp.arange(n, dtype=jnp.int32)
    before = (picks[None, :] < picks[:, None]) | (
        (picks[None, :] == picks[:, None]) & (index[None, :] < index[:, None])
    )
    pos = jnp.sum(before.astype(jnp.int32), axis=1)
    at = pos[None, :] == index[:, None]
    perm = jnp.sum(jnp.where(at, index[None, :], 0), axis=1)
    member_sorted = jnp.sum(jnp.where(at, picks[None, :], 0), axis=1)
    labels = jnp.arange(members, dtype=jnp.int32)[:, None]
    start = jnp.sum((picks[None, :] < labels).astype(jnp.int32), axis=1)
    end = jnp.sum((picks[None, :] <= labels).astype(jnp.int32), axis=1)
    low = jnp.minimum(start, n - 1) // per_block
    high = jnp.where(end > start, (end - 1) // per_block, low - 1)
    return pos, perm, member_sorted, low, high


def on_device_shared(ranks, tokens_in, upstream, member_pick, norm_gain, up_proj, down_proj):
    rows, seq, width = tokens_in.shape
    members, depth, hidden = up_proj.shape
    rank = lax.axis_index("row")
    core = lax.rem(rank, 2)
    x_at = lax.axis_index("grp")
    y_at = lax.rem(rank // 2, 2)
    lines = ranks // 4

    def partner(a):
        return lax.ppermute(a, "row", [(i, i ^ 1) for i in range(ranks)])

    def over_y(a):
        return lax.ppermute(a, "row", [(i, i ^ 2) for i in range(ranks)])

    def over_x(a):
        return lax.ppermute(a, "grp", [(0, 1), (1, 0)])

    def shift_z(a, d):
        return lax.ppermute(a, "row", [(i, (i + 4 * d) % ranks) for i in range(ranks)])

    def after(a, *others):
        return lax.optimization_barrier((a, *others))[0]

    quarter = hidden // 4
    both = jnp.stack([up_proj, down_proj], axis=1)

    def units_of(c):
        return lax.dynamic_slice_in_dim(both, (2 * x_at + c) * quarter, quarter, 3)

    mine = units_of(core)
    theirs = partner(units_of(1 - core))
    even = core == 0
    shard = jnp.concatenate(
        [jnp.where(even, mine, theirs), jnp.where(even, theirs, mine)], axis=2
    ).reshape(members, 4 * depth, quarter)

    unit = quarter // 4
    groups = [
        [(0, 0, unit)],
        [(0, unit, 2 * unit)],
        [(0, 3 * unit, unit), (1, 0, unit)],
        [(1, unit, 2 * unit)],
        [(1, 3 * unit, unit)],
    ]
    send = [
        jnp.concatenate([shard[m, :, at : at + n] for m, at, n in group], axis=1)
        for group in groups
    ]
    here, there = [], []

    def exchange(step, arrived):
        results = []
        if step < len(groups):
            mine = after(send[step], *arrived)
            results += [shift_z(mine, d) for d in range(1, lines)]
        if step > 0:
            there.append(over_y(after(here[step - 1], *arrived)))
            results.append(there[-1])
        if step < len(groups):
            here.append(jnp.stack([send[step], *results[: lines - 1]]))
        return results

    def piece(group, i):
        at = sum(n for _, _, n in groups[group][:i])
        return groups[group][i][2], (here[group], at), (there[group], at)

    pick_own = member_pick[:, 0]
    pick_near = jnp.concatenate([pick_own, over_x(pick_own)])
    pick_far = partner(pick_near)
    pick_pair = jnp.concatenate([pick_own, pick_far[:rows]])
    pick_all = jnp.concatenate([pick_pair, pick_near[rows:], pick_far[rows:]])
    per_block = math.gcd(2 * rows, 4)
    place = jnp.stack([y_at, rank // 4])
    index = jnp.arange(4 * rows, dtype=jnp.int32)
    _, perm, member_sorted, low, high = sort_rows(pick_all, members, per_block)
    scalars = (low, high, member_sorted, place, perm, lax.rem(index, rows))

    near = jnp.stack([tokens_in, upstream])
    over = over_x(near)
    arrived = exchange(0, [])

    arrived = exchange(1, arrived)
    arrived += [over]

    set_1, arrived = arrived, exchange(2, arrived)
    far = partner(after(jnp.stack([near, over]), *set_1))
    arrived += [far]

    set_2, arrived = arrived, exchange(3, arrived)
    lifted, g_sorted = prep(
        perm, member_sorted, near, over, after(far, *set_2), norm_gain
    )
    arrived += [lifted]

    set_3, arrived = arrived, exchange(4, arrived)
    sums = chunk(
        0, (True, False, False), per_block, scalars, after(lifted, *set_3), g_sorted,
        [piece(0, 0), piece(1, 0), piece(2, 0)], None,
    )
    arrived += [sums[0]]

    set_4, arrived = arrived, exchange(5, arrived)
    sums = chunk(
        1, (False, True, False), per_block, scalars, lifted, g_sorted,
        [piece(2, 1), piece(3, 0)], (after(sums[0], *set_4), sums[1]),
    )
    out, back, packed, over_same, over_other = chunk(
        1, (False, False, True), per_block, scalars, lifted, g_sorted, [piece(4, 0)], sums,
        (rows, rows, rows, rows),
    )
    across = over_x((over_same.astype(F32) + partner(over_other).astype(F32)).astype(BF16))
    return tuple(
        finish(
            pick_own, tokens_in, upstream, norm_gain, out, back, partner(packed), across
        )
    )


def solution(mesh):
    ranks = mesh.shape["row"]
    four = mesh.shape["feat"] == 1 and ranks % 4 == 0 and mesh.shape["grp"] == 2

    def on_device(tokens_in, upstream, member_pick, norm_gain, up_proj, down_proj):
        args = (tokens_in, upstream, member_pick, norm_gain, up_proj, down_proj)
        if four and member_pick.shape[1] == 1 and up_proj.shape[0] == 2:
            return on_device_shared(ranks, *args)
        return on_device_general(*args)

    in_specs = (
        P(("grp", "row"), None, "feat"),
        P(("grp", "row"), None, "feat"),
        P(("grp", "row"), None),
        P(),
        P(None, "row", "feat"),
        P(None, "row", "feat"),
    )
    out_specs = (
        P(("grp", "row"), None, "feat"),
        P(("grp", "row"), None, "feat"),
        P(("grp", "row"), None),
    )
    return jax.shard_map(
        on_device, mesh=mesh, in_specs=in_specs, out_specs=out_specs, check_vma=False
    )
```

```python
import functools
import math

import jax
import jax.numpy as jnp
from jax import lax
from jax.experimental import pallas as pl
from jax.experimental.pallas import tpu as pltpu
from jax.sharding import PartitionSpec as P

coef_c = math.sqrt(2.0 / math.pi)


def gelu_tanh(v):
    return 0.5 * v * (1.0 + jnp.tanh(coef_c * (v + 0.044715 * v * v * v)))


def gelu_slope(v):
    inner = jnp.tanh(coef_c * (v + 0.044715 * v * v * v))
    return 0.5 * (1.0 + inner) + 0.5 * v * (1.0 - inner * inner) * coef_c * (
        1.0 + 3.0 * 0.044715 * v * v
    )


def on_device_general(tokens_in, upstream, member_pick, norm_gain, up_proj, down_proj):
    rows, seq, half = tokens_in.shape
    count = rows * seq
    members = up_proj.shape[0]
    pick = member_pick.shape[1]
    whole_x, whole_g = (
        lax.all_gather(tokens_in, "feat", axis=2, tiled=True),
        lax.all_gather(upstream, "feat", axis=2, tiled=True),
    )
    width = whole_x.shape[2]
    flat_x = whole_x.reshape(count, width).astype(jnp.float32)
    flat_g = whole_g.reshape(count, width)
    inv_rms = 1.0 / jnp.sqrt(jnp.mean(flat_x * flat_x, axis=1, keepdims=True) + 1e-06)
    normed = flat_x * inv_rms
    labels = jnp.arange(members, dtype=jnp.int32)
    chosen = (
        jnp.sum((member_pick[:, :, None] == labels[None, None, :]).astype(jnp.float32), axis=1)
        / pick
    )
    chosen_tok = jnp.repeat(chosen, seq, axis=0)
    out_half = jnp.zeros((count, half), jnp.float32)
    back_half = jnp.zeros((count, half), jnp.float32)
    for member in range(members):
        lifted = (normed * norm_gain[member][None, :]).astype(jnp.bfloat16)
        up_full = lax.all_gather(up_proj[member], "row", axis=0, tiled=True)
        hidden = jnp.dot(lifted, up_full, preferred_element_type=jnp.float32)
        act = gelu_tanh(hidden).astype(jnp.bfloat16)
        piece = lax.all_gather(down_proj[member], "row", axis=0, tiled=True)
        block = lax.dot_general(
            act, piece, (((1,), (1,)), ((), ())), preferred_element_type=jnp.float32
        )
        grads = jnp.dot(flat_g, piece, preferred_element_type=jnp.float32)
        pre_grad = (grads * gelu_slope(hidden)).astype(jnp.bfloat16)
        in_grad = lax.dot_general(
            pre_grad, up_full, (((1,), (1,)), ((), ())), preferred_element_type=jnp.float32
        )
        weight_col = chosen_tok[:, member : member + 1]
        out_term = weight_col * block
        back_term = weight_col * norm_gain[member][None, :] * in_grad
        out_part, back_part = (
            lax.psum_scatter(
                out_term.astype(jnp.bfloat16), "feat", scatter_dimension=1, tiled=True
            ).astype(jnp.float32),
            lax.psum_scatter(
                back_term.astype(jnp.bfloat16), "feat", scatter_dimension=1, tiled=True
            ).astype(jnp.float32),
        )
        out_half = out_half + out_part
        back_half = back_half + back_part
    own_x = tokens_in.reshape(count, half).astype(jnp.float32)
    normed_half = own_x * inv_rms
    stat = lax.psum(jnp.sum(normed_half * back_half, axis=1, keepdims=True), "feat") / width
    coupling = stat * math.sqrt(width)
    own_g = upstream.reshape(count, half).astype(jnp.float32)
    value_out = (own_x + out_half).astype(jnp.bfloat16)
    grad_in = (own_g + (back_half - normed_half * stat) * inv_rms).astype(jnp.bfloat16)
    return (
        value_out.reshape(rows, seq, half),
        grad_in.reshape(rows, seq, half),
        coupling.reshape(rows, seq),
    )


VMEM_LIMIT = 56 * 1024 * 1024
BF16 = jnp.bfloat16
F32 = jnp.float32


def prep_kernel(perm_ref, sorted_ref, near_ref, far_ref, gain_ref, lifted_ref, g_out_ref):
    rows = near_ref.shape[1]

    def row(p, carry):
        at = perm_ref[p]
        i = lax.rem(at, rows)

        def emit(ref):
            x = ref[0, i].astype(F32)
            inv = 1.0 / jnp.sqrt(jnp.mean(x * x, axis=1, keepdims=True) + 1e-06)
            gain = gain_ref[pl.ds(sorted_ref[p], 1), :]
            lifted_ref[p] = ((x * inv) * gain).astype(BF16)
            g_out_ref[p] = ref[1, i]

        @pl.when(at < rows)
        def _():
            emit(near_ref)

        @pl.when(at >= rows)
        def _():
            emit(far_ref)

        return carry

    lax.fori_loop(0, lifted_ref.shape[0], row, 0)


def prep(perm, member_sorted, near, far, gain):
    smem = pl.BlockSpec(memory_space=pltpu.SMEM)
    vmem = pl.BlockSpec(memory_space=pltpu.VMEM)
    shape = (perm.shape[0], *near.shape[2:])
    return pl.pallas_call(
        prep_kernel,
        in_specs=[smem, smem, vmem, vmem, vmem],
        out_specs=[vmem, vmem],
        out_shape=[jax.ShapeDtypeStruct(shape, BF16)] * 2,
        compiler_params=pltpu.CompilerParams(vmem_limit_bytes=VMEM_LIMIT),
        cost_estimate=pl.CostEstimate(
            flops=8 * perm.shape[0] * near.shape[2] * near.shape[3],
            bytes_accessed=16 * perm.shape[0] * near.shape[2] * near.shape[3],
            transcendentals=0,
        ),
        name="prep",
    )(perm, member_sorted, near, far, gain)


def chunk_kernel(
    per_block, kind, units, sorted_ref, place_ref, perm_ref, lifted_ref, g_ref, *refs
):
    first, last = kind
    parts = len(units)
    pieces, refs = refs[: 2 * parts], refs[2 * parts :]
    if first:
        *outs, weights_ref, sems = refs
    elif last:
        out_in, back_in, *outs, weights_ref, sems, out_acc, back_acc = refs
    else:
        out_in, back_in, *outs, weights_ref, sems = refs
    if not last:
        out_acc, back_acc = outs
    j = pl.program_id(0)
    lines, _, depth2, _ = weights_ref.shape
    depth = depth2 // 2
    starts = [sum(n for _, n in units[:part]) for part in range(parts)]

    @pl.when(j == 0)
    def _():
        y, z = place_ref[0], place_ref[1]
        copies = []
        for part in range(parts):
            n = units[part][1]
            for to_y, (ref, start) in zip((y, 1 - y), pieces[2 * part : 2 * part + 2]):
                for d in range(lines):
                    from_z = lax.rem(z + lines - d, lines)
                    copies.append(
                        pltpu.make_async_copy(
                            ref.at[d, :, pl.ds(start, n)],
                            weights_ref.at[from_z, to_y, :, pl.ds(starts[part], n)],
                            sems.at[len(copies)],
                        )
                    )
        for copy in copies:
            copy.start()
        for copy in copies:
            copy.wait()

    width = lifted_ref.shape[1]
    seq = lifted_ref.shape[0] // per_block
    here = [sorted_ref[j * per_block + i] for i in range(per_block)]
    if first:
        out_acc[...] = jnp.zeros(out_acc.shape, F32)
        back_acc[...] = jnp.zeros(back_acc.shape, F32)
    else:
        out_acc[...] = out_in[...]
        back_acc[...] = back_in[...]

    for member in sorted(set(m for m, _ in units)):
        used = functools.reduce(jnp.logical_or, [m == member for m in here])

        @pl.when(used)
        def _():
            lifted = lifted_ref[...]
            g = g_ref[...]
            weight = jnp.concatenate(
                [jnp.full((seq, 1), (m == member).astype(F32), F32) for m in here], axis=0
            )
            out_sum = jnp.zeros(lifted.shape, F32)
            back_sum = jnp.zeros(lifted.shape, F32)
            spans = []
            for (m, n), start in zip(units, starts):
                if m == member:
                    spans += [(s, min(s + 512, start + n)) for s in range(start, start + n, 512)]
            for s, e in spans:
                up = weights_ref[:, :, :depth, s:e].reshape(width, e - s)
                down = weights_ref[:, :, depth:, s:e].reshape(width, e - s)
                v = jnp.dot(lifted, up, preferred_element_type=F32)
                grads = jnp.dot(g, down, preferred_element_type=F32)
                square = v * v
                t = jnp.tanh(coef_c * (v + 0.044715 * square * v))
                act = (0.5 * v * (1.0 + t)).astype(BF16)
                slope = 0.5 * (1.0 + t) + 0.5 * v * (1.0 - t * t) * coef_c * (
                    1.0 + 3.0 * 0.044715 * square
                )
                pre = (grads * slope).astype(BF16)
                dims = (((1,), (1,)), ((), ()))
                out_sum += lax.dot_general(act, down, dims, preferred_element_type=F32)
                back_sum += lax.dot_general(pre, up, dims, preferred_element_type=F32)
            out_acc[...] += weight * out_sum
            back_acc[...] += weight * back_sum

    if last:
        for p in range(per_block):
            row = perm_ref[j * per_block + p]
            tokens = pl.ds(p * seq, seq)
            low = 0
            for to_out, to_back in zip(outs[::2], outs[1::2]):
                n = to_out.shape[0]

                @pl.when(jnp.logical_and(row >= low, row < low + n))
                def _():
                    to = jnp.clip(row - low, 0, n - 1)
                    to_out[to] = out_acc[tokens, :].astype(to_out.dtype)
                    to_back[to] = back_acc[tokens, :].astype(to_back.dtype)

                low += n


def chunk(kind, per_block, scalars, lifted, g, pieces, sums, outs=None, weight=1):
    first, last = kind
    rows, seq, width = lifted.shape
    tokens = rows * seq
    units = [(member, n) for member, n, *_ in pieces]
    lines, depth2, _ = pieces[0][2][0].shape
    hidden = sum(n for _, n in units)
    size = per_block * seq

    tok = pl.BlockSpec((size, width), lambda j, *_: (j, 0))
    hbm = pl.BlockSpec(memory_space=pl.ANY)
    args = [*scalars, lifted.reshape(tokens, width), g.reshape(tokens, width)]
    starts = []
    for _, _, *both in pieces:
        args += [array for array, _ in both]
        starts += [start for _, start in both]
    specs = [tok, tok] + [hbm] * len(starts)
    alias = {}
    out_specs = [tok, tok]
    out_shape = [jax.ShapeDtypeStruct((tokens, width), F32)] * 2
    scratch = [
        pltpu.VMEM((lines, 2, depth2, hidden), BF16),
        pltpu.SemaphoreType.DMA((len(pieces) * 2 * lines,)),
    ]
    if not first:
        alias = {len(args): 0, len(args) + 1: 1}
        args += list(sums)
        specs += [tok, tok]
    if last:
        alias = {}
        shape = (rows // len(outs), seq, width)
        out_shape = [jax.ShapeDtypeStruct(shape, dtype) for dtype in outs for _ in range(2)]
        out_specs = [pl.BlockSpec(shape, lambda *_: (0, 0, 0))] * len(out_shape)
        scratch += [pltpu.VMEM((size, width), F32)] * 2

    def kernel(*refs):
        refs = list(refs)
        base = len(scalars) + 2
        for i, start in enumerate(starts):
            refs[base + i] = (refs[base + i], start)
        chunk_kernel(per_block, kind, units, *refs)

    return pl.pallas_call(
        kernel,
        grid_spec=pltpu.PrefetchScalarGridSpec(
            num_scalar_prefetch=len(scalars),
            grid=(tokens // size,),
            in_specs=specs,
            out_specs=out_specs,
            scratch_shapes=scratch,
        ),
        out_shape=out_shape,
        input_output_aliases=alias,
        compiler_params=pltpu.CompilerParams(vmem_limit_bytes=VMEM_LIMIT),
        cost_estimate=pl.CostEstimate(
            flops=weight * 8 * tokens * width * hidden * 2 // 3,
            bytes_accessed=weight * (4 * width * hidden + 20 * lifted.size),
            transcendentals=weight * tokens * hidden,
        ),
        name="chunk",
    )(*args)


def finish_kernel(
    member_ref, x_ref, g_ref, gain_ref, out_ref, back_ref, other_out_ref, other_back_ref,
    across_ref, value_ref, grad_ref, coupling_ref,
):
    rows, seq, width = x_ref.shape
    diagonal = lax.broadcasted_iota(jnp.int32, (seq, seq), 0) == lax.broadcasted_iota(
        jnp.int32, (seq, seq), 1
    )
    for r in range(rows):
        x = x_ref[r].astype(F32)
        inv = 1.0 / jnp.sqrt(jnp.mean(x * x, axis=1, keepdims=True) + 1e-06)
        normed = x * inv
        gain = gain_ref[pl.ds(member_ref[pl.program_id(0) * rows + r], 1), :]
        back = gain * (
            back_ref[r] + other_back_ref[r].astype(F32) + across_ref[1, r].astype(F32)
        )
        stat = jnp.sum(normed * back, axis=1, keepdims=True) / width
        out = out_ref[r] + other_out_ref[r].astype(F32) + across_ref[0, r].astype(F32)
        value_ref[r] = (x + out).astype(BF16)
        grad_ref[r] = (g_ref[r].astype(F32) + (back - normed * stat) * inv).astype(BF16)
        line = jnp.sum(jnp.where(diagonal, stat, 0.0), axis=0, keepdims=True)
        coupling_ref[pl.ds(pl.program_id(0) * rows + r, 1), :] = line * math.sqrt(width)


def finish(member_own, x, g, gain, *sums):
    rows, seq, width = x.shape
    step = math.gcd(rows, 2)
    row = pl.BlockSpec((step, seq, width), lambda r, mem: (r, 0, 0))
    two = pl.BlockSpec((2, step, seq, width), lambda r, mem: (0, r, 0, 0))
    return pl.pallas_call(
        finish_kernel,
        grid_spec=pltpu.PrefetchScalarGridSpec(
            num_scalar_prefetch=1,
            grid=(rows // step,),
            in_specs=[
                row, row, pl.BlockSpec(gain.shape, lambda r, mem: (0, 0)), row, row, row, row, two
            ],
            out_specs=[row, row, pl.BlockSpec((rows, seq), lambda r, mem: (0, 0))],
        ),
        out_shape=[
            jax.ShapeDtypeStruct((rows, seq, width), BF16),
            jax.ShapeDtypeStruct((rows, seq, width), BF16),
            jax.ShapeDtypeStruct((rows, seq), F32),
        ],
        compiler_params=pltpu.CompilerParams(vmem_limit_bytes=VMEM_LIMIT),
        name="finish",
    )(member_own, x, g, gain, *sums)


def sort_rows(picks):
    index = jnp.arange(picks.shape[0], dtype=jnp.int32)
    before = (picks[None, :] < picks[:, None]) | (
        (picks[None, :] == picks[:, None]) & (index[None, :] < index[:, None])
    )
    pos = jnp.sum(before.astype(jnp.int32), axis=1)
    at = pos[None, :] == index[:, None]
    perm = jnp.sum(jnp.where(at, index[None, :], 0), axis=1)
    return perm, jnp.sum(jnp.where(at, picks[None, :], 0), axis=1)


def on_device_shared(ranks, tokens_in, upstream, member_pick, norm_gain, up_proj, down_proj):
    rows, seq, width = tokens_in.shape
    members, depth, hidden = up_proj.shape
    rank = lax.axis_index("row")
    core = lax.rem(rank, 2)
    x_at = lax.axis_index("grp")
    y_at = lax.rem(rank // 2, 2)
    lines = ranks // 4

    def partner(a):
        return lax.ppermute(a, "row", [(i, i ^ 1) for i in range(ranks)])

    def over_y(a):
        return lax.ppermute(a, "row", [(i, i ^ 2) for i in range(ranks)])

    def over_x(a):
        return lax.ppermute(a, "grp", [(0, 1), (1, 0)])

    def shift_z(a, d):
        return lax.ppermute(a, "row", [(i, (i + 4 * d) % ranks) for i in range(ranks)])

    def after(a, *others):
        return lax.optimization_barrier((a, *others))[0]

    unit = hidden // 32
    quarter, half = 7 * unit, 2 * unit
    both = jnp.stack([up_proj, down_proj], axis=1)

    def units_of(c):
        return jnp.concatenate(
            [
                lax.dynamic_slice_in_dim(both, (2 * x_at + c) * quarter, quarter, 3),
                lax.dynamic_slice_in_dim(both, 4 * quarter + c * half, half, 3),
            ],
            axis=3,
        )

    pick_own = member_pick[:, 0]
    pick_near = jnp.concatenate([pick_own, over_x(pick_own)])
    mine = units_of(core)
    theirs = after(partner(units_of(1 - core)), pick_near)
    even = core == 0
    shard = jnp.concatenate(
        [jnp.where(even, mine, theirs), jnp.where(even, theirs, mine)], axis=2
    ).reshape(members, 4 * depth, quarter + half)

    groups = [
        [(0, 0, 2 * unit)],
        [(0, 2 * unit, 4 * unit)],
        [(0, 6 * unit, unit), (1, 0, 3 * unit)],
        [(1, 3 * unit, 4 * unit)],
        [(0, quarter, half), (1, quarter, half)],
    ]
    send = [
        jnp.concatenate([shard[m, :, at : at + n] for m, at, n in group], axis=1)
        for group in groups
    ]
    here, there = [], []

    def exchange(step, arrived):
        results = []
        if step < len(groups):
            mine = after(send[step], *arrived)
            results += [shift_z(mine, d) for d in range(1, lines)]
        if step > 0:
            there.append(over_y(after(here[step - 1], *arrived)))
            results.append(there[-1])
        if step < len(groups):
            here.append(jnp.stack([send[step], *results[: lines - 1]]))
        return results

    def chunk_pieces(*at):
        pieces = []
        for group in at:
            start = 0
            for member, _, n in groups[group]:
                pieces.append((member, n, (here[group], start), (there[group], start)))
                start += n
        return pieces

    per_block = math.gcd(2 * rows, 4)
    place = jnp.stack([y_at, rank // 4])
    pick_far = partner(after(pick_near, theirs))

    arrived = exchange(0, [])
    arrived += [pick_far]
    near = jnp.stack([after(tokens_in, send[0]), upstream])
    over = over_x(near)

    arrived = exchange(1, arrived)
    arrived += [over]

    set_1, arrived = arrived, exchange(2, arrived)
    far = partner(after(jnp.stack([near, over]), *set_1))
    chips = []
    for i, mine in enumerate((near, over)):
        perm, member_sorted = sort_rows(
            jnp.concatenate([pick_near[i * rows : (i + 1) * rows], pick_far[i * rows : (i + 1) * rows]])
        )
        lifted, g_sorted = prep(perm, member_sorted, mine, far[i], norm_gain)
        chips.append(((member_sorted, place, perm), lifted, g_sorted))
        arrived.append(lifted)
    chip, over_chip = chips

    set_2, arrived = arrived, exchange(3, arrived)
    first = chunk_pieces(0, 1)
    sums = chunk((True, False), per_block, *chip, first, None)
    over_sums = chunk((True, False), per_block, *over_chip, first, None)
    arrived += [sums[0], over_sums[0]]

    set_3, arrived = arrived, exchange(4, arrived)
    second = chunk_pieces(2)
    sums = chunk(
        (False, False), per_block, *chip, second, (after(sums[0], *set_3), sums[1])
    )
    over_sums = chunk(
        (False, False), per_block, *over_chip, second, (after(over_sums[0], *set_3), over_sums[1])
    )
    arrived += [sums[0], over_sums[0]]

    set_4 = arrived
    exchange(5, arrived)
    over_sums = (after(over_sums[0], *set_4), over_sums[1])
    *same, other_out, other_back = chunk(
        (False, True), per_block, *over_chip, chunk_pieces(3), over_sums, (BF16, BF16), 0
    )
    others = partner(jnp.stack([other_out, other_back]))
    across = (jnp.stack(same).astype(F32) + others.astype(F32)).astype(BF16)
    sums = (after(sums[0], across), sums[1])
    across = over_x(across)
    out, back, packed_out, packed_back = chunk(
        (False, True), per_block, *chip, chunk_pieces(3, 4), sums, (F32, BF16), 0
    )
    return tuple(
        finish(
            pick_own, tokens_in, upstream, norm_gain, out, back,
            partner(packed_out), partner(packed_back), across,
        )
    )


def solution(mesh):
    ranks = mesh.shape["row"]
    four = mesh.shape["feat"] == 1 and ranks % 4 == 0 and mesh.shape["grp"] == 2

    def on_device(tokens_in, upstream, member_pick, norm_gain, up_proj, down_proj):
        args = (tokens_in, upstream, member_pick, norm_gain, up_proj, down_proj)
        if four and member_pick.shape[1] == 1 and up_proj.shape[0] == 2:
            return on_device_shared(ranks, *args)
        return on_device_general(*args)

    in_specs = (
        P(("grp", "row"), None, "feat"),
        P(("grp", "row"), None, "feat"),
        P(("grp", "row"), None),
        P(),
        P(None, "row", "feat"),
        P(None, "row", "feat"),
    )
    out_specs = (
        P(("grp", "row"), None, "feat"),
        P(("grp", "row"), None, "feat"),
        P(("grp", "row"), None),
    )
    return jax.shard_map(
        on_device, mesh=mesh, in_specs=in_specs, out_specs=out_specs, check_vma=False
    )
```

```python
import functools
import math

import jax
import jax.numpy as jnp
from jax import lax
from jax.experimental import pallas as pl
from jax.experimental.pallas import tpu as pltpu
from jax.sharding import PartitionSpec as P

coef_c = math.sqrt(2.0 / math.pi)


def gelu_tanh(v):
    return 0.5 * v * (1.0 + jnp.tanh(coef_c * (v + 0.044715 * v * v * v)))


def gelu_slope(v):
    inner = jnp.tanh(coef_c * (v + 0.044715 * v * v * v))
    return 0.5 * (1.0 + inner) + 0.5 * v * (1.0 - inner * inner) * coef_c * (
        1.0 + 3.0 * 0.044715 * v * v
    )


def on_device_general(tokens_in, upstream, member_pick, norm_gain, up_proj, down_proj):
    rows, seq, half = tokens_in.shape
    count = rows * seq
    members = up_proj.shape[0]
    pick = member_pick.shape[1]
    whole_x, whole_g = (
        lax.all_gather(tokens_in, "feat", axis=2, tiled=True),
        lax.all_gather(upstream, "feat", axis=2, tiled=True),
    )
    width = whole_x.shape[2]
    flat_x = whole_x.reshape(count, width).astype(jnp.float32)
    flat_g = whole_g.reshape(count, width)
    inv_rms = 1.0 / jnp.sqrt(jnp.mean(flat_x * flat_x, axis=1, keepdims=True) + 1e-06)
    normed = flat_x * inv_rms
    labels = jnp.arange(members, dtype=jnp.int32)
    chosen = (
        jnp.sum((member_pick[:, :, None] == labels[None, None, :]).astype(jnp.float32), axis=1)
        / pick
    )
    chosen_tok = jnp.repeat(chosen, seq, axis=0)
    out_half = jnp.zeros((count, half), jnp.float32)
    back_half = jnp.zeros((count, half), jnp.float32)
    for member in range(members):
        lifted = (normed * norm_gain[member][None, :]).astype(jnp.bfloat16)
        up_full = lax.all_gather(up_proj[member], "row", axis=0, tiled=True)
        hidden = jnp.dot(lifted, up_full, preferred_element_type=jnp.float32)
        act = gelu_tanh(hidden).astype(jnp.bfloat16)
        piece = lax.all_gather(down_proj[member], "row", axis=0, tiled=True)
        block = lax.dot_general(
            act, piece, (((1,), (1,)), ((), ())), preferred_element_type=jnp.float32
        )
        grads = jnp.dot(flat_g, piece, preferred_element_type=jnp.float32)
        pre_grad = (grads * gelu_slope(hidden)).astype(jnp.bfloat16)
        in_grad = lax.dot_general(
            pre_grad, up_full, (((1,), (1,)), ((), ())), preferred_element_type=jnp.float32
        )
        weight_col = chosen_tok[:, member : member + 1]
        out_term = weight_col * block
        back_term = weight_col * norm_gain[member][None, :] * in_grad
        out_part, back_part = (
            lax.psum_scatter(
                out_term.astype(jnp.bfloat16), "feat", scatter_dimension=1, tiled=True
            ).astype(jnp.float32),
            lax.psum_scatter(
                back_term.astype(jnp.bfloat16), "feat", scatter_dimension=1, tiled=True
            ).astype(jnp.float32),
        )
        out_half = out_half + out_part
        back_half = back_half + back_part
    own_x = tokens_in.reshape(count, half).astype(jnp.float32)
    normed_half = own_x * inv_rms
    stat = lax.psum(jnp.sum(normed_half * back_half, axis=1, keepdims=True), "feat") / width
    coupling = stat * math.sqrt(width)
    own_g = upstream.reshape(count, half).astype(jnp.float32)
    value_out = (own_x + out_half).astype(jnp.bfloat16)
    grad_in = (own_g + (back_half - normed_half * stat) * inv_rms).astype(jnp.bfloat16)
    return (
        value_out.reshape(rows, seq, half),
        grad_in.reshape(rows, seq, half),
        coupling.reshape(rows, seq),
    )


VMEM_LIMIT = 56 * 1024 * 1024
BF16 = jnp.bfloat16
F32 = jnp.float32


def chunk_kernel(
    offset, kind, units, sorted_ref, place_ref, perm_ref, near_ref, over_ref, far_ref, *refs
):
    first, last = kind
    parts = len(units)
    pieces, refs = refs[: 2 * parts], refs[2 * parts :]
    if first:
        *outs, weights_ref, sems, lifted_ref, g_ref = refs
    elif last:
        out_in, back_in, *outs, weights_ref, sems, lifted_ref, g_ref, out_acc, back_acc = refs
    else:
        out_in, back_in, *outs, weights_ref, sems, lifted_ref, g_ref = refs
    if not last:
        out_acc, back_acc = outs
    j = pl.program_id(0)
    rows, seq = near_ref.shape[1:3]
    per_block = lifted_ref.shape[0] // seq
    places = [(j + offset) * per_block + i for i in range(per_block)]
    lines, _, depth2, _ = weights_ref.shape
    depth = depth2 // 2
    starts = [sum(n for _, n in units[:part]) for part in range(parts)]

    @pl.when(j == 0)
    def _():
        y, z = place_ref[0], place_ref[1]
        copies = []
        for part in range(parts):
            n = units[part][1]
            for to_y, (ref, start) in zip((y, 1 - y), pieces[2 * part : 2 * part + 2]):
                for d in range(lines):
                    from_z = lax.rem(z + lines - d, lines)
                    copies.append(
                        pltpu.make_async_copy(
                            ref.at[d, :, pl.ds(start, n)],
                            weights_ref.at[from_z, to_y, :, pl.ds(starts[part], n)],
                            sems.at[len(copies)],
                        )
                    )
        for copy in copies:
            copy.start()
        for copy in copies:
            copy.wait()

    for i, at in enumerate(places):
        row = perm_ref[at]
        source = row // rows
        for k, ref in enumerate((near_ref, far_ref.at[0], over_ref, far_ref.at[1])):

            @pl.when(source == k)
            def _():
                tokens = pl.ds(i * seq, seq)
                lifted_ref[tokens, :] = ref[0, row - k * rows]
                g_ref[tokens, :] = ref[1, row - k * rows]

    width = lifted_ref.shape[1]
    here = [sorted_ref[at] for at in places]
    if first:
        out_acc[...] = jnp.zeros(out_acc.shape, F32)
        back_acc[...] = jnp.zeros(back_acc.shape, F32)
    else:
        out_acc[...] = out_in[...]
        back_acc[...] = back_in[...]

    for member in sorted(set(m for m, _ in units)):
        used = functools.reduce(jnp.logical_or, [m == member for m in here])

        @pl.when(used)
        def _():
            lifted = lifted_ref[...]
            g = g_ref[...]
            weight = jnp.concatenate(
                [jnp.full((seq, 1), (m == member).astype(F32), F32) for m in here], axis=0
            )
            out_sum = jnp.zeros(lifted.shape, F32)
            back_sum = jnp.zeros(lifted.shape, F32)
            spans = []
            for (m, n), start in zip(units, starts):
                if m == member:
                    spans += [(s, min(s + 512, start + n)) for s in range(start, start + n, 512)]
            for s, e in spans:
                up = weights_ref[:, :, :depth, s:e].reshape(width, e - s)
                down = weights_ref[:, :, depth:, s:e].reshape(width, e - s)
                v = jnp.dot(lifted, up, preferred_element_type=F32)
                grads = jnp.dot(g, down, preferred_element_type=F32)
                square = v * v
                t = jnp.tanh(coef_c * (v + 0.044715 * square * v))
                act = (0.5 * v * (1.0 + t)).astype(BF16)
                slope = 0.5 * (1.0 + t) + 0.5 * v * (1.0 - t * t) * coef_c * (
                    1.0 + 3.0 * 0.044715 * square
                )
                pre = (grads * slope).astype(BF16)
                dims = (((1,), (1,)), ((), ()))
                out_sum += lax.dot_general(act, down, dims, preferred_element_type=F32)
                back_sum += lax.dot_general(pre, up, dims, preferred_element_type=F32)
            out_acc[...] += weight * out_sum
            back_acc[...] += weight * back_sum

    if last:
        for p, at in enumerate(places):
            row = lax.rem(perm_ref[at], 2 * rows)
            tokens = pl.ds(p * seq, seq)
            low = 0
            for to_out, to_back in zip(outs[::2], outs[1::2]):
                n = to_out.shape[0]

                @pl.when(jnp.logical_and(row >= low, row < low + n))
                def _():
                    to = jnp.clip(row - low, 0, n - 1)
                    to_out[to] = out_acc[tokens, :].astype(to_out.dtype)
                    to_back[to] = back_acc[tokens, :].astype(to_back.dtype)

                low += n


def chunk(kind, blocks, scalars, tokens_of, pieces, sums, outs=None, weight=1):
    first, last = kind
    offset, number, per_block = blocks
    _, rows, seq, width = tokens_of[0].shape
    units = [(member, n) for member, n, *_ in pieces]
    lines, depth2, _ = pieces[0][2][0].shape
    hidden = sum(n for _, n in units)
    size = per_block * seq

    tok = pl.BlockSpec((size, width), lambda j, *_: (j + offset, 0))
    hbm = pl.BlockSpec(memory_space=pl.ANY)
    args = [*scalars, *tokens_of]
    specs = [
        pl.BlockSpec(a.shape, lambda *_, n=a.ndim: (0,) * n, pipeline_mode=pl.Buffered(1))
        for a in tokens_of
    ]
    starts = []
    for _, _, *both in pieces:
        args += [array for array, _ in both]
        starts += [start for _, start in both]
    specs += [hbm] * len(starts)
    alias = {}
    out_specs = [tok, tok]
    out_shape = [jax.ShapeDtypeStruct((4 * rows * seq, width), F32)] * 2
    scratch = [
        pltpu.VMEM((lines, 2, depth2, hidden), BF16),
        pltpu.SemaphoreType.DMA((len(pieces) * 2 * lines,)),
        pltpu.VMEM((size, width), BF16),
        pltpu.VMEM((size, width), BF16),
    ]
    if not first:
        alias = {len(args): 0, len(args) + 1: 1}
        args += list(sums)
        specs += [tok, tok]
    if last:
        alias = {}
        shape = (rows, seq, width)
        out_shape = [jax.ShapeDtypeStruct(shape, dtype) for dtype in outs for _ in range(2)]
        out_specs = [pl.BlockSpec(shape, lambda *_: (0, 0, 0))] * len(out_shape)
        scratch += [pltpu.VMEM((size, width), F32)] * 2

    def kernel(*refs):
        refs = list(refs)
        base = len(scalars) + len(tokens_of)
        for i, start in enumerate(starts):
            refs[base + i] = (refs[base + i], start)
        chunk_kernel(offset, kind, units, *refs)

    return pl.pallas_call(
        kernel,
        grid_spec=pltpu.PrefetchScalarGridSpec(
            num_scalar_prefetch=len(scalars),
            grid=(number,),
            in_specs=specs,
            out_specs=out_specs,
            scratch_shapes=scratch,
        ),
        out_shape=out_shape,
        input_output_aliases=alias,
        compiler_params=pltpu.CompilerParams(vmem_limit_bytes=VMEM_LIMIT),
        cost_estimate=pl.CostEstimate(
            flops=weight * 8 * number * size * width * hidden * 2 // 3,
            bytes_accessed=weight * (4 * width * hidden + 20 * number * size * width),
            transcendentals=weight * number * size * hidden,
        ),
        name="chunk",
    )(*args)


def finish_kernel(
    member_ref, x_ref, g_ref, gain_ref, out_ref, back_ref, other_out_ref, other_back_ref,
    across_ref, value_ref, grad_ref, coupling_ref,
):
    rows, seq, width = x_ref.shape
    diagonal = lax.broadcasted_iota(jnp.int32, (seq, seq), 0) == lax.broadcasted_iota(
        jnp.int32, (seq, seq), 1
    )
    for r in range(rows):
        x = x_ref[r].astype(F32)
        inv = 1.0 / jnp.sqrt(jnp.mean(x * x, axis=1, keepdims=True) + 1e-06)
        normed = x * inv
        gain = gain_ref[pl.ds(member_ref[pl.program_id(0) * rows + r], 1), :]
        back = gain * (
            back_ref[r] + other_back_ref[r].astype(F32) + across_ref[1, r].astype(F32)
        )
        stat = jnp.sum(normed * back, axis=1, keepdims=True) / width
        out = out_ref[r] + other_out_ref[r].astype(F32) + across_ref[0, r].astype(F32)
        value_ref[r] = (x + out).astype(BF16)
        grad_ref[r] = (g_ref[r].astype(F32) + (back - normed * stat) * inv).astype(BF16)
        line = jnp.sum(jnp.where(diagonal, stat, 0.0), axis=0, keepdims=True)
        coupling_ref[pl.ds(pl.program_id(0) * rows + r, 1), :] = line * math.sqrt(width)


def finish(member_own, x, g, gain, *sums):
    rows, seq, width = x.shape
    step = math.gcd(rows, 2)
    row = pl.BlockSpec((step, seq, width), lambda r, mem: (r, 0, 0))
    two = pl.BlockSpec((2, step, seq, width), lambda r, mem: (0, r, 0, 0))
    return pl.pallas_call(
        finish_kernel,
        grid_spec=pltpu.PrefetchScalarGridSpec(
            num_scalar_prefetch=1,
            grid=(rows // step,),
            in_specs=[
                row, row, pl.BlockSpec(gain.shape, lambda r, mem: (0, 0)), row, row, row, row, two
            ],
            out_specs=[row, row, pl.BlockSpec((rows, seq), lambda r, mem: (0, 0))],
        ),
        out_shape=[
            jax.ShapeDtypeStruct((rows, seq, width), BF16),
            jax.ShapeDtypeStruct((rows, seq, width), BF16),
            jax.ShapeDtypeStruct((rows, seq), F32),
        ],
        compiler_params=pltpu.CompilerParams(vmem_limit_bytes=VMEM_LIMIT),
        name="finish",
    )(member_own, x, g, gain, *sums)


def sort_rows(picks):
    index = jnp.arange(picks.shape[0], dtype=jnp.int32)
    before = (picks[None, :] < picks[:, None]) | (
        (picks[None, :] == picks[:, None]) & (index[None, :] < index[:, None])
    )
    pos = jnp.sum(before.astype(jnp.int32), axis=1)
    at = pos[None, :] == index[:, None]
    perm = jnp.sum(jnp.where(at, index[None, :], 0), axis=1)
    return perm, jnp.sum(jnp.where(at, picks[None, :], 0), axis=1)


def on_device_shared(ranks, tokens_in, upstream, member_pick, norm_gain, up_proj, down_proj):
    rows, seq, width = tokens_in.shape
    members, depth, hidden = up_proj.shape
    rank = lax.axis_index("row")
    core = lax.rem(rank, 2)
    x_at = lax.axis_index("grp")
    y_at = lax.rem(rank // 2, 2)
    lines = ranks // 4

    def partner(a):
        return lax.ppermute(a, "row", [(i, i ^ 1) for i in range(ranks)])

    def over_y(a):
        return lax.ppermute(a, "row", [(i, i ^ 2) for i in range(ranks)])

    def over_x(a):
        return lax.ppermute(a, "grp", [(0, 1), (1, 0)])

    def shift_z(a, d):
        return lax.ppermute(a, "row", [(i, (i + 4 * d) % ranks) for i in range(ranks)])

    def after(a, *others):
        return lax.optimization_barrier((a, *others))[0]

    unit = hidden // 32
    quarter, half = 7 * unit, 2 * unit
    both = jnp.stack([up_proj, down_proj], axis=1)

    def units_of(c):
        return jnp.concatenate(
            [
                lax.dynamic_slice_in_dim(both, (2 * x_at + c) * quarter, quarter, 3),
                lax.dynamic_slice_in_dim(both, 4 * quarter + c * half, half, 3),
            ],
            axis=3,
        )

    pick_own = member_pick[:, 0]
    pick_near = jnp.concatenate([pick_own, over_x(pick_own)])
    mine = units_of(core)
    theirs = after(partner(units_of(1 - core)), pick_near)
    even = core == 0
    shard = jnp.concatenate(
        [jnp.where(even, mine, theirs), jnp.where(even, theirs, mine)], axis=2
    ).reshape(members, 4 * depth, quarter + half)

    groups = [
        [(0, 0, 2 * unit)],
        [(0, 2 * unit, 4 * unit)],
        [(0, 6 * unit, unit), (1, 0, 3 * unit)],
        [(1, 3 * unit, 4 * unit)],
        [(0, quarter, half), (1, quarter, half)],
    ]
    send = [
        jnp.concatenate([shard[m, :, at : at + n] for m, at, n in group], axis=1)
        for group in groups
    ]
    here, there = [], []

    def exchange(step, arrived):
        results = []
        if step < len(groups):
            mine = after(send[step], *arrived)
            results += [shift_z(mine, d) for d in range(1, lines)]
        if step > 0:
            there.append(over_y(after(here[step - 1], *arrived)))
            results.append(there[-1])
        if step < len(groups):
            here.append(jnp.stack([send[step], *results[: lines - 1]]))
        return results

    def chunk_pieces(*at):
        pieces = []
        for group in at:
            start = 0
            for member, _, n in groups[group]:
                pieces.append((member, n, (here[group], start), (there[group], start)))
                start += n
        return pieces

    per_block = math.gcd(2 * rows, 4)
    per_chip = 2 * rows // per_block
    pick_far = partner(after(pick_near, theirs))

    arrived = exchange(0, [])
    arrived += [pick_far]
    x = after(tokens_in, send[0]).astype(F32)
    gain = jnp.zeros((rows, width), F32)
    for member in range(members):
        gain = jnp.where(pick_own[:, None] == member, norm_gain[member][None, :], gain)
    normed = x * (1.0 / jnp.sqrt(jnp.mean(x * x, axis=2, keepdims=True) + 1e-06))
    near = jnp.stack([(normed * gain[:, None, :]).astype(BF16), upstream])
    over = over_x(near)

    arrived = exchange(1, arrived)
    arrived += [over]

    set_1, arrived = arrived, exchange(2, arrived)
    far = partner(after(jnp.stack([near, over]), *set_1))
    arrived += [far]
    perm, member_sorted = sort_rows(jnp.concatenate([pick_near[rows:], pick_far[rows:]]))
    perm_own, member_sorted_own = sort_rows(jnp.concatenate([pick_own, pick_far[:rows]]))
    scalars = (
        jnp.concatenate([member_sorted, member_sorted_own]),
        jnp.stack([y_at, rank // 4]),
        jnp.concatenate([perm + 2 * rows, perm_own]),
    )
    tokens_of = (near, over, far)

    set_2, arrived = arrived, exchange(3, arrived)
    whole = (0, 2 * per_chip, per_block)
    sums = chunk(
        (True, False), whole, scalars, (after(near, *set_2), over, far), chunk_pieces(0, 1), None
    )
    arrived += [sums[0]]

    set_3, arrived = arrived, exchange(4, arrived)
    sums = chunk(
        (False, False), whole, scalars, tokens_of, chunk_pieces(2),
        (after(sums[0], *set_3), sums[1]),
    )
    arrived += [sums[0]]

    set_4 = arrived
    exchange(5, arrived)
    sums = (after(sums[0], *set_4), sums[1])
    *same, other_out, other_back = chunk(
        (False, True), (0, per_chip, per_block), scalars, tokens_of, chunk_pieces(3), sums,
        (BF16, BF16), 0,
    )
    others = partner(jnp.stack([other_out, other_back]))
    across = (jnp.stack(same).astype(F32) + others.astype(F32)).astype(BF16)
    sums = (after(sums[0], across), sums[1])
    across = over_x(across)
    out, back, packed_out, packed_back = chunk(
        (False, True), (per_chip, per_chip, per_block), scalars, tokens_of, chunk_pieces(3, 4),
        sums, (F32, BF16), 0,
    )
    return tuple(
        finish(
            pick_own, tokens_in, upstream, norm_gain, out, back,
            partner(packed_out), partner(packed_back), across,
        )
    )


def solution(mesh):
    ranks = mesh.shape["row"]
    four = mesh.shape["feat"] == 1 and ranks % 4 == 0 and mesh.shape["grp"] == 2

    def on_device(tokens_in, upstream, member_pick, norm_gain, up_proj, down_proj):
        args = (tokens_in, upstream, member_pick, norm_gain, up_proj, down_proj)
        if four and member_pick.shape[1] == 1 and up_proj.shape[0] == 2:
            return on_device_shared(ranks, *args)
        return on_device_general(*args)

    in_specs = (
        P(("grp", "row"), None, "feat"),
        P(("grp", "row"), None, "feat"),
        P(("grp", "row"), None),
        P(),
        P(None, "row", "feat"),
        P(None, "row", "feat"),
    )
    out_specs = (
        P(("grp", "row"), None, "feat"),
        P(("grp", "row"), None, "feat"),
        P(("grp", "row"), None),
    )
    return jax.shard_map(
        on_device, mesh=mesh, in_specs=in_specs, out_specs=out_specs, check_vma=False
    )
```

```python
import functools
import math

import jax
import jax.numpy as jnp
from jax import lax
from jax.experimental import pallas as pl
from jax.experimental.pallas import tpu as pltpu
from jax.sharding import PartitionSpec as P

coef_c = math.sqrt(2.0 / math.pi)


def gelu_tanh(v):
    return 0.5 * v * (1.0 + jnp.tanh(coef_c * (v + 0.044715 * v * v * v)))


def gelu_slope(v):
    inner = jnp.tanh(coef_c * (v + 0.044715 * v * v * v))
    return 0.5 * (1.0 + inner) + 0.5 * v * (1.0 - inner * inner) * coef_c * (
        1.0 + 3.0 * 0.044715 * v * v
    )


def on_device_general(tokens_in, upstream, member_pick, norm_gain, up_proj, down_proj):
    rows, seq, half = tokens_in.shape
    count = rows * seq
    members = up_proj.shape[0]
    pick = member_pick.shape[1]
    whole_x, whole_g = (
        lax.all_gather(tokens_in, "feat", axis=2, tiled=True),
        lax.all_gather(upstream, "feat", axis=2, tiled=True),
    )
    width = whole_x.shape[2]
    flat_x = whole_x.reshape(count, width).astype(jnp.float32)
    flat_g = whole_g.reshape(count, width)
    inv_rms = 1.0 / jnp.sqrt(jnp.mean(flat_x * flat_x, axis=1, keepdims=True) + 1e-06)
    normed = flat_x * inv_rms
    labels = jnp.arange(members, dtype=jnp.int32)
    chosen = (
        jnp.sum((member_pick[:, :, None] == labels[None, None, :]).astype(jnp.float32), axis=1)
        / pick
    )
    chosen_tok = jnp.repeat(chosen, seq, axis=0)
    out_half = jnp.zeros((count, half), jnp.float32)
    back_half = jnp.zeros((count, half), jnp.float32)
    for member in range(members):
        lifted = (normed * norm_gain[member][None, :]).astype(jnp.bfloat16)
        up_full = lax.all_gather(up_proj[member], "row", axis=0, tiled=True)
        hidden = jnp.dot(lifted, up_full, preferred_element_type=jnp.float32)
        act = gelu_tanh(hidden).astype(jnp.bfloat16)
        piece = lax.all_gather(down_proj[member], "row", axis=0, tiled=True)
        block = lax.dot_general(
            act, piece, (((1,), (1,)), ((), ())), preferred_element_type=jnp.float32
        )
        grads = jnp.dot(flat_g, piece, preferred_element_type=jnp.float32)
        pre_grad = (grads * gelu_slope(hidden)).astype(jnp.bfloat16)
        in_grad = lax.dot_general(
            pre_grad, up_full, (((1,), (1,)), ((), ())), preferred_element_type=jnp.float32
        )
        weight_col = chosen_tok[:, member : member + 1]
        out_term = weight_col * block
        back_term = weight_col * norm_gain[member][None, :] * in_grad
        out_part, back_part = (
            lax.psum_scatter(
                out_term.astype(jnp.bfloat16), "feat", scatter_dimension=1, tiled=True
            ).astype(jnp.float32),
            lax.psum_scatter(
                back_term.astype(jnp.bfloat16), "feat", scatter_dimension=1, tiled=True
            ).astype(jnp.float32),
        )
        out_half = out_half + out_part
        back_half = back_half + back_part
    own_x = tokens_in.reshape(count, half).astype(jnp.float32)
    normed_half = own_x * inv_rms
    stat = lax.psum(jnp.sum(normed_half * back_half, axis=1, keepdims=True), "feat") / width
    coupling = stat * math.sqrt(width)
    own_g = upstream.reshape(count, half).astype(jnp.float32)
    value_out = (own_x + out_half).astype(jnp.bfloat16)
    grad_in = (own_g + (back_half - normed_half * stat) * inv_rms).astype(jnp.bfloat16)
    return (
        value_out.reshape(rows, seq, half),
        grad_in.reshape(rows, seq, half),
        coupling.reshape(rows, seq),
    )


VMEM_LIMIT = 56 * 1024 * 1024
BF16 = jnp.bfloat16
F32 = jnp.float32


def chunk_kernel(
    offset, kind, units, sorted_ref, place_ref, perm_ref, near_ref, over_ref, far_ref, *refs
):
    first, last = kind
    parts = len(units)
    pieces, refs = refs[: 2 * parts], refs[2 * parts :]
    if first:
        *outs, weights_ref, sems, lifted_ref, g_ref, act_ref, pre_ref = refs
    elif last:
        out_in, back_in, *outs, weights_ref, sems, lifted_ref, g_ref, act_ref, pre_ref = refs[:-2]
        out_acc, back_acc = refs[-2:]
    else:
        out_in, back_in, *outs, weights_ref, sems, lifted_ref, g_ref, act_ref, pre_ref = refs
    if not last:
        out_acc, back_acc = outs
    j = pl.program_id(0)
    rows, seq = near_ref.shape[1:3]
    per_block = lifted_ref.shape[0] // seq
    places = [(j + offset) * per_block + i for i in range(per_block)]
    lines, _, depth2, _ = weights_ref.shape
    depth = depth2 // 2
    starts = [sum(n for _, n in units[:part]) for part in range(parts)]

    @pl.when(j == 0)
    def _():
        y, z = place_ref[0], place_ref[1]
        copies = []
        for part in range(parts):
            n = units[part][1]
            for to_y, (ref, start) in zip((y, 1 - y), pieces[2 * part : 2 * part + 2]):
                for d in range(lines):
                    from_z = lax.rem(z + lines - d, lines)
                    copies.append(
                        pltpu.make_async_copy(
                            ref.at[d, :, pl.ds(start, n)],
                            weights_ref.at[from_z, to_y, :, pl.ds(starts[part], n)],
                            sems.at[len(copies)],
                        )
                    )
        for copy in copies:
            copy.start()
        for copy in copies:
            copy.wait()

    width = lifted_ref.shape[1]
    here = [sorted_ref[at] for at in places]

    def pick_up(member):
        for i, at in enumerate(places):
            row = perm_ref[at]
            source = jnp.where(here[i] == member, row // rows, 4)
            tokens = pl.ds(i * seq, seq)
            for k, ref in enumerate((near_ref, far_ref.at[0], over_ref, far_ref.at[1])):

                @pl.when(source == k)
                def _():
                    lifted_ref[tokens, :] = ref[0, row - k * rows]
                    g_ref[tokens, :] = ref[1, row - k * rows]

            @pl.when(source == 4)
            def _():
                lifted_ref[tokens, :] = jnp.zeros((seq, width), BF16)
                g_ref[tokens, :] = jnp.zeros((seq, width), BF16)

    def sums(member):
        pick_up(member)
        mine = [(start, n) for (m, n), start in zip(units, starts) if m == member]
        low, high = mine[0][0], mine[-1][0] + mine[-1][1]
        for s in range(low, high, 256):
            e = min(s + 256, high)
            up = weights_ref[:, :, :depth, s:e].reshape(width, e - s)
            down = weights_ref[:, :, depth:, s:e].reshape(width, e - s)
            v = jnp.dot(lifted_ref[...], up, preferred_element_type=F32)
            grads = jnp.dot(g_ref[...], down, preferred_element_type=F32)
            square = v * v
            t = jnp.tanh(v * (coef_c + (coef_c * 0.044715) * square))
            half_v = 0.5 * v
            act_ref[:, s - low : e - low] = (half_v + half_v * t).astype(BF16)
            slope = (0.5 + 0.5 * t) + (half_v * (1.0 - t * t)) * (
                coef_c + (3.0 * coef_c * 0.044715) * square
            )
            pre_ref[:, s - low : e - low] = (grads * slope).astype(BF16)
        up = weights_ref[:, :, :depth, low:high].reshape(width, high - low)
        down = weights_ref[:, :, depth:, low:high].reshape(width, high - low)
        dims = (((1,), (1,)), ((), ()))
        return (
            lax.dot_general(act_ref[:, : high - low], down, dims, preferred_element_type=F32),
            lax.dot_general(pre_ref[:, : high - low], up, dims, preferred_element_type=F32),
        )

    for at, member in enumerate(sorted(set(m for m, _ in units))):
        used = functools.reduce(jnp.logical_or, [m == member for m in here])

        @pl.when(used)
        def _():
            out_sum, back_sum = sums(member)
            if at > 0:
                out_acc[...] += out_sum
                back_acc[...] += back_sum
            elif first:
                out_acc[...] = out_sum
                back_acc[...] = back_sum
            else:
                out_acc[...] = out_in[...] + out_sum
                back_acc[...] = back_in[...] + back_sum

        if at == 0:

            @pl.when(jnp.logical_not(used))
            def _():
                out_acc[...] = jnp.zeros(out_acc.shape, F32) if first else out_in[...]
                back_acc[...] = jnp.zeros(back_acc.shape, F32) if first else back_in[...]

    if last:
        for p, at in enumerate(places):
            row = lax.rem(perm_ref[at], 2 * rows)
            tokens = pl.ds(p * seq, seq)
            low = 0
            for to_out, to_back in zip(outs[::2], outs[1::2]):
                n = to_out.shape[0]

                @pl.when(jnp.logical_and(row >= low, row < low + n))
                def _():
                    to = jnp.clip(row - low, 0, n - 1)
                    to_out[to] = out_acc[tokens, :].astype(to_out.dtype)
                    to_back[to] = back_acc[tokens, :].astype(to_back.dtype)

                low += n


def chunk(kind, blocks, scalars, tokens_of, pieces, sums, outs=None, weight=1):
    first, last = kind
    offset, number, per_block = blocks
    _, rows, seq, width = tokens_of[0].shape
    units = [(member, n) for member, n, *_ in pieces]
    lines, depth2, _ = pieces[0][2][0].shape
    hidden = sum(n for _, n in units)
    size = per_block * seq

    tok = pl.BlockSpec((size, width), lambda j, *_: (j + offset, 0))
    hbm = pl.BlockSpec(memory_space=pl.ANY)
    args = [*scalars, *tokens_of]
    specs = [
        pl.BlockSpec(a.shape, lambda *_, n=a.ndim: (0,) * n, pipeline_mode=pl.Buffered(1))
        for a in tokens_of
    ]
    starts = []
    for _, _, *both in pieces:
        args += [array for array, _ in both]
        starts += [start for _, start in both]
    specs += [hbm] * len(starts)
    alias = {}
    out_specs = [tok, tok]
    out_shape = [jax.ShapeDtypeStruct((4 * rows * seq, width), F32)] * 2
    scratch = [
        pltpu.VMEM((lines, 2, depth2, hidden), BF16),
        pltpu.SemaphoreType.DMA((len(pieces) * 2 * lines,)),
        pltpu.VMEM((size, width), BF16),
        pltpu.VMEM((size, width), BF16),
        pltpu.VMEM((size, hidden), BF16),
        pltpu.VMEM((size, hidden), BF16),
    ]
    if not first:
        alias = {len(args): 0, len(args) + 1: 1}
        args += list(sums)
        specs += [tok, tok]
    if last:
        alias = {}
        shape = (rows, seq, width)
        out_shape = [jax.ShapeDtypeStruct(shape, dtype) for dtype in outs for _ in range(2)]
        out_specs = [pl.BlockSpec(shape, lambda *_: (0, 0, 0))] * len(out_shape)
        scratch += [pltpu.VMEM((size, width), F32)] * 2

    def kernel(*refs):
        refs = list(refs)
        base = len(scalars) + len(tokens_of)
        for i, start in enumerate(starts):
            refs[base + i] = (refs[base + i], start)
        chunk_kernel(offset, kind, units, *refs)

    return pl.pallas_call(
        kernel,
        grid_spec=pltpu.PrefetchScalarGridSpec(
            num_scalar_prefetch=len(scalars),
            grid=(number,),
            in_specs=specs,
            out_specs=out_specs,
            scratch_shapes=scratch,
        ),
        out_shape=out_shape,
        input_output_aliases=alias,
        compiler_params=pltpu.CompilerParams(vmem_limit_bytes=VMEM_LIMIT),
        cost_estimate=pl.CostEstimate(
            flops=weight * 8 * number * size * width * hidden * 2 // 3,
            bytes_accessed=weight * (4 * width * hidden + 20 * number * size * width),
            transcendentals=weight * number * size * hidden,
        ),
        name="chunk",
    )(*args)


def finish_kernel(
    member_ref, x_ref, g_ref, gain_ref, out_ref, back_ref, other_out_ref, other_back_ref,
    across_ref, value_ref, grad_ref, coupling_ref,
):
    rows, seq, width = x_ref.shape
    diagonal = lax.broadcasted_iota(jnp.int32, (seq, seq), 0) == lax.broadcasted_iota(
        jnp.int32, (seq, seq), 1
    )
    for r in range(rows):
        x = x_ref[r].astype(F32)
        inv = 1.0 / jnp.sqrt(jnp.mean(x * x, axis=1, keepdims=True) + 1e-06)
        normed = x * inv
        gain = gain_ref[pl.ds(member_ref[pl.program_id(0) * rows + r], 1), :]
        back = gain * (
            back_ref[r] + other_back_ref[r].astype(F32) + across_ref[1, r].astype(F32)
        )
        stat = jnp.sum(normed * back, axis=1, keepdims=True) / width
        out = out_ref[r] + other_out_ref[r].astype(F32) + across_ref[0, r].astype(F32)
        value_ref[r] = (x + out).astype(BF16)
        grad_ref[r] = (g_ref[r].astype(F32) + (back - normed * stat) * inv).astype(BF16)
        line = jnp.sum(jnp.where(diagonal, stat, 0.0), axis=0, keepdims=True)
        coupling_ref[pl.ds(pl.program_id(0) * rows + r, 1), :] = line * math.sqrt(width)


def finish(member_own, x, g, gain, *sums):
    rows, seq, width = x.shape
    step = math.gcd(rows, 2)
    row = pl.BlockSpec((step, seq, width), lambda r, mem: (r, 0, 0))
    two = pl.BlockSpec((2, step, seq, width), lambda r, mem: (0, r, 0, 0))
    return pl.pallas_call(
        finish_kernel,
        grid_spec=pltpu.PrefetchScalarGridSpec(
            num_scalar_prefetch=1,
            grid=(rows // step,),
            in_specs=[
                row, row, pl.BlockSpec(gain.shape, lambda r, mem: (0, 0)), row, row, row, row, two
            ],
            out_specs=[row, row, pl.BlockSpec((rows, seq), lambda r, mem: (0, 0))],
        ),
        out_shape=[
            jax.ShapeDtypeStruct((rows, seq, width), BF16),
            jax.ShapeDtypeStruct((rows, seq, width), BF16),
            jax.ShapeDtypeStruct((rows, seq), F32),
        ],
        compiler_params=pltpu.CompilerParams(vmem_limit_bytes=VMEM_LIMIT),
        name="finish",
    )(member_own, x, g, gain, *sums)


def sort_rows(picks):
    index = jnp.arange(picks.shape[0], dtype=jnp.int32)
    before = (picks[None, :] < picks[:, None]) | (
        (picks[None, :] == picks[:, None]) & (index[None, :] < index[:, None])
    )
    pos = jnp.sum(before.astype(jnp.int32), axis=1)
    at = pos[None, :] == index[:, None]
    perm = jnp.sum(jnp.where(at, index[None, :], 0), axis=1)
    return perm, jnp.sum(jnp.where(at, picks[None, :], 0), axis=1)


def on_device_shared(ranks, tokens_in, upstream, member_pick, norm_gain, up_proj, down_proj):
    rows, seq, width = tokens_in.shape
    members, depth, hidden = up_proj.shape
    rank = lax.axis_index("row")
    core = lax.rem(rank, 2)
    x_at = lax.axis_index("grp")
    y_at = lax.rem(rank // 2, 2)
    lines = ranks // 4

    def partner(a):
        return lax.ppermute(a, "row", [(i, i ^ 1) for i in range(ranks)])

    def over_y(a):
        return lax.ppermute(a, "row", [(i, i ^ 2) for i in range(ranks)])

    def over_x(a):
        return lax.ppermute(a, "grp", [(0, 1), (1, 0)])

    def shift_z(a, d):
        return lax.ppermute(a, "row", [(i, (i + 4 * d) % ranks) for i in range(ranks)])

    def after(a, *others):
        return lax.optimization_barrier((a, *others))[0]

    unit = hidden // 32
    quarter, half = 7 * unit, 2 * unit
    both = jnp.stack([up_proj, down_proj], axis=1)

    def units_of(c):
        return jnp.concatenate(
            [
                lax.dynamic_slice_in_dim(both, (2 * x_at + c) * quarter, quarter, 3),
                lax.dynamic_slice_in_dim(both, 4 * quarter + c * half, half, 3),
            ],
            axis=3,
        )

    pick_own = member_pick[:, 0]
    pick_near = jnp.concatenate([pick_own, over_x(pick_own)])
    mine = units_of(core)
    theirs = after(partner(units_of(1 - core)), pick_near)
    even = core == 0
    shard = jnp.concatenate(
        [jnp.where(even, mine, theirs), jnp.where(even, theirs, mine)], axis=2
    ).reshape(members, 4 * depth, quarter + half)

    groups = [
        [(0, 0, 2 * unit)],
        [(0, 2 * unit, 4 * unit)],
        [(0, 6 * unit, unit), (1, 0, 3 * unit)],
        [(1, 3 * unit, 4 * unit)],
        [(0, quarter, half), (1, quarter, half)],
    ]
    send = [
        jnp.concatenate([shard[m, :, at : at + n] for m, at, n in group], axis=1)
        for group in groups
    ]
    here, there = [], []

    def exchange(step, arrived):
        results = []
        if step < len(groups):
            mine = after(send[step], *arrived)
            results += [shift_z(mine, d) for d in range(1, lines)]
        if step > 0:
            there.append(over_y(after(here[step - 1], *arrived)))
            results.append(there[-1])
        if step < len(groups):
            here.append(jnp.stack([send[step], *results[: lines - 1]]))
        return results

    def chunk_pieces(*at):
        pieces = []
        for group in at:
            start = 0
            for member, _, n in groups[group]:
                pieces.append((member, n, (here[group], start), (there[group], start)))
                start += n
        return pieces

    per_block = math.gcd(2 * rows, 4)
    per_chip = 2 * rows // per_block
    pick_far = partner(after(pick_near, theirs))

    arrived = exchange(0, [])
    x = after(tokens_in, arrived[0]).astype(F32)
    gain = jnp.zeros((rows, width), F32)
    for member in range(members):
        gain = jnp.where(pick_own[:, None] == member, norm_gain[member][None, :], gain)
    normed = x * (1.0 / jnp.sqrt(jnp.mean(x * x, axis=2, keepdims=True) + 1e-06))
    near = jnp.stack([(normed * gain[:, None, :]).astype(BF16), upstream])
    over = over_x(near)
    arrived += [pick_far, *send[1:]]

    perm, member_sorted = sort_rows(jnp.concatenate([pick_near[rows:], pick_far[rows:]]))
    perm_own, member_sorted_own = sort_rows(jnp.concatenate([pick_own, pick_far[:rows]]))
    scalars = (
        jnp.concatenate([member_sorted, member_sorted_own]),
        jnp.stack([y_at, rank // 4]),
        jnp.concatenate([perm + 2 * rows, perm_own]),
    )

    arrived = exchange(1, arrived)
    arrived += [*scalars]

    set_1, arrived = arrived, exchange(2, arrived)
    far = partner(jnp.stack([near, after(over, *set_1)]))
    arrived += [far]
    tokens_of = (near, over, far)

    set_2, arrived = arrived, exchange(3, arrived)
    whole = (0, 2 * per_chip, per_block)
    sums = chunk(
        (True, False), whole, scalars, (after(near, *set_2), over, far), chunk_pieces(0, 1), None
    )
    arrived += [sums[0]]

    set_3, arrived = arrived, exchange(4, arrived)
    sums = chunk(
        (False, False), whole, scalars, tokens_of, chunk_pieces(2),
        (after(sums[0], *set_3), sums[1]),
    )
    arrived += [sums[0]]

    set_4 = arrived
    exchange(5, arrived)
    sums = (after(sums[0], *set_4), sums[1])
    *same, other_out, other_back = chunk(
        (False, True), (0, per_chip, per_block), scalars, tokens_of, chunk_pieces(3), sums,
        (BF16, BF16), 0,
    )
    others = partner(jnp.stack([other_out, other_back]))
    across = (jnp.stack(same).astype(F32) + others.astype(F32)).astype(BF16)
    sums = tuple(after(a, across) for a in sums)
    across = over_x(across)
    own = (per_chip, per_chip, per_block)
    sums = chunk((False, False), own, scalars, tokens_of, chunk_pieces(3), sums, None, 0)
    out, back, packed_out, packed_back = chunk(
        (False, True), own, scalars, tokens_of, chunk_pieces(4), sums, (F32, BF16), 0
    )
    return tuple(
        finish(
            pick_own, tokens_in, upstream, norm_gain, out, back,
            partner(packed_out), partner(packed_back), across,
        )
    )


def solution(mesh):
    ranks = mesh.shape["row"]
    four = mesh.shape["feat"] == 1 and ranks % 4 == 0 and mesh.shape["grp"] == 2

    def on_device(tokens_in, upstream, member_pick, norm_gain, up_proj, down_proj):
        args = (tokens_in, upstream, member_pick, norm_gain, up_proj, down_proj)
        if four and member_pick.shape[1] == 1 and up_proj.shape[0] == 2:
            return on_device_shared(ranks, *args)
        return on_device_general(*args)

    in_specs = (
        P(("grp", "row"), None, "feat"),
        P(("grp", "row"), None, "feat"),
        P(("grp", "row"), None),
        P(),
        P(None, "row", "feat"),
        P(None, "row", "feat"),
    )
    out_specs = (
        P(("grp", "row"), None, "feat"),
        P(("grp", "row"), None, "feat"),
        P(("grp", "row"), None),
    )
    return jax.shard_map(
        on_device, mesh=mesh, in_specs=in_specs, out_specs=out_specs, check_vma=False
    )
```

```python
import functools
import math

import jax
import jax.numpy as jnp
from jax import lax
from jax.experimental import pallas as pl
from jax.experimental.pallas import tpu as pltpu
from jax.sharding import PartitionSpec as P

coef_c = math.sqrt(2.0 / math.pi)


def gelu_tanh(v):
    return 0.5 * v * (1.0 + jnp.tanh(coef_c * (v + 0.044715 * v * v * v)))


def gelu_slope(v):
    inner = jnp.tanh(coef_c * (v + 0.044715 * v * v * v))
    return 0.5 * (1.0 + inner) + 0.5 * v * (1.0 - inner * inner) * coef_c * (
        1.0 + 3.0 * 0.044715 * v * v
    )


def on_device_general(tokens_in, upstream, member_pick, norm_gain, up_proj, down_proj):
    rows, seq, half = tokens_in.shape
    count = rows * seq
    members = up_proj.shape[0]
    pick = member_pick.shape[1]
    whole_x, whole_g = (
        lax.all_gather(tokens_in, "feat", axis=2, tiled=True),
        lax.all_gather(upstream, "feat", axis=2, tiled=True),
    )
    width = whole_x.shape[2]
    flat_x = whole_x.reshape(count, width).astype(jnp.float32)
    flat_g = whole_g.reshape(count, width)
    inv_rms = 1.0 / jnp.sqrt(jnp.mean(flat_x * flat_x, axis=1, keepdims=True) + 1e-06)
    normed = flat_x * inv_rms
    labels = jnp.arange(members, dtype=jnp.int32)
    chosen = (
        jnp.sum((member_pick[:, :, None] == labels[None, None, :]).astype(jnp.float32), axis=1)
        / pick
    )
    chosen_tok = jnp.repeat(chosen, seq, axis=0)
    out_half = jnp.zeros((count, half), jnp.float32)
    back_half = jnp.zeros((count, half), jnp.float32)
    for member in range(members):
        lifted = (normed * norm_gain[member][None, :]).astype(jnp.bfloat16)
        up_full = lax.all_gather(up_proj[member], "row", axis=0, tiled=True)
        hidden = jnp.dot(lifted, up_full, preferred_element_type=jnp.float32)
        act = gelu_tanh(hidden).astype(jnp.bfloat16)
        piece = lax.all_gather(down_proj[member], "row", axis=0, tiled=True)
        block = lax.dot_general(
            act, piece, (((1,), (1,)), ((), ())), preferred_element_type=jnp.float32
        )
        grads = jnp.dot(flat_g, piece, preferred_element_type=jnp.float32)
        pre_grad = (grads * gelu_slope(hidden)).astype(jnp.bfloat16)
        in_grad = lax.dot_general(
            pre_grad, up_full, (((1,), (1,)), ((), ())), preferred_element_type=jnp.float32
        )
        weight_col = chosen_tok[:, member : member + 1]
        out_term = weight_col * block
        back_term = weight_col * norm_gain[member][None, :] * in_grad
        out_part, back_part = (
            lax.psum_scatter(
                out_term.astype(jnp.bfloat16), "feat", scatter_dimension=1, tiled=True
            ).astype(jnp.float32),
            lax.psum_scatter(
                back_term.astype(jnp.bfloat16), "feat", scatter_dimension=1, tiled=True
            ).astype(jnp.float32),
        )
        out_half = out_half + out_part
        back_half = back_half + back_part
    own_x = tokens_in.reshape(count, half).astype(jnp.float32)
    normed_half = own_x * inv_rms
    stat = lax.psum(jnp.sum(normed_half * back_half, axis=1, keepdims=True), "feat") / width
    coupling = stat * math.sqrt(width)
    own_g = upstream.reshape(count, half).astype(jnp.float32)
    value_out = (own_x + out_half).astype(jnp.bfloat16)
    grad_in = (own_g + (back_half - normed_half * stat) * inv_rms).astype(jnp.bfloat16)
    return (
        value_out.reshape(rows, seq, half),
        grad_in.reshape(rows, seq, half),
        coupling.reshape(rows, seq),
    )


VMEM_LIMIT = 40 * 1024 * 1024
BF16 = jnp.bfloat16
F32 = jnp.float32


def chunk_kernel(
    offset, kind, units, chips, sorted_ref, place_ref, perm_ref, *refs
):
    first, last = kind
    parts = len(units)
    tokens_of, refs = refs[: len(chips) + 1], refs[len(chips) + 1 :]
    pieces, refs = refs[: 2 * parts], refs[2 * parts :]
    if first:
        *outs, tokens_ref, weights_ref, sems, lifted_ref, g_ref, act_ref, pre_ref = refs
    elif last:
        out_in, back_in, *outs, tokens_ref, weights_ref, sems = refs[:-6]
        lifted_ref, g_ref, act_ref, pre_ref = refs[-6:-2]
        out_acc, back_acc = refs[-2:]
    else:
        out_in, back_in, *outs, tokens_ref, weights_ref, sems = refs[:-4]
        lifted_ref, g_ref, act_ref, pre_ref = refs[-4:]
    if not last:
        out_acc, back_acc = outs
    j = pl.program_id(0)
    rows, seq = tokens_ref.shape[2:4]
    per_block = lifted_ref.shape[0] // seq
    places = [(j + offset) * per_block + i for i in range(per_block)]
    lines, _, depth2, _ = weights_ref.shape
    depth = depth2 // 2
    starts = [sum(n for _, n in units[:part]) for part in range(parts)]

    @pl.when(j == 0)
    def _():
        y, z = place_ref[0], place_ref[1]
        copies = []
        for i, chip in enumerate(chips):
            for k, ref in enumerate((tokens_of[i], tokens_of[-1].at[chip])):
                copies.append(
                    pltpu.make_async_copy(ref, tokens_ref.at[2 * i + k], sems.at[len(copies)])
                )
        for part in range(parts):
            n = units[part][1]
            for to_y, (ref, start) in zip((y, 1 - y), pieces[2 * part : 2 * part + 2]):
                for d in range(lines):
                    from_z = lax.rem(z + lines - d, lines)
                    copies.append(
                        pltpu.make_async_copy(
                            ref.at[d, :, pl.ds(start, n)],
                            weights_ref.at[from_z, to_y, :, pl.ds(starts[part], n)],
                            sems.at[len(copies)],
                        )
                    )
        for copy in copies:
            copy.start()
        for copy in copies:
            copy.wait()

    width = lifted_ref.shape[1]
    here = [sorted_ref[at] for at in places]

    def pick_up(member):
        for i, at in enumerate(places):
            row = perm_ref[at]
            source = row // rows - 2 * chips[0]
            tokens = pl.ds(i * seq, seq)

            @pl.when(here[i] == member)
            def _():
                lifted_ref[tokens, :] = tokens_ref[source, 0, lax.rem(row, rows)]
                g_ref[tokens, :] = tokens_ref[source, 1, lax.rem(row, rows)]

            @pl.when(here[i] != member)
            def _():
                lifted_ref[tokens, :] = jnp.zeros((seq, width), BF16)
                g_ref[tokens, :] = jnp.zeros((seq, width), BF16)

    def sums(member):
        pick_up(member)
        mine = [(start, n) for (m, n), start in zip(units, starts) if m == member]
        low, high = mine[0][0], mine[-1][0] + mine[-1][1]
        for s in range(low, high, 256):
            e = min(s + 256, high)
            up = weights_ref[:, :, :depth, s:e].reshape(width, e - s)
            down = weights_ref[:, :, depth:, s:e].reshape(width, e - s)
            v = jnp.dot(lifted_ref[...], up, preferred_element_type=F32)
            grads = jnp.dot(g_ref[...], down, preferred_element_type=F32)
            square = v * v
            t = jnp.tanh(v * (coef_c + (coef_c * 0.044715) * square))
            half_v = 0.5 * v
            act_ref[:, s - low : e - low] = (half_v + half_v * t).astype(BF16)
            slope = (0.5 + 0.5 * t) + (half_v * (1.0 - t * t)) * (
                coef_c + (3.0 * coef_c * 0.044715) * square
            )
            pre_ref[:, s - low : e - low] = (grads * slope).astype(BF16)
        up = weights_ref[:, :, :depth, low:high].reshape(width, high - low)
        down = weights_ref[:, :, depth:, low:high].reshape(width, high - low)
        dims = (((1,), (1,)), ((), ()))
        return (
            lax.dot_general(act_ref[:, : high - low], down, dims, preferred_element_type=F32),
            lax.dot_general(pre_ref[:, : high - low], up, dims, preferred_element_type=F32),
        )

    for at, member in enumerate(sorted(set(m for m, _ in units))):
        used = functools.reduce(jnp.logical_or, [m == member for m in here])

        @pl.when(used)
        def _():
            out_sum, back_sum = sums(member)
            if at > 0:
                out_acc[...] += out_sum
                back_acc[...] += back_sum
            elif first:
                out_acc[...] = out_sum
                back_acc[...] = back_sum
            else:
                out_acc[...] = out_in[...] + out_sum
                back_acc[...] = back_in[...] + back_sum

        if at == 0:

            @pl.when(jnp.logical_not(used))
            def _():
                out_acc[...] = jnp.zeros(out_acc.shape, F32) if first else out_in[...]
                back_acc[...] = jnp.zeros(back_acc.shape, F32) if first else back_in[...]

    if last:
        for p, at in enumerate(places):
            row = lax.rem(perm_ref[at], 2 * rows)
            tokens = pl.ds(p * seq, seq)
            low = 0
            for to_out, to_back in zip(outs[::2], outs[1::2]):
                n = to_out.shape[0]

                @pl.when(jnp.logical_and(row >= low, row < low + n))
                def _():
                    to = jnp.clip(row - low, 0, n - 1)
                    to_out[to] = out_acc[tokens, :].astype(to_out.dtype)
                    to_back[to] = back_acc[tokens, :].astype(to_back.dtype)

                low += n


def chunk(kind, blocks, chips, scalars, tokens_of, pieces, sums, outs=None, weight=1):
    first, last = kind
    offset, number, per_block = blocks
    _, rows, seq, width = tokens_of[0].shape
    units = [(member, n) for member, n, *_ in pieces]
    lines, depth2, _ = pieces[0][2][0].shape
    hidden = sum(n for _, n in units)
    size = per_block * seq

    tok = pl.BlockSpec((size, width), lambda j, *_: (j + offset, 0))
    hbm = pl.BlockSpec(memory_space=pl.ANY)
    args = [*scalars, *(tokens_of[chip] for chip in chips), tokens_of[-1]]
    specs = [hbm] * (len(chips) + 1)
    starts = []
    for _, _, *both in pieces:
        args += [array for array, _ in both]
        starts += [start for _, start in both]
    specs += [hbm] * len(starts)
    alias = {}
    out_specs = [tok, tok]
    out_shape = [jax.ShapeDtypeStruct((4 * rows * seq, width), F32)] * 2
    scratch = [
        pltpu.VMEM((2 * len(chips), 2, rows, seq, width), BF16),
        pltpu.VMEM((lines, 2, depth2, hidden), BF16),
        pltpu.SemaphoreType.DMA((len(pieces) * 2 * lines + 2 * len(chips),)),
        pltpu.VMEM((size, width), BF16),
        pltpu.VMEM((size, width), BF16),
        pltpu.VMEM((size, hidden), BF16),
        pltpu.VMEM((size, hidden), BF16),
    ]
    if not first:
        alias = {len(args): 0, len(args) + 1: 1}
        args += list(sums)
        specs += [tok, tok]
    if last:
        alias = {}
        shape = (rows, seq, width)
        out_shape = [jax.ShapeDtypeStruct(shape, dtype) for dtype in outs for _ in range(2)]
        out_specs = [pl.BlockSpec(shape, lambda *_: (0, 0, 0))] * len(out_shape)
        scratch += [pltpu.VMEM((size, width), F32)] * 2

    def kernel(*refs):
        refs = list(refs)
        base = len(scalars) + len(chips) + 1
        for i, start in enumerate(starts):
            refs[base + i] = (refs[base + i], start)
        chunk_kernel(offset, kind, units, chips, *refs)

    return pl.pallas_call(
        kernel,
        grid_spec=pltpu.PrefetchScalarGridSpec(
            num_scalar_prefetch=len(scalars),
            grid=(number,),
            in_specs=specs,
            out_specs=out_specs,
            scratch_shapes=scratch,
        ),
        out_shape=out_shape,
        input_output_aliases=alias,
        compiler_params=pltpu.CompilerParams(vmem_limit_bytes=VMEM_LIMIT),
        cost_estimate=pl.CostEstimate(
            flops=weight * 8 * number * size * width * hidden * 2 // 3,
            bytes_accessed=weight * (4 * width * hidden + 20 * number * size * width),
            transcendentals=weight * number * size * hidden,
        ),
        name="chunk",
    )(*args)


def finish_kernel(
    member_ref, x_ref, g_ref, gain_ref, out_ref, back_ref, other_out_ref, other_back_ref,
    across_ref, value_ref, grad_ref, coupling_ref,
):
    rows, seq, width = x_ref.shape
    diagonal = lax.broadcasted_iota(jnp.int32, (seq, seq), 0) == lax.broadcasted_iota(
        jnp.int32, (seq, seq), 1
    )
    for r in range(rows):
        x = x_ref[r].astype(F32)
        inv = 1.0 / jnp.sqrt(jnp.mean(x * x, axis=1, keepdims=True) + 1e-06)
        normed = x * inv
        gain = gain_ref[pl.ds(member_ref[pl.program_id(0) * rows + r], 1), :]
        back = gain * (
            back_ref[r] + other_back_ref[r].astype(F32) + across_ref[1, r].astype(F32)
        )
        stat = jnp.sum(normed * back, axis=1, keepdims=True) / width
        out = out_ref[r] + other_out_ref[r].astype(F32) + across_ref[0, r].astype(F32)
        value_ref[r] = (x + out).astype(BF16)
        grad_ref[r] = (g_ref[r].astype(F32) + (back - normed * stat) * inv).astype(BF16)
        line = jnp.sum(jnp.where(diagonal, stat, 0.0), axis=0, keepdims=True)
        coupling_ref[pl.ds(pl.program_id(0) * rows + r, 1), :] = line * math.sqrt(width)


def finish(member_own, x, g, gain, *sums):
    rows, seq, width = x.shape
    step = math.gcd(rows, 2)
    row = pl.BlockSpec((step, seq, width), lambda r, mem: (r, 0, 0))
    two = pl.BlockSpec((2, step, seq, width), lambda r, mem: (0, r, 0, 0))
    return pl.pallas_call(
        finish_kernel,
        grid_spec=pltpu.PrefetchScalarGridSpec(
            num_scalar_prefetch=1,
            grid=(rows // step,),
            in_specs=[
                row, row, pl.BlockSpec(gain.shape, lambda r, mem: (0, 0)), row, row, row, row, two
            ],
            out_specs=[row, row, pl.BlockSpec((rows, seq), lambda r, mem: (0, 0))],
        ),
        out_shape=[
            jax.ShapeDtypeStruct((rows, seq, width), BF16),
            jax.ShapeDtypeStruct((rows, seq, width), BF16),
            jax.ShapeDtypeStruct((rows, seq), F32),
        ],
        compiler_params=pltpu.CompilerParams(vmem_limit_bytes=VMEM_LIMIT),
        name="finish",
    )(member_own, x, g, gain, *sums)


def sort_rows(picks):
    index = jnp.arange(picks.shape[0], dtype=jnp.int32)
    before = (picks[None, :] < picks[:, None]) | (
        (picks[None, :] == picks[:, None]) & (index[None, :] < index[:, None])
    )
    pos = jnp.sum(before.astype(jnp.int32), axis=1)
    at = pos[None, :] == index[:, None]
    perm = jnp.sum(jnp.where(at, index[None, :], 0), axis=1)
    return perm, jnp.sum(jnp.where(at, picks[None, :], 0), axis=1)


def on_device_shared(ranks, tokens_in, upstream, member_pick, norm_gain, up_proj, down_proj):
    rows, seq, width = tokens_in.shape
    members, depth, hidden = up_proj.shape
    rank = lax.axis_index("row")
    core = lax.rem(rank, 2)
    x_at = lax.axis_index("grp")
    y_at = lax.rem(rank // 2, 2)
    lines = ranks // 4

    def partner(a):
        return lax.ppermute(a, "row", [(i, i ^ 1) for i in range(ranks)])

    def over_y(a):
        return lax.ppermute(a, "row", [(i, i ^ 2) for i in range(ranks)])

    def over_x(a):
        return lax.ppermute(a, "grp", [(0, 1), (1, 0)])

    def shift_z(a, d):
        return lax.ppermute(a, "row", [(i, (i + 4 * d) % ranks) for i in range(ranks)])

    def after(a, *others):
        return lax.optimization_barrier((a, *others))[0]

    unit = hidden // 32
    quarter, half = 7 * unit, 2 * unit
    both = jnp.stack([up_proj, down_proj], axis=1)

    def units_of(c):
        return jnp.concatenate(
            [
                lax.dynamic_slice_in_dim(both, (2 * x_at + c) * quarter, quarter, 3),
                lax.dynamic_slice_in_dim(both, 4 * quarter + c * half, half, 3),
            ],
            axis=3,
        )

    pick_own = member_pick[:, 0]
    pick_near = jnp.concatenate([pick_own, over_x(pick_own)])
    def both_cores(mine, theirs):
        even = core == 0
        whole = jnp.concatenate(
            [jnp.where(even, mine, theirs), jnp.where(even, theirs, mine)], axis=2
        )
        return whole.reshape(mine.shape[0], 4 * depth, mine.shape[3])

    mine, given = units_of(core), units_of(1 - core)
    head = 2 * unit
    head_theirs = after(partner(given[:1, :, :, :head]), pick_near)
    shard_head = both_cores(mine[:1, :, :, :head], head_theirs)
    theirs = partner(after(given, head_theirs))
    shard = both_cores(mine, theirs)

    groups = [
        [(0, 0, 2 * unit)],
        [(0, 2 * unit, 4 * unit)],
        [(0, 6 * unit, unit), (1, 0, 3 * unit)],
        [(1, 3 * unit, 4 * unit)],
        [(0, quarter, half), (1, quarter, half)],
    ]
    send = [shard_head[0]] + [
        jnp.concatenate([shard[m, :, at : at + n] for m, at, n in group], axis=1)
        for group in groups[1:]
    ]
    here, there = [], []

    def exchange(step, arrived):
        results = []
        if step < len(groups):
            mine = after(send[step], *arrived)
            results += [shift_z(mine, d) for d in range(1, lines)]
        if step > 0:
            there.append(over_y(after(here[step - 1], *arrived)))
            results.append(there[-1])
        if step < len(groups):
            here.append(jnp.stack([send[step], *results[: lines - 1]]))
        return results

    def chunk_pieces(*at):
        pieces = []
        for group in at:
            start = 0
            for member, _, n in groups[group]:
                pieces.append((member, n, (here[group], start), (there[group], start)))
                start += n
        return pieces

    per_block = math.gcd(2 * rows, 4)
    per_chip = 2 * rows // per_block
    pick_far = partner(after(pick_near, head_theirs))

    arrived = exchange(0, [])
    x = after(tokens_in, arrived[0]).astype(F32)
    gain = jnp.zeros((rows, width), F32)
    for member in range(members):
        gain = jnp.where(pick_own[:, None] == member, norm_gain[member][None, :], gain)
    normed = x * (1.0 / jnp.sqrt(jnp.mean(x * x, axis=2, keepdims=True) + 1e-06))
    near = jnp.stack([(normed * gain[:, None, :]).astype(BF16), upstream])
    over = over_x(near)
    arrived += [pick_far, *send[1:]]

    perm, member_sorted = sort_rows(jnp.concatenate([pick_near[rows:], pick_far[rows:]]))
    perm_own, member_sorted_own = sort_rows(jnp.concatenate([pick_own, pick_far[:rows]]))
    scalars = (
        jnp.concatenate([member_sorted, member_sorted_own]),
        jnp.stack([y_at, rank // 4]),
        jnp.concatenate([perm + 2 * rows, perm_own]),
    )

    arrived = exchange(1, arrived)
    arrived += [*scalars]

    arrived = exchange(2, arrived)
    arrived += [over]

    set_2, arrived = arrived, exchange(3, arrived)
    far = partner(after(jnp.stack([near, over]), *set_2))
    arrived += [far]
    tokens_of = (near, over, far)

    set_3, arrived = arrived, exchange(4, arrived)
    sums = chunk(
        (True, False), (0, 2 * per_chip, per_block), (0, 1), scalars,
        (after(near, *set_3), over, far), chunk_pieces(0, 1, 2), None,
    )
    arrived += [sums[0]]

    set_4 = arrived
    exchange(5, arrived)
    sums = (after(sums[0], *set_4), sums[1])
    *same, other_out, other_back = chunk(
        (False, True), (0, per_chip, per_block), (1,), scalars, tokens_of, chunk_pieces(3), sums,
        (BF16, BF16), 0,
    )
    across = jnp.stack(
        [
            (a.astype(F32) + partner(b).astype(F32)).astype(BF16)
            for a, b in zip(same, (other_out, other_back))
        ]
    )
    sums = tuple(after(a, across) for a in sums)
    across = over_x(across)
    own = (per_chip, per_chip, per_block)
    sums = chunk((False, False), own, (0,), scalars, tokens_of, chunk_pieces(3), sums, None, 0)
    out, back, packed_out, packed_back = chunk(
        (False, True), own, (0,), scalars, tokens_of, chunk_pieces(4), sums, (F32, BF16), 0
    )
    return tuple(
        finish(
            pick_own, tokens_in, upstream, norm_gain, out, back,
            partner(packed_out), partner(packed_back), across,
        )
    )


def solution(mesh):
    ranks = mesh.shape["row"]
    four = mesh.shape["feat"] == 1 and ranks % 4 == 0 and mesh.shape["grp"] == 2

    def on_device(tokens_in, upstream, member_pick, norm_gain, up_proj, down_proj):
        args = (tokens_in, upstream, member_pick, norm_gain, up_proj, down_proj)
        if four and member_pick.shape[1] == 1 and up_proj.shape[0] == 2:
            return on_device_shared(ranks, *args)
        return on_device_general(*args)

    in_specs = (
        P(("grp", "row"), None, "feat"),
        P(("grp", "row"), None, "feat"),
        P(("grp", "row"), None),
        P(),
        P(None, "row", "feat"),
        P(None, "row", "feat"),
    )
    out_specs = (
        P(("grp", "row"), None, "feat"),
        P(("grp", "row"), None, "feat"),
        P(("grp", "row"), None),
    )
    return jax.shard_map(
        on_device, mesh=mesh, in_specs=in_specs, out_specs=out_specs, check_vma=False
    )
```

```python
import functools
import math

import jax
import jax.numpy as jnp
from jax import lax
from jax.experimental import pallas as pl
from jax.experimental.pallas import tpu as pltpu
from jax.sharding import PartitionSpec as P

coef_c = math.sqrt(2.0 / math.pi)


def gelu_tanh(v):
    return 0.5 * v * (1.0 + jnp.tanh(coef_c * (v + 0.044715 * v * v * v)))


def gelu_slope(v):
    inner = jnp.tanh(coef_c * (v + 0.044715 * v * v * v))
    return 0.5 * (1.0 + inner) + 0.5 * v * (1.0 - inner * inner) * coef_c * (
        1.0 + 3.0 * 0.044715 * v * v
    )


def on_device_general(tokens_in, upstream, member_pick, norm_gain, up_proj, down_proj):
    rows, seq, half = tokens_in.shape
    count = rows * seq
    members = up_proj.shape[0]
    pick = member_pick.shape[1]
    whole_x, whole_g = (
        lax.all_gather(tokens_in, "feat", axis=2, tiled=True),
        lax.all_gather(upstream, "feat", axis=2, tiled=True),
    )
    width = whole_x.shape[2]
    flat_x = whole_x.reshape(count, width).astype(jnp.float32)
    flat_g = whole_g.reshape(count, width)
    inv_rms = 1.0 / jnp.sqrt(jnp.mean(flat_x * flat_x, axis=1, keepdims=True) + 1e-06)
    normed = flat_x * inv_rms
    labels = jnp.arange(members, dtype=jnp.int32)
    chosen = (
        jnp.sum((member_pick[:, :, None] == labels[None, None, :]).astype(jnp.float32), axis=1)
        / pick
    )
    chosen_tok = jnp.repeat(chosen, seq, axis=0)
    out_half = jnp.zeros((count, half), jnp.float32)
    back_half = jnp.zeros((count, half), jnp.float32)
    for member in range(members):
        lifted = (normed * norm_gain[member][None, :]).astype(jnp.bfloat16)
        up_full = lax.all_gather(up_proj[member], "row", axis=0, tiled=True)
        hidden = jnp.dot(lifted, up_full, preferred_element_type=jnp.float32)
        act = gelu_tanh(hidden).astype(jnp.bfloat16)
        piece = lax.all_gather(down_proj[member], "row", axis=0, tiled=True)
        block = lax.dot_general(
            act, piece, (((1,), (1,)), ((), ())), preferred_element_type=jnp.float32
        )
        grads = jnp.dot(flat_g, piece, preferred_element_type=jnp.float32)
        pre_grad = (grads * gelu_slope(hidden)).astype(jnp.bfloat16)
        in_grad = lax.dot_general(
            pre_grad, up_full, (((1,), (1,)), ((), ())), preferred_element_type=jnp.float32
        )
        weight_col = chosen_tok[:, member : member + 1]
        out_term = weight_col * block
        back_term = weight_col * norm_gain[member][None, :] * in_grad
        out_part, back_part = (
            lax.psum_scatter(
                out_term.astype(jnp.bfloat16), "feat", scatter_dimension=1, tiled=True
            ).astype(jnp.float32),
            lax.psum_scatter(
                back_term.astype(jnp.bfloat16), "feat", scatter_dimension=1, tiled=True
            ).astype(jnp.float32),
        )
        out_half = out_half + out_part
        back_half = back_half + back_part
    own_x = tokens_in.reshape(count, half).astype(jnp.float32)
    normed_half = own_x * inv_rms
    stat = lax.psum(jnp.sum(normed_half * back_half, axis=1, keepdims=True), "feat") / width
    coupling = stat * math.sqrt(width)
    own_g = upstream.reshape(count, half).astype(jnp.float32)
    value_out = (own_x + out_half).astype(jnp.bfloat16)
    grad_in = (own_g + (back_half - normed_half * stat) * inv_rms).astype(jnp.bfloat16)
    return (
        value_out.reshape(rows, seq, half),
        grad_in.reshape(rows, seq, half),
        coupling.reshape(rows, seq),
    )


VMEM_LIMIT = 40 * 1024 * 1024
BF16 = jnp.bfloat16
F32 = jnp.float32


def chunk_kernel(
    offset, kind, units, chips, sorted_ref, place_ref, perm_ref, *refs
):
    first, last = kind
    parts = len(units)
    tokens_of, refs = refs[: len(chips) + 1], refs[len(chips) + 1 :]
    pieces, refs = refs[: 2 * parts], refs[2 * parts :]
    if first:
        *outs, tokens_ref, weights_ref, sems, lifted_ref, g_ref, act_ref, pre_ref = refs
    elif last:
        out_in, back_in, *outs, tokens_ref, weights_ref, sems = refs[:-6]
        lifted_ref, g_ref, act_ref, pre_ref = refs[-6:-2]
        out_acc, back_acc = refs[-2:]
    else:
        out_in, back_in, *outs, tokens_ref, weights_ref, sems = refs[:-4]
        lifted_ref, g_ref, act_ref, pre_ref = refs[-4:]
    if not last:
        out_acc, back_acc = outs
    j = pl.program_id(0)
    rows, seq = tokens_ref.shape[2:4]
    per_block = lifted_ref.shape[0] // seq
    places = [(j + offset) * per_block + i for i in range(per_block)]
    lines, _, depth2, _ = weights_ref.shape
    depth = depth2 // 2
    starts = [sum(n for _, n in units[:part]) for part in range(parts)]

    @pl.when(j == 0)
    def _():
        y, z = place_ref[0], place_ref[1]
        copies = []
        for i, chip in enumerate(chips):
            for k, ref in enumerate((tokens_of[i], tokens_of[-1].at[chip])):
                copies.append(
                    pltpu.make_async_copy(ref, tokens_ref.at[2 * i + k], sems.at[len(copies)])
                )
        for part in range(parts):
            n = units[part][1]
            for to_y, (ref, start) in zip((y, 1 - y), pieces[2 * part : 2 * part + 2]):
                for d in range(lines):
                    from_z = lax.rem(z + lines - d, lines)
                    copies.append(
                        pltpu.make_async_copy(
                            ref.at[d, :, pl.ds(start, n)],
                            weights_ref.at[from_z, to_y, :, pl.ds(starts[part], n)],
                            sems.at[len(copies)],
                        )
                    )
        for copy in copies:
            copy.start()
        for copy in copies:
            copy.wait()

    width = lifted_ref.shape[1]
    here = [sorted_ref[at] for at in places]

    def pick_up(member):
        for i, at in enumerate(places):
            row = perm_ref[at]
            source = row // rows - 2 * chips[0]
            tokens = pl.ds(i * seq, seq)

            @pl.when(here[i] == member)
            def _():
                lifted_ref[tokens, :] = tokens_ref[source, 0, lax.rem(row, rows)]
                g_ref[tokens, :] = tokens_ref[source, 1, lax.rem(row, rows)]

            @pl.when(here[i] != member)
            def _():
                lifted_ref[tokens, :] = jnp.zeros((seq, width), BF16)
                g_ref[tokens, :] = jnp.zeros((seq, width), BF16)

    def sums(member):
        pick_up(member)
        mine = [(start, n) for (m, n), start in zip(units, starts) if m == member]
        low, high = mine[0][0], mine[-1][0] + mine[-1][1]
        for s in range(low, high, 256):
            e = min(s + 256, high)
            up = weights_ref[:, :, :depth, s:e].reshape(width, e - s)
            down = weights_ref[:, :, depth:, s:e].reshape(width, e - s)
            v = jnp.dot(lifted_ref[...], up, preferred_element_type=F32)
            grads = jnp.dot(g_ref[...], down, preferred_element_type=F32)
            square = v * v
            t = jnp.tanh(v * (coef_c + (coef_c * 0.044715) * square))
            half_v = 0.5 * v
            act_ref[:, s - low : e - low] = (half_v + half_v * t).astype(BF16)
            slope = (0.5 + 0.5 * t) + (half_v * (1.0 - t * t)) * (
                coef_c + (3.0 * coef_c * 0.044715) * square
            )
            pre_ref[:, s - low : e - low] = (grads * slope).astype(BF16)
        up = weights_ref[:, :, :depth, low:high].reshape(width, high - low)
        down = weights_ref[:, :, depth:, low:high].reshape(width, high - low)
        dims = (((1,), (1,)), ((), ()))
        return (
            lax.dot_general(act_ref[:, : high - low], down, dims, preferred_element_type=F32),
            lax.dot_general(pre_ref[:, : high - low], up, dims, preferred_element_type=F32),
        )

    for at, member in enumerate(sorted(set(m for m, _ in units))):
        used = functools.reduce(jnp.logical_or, [m == member for m in here])

        @pl.when(used)
        def _():
            out_sum, back_sum = sums(member)
            if at > 0:
                out_acc[...] += out_sum
                back_acc[...] += back_sum
            elif first:
                out_acc[...] = out_sum
                back_acc[...] = back_sum
            else:
                out_acc[...] = out_in[...] + out_sum
                back_acc[...] = back_in[...] + back_sum

        if at == 0:

            @pl.when(jnp.logical_not(used))
            def _():
                out_acc[...] = jnp.zeros(out_acc.shape, F32) if first else out_in[...]
                back_acc[...] = jnp.zeros(back_acc.shape, F32) if first else back_in[...]

    if last:
        for p, at in enumerate(places):
            row = lax.rem(perm_ref[at], 2 * rows)
            tokens = pl.ds(p * seq, seq)
            low = 0
            for to_out, to_back in zip(outs[::2], outs[1::2]):
                n = to_out.shape[0]

                @pl.when(jnp.logical_and(row >= low, row < low + n))
                def _():
                    to = jnp.clip(row - low, 0, n - 1)
                    to_out[to] = out_acc[tokens, :].astype(to_out.dtype)
                    to_back[to] = back_acc[tokens, :].astype(to_back.dtype)

                low += n


def chunk(kind, blocks, chips, scalars, tokens_of, pieces, sums, outs=None, weight=1):
    first, last = kind
    offset, number, per_block = blocks
    _, rows, seq, width = tokens_of[0].shape
    units = [(member, n) for member, n, *_ in pieces]
    lines, depth2, _ = pieces[0][2][0].shape
    hidden = sum(n for _, n in units)
    size = per_block * seq

    tok = pl.BlockSpec((size, width), lambda j, *_: (j + offset, 0))
    hbm = pl.BlockSpec(memory_space=pl.ANY)
    args = [*scalars, *(tokens_of[chip] for chip in chips), tokens_of[-1]]
    specs = [hbm] * (len(chips) + 1)
    starts = []
    for _, _, *both in pieces:
        args += [array for array, _ in both]
        starts += [start for _, start in both]
    specs += [hbm] * len(starts)
    alias = {}
    out_specs = [tok, tok]
    out_shape = [jax.ShapeDtypeStruct((4 * rows * seq, width), F32)] * 2
    scratch = [
        pltpu.VMEM((2 * len(chips), 2, rows, seq, width), BF16),
        pltpu.VMEM((lines, 2, depth2, hidden), BF16),
        pltpu.SemaphoreType.DMA((len(pieces) * 2 * lines + 2 * len(chips),)),
        pltpu.VMEM((size, width), BF16),
        pltpu.VMEM((size, width), BF16),
        pltpu.VMEM((size, hidden), BF16),
        pltpu.VMEM((size, hidden), BF16),
    ]
    if not first:
        alias = {len(args): 0, len(args) + 1: 1}
        args += list(sums)
        specs += [tok, tok]
    if last:
        alias = {}
        shape = (rows, seq, width)
        out_shape = [jax.ShapeDtypeStruct(shape, dtype) for dtype in outs for _ in range(2)]
        out_specs = [pl.BlockSpec(shape, lambda *_: (0, 0, 0))] * len(out_shape)
        scratch += [pltpu.VMEM((size, width), F32)] * 2

    def kernel(*refs):
        refs = list(refs)
        base = len(scalars) + len(chips) + 1
        for i, start in enumerate(starts):
            refs[base + i] = (refs[base + i], start)
        chunk_kernel(offset, kind, units, chips, *refs)

    return pl.pallas_call(
        kernel,
        grid_spec=pltpu.PrefetchScalarGridSpec(
            num_scalar_prefetch=len(scalars),
            grid=(number,),
            in_specs=specs,
            out_specs=out_specs,
            scratch_shapes=scratch,
        ),
        out_shape=out_shape,
        input_output_aliases=alias,
        compiler_params=pltpu.CompilerParams(vmem_limit_bytes=VMEM_LIMIT),
        cost_estimate=pl.CostEstimate(
            flops=weight * 8 * number * size * width * hidden * 2 // 3,
            bytes_accessed=weight * (4 * width * hidden + 20 * number * size * width),
            transcendentals=weight * number * size * hidden,
        ),
        name="chunk",
    )(*args)


def finish_kernel(member_ref, gain_ref, *refs):
    sources, (value_ref, grad_ref, coupling_ref), buffers, sems = (
        refs[:7], refs[7:10], refs[10:17], refs[17]
    )
    rows, seq, width = value_ref.shape
    copies = []
    for r in range(rows):
        for i, (source, buffer) in enumerate(zip(sources, buffers)):
            at = (slice(None), r) if len(source.shape) == 4 else (r,)
            copies.append(
                pltpu.make_async_copy(source.at[at], buffer.at[at], sems.at[i, r])
            )
    for copy in copies:
        copy.start()
    x_ref, g_ref, out_ref, back_ref, other_out_ref, other_back_ref, across_ref = buffers
    diagonal = lax.broadcasted_iota(jnp.int32, (seq, seq), 0) == lax.broadcasted_iota(
        jnp.int32, (seq, seq), 1
    )
    for r in range(rows):
        for copy in copies[7 * r : 7 * r + 7]:
            copy.wait()
        x = x_ref[r].astype(F32)
        inv = 1.0 / jnp.sqrt(jnp.mean(x * x, axis=1, keepdims=True) + 1e-06)
        normed = x * inv
        gain = gain_ref[pl.ds(member_ref[r], 1), :]
        back = gain * (
            back_ref[r] + other_back_ref[r].astype(F32) + across_ref[1, r].astype(F32)
        )
        stat = jnp.sum(normed * back, axis=1, keepdims=True) / width
        out = out_ref[r] + other_out_ref[r].astype(F32) + across_ref[0, r].astype(F32)
        value_ref[r] = (x + out).astype(BF16)
        grad_ref[r] = (g_ref[r].astype(F32) + (back - normed * stat) * inv).astype(BF16)
        line = jnp.sum(jnp.where(diagonal, stat, 0.0), axis=0, keepdims=True)
        coupling_ref[pl.ds(r, 1), :] = line * math.sqrt(width)


def finish(member_own, gain, *sources):
    rows, seq, width = sources[0].shape
    vmem = pl.BlockSpec(memory_space=pltpu.VMEM)
    return pl.pallas_call(
        finish_kernel,
        in_specs=[pl.BlockSpec(memory_space=pltpu.SMEM), vmem]
        + [pl.BlockSpec(memory_space=pl.ANY)] * 7,
        out_specs=[vmem] * 3,
        out_shape=[
            jax.ShapeDtypeStruct((rows, seq, width), BF16),
            jax.ShapeDtypeStruct((rows, seq, width), BF16),
            jax.ShapeDtypeStruct((rows, seq), F32),
        ],
        scratch_shapes=[pltpu.VMEM(a.shape, a.dtype) for a in sources]
        + [pltpu.SemaphoreType.DMA((7, rows))],
        compiler_params=pltpu.CompilerParams(vmem_limit_bytes=VMEM_LIMIT // 2),
        name="finish",
    )(member_own, gain, *sources)


def sort_rows(picks):
    index = jnp.arange(picks.shape[0], dtype=jnp.int32)
    before = (picks[None, :] < picks[:, None]) | (
        (picks[None, :] == picks[:, None]) & (index[None, :] < index[:, None])
    )
    pos = jnp.sum(before.astype(jnp.int32), axis=1)
    at = pos[None, :] == index[:, None]
    perm = jnp.sum(jnp.where(at, index[None, :], 0), axis=1)
    return perm, jnp.sum(jnp.where(at, picks[None, :], 0), axis=1)


def on_device_shared(ranks, tokens_in, upstream, member_pick, norm_gain, up_proj, down_proj):
    rows, seq, width = tokens_in.shape
    members, depth, hidden = up_proj.shape
    rank = lax.axis_index("row")
    core = lax.rem(rank, 2)
    x_at = lax.axis_index("grp")
    y_at = lax.rem(rank // 2, 2)
    lines = ranks // 4

    def partner(a):
        return lax.ppermute(a, "row", [(i, i ^ 1) for i in range(ranks)])

    def over_y(a):
        return lax.ppermute(a, "row", [(i, i ^ 2) for i in range(ranks)])

    def over_x(a):
        return lax.ppermute(a, "grp", [(0, 1), (1, 0)])

    def shift_z(a, d):
        return lax.ppermute(a, "row", [(i, (i + 4 * d) % ranks) for i in range(ranks)])

    def after(a, *others):
        return lax.optimization_barrier((a, *others))[0]

    unit = hidden // 32
    quarter, half = 7 * unit, 2 * unit
    both = jnp.stack([up_proj, down_proj], axis=1)

    def units_of(c):
        return jnp.concatenate(
            [
                lax.dynamic_slice_in_dim(both, (2 * x_at + c) * quarter, quarter, 3),
                lax.dynamic_slice_in_dim(both, 4 * quarter + c * half, half, 3),
            ],
            axis=3,
        )

    def both_cores(mine, theirs):
        even = core == 0
        whole = jnp.concatenate(
            [jnp.where(even, mine, theirs), jnp.where(even, theirs, mine)], axis=2
        )
        return whole.reshape(mine.shape[0], 4 * depth, mine.shape[3])

    def head_of(c):
        at = (2 * x_at + c) * quarter
        return jnp.stack(
            [lax.dynamic_slice(a, (0, 0, at), (1, depth, 2 * unit)) for a in (up_proj, down_proj)],
            axis=1,
        )

    head_theirs = partner(head_of(1 - core))
    shard_head = both_cores(head_of(core), head_theirs)
    theirs = partner(after(units_of(1 - core), head_theirs))
    shard = both_cores(units_of(core), theirs)

    groups = [
        [(0, 0, 2 * unit)],
        [(0, 2 * unit, 4 * unit)],
        [(0, 6 * unit, unit), (1, 0, 3 * unit)],
        [(1, 3 * unit, 4 * unit)],
        [(0, quarter, half), (1, quarter, half)],
    ]
    send = [shard_head[0]] + [
        jnp.concatenate([shard[m, :, at : at + n] for m, at, n in group], axis=1)
        for group in groups[1:]
    ]
    here, there, shifted = [], [], []

    def along_z(step, *waits):
        results = []
        for d in range(1, lines):
            mine = send[step]
            if step:
                mine = after(mine, *shifted[-1], *waits)
            results.append(shift_z(mine, d))
        shifted.append(results)
        here.append(jnp.stack([send[step], *results]))

    def across_y(step, *waits):
        there.append(over_y(after(here[step], *there[-1:], *waits)))

    def chunk_pieces(*at):
        pieces = []
        for group in at:
            start = 0
            for member, _, n in groups[group]:
                pieces.append((member, n, (here[group], start), (there[group], start)))
                start += n
        return pieces

    per_block = math.gcd(2 * rows, 4)
    per_chip = 2 * rows // per_block
    along_z(0)
    pick_own = member_pick[:, 0]
    pick_near = jnp.concatenate([pick_own, over_x(after(pick_own, send[0]))])
    x = after(tokens_in, shifted[0][0]).astype(F32)
    gain = jnp.zeros((rows, width), F32)
    for member in range(members):
        gain = jnp.where(pick_own[:, None] == member, norm_gain[member][None, :], gain)
    normed = x * (1.0 / jnp.sqrt(jnp.mean(x * x, axis=2, keepdims=True) + 1e-06))
    near = jnp.stack([(normed * gain[:, None, :]).astype(BF16), upstream])
    over = over_x(near)
    along_z(1, pick_near, *send[2:])
    across_y(0)
    pick_far = partner(after(pick_near, shifted[0][-1]))

    perm, member_sorted = sort_rows(jnp.concatenate([pick_near[rows:], pick_far[rows:]]))
    perm_own, member_sorted_own = sort_rows(jnp.concatenate([pick_own, pick_far[:rows]]))
    scalars = (
        jnp.concatenate([member_sorted, member_sorted_own]),
        jnp.stack([y_at, rank // 4]),
        jnp.concatenate([perm + 2 * rows, perm_own]),
    )

    along_z(2, there[0], *scalars)
    across_y(1)
    along_z(3, there[1], over)
    across_y(2)
    far = partner(after(jnp.stack([near, over]), *shifted[2], there[1]))
    along_z(4, there[2], far)
    across_y(3)
    tokens_of = (near, over, far)
    sums = chunk(
        (True, False), (0, 2 * per_chip, per_block), (0, 1), scalars,
        (after(near, *shifted[3]), over, far), chunk_pieces(0, 1, 2), None,
    )
    across_y(4)
    sums = (after(sums[0], *shifted[4]), sums[1])
    *same, other_out, other_back = chunk(
        (False, True), (0, per_chip, per_block), (1,), scalars, tokens_of, chunk_pieces(3), sums,
        (BF16, BF16), 0,
    )
    across = jnp.stack(
        [
            (a.astype(F32) + partner(b).astype(F32)).astype(BF16)
            for a, b in zip(same, (other_out, other_back))
        ]
    )
    sums = tuple(after(a, across) for a in sums)
    across = over_x(across)
    own = (per_chip, per_chip, per_block)
    sums = chunk((False, False), own, (0,), scalars, tokens_of, chunk_pieces(3), sums, None, 0)
    out, back, packed_out, packed_back = chunk(
        (False, True), own, (0,), scalars, tokens_of, chunk_pieces(4), sums, (F32, BF16), 0
    )
    return tuple(
        finish(
            pick_own, norm_gain, tokens_in, upstream, out, back,
            partner(packed_out), partner(packed_back), across,
        )
    )


def solution(mesh):
    ranks = mesh.shape["row"]
    four = mesh.shape["feat"] == 1 and ranks % 4 == 0 and mesh.shape["grp"] == 2

    def on_device(tokens_in, upstream, member_pick, norm_gain, up_proj, down_proj):
        args = (tokens_in, upstream, member_pick, norm_gain, up_proj, down_proj)
        if four and member_pick.shape[1] == 1 and up_proj.shape[0] == 2:
            return on_device_shared(ranks, *args)
        return on_device_general(*args)

    in_specs = (
        P(("grp", "row"), None, "feat"),
        P(("grp", "row"), None, "feat"),
        P(("grp", "row"), None),
        P(),
        P(None, "row", "feat"),
        P(None, "row", "feat"),
    )
    out_specs = (
        P(("grp", "row"), None, "feat"),
        P(("grp", "row"), None, "feat"),
        P(("grp", "row"), None),
    )
    return jax.shard_map(
        on_device, mesh=mesh, in_specs=in_specs, out_specs=out_specs, check_vma=False
    )
```

```python
import functools
import math

import jax
import jax.numpy as jnp
from jax import lax
from jax.experimental import pallas as pl
from jax.experimental.pallas import tpu as pltpu
from jax.sharding import PartitionSpec as P

coef_c = math.sqrt(2.0 / math.pi)


def gelu_tanh(v):
    return 0.5 * v * (1.0 + jnp.tanh(coef_c * (v + 0.044715 * v * v * v)))


def gelu_slope(v):
    inner = jnp.tanh(coef_c * (v + 0.044715 * v * v * v))
    return 0.5 * (1.0 + inner) + 0.5 * v * (1.0 - inner * inner) * coef_c * (
        1.0 + 3.0 * 0.044715 * v * v
    )


def on_device_general(tokens_in, upstream, member_pick, norm_gain, up_proj, down_proj):
    rows, seq, half = tokens_in.shape
    count = rows * seq
    members = up_proj.shape[0]
    pick = member_pick.shape[1]
    whole_x, whole_g = (
        lax.all_gather(tokens_in, "feat", axis=2, tiled=True),
        lax.all_gather(upstream, "feat", axis=2, tiled=True),
    )
    width = whole_x.shape[2]
    flat_x = whole_x.reshape(count, width).astype(jnp.float32)
    flat_g = whole_g.reshape(count, width)
    inv_rms = 1.0 / jnp.sqrt(jnp.mean(flat_x * flat_x, axis=1, keepdims=True) + 1e-06)
    normed = flat_x * inv_rms
    labels = jnp.arange(members, dtype=jnp.int32)
    chosen = (
        jnp.sum((member_pick[:, :, None] == labels[None, None, :]).astype(jnp.float32), axis=1)
        / pick
    )
    chosen_tok = jnp.repeat(chosen, seq, axis=0)
    out_half = jnp.zeros((count, half), jnp.float32)
    back_half = jnp.zeros((count, half), jnp.float32)
    for member in range(members):
        lifted = (normed * norm_gain[member][None, :]).astype(jnp.bfloat16)
        up_full = lax.all_gather(up_proj[member], "row", axis=0, tiled=True)
        hidden = jnp.dot(lifted, up_full, preferred_element_type=jnp.float32)
        act = gelu_tanh(hidden).astype(jnp.bfloat16)
        piece = lax.all_gather(down_proj[member], "row", axis=0, tiled=True)
        block = lax.dot_general(
            act, piece, (((1,), (1,)), ((), ())), preferred_element_type=jnp.float32
        )
        grads = jnp.dot(flat_g, piece, preferred_element_type=jnp.float32)
        pre_grad = (grads * gelu_slope(hidden)).astype(jnp.bfloat16)
        in_grad = lax.dot_general(
            pre_grad, up_full, (((1,), (1,)), ((), ())), preferred_element_type=jnp.float32
        )
        weight_col = chosen_tok[:, member : member + 1]
        out_term = weight_col * block
        back_term = weight_col * norm_gain[member][None, :] * in_grad
        out_part, back_part = (
            lax.psum_scatter(
                out_term.astype(jnp.bfloat16), "feat", scatter_dimension=1, tiled=True
            ).astype(jnp.float32),
            lax.psum_scatter(
                back_term.astype(jnp.bfloat16), "feat", scatter_dimension=1, tiled=True
            ).astype(jnp.float32),
        )
        out_half = out_half + out_part
        back_half = back_half + back_part
    own_x = tokens_in.reshape(count, half).astype(jnp.float32)
    normed_half = own_x * inv_rms
    stat = lax.psum(jnp.sum(normed_half * back_half, axis=1, keepdims=True), "feat") / width
    coupling = stat * math.sqrt(width)
    own_g = upstream.reshape(count, half).astype(jnp.float32)
    value_out = (own_x + out_half).astype(jnp.bfloat16)
    grad_in = (own_g + (back_half - normed_half * stat) * inv_rms).astype(jnp.bfloat16)
    return (
        value_out.reshape(rows, seq, half),
        grad_in.reshape(rows, seq, half),
        coupling.reshape(rows, seq),
    )


VMEM_LIMIT = 40 * 1024 * 1024
BF16 = jnp.bfloat16
F32 = jnp.float32


def chunk_kernel(
    offset, kind, units, chips, sorted_ref, place_ref, perm_ref, *refs
):
    first, last = kind
    parts = len(units)
    tokens_of, refs = refs[: len(chips) + 1], refs[len(chips) + 1 :]
    pieces, refs = refs[: 2 * parts], refs[2 * parts :]
    if first:
        *outs, tokens_ref, weights_ref, sems, lifted_ref, g_ref, act_ref, pre_ref = refs
    elif last:
        out_in, back_in, *outs, tokens_ref, weights_ref, sems = refs[:-6]
        lifted_ref, g_ref, act_ref, pre_ref = refs[-6:-2]
        out_acc, back_acc = refs[-2:]
    else:
        out_in, back_in, *outs, tokens_ref, weights_ref, sems = refs[:-4]
        lifted_ref, g_ref, act_ref, pre_ref = refs[-4:]
    if not last:
        out_acc, back_acc = outs
    j = pl.program_id(0)
    rows, seq = tokens_ref.shape[2:4]
    per_block = lifted_ref.shape[0] // seq
    places = [(j + offset) * per_block + i for i in range(per_block)]
    lines, _, depth2, _ = weights_ref.shape
    depth = depth2 // 2
    starts = [sum(n for _, n in units[:part]) for part in range(parts)]

    @pl.when(j == 0)
    def _():
        y, z = place_ref[0], place_ref[1]
        copies = []
        for i, chip in enumerate(chips):
            for k, ref in enumerate((tokens_of[i], tokens_of[-1].at[chip])):
                copies.append(
                    pltpu.make_async_copy(ref, tokens_ref.at[2 * i + k], sems.at[len(copies)])
                )
        for part in range(parts):
            n = units[part][1]
            for to_y, (ref, start) in zip((y, 1 - y), pieces[2 * part : 2 * part + 2]):
                for d in range(lines):
                    from_z = lax.rem(z + lines - d, lines)
                    copies.append(
                        pltpu.make_async_copy(
                            ref.at[d, :, pl.ds(start, n)],
                            weights_ref.at[from_z, to_y, :, pl.ds(starts[part], n)],
                            sems.at[len(copies)],
                        )
                    )
        for copy in copies:
            copy.start()
        for copy in copies:
            copy.wait()

    width = lifted_ref.shape[1]
    here = [sorted_ref[at] for at in places]

    def pick_up(member):
        for i, at in enumerate(places):
            row = perm_ref[at]
            source = row // rows - 2 * chips[0]
            tokens = pl.ds(i * seq, seq)

            @pl.when(here[i] == member)
            def _():
                lifted_ref[tokens, :] = tokens_ref[source, 0, lax.rem(row, rows)]
                g_ref[tokens, :] = tokens_ref[source, 1, lax.rem(row, rows)]

            @pl.when(here[i] != member)
            def _():
                lifted_ref[tokens, :] = jnp.zeros((seq, width), BF16)
                g_ref[tokens, :] = jnp.zeros((seq, width), BF16)

    def sums(member):
        pick_up(member)
        mine = [(start, n) for (m, n), start in zip(units, starts) if m == member]
        low, high = mine[0][0], mine[-1][0] + mine[-1][1]
        for s in range(low, high, 256):
            e = min(s + 256, high)
            up = weights_ref[:, :, :depth, s:e].reshape(width, e - s)
            down = weights_ref[:, :, depth:, s:e].reshape(width, e - s)
            v = jnp.dot(lifted_ref[...], up, preferred_element_type=F32)
            grads = jnp.dot(g_ref[...], down, preferred_element_type=F32)
            square = v * v
            t = jnp.tanh(v * (coef_c + (coef_c * 0.044715) * square))
            half_v = 0.5 * v
            act_ref[:, s - low : e - low] = (half_v + half_v * t).astype(BF16)
            slope = (0.5 + 0.5 * t) + (half_v * (1.0 - t * t)) * (
                coef_c + (3.0 * coef_c * 0.044715) * square
            )
            pre_ref[:, s - low : e - low] = (grads * slope).astype(BF16)
        up = weights_ref[:, :, :depth, low:high].reshape(width, high - low)
        down = weights_ref[:, :, depth:, low:high].reshape(width, high - low)
        dims = (((1,), (1,)), ((), ()))
        return (
            lax.dot_general(act_ref[:, : high - low], down, dims, preferred_element_type=F32),
            lax.dot_general(pre_ref[:, : high - low], up, dims, preferred_element_type=F32),
        )

    for at, member in enumerate(sorted(set(m for m, _ in units))):
        used = functools.reduce(jnp.logical_or, [m == member for m in here])

        @pl.when(used)
        def _():
            out_sum, back_sum = sums(member)
            if at > 0:
                out_acc[...] += out_sum
                back_acc[...] += back_sum
            elif first:
                out_acc[...] = out_sum
                back_acc[...] = back_sum
            else:
                out_acc[...] = out_in[...] + out_sum
                back_acc[...] = back_in[...] + back_sum

        if at == 0:

            @pl.when(jnp.logical_not(used))
            def _():
                out_acc[...] = jnp.zeros(out_acc.shape, F32) if first else out_in[...]
                back_acc[...] = jnp.zeros(back_acc.shape, F32) if first else back_in[...]

    if last:
        for p, at in enumerate(places):
            row = lax.rem(perm_ref[at], 2 * rows)
            tokens = pl.ds(p * seq, seq)
            low = 0
            for to_out, to_back in zip(outs[::2], outs[1::2]):
                n = to_out.shape[0]

                @pl.when(jnp.logical_and(row >= low, row < low + n))
                def _():
                    to = jnp.clip(row - low, 0, n - 1)
                    to_out[to] = out_acc[tokens, :].astype(to_out.dtype)
                    to_back[to] = back_acc[tokens, :].astype(to_back.dtype)

                low += n


def chunk(kind, blocks, chips, scalars, tokens_of, pieces, sums, outs=None, weight=1):
    first, last = kind
    offset, number, per_block = blocks
    _, rows, seq, width = tokens_of[0].shape
    units = [(member, n) for member, n, *_ in pieces]
    lines, depth2, _ = pieces[0][2][0].shape
    hidden = sum(n for _, n in units)
    size = per_block * seq

    tok = pl.BlockSpec((size, width), lambda j, *_: (j, 0))
    hbm = pl.BlockSpec(memory_space=pl.ANY)
    args = [*scalars, *(tokens_of[chip] for chip in chips), tokens_of[-1]]
    specs = [hbm] * (len(chips) + 1)
    starts = []
    for _, _, *both in pieces:
        args += [array for array, _ in both]
        starts += [start for _, start in both]
    specs += [hbm] * len(starts)
    alias = {}
    out_specs = [tok, tok]
    out_shape = [jax.ShapeDtypeStruct((number * size, width), F32)] * 2
    scratch = [
        pltpu.VMEM((2 * len(chips), 2, rows, seq, width), BF16),
        pltpu.VMEM((lines, 2, depth2, hidden), BF16),
        pltpu.SemaphoreType.DMA((len(pieces) * 2 * lines + 2 * len(chips),)),
        pltpu.VMEM((size, width), BF16),
        pltpu.VMEM((size, width), BF16),
        pltpu.VMEM((size, hidden), BF16),
        pltpu.VMEM((size, hidden), BF16),
    ]
    if not first:
        alias = {len(args): 0, len(args) + 1: 1}
        args += list(sums)
        specs += [tok, tok]
    if last:
        alias = {}
        shape = (rows, seq, width)
        out_shape = [jax.ShapeDtypeStruct(shape, dtype) for dtype in outs for _ in range(2)]
        out_specs = [pl.BlockSpec(shape, lambda *_: (0, 0, 0))] * len(out_shape)
        scratch += [pltpu.VMEM((size, width), F32)] * 2

    def kernel(*refs):
        refs = list(refs)
        base = len(scalars) + len(chips) + 1
        for i, start in enumerate(starts):
            refs[base + i] = (refs[base + i], start)
        chunk_kernel(offset, kind, units, chips, *refs)

    return pl.pallas_call(
        kernel,
        grid_spec=pltpu.PrefetchScalarGridSpec(
            num_scalar_prefetch=len(scalars),
            grid=(number,),
            in_specs=specs,
            out_specs=out_specs,
            scratch_shapes=scratch,
        ),
        out_shape=out_shape,
        input_output_aliases=alias,
        compiler_params=pltpu.CompilerParams(vmem_limit_bytes=VMEM_LIMIT),
        cost_estimate=pl.CostEstimate(
            flops=weight * 8 * number * size * width * hidden * 2 // 3,
            bytes_accessed=weight * (4 * width * hidden + 20 * number * size * width),
            transcendentals=weight * number * size * hidden,
        ),
        name="chunk",
    )(*args)


def finish_kernel(
    member_ref, x_ref, g_ref, gain_ref, out_ref, back_ref, other_out_ref, other_back_ref,
    across_ref, value_ref, grad_ref, coupling_ref,
):
    rows, seq, width = x_ref.shape
    diagonal = lax.broadcasted_iota(jnp.int32, (seq, seq), 0) == lax.broadcasted_iota(
        jnp.int32, (seq, seq), 1
    )
    for r in range(rows):
        x = x_ref[r].astype(F32)
        inv = 1.0 / jnp.sqrt(jnp.mean(x * x, axis=1, keepdims=True) + 1e-06)
        normed = x * inv
        gain = gain_ref[pl.ds(member_ref[pl.program_id(0) * rows + r], 1), :]
        back = gain * (
            back_ref[r] + other_back_ref[r].astype(F32) + across_ref[1, r].astype(F32)
        )
        stat = jnp.sum(normed * back, axis=1, keepdims=True) / width
        out = out_ref[r] + other_out_ref[r].astype(F32) + across_ref[0, r].astype(F32)
        value_ref[r] = (x + out).astype(BF16)
        grad_ref[r] = (g_ref[r].astype(F32) + (back - normed * stat) * inv).astype(BF16)
        line = jnp.sum(jnp.where(diagonal, stat, 0.0), axis=0, keepdims=True)
        coupling_ref[pl.ds(pl.program_id(0) * rows + r, 1), :] = line * math.sqrt(width)


def finish(member_own, x, g, gain, *sums):
    rows, seq, width = x.shape
    step = math.gcd(rows, 2)
    row = pl.BlockSpec((step, seq, width), lambda r, mem: (r, 0, 0))
    two = pl.BlockSpec((2, step, seq, width), lambda r, mem: (0, r, 0, 0))
    return pl.pallas_call(
        finish_kernel,
        grid_spec=pltpu.PrefetchScalarGridSpec(
            num_scalar_prefetch=1,
            grid=(rows // step,),
            in_specs=[
                row, row, pl.BlockSpec(gain.shape, lambda r, mem: (0, 0)), row, row, row, row, two
            ],
            out_specs=[row, row, pl.BlockSpec((rows, seq), lambda r, mem: (0, 0))],
        ),
        out_shape=[
            jax.ShapeDtypeStruct((rows, seq, width), BF16),
            jax.ShapeDtypeStruct((rows, seq, width), BF16),
            jax.ShapeDtypeStruct((rows, seq), F32),
        ],
        compiler_params=pltpu.CompilerParams(vmem_limit_bytes=VMEM_LIMIT // 2),
        name="finish",
    )(member_own, x, g, gain, *sums)


def sort_rows(picks):
    index = jnp.arange(picks.shape[0], dtype=jnp.int32)
    before = (picks[None, :] < picks[:, None]) | (
        (picks[None, :] == picks[:, None]) & (index[None, :] < index[:, None])
    )
    pos = jnp.sum(before.astype(jnp.int32), axis=1)
    at = pos[None, :] == index[:, None]
    perm = jnp.sum(jnp.where(at, index[None, :], 0), axis=1)
    return perm, jnp.sum(jnp.where(at, picks[None, :], 0), axis=1)


def on_device_shared(ranks, tokens_in, upstream, member_pick, norm_gain, up_proj, down_proj):
    rows, seq, width = tokens_in.shape
    members, depth, hidden = up_proj.shape
    rank = lax.axis_index("row")
    core = lax.rem(rank, 2)
    x_at = lax.axis_index("grp")
    y_at = lax.rem(rank // 2, 2)
    lines = ranks // 4

    def partner(a):
        return lax.ppermute(a, "row", [(i, i ^ 1) for i in range(ranks)])

    def over_y(a):
        return lax.ppermute(a, "row", [(i, i ^ 2) for i in range(ranks)])

    def over_x(a):
        return lax.ppermute(a, "grp", [(0, 1), (1, 0)])

    def shift_z(a, d):
        return lax.ppermute(a, "row", [(i, (i + 4 * d) % ranks) for i in range(ranks)])

    def after(a, *others):
        return lax.optimization_barrier((a, *others))[0]

    unit = hidden // 32
    quarter, half = 7 * unit, 2 * unit

    def units_of(c, both):
        return jnp.concatenate(
            [
                lax.dynamic_slice_in_dim(both, (2 * x_at + c) * quarter, quarter, 3),
                lax.dynamic_slice_in_dim(both, 4 * quarter + c * half, half, 3),
            ],
            axis=3,
        )

    def both_cores(mine, theirs):
        even = core == 0
        whole = jnp.concatenate(
            [jnp.where(even, mine, theirs), jnp.where(even, theirs, mine)], axis=2
        )
        return whole.reshape(mine.shape[0], 4 * depth, mine.shape[3])

    def head_of(c):
        at = (2 * x_at + c) * quarter
        return jnp.stack(
            [lax.dynamic_slice(a, (0, 0, at), (1, depth, 2 * unit)) for a in (up_proj, down_proj)],
            axis=1,
        )

    head_theirs = partner(head_of(1 - core))
    shard_head = both_cores(head_of(core), head_theirs)
    both = jnp.stack([after(up_proj, shard_head), down_proj], axis=1)
    theirs = partner(units_of(1 - core, both))
    shard = both_cores(units_of(core, both), theirs)

    groups = [
        [(0, 0, 2 * unit)],
        [(0, 2 * unit, 4 * unit)],
        [(0, 6 * unit, unit), (1, 0, 3 * unit)],
        [(1, 3 * unit, 4 * unit)],
        [(0, quarter, half), (1, quarter, half)],
    ]
    send = [shard_head[0]] + [
        jnp.concatenate([shard[m, :, at : at + n] for m, at, n in group], axis=1)
        for group in groups[1:]
    ]
    here, there, shifted = [], [], []

    def along_z(step, *waits):
        results = []
        for d in range(1, lines):
            mine = send[step]
            if step:
                mine = after(mine, *shifted[-1], *waits)
            results.append(shift_z(mine, d))
        shifted.append(results)
        here.append(jnp.stack([send[step], *results]))

    def across_y(step, *waits):
        there.append(over_y(after(here[step], *there[-1:], *waits)))

    def chunk_pieces(*at):
        pieces = []
        for group in at:
            start = 0
            for member, _, n in groups[group]:
                pieces.append((member, n, (here[group], start), (there[group], start)))
                start += n
        return pieces

    per_block = math.gcd(2 * rows, 4)
    per_chip = 2 * rows // per_block
    along_z(0)
    pick_own = member_pick[:, 0]
    pick_near = jnp.concatenate([pick_own, over_x(after(pick_own, send[0]))])
    x = after(tokens_in, shifted[0][0]).astype(F32)
    gain = jnp.zeros((rows, width), F32)
    for member in range(members):
        gain = jnp.where(pick_own[:, None] == member, norm_gain[member][None, :], gain)
    normed = x * (1.0 / jnp.sqrt(jnp.mean(x * x, axis=2, keepdims=True) + 1e-06))
    near = jnp.stack([(normed * gain[:, None, :]).astype(BF16), upstream])
    over = over_x(near)
    along_z(1, pick_near, *send[2:])
    across_y(0)
    pick_far = partner(after(pick_near, shifted[0][-1]))

    perm, member_sorted = sort_rows(jnp.concatenate([pick_near[rows:], pick_far[rows:]]))
    perm_own, member_sorted_own = sort_rows(jnp.concatenate([pick_own, pick_far[:rows]]))
    scalars = (
        jnp.concatenate([member_sorted, member_sorted_own]),
        jnp.stack([y_at, rank // 4]),
        jnp.concatenate([perm + 2 * rows, perm_own]),
    )

    along_z(2, there[0], *scalars)
    across_y(1)
    along_z(3, there[1], over)
    across_y(2)
    far = partner(after(jnp.stack([near, over]), *shifted[2], there[1]))
    along_z(4, there[2], far)
    across_y(3)
    tokens_of = (near, over, far)
    other_rows, own_rows = (0, per_chip, per_block), (per_chip, per_chip, per_block)
    sums = chunk(
        (True, False), other_rows, (1,), scalars,
        (near, after(over, *shifted[3]), far), chunk_pieces(0, 1, 2), None,
    )
    across_y(4)
    sums = (after(sums[0], *shifted[4]), sums[1])
    *same, other_out, other_back = chunk(
        (False, True), other_rows, (1,), scalars, tokens_of, chunk_pieces(3), sums,
        (BF16, BF16), 0,
    )
    across = jnp.stack(
        [
            (a.astype(F32) + partner(b).astype(F32)).astype(BF16)
            for a, b in zip(same, (other_out, other_back))
        ]
    )
    tokens_of = (after(near, across), over, far)
    across = over_x(across)
    sums = chunk(
        (True, False), own_rows, (0,), scalars, tokens_of, chunk_pieces(0, 1, 2, 3), None, None, 0
    )
    out, back, packed_out, packed_back = chunk(
        (False, True), own_rows, (0,), scalars, tokens_of, chunk_pieces(4), sums, (F32, BF16), 0
    )
    return tuple(
        finish(
            pick_own, tokens_in, upstream, norm_gain, out, back,
            partner(packed_out), partner(packed_back), across,
        )
    )


def solution(mesh):
    ranks = mesh.shape["row"]
    four = mesh.shape["feat"] == 1 and ranks % 4 == 0 and mesh.shape["grp"] == 2

    def on_device(tokens_in, upstream, member_pick, norm_gain, up_proj, down_proj):
        args = (tokens_in, upstream, member_pick, norm_gain, up_proj, down_proj)
        if four and member_pick.shape[1] == 1 and up_proj.shape[0] == 2:
            return on_device_shared(ranks, *args)
        return on_device_general(*args)

    in_specs = (
        P(("grp", "row"), None, "feat"),
        P(("grp", "row"), None, "feat"),
        P(("grp", "row"), None),
        P(),
        P(None, "row", "feat"),
        P(None, "row", "feat"),
    )
    out_specs = (
        P(("grp", "row"), None, "feat"),
        P(("grp", "row"), None, "feat"),
        P(("grp", "row"), None),
    )
    return jax.shard_map(
        on_device, mesh=mesh, in_specs=in_specs, out_specs=out_specs, check_vma=False
    )
```

```python
import functools
import math

import jax
import jax.numpy as jnp
from jax import lax
from jax.experimental import pallas as pl
from jax.experimental.pallas import tpu as pltpu
from jax.sharding import PartitionSpec as P

coef_c = math.sqrt(2.0 / math.pi)


def gelu_tanh(v):
    return 0.5 * v * (1.0 + jnp.tanh(coef_c * (v + 0.044715 * v * v * v)))


def gelu_slope(v):
    inner = jnp.tanh(coef_c * (v + 0.044715 * v * v * v))
    return 0.5 * (1.0 + inner) + 0.5 * v * (1.0 - inner * inner) * coef_c * (
        1.0 + 3.0 * 0.044715 * v * v
    )


def on_device_general(tokens_in, upstream, member_pick, norm_gain, up_proj, down_proj):
    rows, seq, half = tokens_in.shape
    count = rows * seq
    members = up_proj.shape[0]
    pick = member_pick.shape[1]
    whole_x, whole_g = (
        lax.all_gather(tokens_in, "feat", axis=2, tiled=True),
        lax.all_gather(upstream, "feat", axis=2, tiled=True),
    )
    width = whole_x.shape[2]
    flat_x = whole_x.reshape(count, width).astype(jnp.float32)
    flat_g = whole_g.reshape(count, width)
    inv_rms = 1.0 / jnp.sqrt(jnp.mean(flat_x * flat_x, axis=1, keepdims=True) + 1e-06)
    normed = flat_x * inv_rms
    labels = jnp.arange(members, dtype=jnp.int32)
    chosen = (
        jnp.sum((member_pick[:, :, None] == labels[None, None, :]).astype(jnp.float32), axis=1)
        / pick
    )
    chosen_tok = jnp.repeat(chosen, seq, axis=0)
    out_half = jnp.zeros((count, half), jnp.float32)
    back_half = jnp.zeros((count, half), jnp.float32)
    for member in range(members):
        lifted = (normed * norm_gain[member][None, :]).astype(jnp.bfloat16)
        up_full = lax.all_gather(up_proj[member], "row", axis=0, tiled=True)
        hidden = jnp.dot(lifted, up_full, preferred_element_type=jnp.float32)
        act = gelu_tanh(hidden).astype(jnp.bfloat16)
        piece = lax.all_gather(down_proj[member], "row", axis=0, tiled=True)
        block = lax.dot_general(
            act, piece, (((1,), (1,)), ((), ())), preferred_element_type=jnp.float32
        )
        grads = jnp.dot(flat_g, piece, preferred_element_type=jnp.float32)
        pre_grad = (grads * gelu_slope(hidden)).astype(jnp.bfloat16)
        in_grad = lax.dot_general(
            pre_grad, up_full, (((1,), (1,)), ((), ())), preferred_element_type=jnp.float32
        )
        weight_col = chosen_tok[:, member : member + 1]
        out_term = weight_col * block
        back_term = weight_col * norm_gain[member][None, :] * in_grad
        out_part, back_part = (
            lax.psum_scatter(
                out_term.astype(jnp.bfloat16), "feat", scatter_dimension=1, tiled=True
            ).astype(jnp.float32),
            lax.psum_scatter(
                back_term.astype(jnp.bfloat16), "feat", scatter_dimension=1, tiled=True
            ).astype(jnp.float32),
        )
        out_half = out_half + out_part
        back_half = back_half + back_part
    own_x = tokens_in.reshape(count, half).astype(jnp.float32)
    normed_half = own_x * inv_rms
    stat = lax.psum(jnp.sum(normed_half * back_half, axis=1, keepdims=True), "feat") / width
    coupling = stat * math.sqrt(width)
    own_g = upstream.reshape(count, half).astype(jnp.float32)
    value_out = (own_x + out_half).astype(jnp.bfloat16)
    grad_in = (own_g + (back_half - normed_half * stat) * inv_rms).astype(jnp.bfloat16)
    return (
        value_out.reshape(rows, seq, half),
        grad_in.reshape(rows, seq, half),
        coupling.reshape(rows, seq),
    )


VMEM_LIMIT = 40 * 1024 * 1024
BF16 = jnp.bfloat16
F32 = jnp.float32


def chunk_kernel(
    offset, kind, units, chips, sources, sorted_ref, place_ref, perm_ref, *refs
):
    first, last = kind
    parts = len(units)
    arrays = 1 + max(i for block in sources for i, _ in block)
    tokens_of, refs = refs[: len(chips) + 1], refs[len(chips) + 1 :]
    here_refs, there_refs, refs = refs[:arrays], refs[arrays : 2 * arrays], refs[2 * arrays :]
    if first:
        *outs, tokens_ref, weights_ref, sems, lifted_ref, g_ref, act_ref, pre_ref = refs
    elif last:
        out_in, back_in, *outs, tokens_ref, weights_ref, sems = refs[:-6]
        lifted_ref, g_ref, act_ref, pre_ref = refs[-6:-2]
        out_acc, back_acc = refs[-2:]
    else:
        out_in, back_in, *outs, tokens_ref, weights_ref, sems = refs[:-4]
        lifted_ref, g_ref, act_ref, pre_ref = refs[-4:]
    if not last:
        out_acc, back_acc = outs
    j = pl.program_id(0)
    rows, seq = tokens_ref.shape[2:4]
    per_block = lifted_ref.shape[0] // seq
    places = [(j + offset) * per_block + i for i in range(per_block)]
    lines, _, depth2, _ = weights_ref.shape
    depth = depth2 // 2
    starts = [sum(n for _, n in units[:part]) for part in range(parts)]

    @pl.when(j == 0)
    def _():
        y, z = place_ref[0], place_ref[1]
        copies = []
        for i, chip in enumerate(chips):
            for k, ref in enumerate((tokens_of[i], tokens_of[-1].at[chip])):
                copies.append(
                    pltpu.make_async_copy(ref, tokens_ref.at[2 * i + k], sems.at[len(copies)])
                )
        for at, block in enumerate(sources):
            for d, (i, place) in enumerate(block):
                from_z = lax.rem(z + lines - d, lines)
                for to_y, ref in ((y, here_refs[i]), (1 - y, there_refs[i])):
                    n = ref.shape[2]
                    copies.append(
                        pltpu.make_async_copy(
                            ref.at[place],
                            weights_ref.at[from_z, to_y, :, pl.ds(at * n, n)],
                            sems.at[len(copies)],
                        )
                    )
        for copy in copies:
            copy.start()
        for copy in copies:
            copy.wait()

    width = lifted_ref.shape[1]
    here = [sorted_ref[at] for at in places]

    def pick_up(member):
        for i, at in enumerate(places):
            row = perm_ref[at]
            source = row // rows - 2 * chips[0]
            tokens = pl.ds(i * seq, seq)

            @pl.when(here[i] == member)
            def _():
                lifted_ref[tokens, :] = tokens_ref[source, 0, lax.rem(row, rows)]
                g_ref[tokens, :] = tokens_ref[source, 1, lax.rem(row, rows)]

            @pl.when(here[i] != member)
            def _():
                lifted_ref[tokens, :] = jnp.zeros((seq, width), BF16)
                g_ref[tokens, :] = jnp.zeros((seq, width), BF16)

    def sums(member):
        pick_up(member)
        mine = [(start, n) for (m, n), start in zip(units, starts) if m == member]
        low, high = mine[0][0], mine[-1][0] + mine[-1][1]
        for s in range(low, high, 256):
            e = min(s + 256, high)
            up = weights_ref[:, :, :depth, s:e].reshape(width, e - s)
            down = weights_ref[:, :, depth:, s:e].reshape(width, e - s)
            v = jnp.dot(lifted_ref[...], up, preferred_element_type=F32)
            grads = jnp.dot(g_ref[...], down, preferred_element_type=F32)
            square = v * v
            t = jnp.tanh(v * (coef_c + (coef_c * 0.044715) * square))
            half_v = 0.5 * v
            act_ref[:, s - low : e - low] = (half_v + half_v * t).astype(BF16)
            slope = (0.5 + 0.5 * t) + (half_v * (1.0 - t * t)) * (
                coef_c + (3.0 * coef_c * 0.044715) * square
            )
            pre_ref[:, s - low : e - low] = (grads * slope).astype(BF16)
        up = weights_ref[:, :, :depth, low:high].reshape(width, high - low)
        down = weights_ref[:, :, depth:, low:high].reshape(width, high - low)
        dims = (((1,), (1,)), ((), ()))
        return (
            lax.dot_general(act_ref[:, : high - low], down, dims, preferred_element_type=F32),
            lax.dot_general(pre_ref[:, : high - low], up, dims, preferred_element_type=F32),
        )

    for at, member in enumerate(sorted(set(m for m, _ in units))):
        used = functools.reduce(jnp.logical_or, [m == member for m in here])

        @pl.when(used)
        def _():
            out_sum, back_sum = sums(member)
            if at > 0:
                out_acc[...] += out_sum
                back_acc[...] += back_sum
            elif first:
                out_acc[...] = out_sum
                back_acc[...] = back_sum
            else:
                out_acc[...] = out_in[...] + out_sum
                back_acc[...] = back_in[...] + back_sum

        if at == 0:

            @pl.when(jnp.logical_not(used))
            def _():
                out_acc[...] = jnp.zeros(out_acc.shape, F32) if first else out_in[...]
                back_acc[...] = jnp.zeros(back_acc.shape, F32) if first else back_in[...]

    if last:
        for p, at in enumerate(places):
            row = lax.rem(perm_ref[at], 2 * rows)
            tokens = pl.ds(p * seq, seq)
            low = 0
            for to_out, to_back in zip(outs[::2], outs[1::2]):
                n = to_out.shape[0]

                @pl.when(jnp.logical_and(row >= low, row < low + n))
                def _():
                    to = jnp.clip(row - low, 0, n - 1)
                    to_out[to] = out_acc[tokens, :].astype(to_out.dtype)
                    to_back[to] = back_acc[tokens, :].astype(to_back.dtype)

                low += n


def chunk(kind, blocks, chips, scalars, tokens_of, weights, sums, outs=None, weight=1):
    first, last = kind
    offset, number, per_block = blocks
    units, here, there, sources = weights
    _, rows, seq, width = tokens_of[0].shape
    lines = len(sources[0])
    depth2 = here[0].shape[1]
    hidden = sum(n for _, n in units)
    size = per_block * seq

    tok = pl.BlockSpec((size, width), lambda j, *_: (j, 0))
    hbm = pl.BlockSpec(memory_space=pl.ANY)
    args = [*scalars, *(tokens_of[chip] for chip in chips), tokens_of[-1], *here, *there]
    specs = [pl.BlockSpec(memory_space=pltpu.HBM)] * (len(chips) + 1) + [hbm] * (2 * len(here))
    alias = {}
    out_specs = [tok, tok]
    out_shape = [jax.ShapeDtypeStruct((number * size, width), F32)] * 2
    scratch = [
        pltpu.VMEM((2 * len(chips), 2, rows, seq, width), BF16),
        pltpu.VMEM((lines, 2, depth2, hidden), BF16),
        pltpu.SemaphoreType.DMA((len(sources) * 2 * lines + 2 * len(chips),)),
        pltpu.VMEM((size, width), BF16),
        pltpu.VMEM((size, width), BF16),
        pltpu.VMEM((size, hidden), BF16),
        pltpu.VMEM((size, hidden), BF16),
    ]
    if not first:
        alias = {len(args): 0, len(args) + 1: 1}
        args += list(sums)
        specs += [tok, tok]
    if last:
        alias = {}
        shape = (rows, seq, width)
        out_shape = [jax.ShapeDtypeStruct(shape, dtype) for dtype in outs for _ in range(2)]
        out_specs = [pl.BlockSpec(shape, lambda *_: (0, 0, 0))] * len(out_shape)
        scratch += [pltpu.VMEM((size, width), F32)] * 2

    return pl.pallas_call(
        functools.partial(chunk_kernel, offset, kind, units, chips, sources),
        grid_spec=pltpu.PrefetchScalarGridSpec(
            num_scalar_prefetch=len(scalars),
            grid=(number,),
            in_specs=specs,
            out_specs=out_specs,
            scratch_shapes=scratch,
        ),
        out_shape=out_shape,
        input_output_aliases=alias,
        compiler_params=pltpu.CompilerParams(vmem_limit_bytes=VMEM_LIMIT),
        cost_estimate=pl.CostEstimate(
            flops=weight * 8 * number * size * width * hidden * 2 // 3,
            bytes_accessed=weight * (4 * width * hidden + 20 * number * size * width),
            transcendentals=weight * number * size * hidden,
        ),
        name="chunk",
    )(*args)


def finish_kernel(
    member_ref, x_ref, g_ref, gain_ref, out_ref, back_ref, other_out_ref, other_back_ref,
    across_ref, value_ref, grad_ref, coupling_ref,
):
    rows, seq, width = x_ref.shape
    diagonal = lax.broadcasted_iota(jnp.int32, (seq, seq), 0) == lax.broadcasted_iota(
        jnp.int32, (seq, seq), 1
    )
    for r in range(rows):
        x = x_ref[r].astype(F32)
        inv = 1.0 / jnp.sqrt(jnp.mean(x * x, axis=1, keepdims=True) + 1e-06)
        normed = x * inv
        gain = gain_ref[pl.ds(member_ref[pl.program_id(0) * rows + r], 1), :]
        back = gain * (
            back_ref[r] + other_back_ref[r].astype(F32) + across_ref[1, r].astype(F32)
        )
        stat = jnp.sum(normed * back, axis=1, keepdims=True) / width
        out = out_ref[r] + other_out_ref[r].astype(F32) + across_ref[0, r].astype(F32)
        value_ref[r] = (x + out).astype(BF16)
        grad_ref[r] = (g_ref[r].astype(F32) + (back - normed * stat) * inv).astype(BF16)
        line = jnp.sum(jnp.where(diagonal, stat, 0.0), axis=0, keepdims=True)
        coupling_ref[pl.ds(pl.program_id(0) * rows + r, 1), :] = line * math.sqrt(width)


def finish(member_own, x, g, gain, *sums):
    rows, seq, width = x.shape
    step = math.gcd(rows, 2)
    row = pl.BlockSpec((step, seq, width), lambda r, mem: (r, 0, 0))
    two = pl.BlockSpec((2, step, seq, width), lambda r, mem: (0, r, 0, 0))
    return pl.pallas_call(
        finish_kernel,
        grid_spec=pltpu.PrefetchScalarGridSpec(
            num_scalar_prefetch=1,
            grid=(rows // step,),
            in_specs=[
                row, row, pl.BlockSpec(gain.shape, lambda r, mem: (0, 0)), row, row, row, row, two
            ],
            out_specs=[row, row, pl.BlockSpec((rows, seq), lambda r, mem: (0, 0))],
        ),
        out_shape=[
            jax.ShapeDtypeStruct((rows, seq, width), BF16),
            jax.ShapeDtypeStruct((rows, seq, width), BF16),
            jax.ShapeDtypeStruct((rows, seq), F32),
        ],
        compiler_params=pltpu.CompilerParams(vmem_limit_bytes=VMEM_LIMIT // 2),
        name="finish",
    )(member_own, x, g, gain, *sums)


def sort_rows(picks):
    index = jnp.arange(picks.shape[0], dtype=jnp.int32)
    before = (picks[None, :] < picks[:, None]) | (
        (picks[None, :] == picks[:, None]) & (index[None, :] < index[:, None])
    )
    pos = jnp.sum(before.astype(jnp.int32), axis=1)
    at = pos[None, :] == index[:, None]
    perm = jnp.sum(jnp.where(at, index[None, :], 0), axis=1)
    return perm, jnp.sum(jnp.where(at, picks[None, :], 0), axis=1)


def on_device_shared(ranks, tokens_in, upstream, member_pick, norm_gain, up_proj, down_proj):
    rows, seq, width = tokens_in.shape
    members, depth, hidden = up_proj.shape
    rank = lax.axis_index("row")
    core = lax.rem(rank, 2)
    x_at = lax.axis_index("grp")
    y_at = lax.rem(rank // 2, 2)
    lines = ranks // 4

    def partner(a):
        return lax.ppermute(a, "row", [(i, i ^ 1) for i in range(ranks)])

    def over_y(a):
        return lax.ppermute(a, "row", [(i, i ^ 2) for i in range(ranks)])

    def over_x(a):
        return lax.ppermute(a, "grp", [(0, 1), (1, 0)])

    def shift_z(a, d):
        return lax.ppermute(a, "row", [(i, (i + 4 * d) % ranks) for i in range(ranks)])

    def after(a, *others):
        return lax.optimization_barrier((a, *others))[0]

    unit = hidden // 32
    quarter, half = 7 * unit, 2 * unit

    def units_of(c, both):
        return jnp.concatenate(
            [
                lax.dynamic_slice_in_dim(both, (2 * x_at + c) * quarter, quarter, 3),
                lax.dynamic_slice_in_dim(both, 4 * quarter + c * half, half, 3),
            ],
            axis=3,
        )

    def both_cores(mine, theirs):
        even = core == 0
        whole = jnp.concatenate(
            [jnp.where(even, mine, theirs), jnp.where(even, theirs, mine)], axis=2
        )
        return whole.reshape(mine.shape[0], 4 * depth, mine.shape[3])

    def head_of(c):
        at = (2 * x_at + c) * quarter
        return jnp.stack(
            [lax.dynamic_slice(a, (0, 0, at), (1, depth, 2 * unit)) for a in (up_proj, down_proj)],
            axis=1,
        )

    head_theirs = partner(head_of(1 - core))
    shard_head = both_cores(head_of(core), head_theirs)
    both = jnp.stack([after(up_proj, shard_head), down_proj], axis=1)
    theirs = partner(units_of(1 - core, both))
    shard = both_cores(units_of(core, both), theirs)

    block = 2 * unit
    groups = [
        [(0, 0, 2 * unit)],
        [(0, 2 * unit, 4 * unit)],
        [(0, 6 * unit, unit), (1, 0, 3 * unit)],
        [(1, 3 * unit, 4 * unit)],
        [(0, quarter, half), (1, quarter, half)],
    ]
    own_with = [[(0, 0), (1, 0), (1, 1), (2, 0)], [(2, 1)], [(3, 0)], [(3, 1)], [(4, 0), (4, 1)]]
    send = [shard_head[0]] + [
        jnp.concatenate([shard[m, :, at : at + n] for m, at, n in group], axis=1)
        for group in groups[1:]
    ]
    here, there, shifted, held = [], [], [], {}

    def along_z(step, *waits):
        mine = after(send[step], *shifted[-1], *waits) if step else send[0]
        shifted.append([shift_z(mine, d) for d in range(1, lines)])

    def across_y(step, *waits):
        blocks = []
        for group, i in own_with[step]:
            held[group, i, 0] = (step, len(blocks))
            blocks.append(send[group][:, i * block : (i + 1) * block])
        for d, rows_from in enumerate(shifted[step]):
            for i in range(rows_from.shape[1] // block):
                held[step, i, d + 1] = (step, len(blocks))
                blocks.append(rows_from[:, i * block : (i + 1) * block])
        here.append(jnp.stack(blocks))
        there.append(over_y(after(here[step], *there[-1:], *waits)))

    def weights_of(*which):
        units = [(member, n) for group in which for member, _, n in groups[group]]
        sources = [
            [held[group, i, d] for d in range(lines)]
            for group in which
            for i in range(send[group].shape[1] // block)
        ]
        used = sorted(set(array for block in sources for array, _ in block))
        return (
            units,
            [here[i] for i in used],
            [there[i] for i in used],
            [[(used.index(i), at) for i, at in block] for block in sources],
        )

    per_block = math.gcd(2 * rows, 4)
    per_chip = 2 * rows // per_block
    along_z(0)
    pick_own = member_pick[:, 0]
    pick_near = jnp.concatenate([pick_own, over_x(after(pick_own, send[0]))])
    x = after(tokens_in, shifted[0][0]).astype(F32)
    gain = jnp.zeros((rows, width), F32)
    for member in range(members):
        gain = jnp.where(pick_own[:, None] == member, norm_gain[member][None, :], gain)
    normed = x * (1.0 / jnp.sqrt(jnp.mean(x * x, axis=2, keepdims=True) + 1e-06))
    lifted = (normed * gain[:, None, :]).astype(BF16)
    near = jnp.stack([lifted, upstream])
    lifted_over = over_x(lifted)
    across_y(0)
    along_z(1)
    pick_far = partner(after(pick_near, shifted[0][-1]))

    perm, member_sorted = sort_rows(jnp.concatenate([pick_near[rows:], pick_far[rows:]]))
    perm_own, member_sorted_own = sort_rows(jnp.concatenate([pick_own, pick_far[:rows]]))
    scalars = (
        jnp.concatenate([member_sorted, member_sorted_own]),
        jnp.stack([y_at, rank // 4]),
        jnp.concatenate([perm + 2 * rows, perm_own]),
    )

    along_z(2, there[0], lifted_over, *scalars)
    across_y(1)
    over = jnp.stack([lifted_over, over_x(after(upstream, there[0], *shifted[1]))])
    along_z(3, there[1], over)
    across_y(2)
    far = partner(after(jnp.stack([near, over]), *shifted[2], there[1]))
    along_z(4, there[2], far)
    across_y(3)
    tokens_of = (near, over, far)
    other_rows, own_rows = (0, per_chip, per_block), (per_chip, per_chip, per_block)
    sums = chunk(
        (True, False), other_rows, (1,), scalars,
        (near, after(over, *shifted[3]), far), weights_of(0, 1, 2), None,
    )
    across_y(4)
    sums = (after(sums[0], *shifted[4]), sums[1])
    *same, other_out, other_back = chunk(
        (False, True), other_rows, (1,), scalars, tokens_of, weights_of(3), sums,
        (BF16, BF16), 0,
    )
    across = jnp.stack(
        [
            (a.astype(F32) + partner(b).astype(F32)).astype(BF16)
            for a, b in zip(same, (other_out, other_back))
        ]
    )
    tokens_of = (after(near, across), over, far)
    across = over_x(across)
    sums = chunk(
        (True, False), own_rows, (0,), scalars, tokens_of, weights_of(0, 1, 2, 3), None, None, 0
    )
    out, back, packed_out, packed_back = chunk(
        (False, True), own_rows, (0,), scalars, tokens_of, weights_of(4), sums, (F32, BF16), 0
    )
    return tuple(
        finish(
            pick_own, tokens_in, upstream, norm_gain, out, back,
            partner(packed_out), partner(packed_back), across,
        )
    )


def solution(mesh):
    ranks = mesh.shape["row"]
    four = mesh.shape["feat"] == 1 and ranks % 4 == 0 and mesh.shape["grp"] == 2

    def on_device(tokens_in, upstream, member_pick, norm_gain, up_proj, down_proj):
        args = (tokens_in, upstream, member_pick, norm_gain, up_proj, down_proj)
        if four and member_pick.shape[1] == 1 and up_proj.shape[0] == 2:
            return on_device_shared(ranks, *args)
        return on_device_general(*args)

    in_specs = (
        P(("grp", "row"), None, "feat"),
        P(("grp", "row"), None, "feat"),
        P(("grp", "row"), None),
        P(),
        P(None, "row", "feat"),
        P(None, "row", "feat"),
    )
    out_specs = (
        P(("grp", "row"), None, "feat"),
        P(("grp", "row"), None, "feat"),
        P(("grp", "row"), None),
    )
    return jax.shard_map(
        on_device, mesh=mesh, in_specs=in_specs, out_specs=out_specs, check_vma=False
    )
```

```python
import functools
import math

import jax
import jax.numpy as jnp
from jax import lax
from jax.experimental import pallas as pl
from jax.experimental.pallas import tpu as pltpu
from jax.sharding import PartitionSpec as P

coef_c = math.sqrt(2.0 / math.pi)


def gelu_tanh(v):
    return 0.5 * v * (1.0 + jnp.tanh(coef_c * (v + 0.044715 * v * v * v)))


def gelu_slope(v):
    inner = jnp.tanh(coef_c * (v + 0.044715 * v * v * v))
    return 0.5 * (1.0 + inner) + 0.5 * v * (1.0 - inner * inner) * coef_c * (
        1.0 + 3.0 * 0.044715 * v * v
    )


def on_device_general(tokens_in, upstream, member_pick, norm_gain, up_proj, down_proj):
    rows, seq, half = tokens_in.shape
    count = rows * seq
    members = up_proj.shape[0]
    pick = member_pick.shape[1]
    whole_x, whole_g = (
        lax.all_gather(tokens_in, "feat", axis=2, tiled=True),
        lax.all_gather(upstream, "feat", axis=2, tiled=True),
    )
    width = whole_x.shape[2]
    flat_x = whole_x.reshape(count, width).astype(jnp.float32)
    flat_g = whole_g.reshape(count, width)
    inv_rms = 1.0 / jnp.sqrt(jnp.mean(flat_x * flat_x, axis=1, keepdims=True) + 1e-06)
    normed = flat_x * inv_rms
    labels = jnp.arange(members, dtype=jnp.int32)
    chosen = (
        jnp.sum((member_pick[:, :, None] == labels[None, None, :]).astype(jnp.float32), axis=1)
        / pick
    )
    chosen_tok = jnp.repeat(chosen, seq, axis=0)
    out_half = jnp.zeros((count, half), jnp.float32)
    back_half = jnp.zeros((count, half), jnp.float32)
    for member in range(members):
        lifted = (normed * norm_gain[member][None, :]).astype(jnp.bfloat16)
        up_full = lax.all_gather(up_proj[member], "row", axis=0, tiled=True)
        hidden = jnp.dot(lifted, up_full, preferred_element_type=jnp.float32)
        act = gelu_tanh(hidden).astype(jnp.bfloat16)
        piece = lax.all_gather(down_proj[member], "row", axis=0, tiled=True)
        block = lax.dot_general(
            act, piece, (((1,), (1,)), ((), ())), preferred_element_type=jnp.float32
        )
        grads = jnp.dot(flat_g, piece, preferred_element_type=jnp.float32)
        pre_grad = (grads * gelu_slope(hidden)).astype(jnp.bfloat16)
        in_grad = lax.dot_general(
            pre_grad, up_full, (((1,), (1,)), ((), ())), preferred_element_type=jnp.float32
        )
        weight_col = chosen_tok[:, member : member + 1]
        out_term = weight_col * block
        back_term = weight_col * norm_gain[member][None, :] * in_grad
        out_part, back_part = (
            lax.psum_scatter(
                out_term.astype(jnp.bfloat16), "feat", scatter_dimension=1, tiled=True
            ).astype(jnp.float32),
            lax.psum_scatter(
                back_term.astype(jnp.bfloat16), "feat", scatter_dimension=1, tiled=True
            ).astype(jnp.float32),
        )
        out_half = out_half + out_part
        back_half = back_half + back_part
    own_x = tokens_in.reshape(count, half).astype(jnp.float32)
    normed_half = own_x * inv_rms
    stat = lax.psum(jnp.sum(normed_half * back_half, axis=1, keepdims=True), "feat") / width
    coupling = stat * math.sqrt(width)
    own_g = upstream.reshape(count, half).astype(jnp.float32)
    value_out = (own_x + out_half).astype(jnp.bfloat16)
    grad_in = (own_g + (back_half - normed_half * stat) * inv_rms).astype(jnp.bfloat16)
    return (
        value_out.reshape(rows, seq, half),
        grad_in.reshape(rows, seq, half),
        coupling.reshape(rows, seq),
    )


VMEM_LIMIT = 20 * 1024 * 1024
BF16 = jnp.bfloat16
F32 = jnp.float32


def chunk_kernel(
    offset, kind, units, chips, sources, sorted_ref, place_ref, perm_ref, *refs
):
    first, last = kind
    parts = len(units)
    arrays = 1 + max(source[0] for source in sources)
    tokens_of, refs = refs[: len(chips) + 1], refs[len(chips) + 1 :]
    here_refs, there_refs, refs = refs[:arrays], refs[arrays : 2 * arrays], refs[2 * arrays :]
    if first:
        *outs, tokens_ref, weights_ref, sems, lifted_ref, g_ref, act_ref, pre_ref = refs
    elif last:
        out_in, back_in, *outs, tokens_ref, weights_ref, sems = refs[:-6]
        lifted_ref, g_ref, act_ref, pre_ref = refs[-6:-2]
        out_acc, back_acc = refs[-2:]
    else:
        out_in, back_in, *outs, tokens_ref, weights_ref, sems = refs[:-4]
        lifted_ref, g_ref, act_ref, pre_ref = refs[-4:]
    if not last:
        out_acc, back_acc = outs
    j = pl.program_id(0)
    rows, seq = tokens_ref.shape[2:4]
    per_block = lifted_ref.shape[0] // seq
    places = [(j + offset) * per_block + i for i in range(per_block)]
    lines, _, depth2, _ = weights_ref.shape
    depth = depth2 // 2
    starts = [sum(n for _, n in units[:part]) for part in range(parts)]

    @pl.when(j == 0)
    def _():
        y, z = place_ref[0], place_ref[1]
        copies = []
        for i, chip in enumerate(chips):
            for k, ref in enumerate((tokens_of[i], tokens_of[-1].at[chip])):
                copies.append(
                    pltpu.make_async_copy(ref, tokens_ref.at[2 * i + k], sems.at[len(copies)])
                )
        for i, start, d, to_row, to_unit, n, wide in sources:
            from_z = lax.rem(z + lines - d, lines)
            for to_y, ref in ((y, here_refs[i]), (1 - y, there_refs[i])):
                to = weights_ref.at[from_z, to_y, pl.ds(to_row, n), pl.ds(to_unit, wide)]
                copies.append(
                    pltpu.make_async_copy(ref.at[pl.ds(start, n)], to, sems.at[len(copies)])
                )
        for copy in copies:
            copy.start()
        for copy in copies:
            copy.wait()

    width = lifted_ref.shape[1]
    here = [sorted_ref[at] for at in places]

    def pick_up(member):
        for i, at in enumerate(places):
            row = perm_ref[at]
            source = row // rows - 2 * chips[0]
            tokens = pl.ds(i * seq, seq)

            @pl.when(here[i] == member)
            def _():
                lifted_ref[tokens, :] = tokens_ref[source, 0, lax.rem(row, rows)]
                g_ref[tokens, :] = tokens_ref[source, 1, lax.rem(row, rows)]

            @pl.when(here[i] != member)
            def _():
                lifted_ref[tokens, :] = jnp.zeros((seq, width), BF16)
                g_ref[tokens, :] = jnp.zeros((seq, width), BF16)

    def sums(member):
        pick_up(member)
        mine = [(start, n) for (m, n), start in zip(units, starts) if m == member]
        low, high = mine[0][0], mine[-1][0] + mine[-1][1]
        for s in range(low, high, 256):
            e = min(s + 256, high)
            up = weights_ref[:, :, :depth, s:e].reshape(width, e - s)
            down = weights_ref[:, :, depth:, s:e].reshape(width, e - s)
            v = jnp.dot(lifted_ref[...], up, preferred_element_type=F32)
            grads = jnp.dot(g_ref[...], down, preferred_element_type=F32)
            square = v * v
            t = jnp.tanh(v * (coef_c + (coef_c * 0.044715) * square))
            half_v = 0.5 * v
            act_ref[:, s - low : e - low] = (half_v + half_v * t).astype(BF16)
            slope = (0.5 + 0.5 * t) + (half_v * (1.0 - t * t)) * (
                coef_c + (3.0 * coef_c * 0.044715) * square
            )
            pre_ref[:, s - low : e - low] = (grads * slope).astype(BF16)
        up = weights_ref[:, :, :depth, low:high].reshape(width, high - low)
        down = weights_ref[:, :, depth:, low:high].reshape(width, high - low)
        dims = (((1,), (1,)), ((), ()))
        return (
            lax.dot_general(act_ref[:, : high - low], down, dims, preferred_element_type=F32),
            lax.dot_general(pre_ref[:, : high - low], up, dims, preferred_element_type=F32),
        )

    for at, member in enumerate(sorted(set(m for m, _ in units))):
        used = functools.reduce(jnp.logical_or, [m == member for m in here])

        @pl.when(used)
        def _():
            out_sum, back_sum = sums(member)
            if at > 0:
                out_acc[...] += out_sum
                back_acc[...] += back_sum
            elif first:
                out_acc[...] = out_sum
                back_acc[...] = back_sum
            else:
                out_acc[...] = out_in[...] + out_sum
                back_acc[...] = back_in[...] + back_sum

        if at == 0:

            @pl.when(jnp.logical_not(used))
            def _():
                out_acc[...] = jnp.zeros(out_acc.shape, F32) if first else out_in[...]
                back_acc[...] = jnp.zeros(back_acc.shape, F32) if first else back_in[...]

    if last:
        for p, at in enumerate(places):
            row = lax.rem(perm_ref[at], 2 * rows)
            tokens = pl.ds(p * seq, seq)
            low = 0
            for to_out, to_back in zip(outs[::2], outs[1::2]):
                n = to_out.shape[0]

                @pl.when(jnp.logical_and(row >= low, row < low + n))
                def _():
                    to = jnp.clip(row - low, 0, n - 1)
                    to_out[to] = out_acc[tokens, :].astype(to_out.dtype)
                    to_back[to] = back_acc[tokens, :].astype(to_back.dtype)

                low += n


def chunk(kind, blocks, chips, scalars, tokens_of, weights, sums, outs=None, weight=1):
    first, last = kind
    offset, number, per_block = blocks
    units, lines, depth2, here, there, sources = weights
    _, rows, seq, width = tokens_of[0].shape
    hidden = sum(n for _, n in units)
    size = per_block * seq

    tok = pl.BlockSpec((size, width), lambda j, *_: (j, 0))
    hbm = pl.BlockSpec(memory_space=pl.ANY)
    args = [*scalars, *(tokens_of[chip] for chip in chips), tokens_of[-1], *here, *there]
    specs = [pl.BlockSpec(memory_space=pltpu.HBM)] * (len(chips) + 1) + [hbm] * (2 * len(here))
    alias = {}
    out_specs = [tok, tok]
    out_shape = [jax.ShapeDtypeStruct((number * size, width), F32)] * 2
    scratch = [
        pltpu.VMEM((2 * len(chips), 2, rows, seq, width), BF16),
        pltpu.VMEM((lines, 2, depth2, hidden), BF16),
        pltpu.SemaphoreType.DMA((2 * len(sources) + 2 * len(chips),)),
        pltpu.VMEM((size, width), BF16),
        pltpu.VMEM((size, width), BF16),
        pltpu.VMEM((size, hidden), BF16),
        pltpu.VMEM((size, hidden), BF16),
    ]
    if not first:
        alias = {len(args): 0, len(args) + 1: 1}
        args += list(sums)
        specs += [tok, tok]
    if last:
        alias = {}
        shape = (rows, seq, width)
        out_shape = [jax.ShapeDtypeStruct(shape, dtype) for dtype in outs for _ in range(2)]
        out_specs = [pl.BlockSpec(shape, lambda *_: (0, 0, 0))] * len(out_shape)
        scratch += [pltpu.VMEM((size, width), F32)] * 2

    return pl.pallas_call(
        functools.partial(chunk_kernel, offset, kind, units, chips, sources),
        grid_spec=pltpu.PrefetchScalarGridSpec(
            num_scalar_prefetch=len(scalars),
            grid=(number,),
            in_specs=specs,
            out_specs=out_specs,
            scratch_shapes=scratch,
        ),
        out_shape=out_shape,
        input_output_aliases=alias,
        compiler_params=pltpu.CompilerParams(vmem_limit_bytes=VMEM_LIMIT),
        cost_estimate=pl.CostEstimate(
            flops=weight * 8 * number * size * width * hidden * 2 // 3,
            bytes_accessed=weight * (4 * width * hidden + 20 * number * size * width),
            transcendentals=weight * number * size * hidden,
        ),
        name="chunk",
    )(*args)


def finish_kernel(
    member_ref, x_ref, g_ref, gain_ref, out_ref, back_ref, other_out_ref, other_back_ref,
    across_ref, value_ref, grad_ref, coupling_ref,
):
    rows, seq, width = x_ref.shape
    diagonal = lax.broadcasted_iota(jnp.int32, (seq, seq), 0) == lax.broadcasted_iota(
        jnp.int32, (seq, seq), 1
    )
    for r in range(rows):
        x = x_ref[r].astype(F32)
        inv = 1.0 / jnp.sqrt(jnp.mean(x * x, axis=1, keepdims=True) + 1e-06)
        normed = x * inv
        gain = gain_ref[pl.ds(member_ref[pl.program_id(0) * rows + r], 1), :]
        back = gain * (
            back_ref[r] + other_back_ref[r].astype(F32) + across_ref[1, r].astype(F32)
        )
        stat = jnp.sum(normed * back, axis=1, keepdims=True) / width
        out = out_ref[r] + other_out_ref[r].astype(F32) + across_ref[0, r].astype(F32)
        value_ref[r] = (x + out).astype(BF16)
        grad_ref[r] = (g_ref[r].astype(F32) + (back - normed * stat) * inv).astype(BF16)
        line = jnp.sum(jnp.where(diagonal, stat, 0.0), axis=0, keepdims=True)
        coupling_ref[pl.ds(pl.program_id(0) * rows + r, 1), :] = line * math.sqrt(width)


def finish(member_own, x, g, gain, *sums):
    rows, seq, width = x.shape
    step = math.gcd(rows, 2)
    row = pl.BlockSpec((step, seq, width), lambda r, mem: (r, 0, 0))
    two = pl.BlockSpec((2, step, seq, width), lambda r, mem: (0, r, 0, 0))
    return pl.pallas_call(
        finish_kernel,
        grid_spec=pltpu.PrefetchScalarGridSpec(
            num_scalar_prefetch=1,
            grid=(rows // step,),
            in_specs=[
                row, row, pl.BlockSpec(gain.shape, lambda r, mem: (0, 0)), row, row, row, row, two
            ],
            out_specs=[row, row, pl.BlockSpec((rows, seq), lambda r, mem: (0, 0))],
        ),
        out_shape=[
            jax.ShapeDtypeStruct((rows, seq, width), BF16),
            jax.ShapeDtypeStruct((rows, seq, width), BF16),
            jax.ShapeDtypeStruct((rows, seq), F32),
        ],
        compiler_params=pltpu.CompilerParams(vmem_limit_bytes=VMEM_LIMIT // 2),
        name="finish",
    )(member_own, x, g, gain, *sums)


def sort_rows(picks):
    index = jnp.arange(picks.shape[0], dtype=jnp.int32)
    before = (picks[None, :] < picks[:, None]) | (
        (picks[None, :] == picks[:, None]) & (index[None, :] < index[:, None])
    )
    pos = jnp.sum(before.astype(jnp.int32), axis=1)
    at = pos[None, :] == index[:, None]
    perm = jnp.sum(jnp.where(at, index[None, :], 0), axis=1)
    return perm, jnp.sum(jnp.where(at, picks[None, :], 0), axis=1)


def on_device_shared(ranks, tokens_in, upstream, member_pick, norm_gain, up_proj, down_proj):
    rows, seq, width = tokens_in.shape
    members, depth, hidden = up_proj.shape
    rank = lax.axis_index("row")
    core = lax.rem(rank, 2)
    x_at = lax.axis_index("grp")
    y_at = lax.rem(rank // 2, 2)
    lines = ranks // 4

    def partner(a):
        return lax.ppermute(a, "row", [(i, i ^ 1) for i in range(ranks)])

    def over_y(a):
        return lax.ppermute(a, "row", [(i, i ^ 2) for i in range(ranks)])

    def over_x(a):
        return lax.ppermute(a, "grp", [(0, 1), (1, 0)])

    def shift_z(a, d):
        return lax.ppermute(a, "row", [(i, (i + 4 * d) % ranks) for i in range(ranks)])

    def after(a, *others):
        return lax.optimization_barrier((a, *others))[0]

    unit = hidden // 32
    quarter, half = 7 * unit, 2 * unit

    def units_of(c, both):
        return jnp.concatenate(
            [
                lax.dynamic_slice_in_dim(both, (2 * x_at + c) * quarter, quarter, 3),
                lax.dynamic_slice_in_dim(both, 4 * quarter + c * half, half, 3),
            ],
            axis=3,
        )

    def both_cores(mine, theirs):
        even = core == 0
        whole = jnp.concatenate(
            [jnp.where(even, mine, theirs), jnp.where(even, theirs, mine)], axis=2
        )
        return whole.reshape(mine.shape[0], 4 * depth, mine.shape[3])

    def head_of(c):
        at = (2 * x_at + c) * quarter
        return jnp.stack(
            [lax.dynamic_slice(a, (0, 0, at), (1, depth, 2 * unit)) for a in (up_proj, down_proj)],
            axis=1,
        )

    head_theirs = partner(head_of(1 - core))
    shard_head = both_cores(head_of(core), head_theirs)
    both = jnp.stack([after(up_proj, shard_head), after(down_proj, shard_head)], axis=1)
    theirs = partner(after(units_of(1 - core, both), shard_head))
    shard = both_cores(units_of(core, both), theirs)

    groups = [
        [(0, 0, 2 * unit)],
        [(0, 2 * unit, 4 * unit)],
        [(0, 6 * unit, unit), (1, 0, 3 * unit)],
        [(1, 3 * unit, 4 * unit)],
        [(0, quarter, half), (1, quarter, half)],
    ]
    own_rows = 4 * depth
    own_with = [
        [(0, 0, own_rows), (1, 0, own_rows), (2, 0, own_rows // 2)],
        [(2, own_rows // 2, own_rows // 2)],
        [(3, 0, own_rows // 2)],
        [(3, own_rows // 2, own_rows // 2)],
        [(4, 0, own_rows)],
    ]

    def own(group, row, n, first=0, wide=None):
        parts = []
        last = first + (wide or sum(k for _, _, k in groups[group]))
        at = 0
        for member, start, k in groups[group]:
            low, high = max(first, at), min(last, at + k)
            if low < high:
                parts.append(shard[member, row : row + n, start + low - at : start + high - at])
            at += k
        return jnp.concatenate(parts, axis=1)

    send = [shard_head[0]] + [own(group, 0, own_rows) for group in range(1, len(groups))]
    here, there, shifted, held = [], [], [], [[] for _ in groups]

    def along_z(step, *waits):
        mine = after(send[step], *shifted[-1], *waits) if step else send[0]
        shifted.append([shift_z(mine, d) for d in range(1, lines)])

    def across_y(step, *waits):
        wide = send[step].shape[1]
        parts = []

        def add(array, group, d, row, first):
            start = sum(a.shape[0] for a in parts)
            held[group].append((step, start, d, row, first, array.shape[0], wide))
            parts.append(array)

        for group, row, n in own_with[step]:
            for first in range(0, send[group].shape[1], wide):
                mine = send[0] if group == 0 else own(group, row, n, first, wide)
                add(mine, group, 0, row, first)
        for d, rows_from in enumerate(shifted[step]):
            add(rows_from, step, d + 1, 0, 0)
        here.append(jnp.concatenate(parts))
        there.append(over_y(after(here[step], *there[-1:], *waits)))

    def weights_of(*which):
        units = [(member, n) for group in which for member, _, n in groups[group]]
        used = sorted(set(source[0] for group in which for source in held[group]))
        sources = []
        at = 0
        for group in which:
            for i, start, d, row, first, n, wide in held[group]:
                sources.append((used.index(i), start, d, row, at + first, n, wide))
            at += send[group].shape[1]
        arrays = [here[i] for i in used], [there[i] for i in used]
        return units, lines, own_rows, *arrays, sources

    per_block = math.gcd(2 * rows, 4)
    per_chip = 2 * rows // per_block
    along_z(0)
    pick_own = member_pick[:, 0]
    pick_near = jnp.concatenate([pick_own, over_x(after(pick_own, send[0]))])
    x = after(tokens_in, shifted[0][0]).astype(F32)
    gain = jnp.zeros((rows, width), F32)
    for member in range(members):
        gain = jnp.where(pick_own[:, None] == member, norm_gain[member][None, :], gain)
    normed = x * (1.0 / jnp.sqrt(jnp.mean(x * x, axis=2, keepdims=True) + 1e-06))
    lifted = (normed * gain[:, None, :]).astype(BF16)
    near = jnp.stack([lifted, upstream])
    lifted_over = over_x(lifted)
    across_y(0)
    along_z(1)
    pick_far = partner(after(pick_near, shifted[0][-1]))

    perm, member_sorted = sort_rows(jnp.concatenate([pick_near[rows:], pick_far[rows:]]))
    perm_own, member_sorted_own = sort_rows(jnp.concatenate([pick_own, pick_far[:rows]]))
    scalars = (
        jnp.concatenate([member_sorted, member_sorted_own]),
        jnp.stack([y_at, rank // 4]),
        jnp.concatenate([perm + 2 * rows, perm_own]),
    )

    along_z(2, there[0], lifted_over, *scalars)
    across_y(1)
    over = jnp.stack([lifted_over, over_x(after(upstream, there[0], *shifted[1]))])
    along_z(3, there[1], over)
    across_y(2)
    far = partner(after(jnp.stack([near, over]), *shifted[2], there[1]))
    along_z(4, there[2], far)
    across_y(3)
    tokens_of = (near, over, far)
    over_blocks, own_blocks = (0, per_chip, per_block), (per_chip, per_chip, per_block)
    sums = chunk(
        (True, False), over_blocks, (1,), scalars,
        (near, after(over, *shifted[3]), far), weights_of(0, 1, 2), None,
    )
    across_y(4)
    sums = (after(sums[0], *shifted[4]), sums[1])
    *same, other_out, other_back = chunk(
        (False, True), over_blocks, (1,), scalars, tokens_of, weights_of(3), sums,
        (BF16, BF16), 0,
    )
    across = jnp.stack(
        [
            (a.astype(F32) + partner(b).astype(F32)).astype(BF16)
            for a, b in zip(same, (other_out, other_back))
        ]
    )
    tokens_of = (after(near, across), over, far)
    across = over_x(across)
    sums = chunk(
        (True, False), own_blocks, (0,), scalars, tokens_of, weights_of(0, 1, 2, 3), None, None, 0
    )
    out, back, packed_out, packed_back = chunk(
        (False, True), own_blocks, (0,), scalars, tokens_of, weights_of(4), sums, (F32, BF16), 0
    )
    return tuple(
        finish(
            pick_own, tokens_in, upstream, norm_gain, out, back,
            partner(packed_out), partner(packed_back), across,
        )
    )


def solution(mesh):
    ranks = mesh.shape["row"]
    four = mesh.shape["feat"] == 1 and ranks % 4 == 0 and mesh.shape["grp"] == 2

    def on_device(tokens_in, upstream, member_pick, norm_gain, up_proj, down_proj):
        args = (tokens_in, upstream, member_pick, norm_gain, up_proj, down_proj)
        if four and member_pick.shape[1] == 1 and up_proj.shape[0] == 2:
            return on_device_shared(ranks, *args)
        return on_device_general(*args)

    in_specs = (
        P(("grp", "row"), None, "feat"),
        P(("grp", "row"), None, "feat"),
        P(("grp", "row"), None),
        P(),
        P(None, "row", "feat"),
        P(None, "row", "feat"),
    )
    out_specs = (
        P(("grp", "row"), None, "feat"),
        P(("grp", "row"), None, "feat"),
        P(("grp", "row"), None),
    )
    return jax.shard_map(
        on_device, mesh=mesh, in_specs=in_specs, out_specs=out_specs, check_vma=False
    )
```

```python
import functools
import math

import jax
import jax.numpy as jnp
from jax import lax
from jax.experimental import pallas as pl
from jax.experimental.pallas import tpu as pltpu
from jax.sharding import PartitionSpec as P

coef_c = math.sqrt(2.0 / math.pi)


def gelu_tanh(v):
    return 0.5 * v * (1.0 + jnp.tanh(coef_c * (v + 0.044715 * v * v * v)))


def gelu_slope(v):
    inner = jnp.tanh(coef_c * (v + 0.044715 * v * v * v))
    return 0.5 * (1.0 + inner) + 0.5 * v * (1.0 - inner * inner) * coef_c * (
        1.0 + 3.0 * 0.044715 * v * v
    )


def on_device_general(tokens_in, upstream, member_pick, norm_gain, up_proj, down_proj):
    rows, seq, half = tokens_in.shape
    count = rows * seq
    members = up_proj.shape[0]
    pick = member_pick.shape[1]
    whole_x, whole_g = (
        lax.all_gather(tokens_in, "feat", axis=2, tiled=True),
        lax.all_gather(upstream, "feat", axis=2, tiled=True),
    )
    width = whole_x.shape[2]
    flat_x = whole_x.reshape(count, width).astype(jnp.float32)
    flat_g = whole_g.reshape(count, width)
    inv_rms = 1.0 / jnp.sqrt(jnp.mean(flat_x * flat_x, axis=1, keepdims=True) + 1e-06)
    normed = flat_x * inv_rms
    labels = jnp.arange(members, dtype=jnp.int32)
    chosen = (
        jnp.sum((member_pick[:, :, None] == labels[None, None, :]).astype(jnp.float32), axis=1)
        / pick
    )
    chosen_tok = jnp.repeat(chosen, seq, axis=0)
    out_half = jnp.zeros((count, half), jnp.float32)
    back_half = jnp.zeros((count, half), jnp.float32)
    for member in range(members):
        lifted = (normed * norm_gain[member][None, :]).astype(jnp.bfloat16)
        up_full = lax.all_gather(up_proj[member], "row", axis=0, tiled=True)
        hidden = jnp.dot(lifted, up_full, preferred_element_type=jnp.float32)
        act = gelu_tanh(hidden).astype(jnp.bfloat16)
        piece = lax.all_gather(down_proj[member], "row", axis=0, tiled=True)
        block = lax.dot_general(
            act, piece, (((1,), (1,)), ((), ())), preferred_element_type=jnp.float32
        )
        grads = jnp.dot(flat_g, piece, preferred_element_type=jnp.float32)
        pre_grad = (grads * gelu_slope(hidden)).astype(jnp.bfloat16)
        in_grad = lax.dot_general(
            pre_grad, up_full, (((1,), (1,)), ((), ())), preferred_element_type=jnp.float32
        )
        weight_col = chosen_tok[:, member : member + 1]
        out_term = weight_col * block
        back_term = weight_col * norm_gain[member][None, :] * in_grad
        out_part, back_part = (
            lax.psum_scatter(
                out_term.astype(jnp.bfloat16), "feat", scatter_dimension=1, tiled=True
            ).astype(jnp.float32),
            lax.psum_scatter(
                back_term.astype(jnp.bfloat16), "feat", scatter_dimension=1, tiled=True
            ).astype(jnp.float32),
        )
        out_half = out_half + out_part
        back_half = back_half + back_part
    own_x = tokens_in.reshape(count, half).astype(jnp.float32)
    normed_half = own_x * inv_rms
    stat = lax.psum(jnp.sum(normed_half * back_half, axis=1, keepdims=True), "feat") / width
    coupling = stat * math.sqrt(width)
    own_g = upstream.reshape(count, half).astype(jnp.float32)
    value_out = (own_x + out_half).astype(jnp.bfloat16)
    grad_in = (own_g + (back_half - normed_half * stat) * inv_rms).astype(jnp.bfloat16)
    return (
        value_out.reshape(rows, seq, half),
        grad_in.reshape(rows, seq, half),
        coupling.reshape(rows, seq),
    )


VMEM_LIMIT = 20 * 1024 * 1024
BF16 = jnp.bfloat16
F32 = jnp.float32


def along(z, d, lines):
    return z ^ d if lines & (lines - 1) == 0 else (z + lines - d) % lines


def chunk_kernel(
    offset, kind, units, chips, sources, sorted_ref, place_ref, perm_ref, *refs
):
    first, last = kind
    parts = len(units)
    arrays = 1 + max(source[0] for source in sources)
    tokens_of, refs = refs[: len(chips) + 1], refs[len(chips) + 1 :]
    here_refs, there_refs, refs = refs[:arrays], refs[arrays : 2 * arrays], refs[2 * arrays :]
    if first:
        *outs, tokens_ref, weights_ref, sems, lifted_ref, g_ref, act_ref, pre_ref = refs
    elif last:
        out_in, back_in, *outs, tokens_ref, weights_ref, sems = refs[:-6]
        lifted_ref, g_ref, act_ref, pre_ref = refs[-6:-2]
        out_acc, back_acc = refs[-2:]
    else:
        out_in, back_in, *outs, tokens_ref, weights_ref, sems = refs[:-4]
        lifted_ref, g_ref, act_ref, pre_ref = refs[-4:]
    if not last:
        out_acc, back_acc = outs
    j = pl.program_id(0)
    rows, seq = tokens_ref.shape[2:4]
    per_block = lifted_ref.shape[0] // seq
    places = [(j + offset) * per_block + i for i in range(per_block)]
    lines, _, depth2, _ = weights_ref.shape
    depth = depth2 // 2
    starts = [sum(n for _, n in units[:part]) for part in range(parts)]

    @pl.when(j == 0)
    def _():
        y, z = place_ref[0], place_ref[1]
        copies = []
        for i, chip in enumerate(chips):
            for k, ref in enumerate((tokens_of[i], tokens_of[-1].at[chip])):
                copies.append(
                    pltpu.make_async_copy(ref, tokens_ref.at[2 * i + k], sems.at[len(copies)])
                )
        for i, start, d, to_row, to_unit, n, wide in sources:
            from_z = along(z, d, lines)
            for to_y, ref in ((y, here_refs[i]), (1 - y, there_refs[i])):
                to = weights_ref.at[from_z, to_y, pl.ds(to_row, n), pl.ds(to_unit, wide)]
                copies.append(
                    pltpu.make_async_copy(ref.at[pl.ds(start, n)], to, sems.at[len(copies)])
                )
        for copy in copies:
            copy.start()
        for copy in copies:
            copy.wait()

    width = lifted_ref.shape[1]
    here = [sorted_ref[at] for at in places]

    def pick_up(member):
        for i, at in enumerate(places):
            row = perm_ref[at]
            source = row // rows - 2 * chips[0]
            tokens = pl.ds(i * seq, seq)

            @pl.when(here[i] == member)
            def _():
                lifted_ref[tokens, :] = tokens_ref[source, 0, lax.rem(row, rows)]
                g_ref[tokens, :] = tokens_ref[source, 1, lax.rem(row, rows)]

            @pl.when(here[i] != member)
            def _():
                lifted_ref[tokens, :] = jnp.zeros((seq, width), BF16)
                g_ref[tokens, :] = jnp.zeros((seq, width), BF16)

    def sums(member):
        pick_up(member)
        mine = [(start, n) for (m, n), start in zip(units, starts) if m == member]
        low, high = mine[0][0], mine[-1][0] + mine[-1][1]
        for s in range(low, high, 256):
            e = min(s + 256, high)
            up = weights_ref[:, :, :depth, s:e].reshape(width, e - s)
            down = weights_ref[:, :, depth:, s:e].reshape(width, e - s)
            v = jnp.dot(lifted_ref[...], up, preferred_element_type=F32)
            grads = jnp.dot(g_ref[...], down, preferred_element_type=F32)
            square = v * v
            t = jnp.tanh(v * (coef_c + (coef_c * 0.044715) * square))
            half_v = 0.5 * v
            act_ref[:, s - low : e - low] = (half_v + half_v * t).astype(BF16)
            slope = (0.5 + 0.5 * t) + (half_v * (1.0 - t * t)) * (
                coef_c + (3.0 * coef_c * 0.044715) * square
            )
            pre_ref[:, s - low : e - low] = (grads * slope).astype(BF16)
        up = weights_ref[:, :, :depth, low:high].reshape(width, high - low)
        down = weights_ref[:, :, depth:, low:high].reshape(width, high - low)
        dims = (((1,), (1,)), ((), ()))
        return (
            lax.dot_general(act_ref[:, : high - low], down, dims, preferred_element_type=F32),
            lax.dot_general(pre_ref[:, : high - low], up, dims, preferred_element_type=F32),
        )

    for at, member in enumerate(sorted(set(m for m, _ in units))):
        used = functools.reduce(jnp.logical_or, [m == member for m in here])

        @pl.when(used)
        def _():
            out_sum, back_sum = sums(member)
            if at > 0:
                out_acc[...] += out_sum
                back_acc[...] += back_sum
            elif first:
                out_acc[...] = out_sum
                back_acc[...] = back_sum
            else:
                out_acc[...] = out_in[...] + out_sum
                back_acc[...] = back_in[...] + back_sum

        if at == 0:

            @pl.when(jnp.logical_not(used))
            def _():
                out_acc[...] = jnp.zeros(out_acc.shape, F32) if first else out_in[...]
                back_acc[...] = jnp.zeros(back_acc.shape, F32) if first else back_in[...]

    if last:
        for p, at in enumerate(places):
            row = lax.rem(perm_ref[at], 2 * rows)
            tokens = pl.ds(p * seq, seq)
            low = 0
            for to_out, to_back in zip(outs[::2], outs[1::2]):
                n = to_out.shape[0]

                @pl.when(jnp.logical_and(row >= low, row < low + n))
                def _():
                    to = jnp.clip(row - low, 0, n - 1)
                    to_out[to] = out_acc[tokens, :].astype(to_out.dtype)
                    to_back[to] = back_acc[tokens, :].astype(to_back.dtype)

                low += n


def chunk(kind, blocks, chips, scalars, tokens_of, weights, sums, outs=None, weight=1):
    first, last = kind
    offset, number, per_block = blocks
    units, lines, depth2, here, there, sources = weights
    _, rows, seq, width = tokens_of[0].shape
    hidden = sum(n for _, n in units)
    size = per_block * seq

    tok = pl.BlockSpec((size, width), lambda j, *_: (j, 0))
    hbm = pl.BlockSpec(memory_space=pl.ANY)
    args = [*scalars, *(tokens_of[chip] for chip in chips), tokens_of[-1], *here, *there]
    specs = [pl.BlockSpec(memory_space=pltpu.HBM)] * (len(chips) + 1) + [hbm] * (2 * len(here))
    alias = {}
    out_specs = [tok, tok]
    out_shape = [jax.ShapeDtypeStruct((number * size, width), F32)] * 2
    scratch = [
        pltpu.VMEM((2 * len(chips), 2, rows, seq, width), BF16),
        pltpu.VMEM((lines, 2, depth2, hidden), BF16),
        pltpu.SemaphoreType.DMA((2 * len(sources) + 2 * len(chips),)),
        pltpu.VMEM((size, width), BF16),
        pltpu.VMEM((size, width), BF16),
        pltpu.VMEM((size, hidden), BF16),
        pltpu.VMEM((size, hidden), BF16),
    ]
    if not first:
        alias = {len(args): 0, len(args) + 1: 1}
        args += list(sums)
        specs += [tok, tok]
    if last:
        alias = {}
        shape = (rows, seq, width)
        out_shape = [jax.ShapeDtypeStruct(shape, dtype) for dtype in outs for _ in range(2)]
        out_specs = [pl.BlockSpec(shape, lambda *_: (0, 0, 0))] * len(out_shape)
        scratch += [pltpu.VMEM((size, width), F32)] * 2

    return pl.pallas_call(
        functools.partial(chunk_kernel, offset, kind, units, chips, sources),
        grid_spec=pltpu.PrefetchScalarGridSpec(
            num_scalar_prefetch=len(scalars),
            grid=(number,),
            in_specs=specs,
            out_specs=out_specs,
            scratch_shapes=scratch,
        ),
        out_shape=out_shape,
        input_output_aliases=alias,
        compiler_params=pltpu.CompilerParams(vmem_limit_bytes=VMEM_LIMIT),
        cost_estimate=pl.CostEstimate(
            flops=weight * 8 * number * size * width * hidden * 2 // 3,
            bytes_accessed=weight * (4 * width * hidden + 20 * number * size * width),
            transcendentals=weight * number * size * hidden,
        ),
        name="chunk",
    )(*args)


def finish_kernel(
    member_ref, x_ref, g_ref, gain_ref, out_ref, back_ref, other_out_ref, other_back_ref,
    across_ref, value_ref, grad_ref, coupling_ref,
):
    rows, seq, width = x_ref.shape
    diagonal = lax.broadcasted_iota(jnp.int32, (seq, seq), 0) == lax.broadcasted_iota(
        jnp.int32, (seq, seq), 1
    )
    for r in range(rows):
        x = x_ref[r].astype(F32)
        inv = 1.0 / jnp.sqrt(jnp.mean(x * x, axis=1, keepdims=True) + 1e-06)
        normed = x * inv
        gain = gain_ref[pl.ds(member_ref[pl.program_id(0) * rows + r], 1), :]
        back = gain * (
            back_ref[r] + other_back_ref[r].astype(F32) + across_ref[1, r].astype(F32)
        )
        stat = jnp.sum(normed * back, axis=1, keepdims=True) / width
        out = out_ref[r] + other_out_ref[r].astype(F32) + across_ref[0, r].astype(F32)
        value_ref[r] = (x + out).astype(BF16)
        grad_ref[r] = (g_ref[r].astype(F32) + (back - normed * stat) * inv).astype(BF16)
        line = jnp.sum(jnp.where(diagonal, stat, 0.0), axis=0, keepdims=True)
        coupling_ref[pl.ds(pl.program_id(0) * rows + r, 1), :] = line * math.sqrt(width)


def finish(member_own, x, g, gain, *sums):
    rows, seq, width = x.shape
    step = math.gcd(rows, 2)
    row = pl.BlockSpec((step, seq, width), lambda r, mem: (r, 0, 0))
    two = pl.BlockSpec((2, step, seq, width), lambda r, mem: (0, r, 0, 0))
    return pl.pallas_call(
        finish_kernel,
        grid_spec=pltpu.PrefetchScalarGridSpec(
            num_scalar_prefetch=1,
            grid=(rows // step,),
            in_specs=[
                row, row, pl.BlockSpec(gain.shape, lambda r, mem: (0, 0)), row, row, row, row, two
            ],
            out_specs=[row, row, pl.BlockSpec((rows, seq), lambda r, mem: (0, 0))],
        ),
        out_shape=[
            jax.ShapeDtypeStruct((rows, seq, width), BF16),
            jax.ShapeDtypeStruct((rows, seq, width), BF16),
            jax.ShapeDtypeStruct((rows, seq), F32),
        ],
        compiler_params=pltpu.CompilerParams(vmem_limit_bytes=VMEM_LIMIT // 2),
        name="finish",
    )(member_own, x, g, gain, *sums)


def sort_rows(picks):
    index = jnp.arange(picks.shape[0], dtype=jnp.int32)
    before = (picks[None, :] < picks[:, None]) | (
        (picks[None, :] == picks[:, None]) & (index[None, :] < index[:, None])
    )
    pos = jnp.sum(before.astype(jnp.int32), axis=1)
    at = pos[None, :] == index[:, None]
    perm = jnp.sum(jnp.where(at, index[None, :], 0), axis=1)
    return perm, jnp.sum(jnp.where(at, picks[None, :], 0), axis=1)


def on_device_shared(ranks, tokens_in, upstream, member_pick, norm_gain, up_proj, down_proj):
    rows, seq, width = tokens_in.shape
    members, depth, hidden = up_proj.shape
    rank = lax.axis_index("row")
    core = lax.rem(rank, 2)
    x_at = lax.axis_index("grp")
    y_at = lax.rem(rank // 2, 2)
    lines = ranks // 4

    def partner(a):
        return lax.ppermute(a, "row", [(i, i ^ 1) for i in range(ranks)])

    def over_y(a):
        return lax.ppermute(a, "row", [(i, i ^ 2) for i in range(ranks)])

    def over_x(a):
        return lax.ppermute(a, "grp", [(0, 1), (1, 0)])

    def shift_z(a, d):
        pairs = [(4 * along(i // 4, d, lines) + i % 4, i) for i in range(ranks)]
        return lax.ppermute(a, "row", pairs)

    def after(a, *others):
        return lax.optimization_barrier((a, *others))[0]

    unit = hidden // 32
    quarter, half = 7 * unit, 2 * unit

    def units_of(c, both):
        return jnp.concatenate(
            [
                lax.dynamic_slice_in_dim(both, (2 * x_at + c) * quarter, quarter, 3),
                lax.dynamic_slice_in_dim(both, 4 * quarter + c * half, half, 3),
            ],
            axis=3,
        )

    def both_cores(mine, theirs):
        even = core == 0
        whole = jnp.concatenate(
            [jnp.where(even, mine, theirs), jnp.where(even, theirs, mine)], axis=2
        )
        return whole.reshape(mine.shape[0], 4 * depth, mine.shape[3])

    def head_of(c):
        at = (2 * x_at + c) * quarter
        return jnp.stack(
            [lax.dynamic_slice(a, (0, 0, at), (1, depth, 2 * unit)) for a in (up_proj, down_proj)],
            axis=1,
        )

    head_theirs = partner(head_of(1 - core))
    shard_head = both_cores(head_of(core), head_theirs)
    both = jnp.stack([after(up_proj, shard_head), after(down_proj, shard_head)], axis=1)
    theirs = partner(after(units_of(1 - core, both), shard_head))
    shard = both_cores(units_of(core, both), theirs)

    groups = [
        [(0, 0, 2 * unit)],
        [(0, 2 * unit, 4 * unit)],
        [(0, 6 * unit, unit), (1, 0, 3 * unit)],
        [(1, 3 * unit, 4 * unit)],
        [(0, quarter, half), (1, quarter, half)],
    ]
    own_rows = 4 * depth
    own_with = [
        [(0, 0, own_rows), (1, 0, own_rows), (2, 0, own_rows // 2)],
        [(2, own_rows // 2, own_rows // 2)],
        [(3, 0, own_rows // 2)],
        [(3, own_rows // 2, own_rows // 2)],
        [(4, 0, own_rows)],
    ]

    def own(group, row, n, first=0, wide=None):
        parts = []
        last = first + (wide or sum(k for _, _, k in groups[group]))
        at = 0
        for member, start, k in groups[group]:
            low, high = max(first, at), min(last, at + k)
            if low < high:
                parts.append(shard[member, row : row + n, start + low - at : start + high - at])
            at += k
        return jnp.concatenate(parts, axis=1)

    send = [shard_head[0]] + [own(group, 0, own_rows) for group in range(1, len(groups))]
    here, there, shifted, held = [], [], [], [[] for _ in groups]

    def along_z(step, *waits):
        mine = after(send[step], *shifted[-1], *waits) if step else send[0]
        shifted.append([shift_z(mine, d) for d in range(1, lines)])

    def across_y(step, *waits):
        wide = send[step].shape[1]
        parts = []

        def add(array, group, d, row, first):
            start = sum(a.shape[0] for a in parts)
            held[group].append((step, start, d, row, first, array.shape[0], wide))
            parts.append(array)

        for group, row, n in own_with[step]:
            for first in range(0, send[group].shape[1], wide):
                mine = send[0] if group == 0 else own(group, row, n, first, wide)
                add(mine, group, 0, row, first)
        for d, rows_from in enumerate(shifted[step]):
            add(rows_from, step, d + 1, 0, 0)
        here.append(jnp.concatenate(parts))
        there.append(over_y(after(here[step], *there[-1:], *waits)))

    def weights_of(*which):
        units = [(member, n) for group in which for member, _, n in groups[group]]
        used = sorted(set(source[0] for group in which for source in held[group]))
        sources = []
        at = 0
        for group in which:
            for i, start, d, row, first, n, wide in held[group]:
                sources.append((used.index(i), start, d, row, at + first, n, wide))
            at += send[group].shape[1]
        arrays = [here[i] for i in used], [there[i] for i in used]
        return units, lines, own_rows, *arrays, sources

    per_block = math.gcd(2 * rows, 4)
    per_chip = 2 * rows // per_block
    along_z(0)
    pick_own = member_pick[:, 0]
    pick_near = jnp.concatenate([pick_own, over_x(after(pick_own, send[0]))])
    x = after(tokens_in, shifted[0][0]).astype(F32)
    gain = jnp.zeros((rows, width), F32)
    for member in range(members):
        gain = jnp.where(pick_own[:, None] == member, norm_gain[member][None, :], gain)
    normed = x * (1.0 / jnp.sqrt(jnp.mean(x * x, axis=2, keepdims=True) + 1e-06))
    lifted = (normed * gain[:, None, :]).astype(BF16)
    near = jnp.stack([lifted, upstream])
    lifted_over = over_x(lifted)
    across_y(0)
    along_z(1)
    pick_far = partner(after(pick_near, shifted[0][-1]))

    perm, member_sorted = sort_rows(jnp.concatenate([pick_near[rows:], pick_far[rows:]]))
    perm_own, member_sorted_own = sort_rows(jnp.concatenate([pick_own, pick_far[:rows]]))
    scalars = (
        jnp.concatenate([member_sorted, member_sorted_own]),
        jnp.stack([y_at, rank // 4]),
        jnp.concatenate([perm + 2 * rows, perm_own]),
    )

    along_z(2, there[0], lifted_over, *scalars)
    across_y(1)
    over = jnp.stack([lifted_over, over_x(after(upstream, there[0], *shifted[1]))])
    along_z(3, there[1], over)
    across_y(2)
    far = partner(after(jnp.stack([near, over]), *shifted[2], there[1]))
    along_z(4, there[2], far)
    across_y(3)
    tokens_of = (near, over, far)
    over_blocks, own_blocks = (0, per_chip, per_block), (per_chip, per_chip, per_block)
    sums = chunk(
        (True, False), over_blocks, (1,), scalars,
        (near, after(over, *shifted[3]), far), weights_of(0, 1, 2), None,
    )
    across_y(4)
    sums = (after(sums[0], *shifted[4]), sums[1])
    *same, other_out, other_back = chunk(
        (False, True), over_blocks, (1,), scalars, tokens_of, weights_of(3), sums,
        (BF16, BF16), 0,
    )
    across = jnp.stack(
        [
            (a.astype(F32) + partner(b).astype(F32)).astype(BF16)
            for a, b in zip(same, (other_out, other_back))
        ]
    )
    tokens_of = (after(near, across), over, far)
    across = over_x(across)
    sums = chunk(
        (True, False), own_blocks, (0,), scalars, tokens_of, weights_of(0, 1, 2, 3), None, None, 0
    )
    out, back, packed_out, packed_back = chunk(
        (False, True), own_blocks, (0,), scalars, tokens_of, weights_of(4), sums, (F32, BF16), 0
    )
    return tuple(
        finish(
            pick_own, tokens_in, upstream, norm_gain, out, back,
            partner(packed_out), partner(packed_back), across,
        )
    )


def solution(mesh):
    ranks = mesh.shape["row"]
    four = mesh.shape["feat"] == 1 and ranks % 4 == 0 and mesh.shape["grp"] == 2

    def on_device(tokens_in, upstream, member_pick, norm_gain, up_proj, down_proj):
        args = (tokens_in, upstream, member_pick, norm_gain, up_proj, down_proj)
        if four and member_pick.shape[1] == 1 and up_proj.shape[0] == 2:
            return on_device_shared(ranks, *args)
        return on_device_general(*args)

    in_specs = (
        P(("grp", "row"), None, "feat"),
        P(("grp", "row"), None, "feat"),
        P(("grp", "row"), None),
        P(),
        P(None, "row", "feat"),
        P(None, "row", "feat"),
    )
    out_specs = (
        P(("grp", "row"), None, "feat"),
        P(("grp", "row"), None, "feat"),
        P(("grp", "row"), None),
    )
    return jax.shard_map(
        on_device, mesh=mesh, in_specs=in_specs, out_specs=out_specs, check_vma=False
    )
```

```python
import functools
import math

import jax
import jax.numpy as jnp
from jax import lax
from jax.experimental import pallas as pl
from jax.experimental.pallas import tpu as pltpu
from jax.sharding import PartitionSpec as P

coef_c = math.sqrt(2.0 / math.pi)


def gelu_tanh(v):
    return 0.5 * v * (1.0 + jnp.tanh(coef_c * (v + 0.044715 * v * v * v)))


def gelu_slope(v):
    inner = jnp.tanh(coef_c * (v + 0.044715 * v * v * v))
    return 0.5 * (1.0 + inner) + 0.5 * v * (1.0 - inner * inner) * coef_c * (
        1.0 + 3.0 * 0.044715 * v * v
    )


def on_device_general(tokens_in, upstream, member_pick, norm_gain, up_proj, down_proj):
    rows, seq, half = tokens_in.shape
    count = rows * seq
    members = up_proj.shape[0]
    pick = member_pick.shape[1]
    whole_x, whole_g = (
        lax.all_gather(tokens_in, "feat", axis=2, tiled=True),
        lax.all_gather(upstream, "feat", axis=2, tiled=True),
    )
    width = whole_x.shape[2]
    flat_x = whole_x.reshape(count, width).astype(jnp.float32)
    flat_g = whole_g.reshape(count, width)
    inv_rms = 1.0 / jnp.sqrt(jnp.mean(flat_x * flat_x, axis=1, keepdims=True) + 1e-06)
    normed = flat_x * inv_rms
    labels = jnp.arange(members, dtype=jnp.int32)
    chosen = (
        jnp.sum((member_pick[:, :, None] == labels[None, None, :]).astype(jnp.float32), axis=1)
        / pick
    )
    chosen_tok = jnp.repeat(chosen, seq, axis=0)
    out_half = jnp.zeros((count, half), jnp.float32)
    back_half = jnp.zeros((count, half), jnp.float32)
    for member in range(members):
        lifted = (normed * norm_gain[member][None, :]).astype(jnp.bfloat16)
        up_full = lax.all_gather(up_proj[member], "row", axis=0, tiled=True)
        hidden = jnp.dot(lifted, up_full, preferred_element_type=jnp.float32)
        act = gelu_tanh(hidden).astype(jnp.bfloat16)
        piece = lax.all_gather(down_proj[member], "row", axis=0, tiled=True)
        block = lax.dot_general(
            act, piece, (((1,), (1,)), ((), ())), preferred_element_type=jnp.float32
        )
        grads = jnp.dot(flat_g, piece, preferred_element_type=jnp.float32)
        pre_grad = (grads * gelu_slope(hidden)).astype(jnp.bfloat16)
        in_grad = lax.dot_general(
            pre_grad, up_full, (((1,), (1,)), ((), ())), preferred_element_type=jnp.float32
        )
        weight_col = chosen_tok[:, member : member + 1]
        out_term = weight_col * block
        back_term = weight_col * norm_gain[member][None, :] * in_grad
        out_part, back_part = (
            lax.psum_scatter(
                out_term.astype(jnp.bfloat16), "feat", scatter_dimension=1, tiled=True
            ).astype(jnp.float32),
            lax.psum_scatter(
                back_term.astype(jnp.bfloat16), "feat", scatter_dimension=1, tiled=True
            ).astype(jnp.float32),
        )
        out_half = out_half + out_part
        back_half = back_half + back_part
    own_x = tokens_in.reshape(count, half).astype(jnp.float32)
    normed_half = own_x * inv_rms
    stat = lax.psum(jnp.sum(normed_half * back_half, axis=1, keepdims=True), "feat") / width
    coupling = stat * math.sqrt(width)
    own_g = upstream.reshape(count, half).astype(jnp.float32)
    value_out = (own_x + out_half).astype(jnp.bfloat16)
    grad_in = (own_g + (back_half - normed_half * stat) * inv_rms).astype(jnp.bfloat16)
    return (
        value_out.reshape(rows, seq, half),
        grad_in.reshape(rows, seq, half),
        coupling.reshape(rows, seq),
    )


VMEM_LIMIT = 20 * 1024 * 1024
BF16 = jnp.bfloat16
F32 = jnp.float32


def along(z, d, lines):
    return z ^ d if lines & (lines - 1) == 0 else (z + lines - d) % lines


def chunk_kernel(
    offset, kind, units, chips, sources, sorted_ref, place_ref, perm_ref, *refs
):
    first, last = kind
    parts = len(units)
    arrays = 1 + max(source[0] for source in sources)
    tokens_of, refs = refs[: len(chips) + 1], refs[len(chips) + 1 :]
    here_refs, there_refs, refs = refs[:arrays], refs[arrays : 2 * arrays], refs[2 * arrays :]
    if first:
        *outs, tokens_ref, weights_ref, sems, lifted_ref, g_ref, act_ref, pre_ref = refs
    elif last:
        out_in, back_in, *outs, tokens_ref, weights_ref, sems = refs[:-6]
        lifted_ref, g_ref, act_ref, pre_ref = refs[-6:-2]
        out_acc, back_acc = refs[-2:]
    else:
        out_in, back_in, *outs, tokens_ref, weights_ref, sems = refs[:-4]
        lifted_ref, g_ref, act_ref, pre_ref = refs[-4:]
    if not last:
        out_acc, back_acc = outs
    j = pl.program_id(0)
    rows, seq = tokens_ref.shape[2:4]
    per_block = lifted_ref.shape[0] // seq
    places = [(j + offset) * per_block + i for i in range(per_block)]
    lines, _, depth2, _ = weights_ref.shape
    depth = depth2 // 2
    starts = [sum(n for _, n in units[:part]) for part in range(parts)]

    @pl.when(j == 0)
    def _():
        y, z = place_ref[0], place_ref[1]
        copies = []
        for i, chip in enumerate(chips):
            for k, ref in enumerate((tokens_of[i], tokens_of[-1].at[chip])):
                copies.append(
                    pltpu.make_async_copy(ref, tokens_ref.at[2 * i + k], sems.at[len(copies)])
                )
        for i, start, d, to_row, to_unit, n, wide in sources:
            from_z = along(z, d, lines)
            for to_y, ref in ((y, here_refs[i]), (1 - y, there_refs[i])):
                to = weights_ref.at[from_z, to_y, pl.ds(to_row, n), pl.ds(to_unit, wide)]
                copies.append(
                    pltpu.make_async_copy(ref.at[pl.ds(start, n)], to, sems.at[len(copies)])
                )
        for copy in copies:
            copy.start()
        for copy in copies:
            copy.wait()

    width = lifted_ref.shape[1]
    here = [sorted_ref[at] for at in places]

    def pick_up(member):
        for i, at in enumerate(places):
            row = perm_ref[at]
            source = row // rows - 2 * chips[0]
            tokens = pl.ds(i * seq, seq)

            @pl.when(here[i] == member)
            def _():
                lifted_ref[tokens, :] = tokens_ref[source, 0, lax.rem(row, rows)]
                g_ref[tokens, :] = tokens_ref[source, 1, lax.rem(row, rows)]

            @pl.when(here[i] != member)
            def _():
                lifted_ref[tokens, :] = jnp.zeros((seq, width), BF16)
                g_ref[tokens, :] = jnp.zeros((seq, width), BF16)

    def sums(member):
        pick_up(member)
        mine = [(start, n) for (m, n), start in zip(units, starts) if m == member]
        low, high = mine[0][0], mine[-1][0] + mine[-1][1]
        for s in range(low, high, 256):
            e = min(s + 256, high)
            up = weights_ref[:, :, :depth, s:e].reshape(width, e - s)
            down = weights_ref[:, :, depth:, s:e].reshape(width, e - s)
            v = jnp.dot(lifted_ref[...], up, preferred_element_type=F32)
            grads = jnp.dot(g_ref[...], down, preferred_element_type=F32)
            square = v * v
            t = jnp.tanh(v * (coef_c + (coef_c * 0.044715) * square))
            half_v = 0.5 * v
            act_ref[:, s - low : e - low] = (half_v + half_v * t).astype(BF16)
            slope = (0.5 + 0.5 * t) + (half_v * (1.0 - t * t)) * (
                coef_c + (3.0 * coef_c * 0.044715) * square
            )
            pre_ref[:, s - low : e - low] = (grads * slope).astype(BF16)
        up = weights_ref[:, :, :depth, low:high].reshape(width, high - low)
        down = weights_ref[:, :, depth:, low:high].reshape(width, high - low)
        dims = (((1,), (1,)), ((), ()))
        return (
            lax.dot_general(act_ref[:, : high - low], down, dims, preferred_element_type=F32),
            lax.dot_general(pre_ref[:, : high - low], up, dims, preferred_element_type=F32),
        )

    for at, member in enumerate(sorted(set(m for m, _ in units))):
        used = functools.reduce(jnp.logical_or, [m == member for m in here])

        @pl.when(used)
        def _():
            out_sum, back_sum = sums(member)
            if at > 0:
                out_acc[...] += out_sum
                back_acc[...] += back_sum
            elif first:
                out_acc[...] = out_sum
                back_acc[...] = back_sum
            else:
                out_acc[...] = out_in[...] + out_sum
                back_acc[...] = back_in[...] + back_sum

        if at == 0:

            @pl.when(jnp.logical_not(used))
            def _():
                out_acc[...] = jnp.zeros(out_acc.shape, F32) if first else out_in[...]
                back_acc[...] = jnp.zeros(back_acc.shape, F32) if first else back_in[...]

    if last:
        for p, at in enumerate(places):
            row = lax.rem(perm_ref[at], 2 * rows)
            tokens = pl.ds(p * seq, seq)
            low = 0
            for to_out, to_back in zip(outs[::2], outs[1::2]):
                n = to_out.shape[0]

                @pl.when(jnp.logical_and(row >= low, row < low + n))
                def _():
                    to = jnp.clip(row - low, 0, n - 1)
                    to_out[to] = out_acc[tokens, :].astype(to_out.dtype)
                    to_back[to] = back_acc[tokens, :].astype(to_back.dtype)

                low += n


def chunk(kind, blocks, chips, scalars, tokens_of, weights, sums, outs=None, weight=1):
    first, last = kind
    offset, number, per_block = blocks
    units, lines, depth2, here, there, sources = weights
    _, rows, seq, width = tokens_of[0].shape
    hidden = sum(n for _, n in units)
    size = per_block * seq

    tok = pl.BlockSpec((size, width), lambda j, *_: (j, 0))
    hbm = pl.BlockSpec(memory_space=pl.ANY)
    args = [*scalars, *(tokens_of[chip] for chip in chips), tokens_of[-1], *here, *there]
    specs = [pl.BlockSpec(memory_space=pltpu.HBM)] * (len(chips) + 1) + [hbm] * (2 * len(here))
    alias = {}
    out_specs = [tok, tok]
    out_shape = [jax.ShapeDtypeStruct((number * size, width), F32)] * 2
    scratch = [
        pltpu.VMEM((2 * len(chips), 2, rows, seq, width), BF16),
        pltpu.VMEM((lines, 2, depth2, hidden), BF16),
        pltpu.SemaphoreType.DMA((2 * len(sources) + 2 * len(chips),)),
        pltpu.VMEM((size, width), BF16),
        pltpu.VMEM((size, width), BF16),
        pltpu.VMEM((size, hidden), BF16),
        pltpu.VMEM((size, hidden), BF16),
    ]
    if not first:
        alias = {len(args): 0, len(args) + 1: 1}
        args += list(sums)
        specs += [tok, tok]
    if last:
        alias = {}
        shape = (rows, seq, width)
        out_shape = [jax.ShapeDtypeStruct(shape, dtype) for dtype in outs for _ in range(2)]
        out_specs = [pl.BlockSpec(shape, lambda *_: (0, 0, 0))] * len(out_shape)
        scratch += [pltpu.VMEM((size, width), F32)] * 2

    return pl.pallas_call(
        functools.partial(chunk_kernel, offset, kind, units, chips, sources),
        grid_spec=pltpu.PrefetchScalarGridSpec(
            num_scalar_prefetch=len(scalars),
            grid=(number,),
            in_specs=specs,
            out_specs=out_specs,
            scratch_shapes=scratch,
        ),
        out_shape=out_shape,
        input_output_aliases=alias,
        compiler_params=pltpu.CompilerParams(vmem_limit_bytes=VMEM_LIMIT),
        cost_estimate=pl.CostEstimate(
            flops=weight * 8 * number * size * width * hidden * 2 // 3,
            bytes_accessed=weight * (4 * width * hidden + 20 * number * size * width),
            transcendentals=weight * number * size * hidden,
        ),
        name="chunk",
    )(*args)


def finish_kernel(
    member_ref, x_ref, g_ref, gain_ref, out_ref, back_ref, other_out_ref, other_back_ref,
    across_ref, value_ref, grad_ref, coupling_ref,
):
    rows, seq, width = x_ref.shape
    diagonal = lax.broadcasted_iota(jnp.int32, (seq, seq), 0) == lax.broadcasted_iota(
        jnp.int32, (seq, seq), 1
    )
    for r in range(rows):
        x = x_ref[r].astype(F32)
        inv = 1.0 / jnp.sqrt(jnp.mean(x * x, axis=1, keepdims=True) + 1e-06)
        normed = x * inv
        gain = gain_ref[pl.ds(member_ref[pl.program_id(0) * rows + r], 1), :]
        back = gain * (
            back_ref[r] + other_back_ref[r].astype(F32) + across_ref[1, r].astype(F32)
        )
        stat = jnp.sum(normed * back, axis=1, keepdims=True) / width
        out = out_ref[r] + other_out_ref[r].astype(F32) + across_ref[0, r].astype(F32)
        value_ref[r] = (x + out).astype(BF16)
        grad_ref[r] = (g_ref[r].astype(F32) + (back - normed * stat) * inv).astype(BF16)
        line = jnp.sum(jnp.where(diagonal, stat, 0.0), axis=0, keepdims=True)
        coupling_ref[pl.ds(pl.program_id(0) * rows + r, 1), :] = line * math.sqrt(width)


def finish(member_own, x, g, gain, *sums):
    rows, seq, width = x.shape
    step = math.gcd(rows, 2)
    row = pl.BlockSpec((step, seq, width), lambda r, mem: (r, 0, 0))
    two = pl.BlockSpec((2, step, seq, width), lambda r, mem: (0, r, 0, 0))
    return pl.pallas_call(
        finish_kernel,
        grid_spec=pltpu.PrefetchScalarGridSpec(
            num_scalar_prefetch=1,
            grid=(rows // step,),
            in_specs=[
                row, row, pl.BlockSpec(gain.shape, lambda r, mem: (0, 0)), row, row, row, row, two
            ],
            out_specs=[row, row, pl.BlockSpec((rows, seq), lambda r, mem: (0, 0))],
        ),
        out_shape=[
            jax.ShapeDtypeStruct((rows, seq, width), BF16),
            jax.ShapeDtypeStruct((rows, seq, width), BF16),
            jax.ShapeDtypeStruct((rows, seq), F32),
        ],
        compiler_params=pltpu.CompilerParams(vmem_limit_bytes=VMEM_LIMIT // 2),
        name="finish",
    )(member_own, x, g, gain, *sums)


def sort_rows(picks):
    index = jnp.arange(picks.shape[0], dtype=jnp.int32)
    before = (picks[None, :] < picks[:, None]) | (
        (picks[None, :] == picks[:, None]) & (index[None, :] < index[:, None])
    )
    pos = jnp.sum(before.astype(jnp.int32), axis=1)
    at = pos[None, :] == index[:, None]
    perm = jnp.sum(jnp.where(at, index[None, :], 0), axis=1)
    return perm, jnp.sum(jnp.where(at, picks[None, :], 0), axis=1)


def on_device_shared(ranks, tokens_in, upstream, member_pick, norm_gain, up_proj, down_proj):
    rows, seq, width = tokens_in.shape
    members, depth, hidden = up_proj.shape
    rank = lax.axis_index("row")
    core = lax.rem(rank, 2)
    x_at = lax.axis_index("grp")
    y_at = lax.rem(rank // 2, 2)
    lines = ranks // 4

    def partner(a):
        return lax.ppermute(a, "row", [(i, i ^ 1) for i in range(ranks)])

    def over_y(a):
        return lax.ppermute(a, "row", [(i, i ^ 2) for i in range(ranks)])

    def over_x(a):
        return lax.ppermute(a, "grp", [(0, 1), (1, 0)])

    def shift_z(a, d):
        pairs = [(4 * along(i // 4, d, lines) + i % 4, i) for i in range(ranks)]
        return lax.ppermute(a, "row", pairs)

    def after(a, *others):
        return lax.optimization_barrier((a, *others))[0]

    unit = hidden // 32
    quarter, half = 7 * unit, 2 * unit

    def units_of(c, both):
        return jnp.concatenate(
            [
                lax.dynamic_slice_in_dim(both, (2 * x_at + c) * quarter, quarter, 3),
                lax.dynamic_slice_in_dim(both, 4 * quarter + c * half, half, 3),
            ],
            axis=3,
        )

    def both_cores(mine, theirs):
        even = core == 0
        whole = jnp.concatenate(
            [jnp.where(even, mine, theirs), jnp.where(even, theirs, mine)], axis=2
        )
        return whole.reshape(mine.shape[0], 4 * depth, mine.shape[3])

    def head_of(c):
        at = (2 * x_at + c) * quarter
        return jnp.stack(
            [lax.dynamic_slice(a, (0, 0, at), (1, depth, 2 * unit)) for a in (up_proj, down_proj)],
            axis=1,
        )

    head_theirs = partner(head_of(1 - core))
    shard_head = both_cores(head_of(core), head_theirs)
    both = jnp.stack([after(up_proj, shard_head), after(down_proj, shard_head)], axis=1)
    theirs = partner(after(units_of(1 - core, both), shard_head))
    shard = both_cores(units_of(core, both), theirs)

    groups = [
        [(0, 0, 2 * unit)],
        [(0, 2 * unit, 4 * unit)],
        [(0, 6 * unit, unit), (1, 0, 3 * unit)],
        [(1, 3 * unit, 4 * unit)],
        [(0, quarter, half), (1, quarter, half)],
    ]
    own_rows = 4 * depth
    own_with = [
        [(0, 0, own_rows), (1, 0, own_rows), (2, 0, own_rows // 2)],
        [(2, own_rows // 2, own_rows // 2)],
        [(3, 0, own_rows // 2)],
        [(3, own_rows // 2, own_rows // 2)],
        [(4, 0, own_rows)],
    ]

    def own(group, row, n, first=0, wide=None):
        parts = []
        last = first + (wide or sum(k for _, _, k in groups[group]))
        at = 0
        for member, start, k in groups[group]:
            low, high = max(first, at), min(last, at + k)
            if low < high:
                parts.append(shard[member, row : row + n, start + low - at : start + high - at])
            at += k
        return jnp.concatenate(parts, axis=1)

    send = [shard_head[0]] + [own(group, 0, own_rows) for group in range(1, len(groups))]
    here, there, shifted, held = [], [], [], [[] for _ in groups]

    def along_z(step, *waits):
        mine = after(send[step], *shifted[-1], *waits) if step else send[0]
        shifted.append([shift_z(mine, d) for d in range(1, lines)])

    def across_y(step, *waits):
        wide = send[step].shape[1]
        parts = []

        def add(array, group, d, row, first):
            start = sum(a.shape[0] for a in parts)
            held[group].append((step, start, d, row, first, array.shape[0], wide))
            parts.append(array)

        for group, row, n in own_with[step]:
            for first in range(0, send[group].shape[1], wide):
                mine = send[0] if group == 0 else own(group, row, n, first, wide)
                add(mine, group, 0, row, first)
        for d, rows_from in enumerate(shifted[step]):
            add(rows_from, step, d + 1, 0, 0)
        here.append(jnp.concatenate(parts))
        there.append(over_y(after(here[step], *there[-1:], *waits)))

    def weights_of(*which):
        units = [(member, n) for group in which for member, _, n in groups[group]]
        used = sorted(set(source[0] for group in which for source in held[group]))
        sources = []
        at = 0
        for group in which:
            for i, start, d, row, first, n, wide in held[group]:
                sources.append((used.index(i), start, d, row, at + first, n, wide))
            at += send[group].shape[1]
        arrays = [here[i] for i in used], [there[i] for i in used]
        return units, lines, own_rows, *arrays, sources

    per_block = math.gcd(2 * rows, 4)
    per_chip = 2 * rows // per_block
    along_z(0)
    pick_own = member_pick[:, 0]
    pick_near = jnp.concatenate([pick_own, over_x(after(pick_own, send[0]))])
    x = after(tokens_in, shifted[0][0]).astype(F32)
    gain = jnp.zeros((rows, width), F32)
    for member in range(members):
        gain = jnp.where(pick_own[:, None] == member, norm_gain[member][None, :], gain)
    normed = x * (1.0 / jnp.sqrt(jnp.mean(x * x, axis=2, keepdims=True) + 1e-06))
    lifted = (normed * gain[:, None, :]).astype(BF16)
    near = jnp.stack([lifted, upstream])
    lifted_over = over_x(lifted)
    across_y(0)
    along_z(1)
    pick_far = partner(after(pick_near, shifted[0][-1]))

    perm, member_sorted = sort_rows(jnp.concatenate([pick_near[rows:], pick_far[rows:]]))
    perm_own, member_sorted_own = sort_rows(jnp.concatenate([pick_own, pick_far[:rows]]))
    scalars = (
        jnp.concatenate([member_sorted, member_sorted_own]),
        jnp.stack([y_at, rank // 4]),
        jnp.concatenate([perm + 2 * rows, perm_own]),
    )

    along_z(2, there[0], lifted_over, *scalars)
    across_y(1)
    over = jnp.stack([lifted_over, over_x(after(upstream, there[0], *shifted[1]))])
    along_z(3, there[1], over)
    across_y(2)
    far = partner(after(jnp.stack([near, over]), *shifted[2], there[1]))
    along_z(4, there[2], far)
    across_y(3)
    tokens_of = (near, over, far)
    over_blocks, own_blocks = (0, per_chip, per_block), (per_chip, per_chip, per_block)
    sums = chunk(
        (True, False), over_blocks, (1,), scalars,
        (near, after(over, *shifted[3]), far), weights_of(0, 1, 2), None,
    )
    sums = (after(sums[0], *shifted[4]), sums[1])
    *same, other_out, other_back = chunk(
        (False, True), over_blocks, (1,), scalars, tokens_of, weights_of(3), sums,
        (BF16, BF16), 0,
    )
    across = jnp.stack(
        [
            (a.astype(F32) + partner(b).astype(F32)).astype(BF16)
            for a, b in zip(same, (other_out, other_back))
        ]
    )
    across_y(4, across)
    tokens_of = (after(near, across), over, far)
    across = over_x(across)
    sums = chunk(
        (True, False), own_blocks, (0,), scalars, tokens_of, weights_of(0, 1, 2, 3), None, None, 0
    )
    out, back, packed_out, packed_back = chunk(
        (False, True), own_blocks, (0,), scalars, tokens_of, weights_of(4), sums, (F32, BF16), 0
    )
    return tuple(
        finish(
            pick_own, tokens_in, upstream, norm_gain, out, back,
            partner(packed_out), partner(packed_back), across,
        )
    )


def solution(mesh):
    ranks = mesh.shape["row"]
    four = mesh.shape["feat"] == 1 and ranks % 4 == 0 and mesh.shape["grp"] == 2

    def on_device(tokens_in, upstream, member_pick, norm_gain, up_proj, down_proj):
        args = (tokens_in, upstream, member_pick, norm_gain, up_proj, down_proj)
        if four and member_pick.shape[1] == 1 and up_proj.shape[0] == 2:
            return on_device_shared(ranks, *args)
        return on_device_general(*args)

    in_specs = (
        P(("grp", "row"), None, "feat"),
        P(("grp", "row"), None, "feat"),
        P(("grp", "row"), None),
        P(),
        P(None, "row", "feat"),
        P(None, "row", "feat"),
    )
    out_specs = (
        P(("grp", "row"), None, "feat"),
        P(("grp", "row"), None, "feat"),
        P(("grp", "row"), None),
    )
    return jax.shard_map(
        on_device, mesh=mesh, in_specs=in_specs, out_specs=out_specs, check_vma=False
    )
```

```python
import functools
import math

import jax
import jax.numpy as jnp
from jax import lax
from jax.experimental import pallas as pl
from jax.experimental.pallas import tpu as pltpu
from jax.sharding import PartitionSpec as P

coef_c = math.sqrt(2.0 / math.pi)


def gelu_tanh(v):
    return 0.5 * v * (1.0 + jnp.tanh(coef_c * (v + 0.044715 * v * v * v)))


def gelu_slope(v):
    inner = jnp.tanh(coef_c * (v + 0.044715 * v * v * v))
    return 0.5 * (1.0 + inner) + 0.5 * v * (1.0 - inner * inner) * coef_c * (
        1.0 + 3.0 * 0.044715 * v * v
    )


def on_device_general(tokens_in, upstream, member_pick, norm_gain, up_proj, down_proj):
    rows, seq, half = tokens_in.shape
    count = rows * seq
    members = up_proj.shape[0]
    pick = member_pick.shape[1]
    whole_x, whole_g = (
        lax.all_gather(tokens_in, "feat", axis=2, tiled=True),
        lax.all_gather(upstream, "feat", axis=2, tiled=True),
    )
    width = whole_x.shape[2]
    flat_x = whole_x.reshape(count, width).astype(jnp.float32)
    flat_g = whole_g.reshape(count, width)
    inv_rms = 1.0 / jnp.sqrt(jnp.mean(flat_x * flat_x, axis=1, keepdims=True) + 1e-06)
    normed = flat_x * inv_rms
    labels = jnp.arange(members, dtype=jnp.int32)
    chosen = (
        jnp.sum((member_pick[:, :, None] == labels[None, None, :]).astype(jnp.float32), axis=1)
        / pick
    )
    chosen_tok = jnp.repeat(chosen, seq, axis=0)
    out_half = jnp.zeros((count, half), jnp.float32)
    back_half = jnp.zeros((count, half), jnp.float32)
    for member in range(members):
        lifted = (normed * norm_gain[member][None, :]).astype(jnp.bfloat16)
        up_full = lax.all_gather(up_proj[member], "row", axis=0, tiled=True)
        hidden = jnp.dot(lifted, up_full, preferred_element_type=jnp.float32)
        act = gelu_tanh(hidden).astype(jnp.bfloat16)
        piece = lax.all_gather(down_proj[member], "row", axis=0, tiled=True)
        block = lax.dot_general(
            act, piece, (((1,), (1,)), ((), ())), preferred_element_type=jnp.float32
        )
        grads = jnp.dot(flat_g, piece, preferred_element_type=jnp.float32)
        pre_grad = (grads * gelu_slope(hidden)).astype(jnp.bfloat16)
        in_grad = lax.dot_general(
            pre_grad, up_full, (((1,), (1,)), ((), ())), preferred_element_type=jnp.float32
        )
        weight_col = chosen_tok[:, member : member + 1]
        out_term = weight_col * block
        back_term = weight_col * norm_gain[member][None, :] * in_grad
        out_part, back_part = (
            lax.psum_scatter(
                out_term.astype(jnp.bfloat16), "feat", scatter_dimension=1, tiled=True
            ).astype(jnp.float32),
            lax.psum_scatter(
                back_term.astype(jnp.bfloat16), "feat", scatter_dimension=1, tiled=True
            ).astype(jnp.float32),
        )
        out_half = out_half + out_part
        back_half = back_half + back_part
    own_x = tokens_in.reshape(count, half).astype(jnp.float32)
    normed_half = own_x * inv_rms
    stat = lax.psum(jnp.sum(normed_half * back_half, axis=1, keepdims=True), "feat") / width
    coupling = stat * math.sqrt(width)
    own_g = upstream.reshape(count, half).astype(jnp.float32)
    value_out = (own_x + out_half).astype(jnp.bfloat16)
    grad_in = (own_g + (back_half - normed_half * stat) * inv_rms).astype(jnp.bfloat16)
    return (
        value_out.reshape(rows, seq, half),
        grad_in.reshape(rows, seq, half),
        coupling.reshape(rows, seq),
    )


VMEM_LIMIT = 20 * 1024 * 1024
BF16 = jnp.bfloat16
F32 = jnp.float32


def chunk_kernel(
    offset, kind, units, chips, sources, sorted_ref, place_ref, perm_ref, *refs
):
    first, last = kind
    parts = len(units)
    arrays = 1 + max(source[0] for source in sources)
    tokens_of, refs = refs[: len(chips) + 1], refs[len(chips) + 1 :]
    here_refs, there_refs, refs = refs[:arrays], refs[arrays : 2 * arrays], refs[2 * arrays :]
    if first:
        *outs, tokens_ref, weights_ref, sems, lifted_ref, g_ref, act_ref, pre_ref = refs
    elif last:
        out_in, back_in, *outs, tokens_ref, weights_ref, sems = refs[:-6]
        lifted_ref, g_ref, act_ref, pre_ref = refs[-6:-2]
        out_acc, back_acc = refs[-2:]
    else:
        out_in, back_in, *outs, tokens_ref, weights_ref, sems = refs[:-4]
        lifted_ref, g_ref, act_ref, pre_ref = refs[-4:]
    if not last:
        out_acc, back_acc = outs
    j = pl.program_id(0)
    rows, seq = tokens_ref.shape[2:4]
    per_block = lifted_ref.shape[0] // seq
    places = [(j + offset) * per_block + i for i in range(per_block)]
    lines, _, depth2, _ = weights_ref.shape
    depth = depth2 // 2
    starts = [sum(n for _, n in units[:part]) for part in range(parts)]

    @pl.when(j == 0)
    def _():
        y, z = place_ref[0], place_ref[1]
        copies = []
        for i, chip in enumerate(chips):
            for k, ref in enumerate((tokens_of[i], tokens_of[-1].at[chip])):
                copies.append(
                    pltpu.make_async_copy(ref, tokens_ref.at[2 * i + k], sems.at[len(copies)])
                )
        for i, start, d, to_row, to_unit, n, wide in sources:
            from_z = lax.rem(z + lines - d, lines)
            for to_y, ref in ((y, here_refs[i]), (1 - y, there_refs[i])):
                to = weights_ref.at[from_z, to_y, pl.ds(to_row, n), pl.ds(to_unit, wide)]
                copies.append(
                    pltpu.make_async_copy(ref.at[pl.ds(start, n)], to, sems.at[len(copies)])
                )
        for copy in copies:
            copy.start()
        for copy in copies:
            copy.wait()

    width = lifted_ref.shape[1]
    here = [sorted_ref[at] for at in places]

    def pick_up(member):
        for i, at in enumerate(places):
            row = perm_ref[at]
            source = row // rows - 2 * chips[0]
            tokens = pl.ds(i * seq, seq)

            @pl.when(here[i] == member)
            def _():
                lifted_ref[tokens, :] = tokens_ref[source, 0, lax.rem(row, rows)]
                g_ref[tokens, :] = tokens_ref[source, 1, lax.rem(row, rows)]

            @pl.when(here[i] != member)
            def _():
                lifted_ref[tokens, :] = jnp.zeros((seq, width), BF16)
                g_ref[tokens, :] = jnp.zeros((seq, width), BF16)

    def sums(member):
        pick_up(member)
        mine = [(start, n) for (m, n), start in zip(units, starts) if m == member]
        low, high = mine[0][0], mine[-1][0] + mine[-1][1]
        for s in range(low, high, 256):
            e = min(s + 256, high)
            up = weights_ref[:, :, :depth, s:e].reshape(width, e - s)
            down = weights_ref[:, :, depth:, s:e].reshape(width, e - s)
            v = jnp.dot(lifted_ref[...], up, preferred_element_type=F32)
            grads = jnp.dot(g_ref[...], down, preferred_element_type=F32)
            square = v * v
            t = jnp.tanh(v * (coef_c + (coef_c * 0.044715) * square))
            half_v = 0.5 * v
            act_ref[:, s - low : e - low] = (half_v + half_v * t).astype(BF16)
            slope = (0.5 + 0.5 * t) + (half_v * (1.0 - t * t)) * (
                coef_c + (3.0 * coef_c * 0.044715) * square
            )
            pre_ref[:, s - low : e - low] = (grads * slope).astype(BF16)
        up = weights_ref[:, :, :depth, low:high].reshape(width, high - low)
        down = weights_ref[:, :, depth:, low:high].reshape(width, high - low)
        dims = (((1,), (1,)), ((), ()))
        return (
            lax.dot_general(act_ref[:, : high - low], down, dims, preferred_element_type=F32),
            lax.dot_general(pre_ref[:, : high - low], up, dims, preferred_element_type=F32),
        )

    for at, member in enumerate(sorted(set(m for m, _ in units))):
        used = functools.reduce(jnp.logical_or, [m == member for m in here])

        @pl.when(used)
        def _():
            out_sum, back_sum = sums(member)
            if at > 0:
                out_acc[...] += out_sum
                back_acc[...] += back_sum
            elif first:
                out_acc[...] = out_sum
                back_acc[...] = back_sum
            else:
                out_acc[...] = out_in[...] + out_sum
                back_acc[...] = back_in[...] + back_sum

        if at == 0:

            @pl.when(jnp.logical_not(used))
            def _():
                out_acc[...] = jnp.zeros(out_acc.shape, F32) if first else out_in[...]
                back_acc[...] = jnp.zeros(back_acc.shape, F32) if first else back_in[...]

    if last:
        for p, at in enumerate(places):
            row = lax.rem(perm_ref[at], 2 * rows)
            tokens = pl.ds(p * seq, seq)
            low = 0
            for to_out, to_back in zip(outs[::2], outs[1::2]):
                n = to_out.shape[0]

                @pl.when(jnp.logical_and(row >= low, row < low + n))
                def _():
                    to = jnp.clip(row - low, 0, n - 1)
                    to_out[to] = out_acc[tokens, :].astype(to_out.dtype)
                    to_back[to] = back_acc[tokens, :].astype(to_back.dtype)

                low += n


def chunk(kind, blocks, chips, scalars, tokens_of, weights, sums, outs=None, weight=1):
    first, last = kind
    offset, number, per_block = blocks
    units, lines, depth2, here, there, sources = weights
    _, rows, seq, width = tokens_of[0].shape
    hidden = sum(n for _, n in units)
    size = per_block * seq

    tok = pl.BlockSpec((size, width), lambda j, *_: (j, 0))
    hbm = pl.BlockSpec(memory_space=pl.ANY)
    args = [*scalars, *(tokens_of[chip] for chip in chips), tokens_of[-1], *here, *there]
    specs = [pl.BlockSpec(memory_space=pltpu.HBM)] * (len(chips) + 1) + [hbm] * (2 * len(here))
    alias = {}
    out_specs = [tok, tok]
    out_shape = [jax.ShapeDtypeStruct((number * size, width), F32)] * 2
    scratch = [
        pltpu.VMEM((2 * len(chips), 2, rows, seq, width), BF16),
        pltpu.VMEM((lines, 2, depth2, hidden), BF16),
        pltpu.SemaphoreType.DMA((2 * len(sources) + 2 * len(chips),)),
        pltpu.VMEM((size, width), BF16),
        pltpu.VMEM((size, width), BF16),
        pltpu.VMEM((size, hidden), BF16),
        pltpu.VMEM((size, hidden), BF16),
    ]
    if not first:
        alias = {len(args): 0, len(args) + 1: 1}
        args += list(sums)
        specs += [tok, tok]
    if last:
        alias = {}
        shape = (rows, seq, width)
        out_shape = [jax.ShapeDtypeStruct(shape, dtype) for dtype in outs for _ in range(2)]
        out_specs = [pl.BlockSpec(shape, lambda *_: (0, 0, 0))] * len(out_shape)
        scratch += [pltpu.VMEM((size, width), F32)] * 2

    return pl.pallas_call(
        functools.partial(chunk_kernel, offset, kind, units, chips, sources),
        grid_spec=pltpu.PrefetchScalarGridSpec(
            num_scalar_prefetch=len(scalars),
            grid=(number,),
            in_specs=specs,
            out_specs=out_specs,
            scratch_shapes=scratch,
        ),
        out_shape=out_shape,
        input_output_aliases=alias,
        compiler_params=pltpu.CompilerParams(vmem_limit_bytes=VMEM_LIMIT),
        cost_estimate=pl.CostEstimate(
            flops=weight * 8 * number * size * width * hidden * 2 // 3,
            bytes_accessed=weight * (4 * width * hidden + 20 * number * size * width),
            transcendentals=weight * number * size * hidden,
        ),
        name="chunk",
    )(*args)


def finish_kernel(
    member_ref, x_ref, g_ref, gain_ref, out_ref, back_ref, other_out_ref, other_back_ref,
    across_out_ref, across_back_ref, value_ref, grad_ref, coupling_ref,
):
    rows, seq, width = x_ref.shape
    diagonal = lax.broadcasted_iota(jnp.int32, (seq, seq), 0) == lax.broadcasted_iota(
        jnp.int32, (seq, seq), 1
    )
    for r in range(rows):
        x = x_ref[r].astype(F32)
        inv = 1.0 / jnp.sqrt(jnp.mean(x * x, axis=1, keepdims=True) + 1e-06)
        normed = x * inv
        gain = gain_ref[pl.ds(member_ref[pl.program_id(0) * rows + r], 1), :]
        back = gain * (
            back_ref[r] + other_back_ref[r].astype(F32) + across_back_ref[r].astype(F32)
        )
        stat = jnp.sum(normed * back, axis=1, keepdims=True) / width
        out = out_ref[r] + other_out_ref[r].astype(F32) + across_out_ref[r].astype(F32)
        value_ref[r] = (x + out).astype(BF16)
        grad_ref[r] = (g_ref[r].astype(F32) + (back - normed * stat) * inv).astype(BF16)
        line = jnp.sum(jnp.where(diagonal, stat, 0.0), axis=0, keepdims=True)
        coupling_ref[pl.ds(pl.program_id(0) * rows + r, 1), :] = line * math.sqrt(width)


def finish(member_own, x, g, gain, *sums):
    rows, seq, width = x.shape
    step = math.gcd(rows, 2)
    row = pl.BlockSpec((step, seq, width), lambda r, mem: (r, 0, 0))
    return pl.pallas_call(
        finish_kernel,
        grid_spec=pltpu.PrefetchScalarGridSpec(
            num_scalar_prefetch=1,
            grid=(rows // step,),
            in_specs=[
                row, row, pl.BlockSpec(gain.shape, lambda r, mem: (0, 0)), row, row, row, row, row, row
            ],
            out_specs=[row, row, pl.BlockSpec((rows, seq), lambda r, mem: (0, 0))],
        ),
        out_shape=[
            jax.ShapeDtypeStruct((rows, seq, width), BF16),
            jax.ShapeDtypeStruct((rows, seq, width), BF16),
            jax.ShapeDtypeStruct((rows, seq), F32),
        ],
        compiler_params=pltpu.CompilerParams(vmem_limit_bytes=VMEM_LIMIT // 2),
        name="finish",
    )(member_own, x, g, gain, *sums)


def sort_rows(picks):
    index = jnp.arange(picks.shape[0], dtype=jnp.int32)
    before = (picks[None, :] < picks[:, None]) | (
        (picks[None, :] == picks[:, None]) & (index[None, :] < index[:, None])
    )
    pos = jnp.sum(before.astype(jnp.int32), axis=1)
    at = pos[None, :] == index[:, None]
    perm = jnp.sum(jnp.where(at, index[None, :], 0), axis=1)
    return perm, jnp.sum(jnp.where(at, picks[None, :], 0), axis=1)


def on_device_shared(ranks, tokens_in, upstream, member_pick, norm_gain, up_proj, down_proj):
    rows, seq, width = tokens_in.shape
    members, depth, hidden = up_proj.shape
    rank = lax.axis_index("row")
    core = lax.rem(rank, 2)
    x_at = lax.axis_index("grp")
    y_at = lax.rem(rank // 2, 2)
    lines = ranks // 4

    def partner(a):
        return lax.ppermute(a, "row", [(i, i ^ 1) for i in range(ranks)])

    def over_y(a):
        return lax.ppermute(a, "row", [(i, i ^ 2) for i in range(ranks)])

    def over_x(a):
        return lax.ppermute(a, "grp", [(0, 1), (1, 0)])

    def shift_z(a, d):
        return lax.ppermute(a, "row", [(i, (i + 4 * d) % ranks) for i in range(ranks)])

    def after(a, *others):
        return lax.optimization_barrier((a, *others))[0]

    unit = hidden // 32
    quarter, half = 7 * unit, 2 * unit

    def units_of(c, both):
        return jnp.concatenate(
            [
                lax.dynamic_slice_in_dim(both, (2 * x_at + c) * quarter, quarter, 3),
                lax.dynamic_slice_in_dim(both, 4 * quarter + c * half, half, 3),
            ],
            axis=3,
        )

    def both_cores(mine, theirs):
        even = core == 0
        whole = jnp.concatenate(
            [jnp.where(even, mine, theirs), jnp.where(even, theirs, mine)], axis=2
        )
        return whole.reshape(mine.shape[0], 4 * depth, mine.shape[3])

    def head_of(c):
        at = (2 * x_at + c) * quarter
        return jnp.stack(
            [lax.dynamic_slice(a, (0, 0, at), (1, depth, 2 * unit)) for a in (up_proj, down_proj)],
            axis=1,
        )

    head_theirs = partner(head_of(1 - core))
    shard_head = both_cores(head_of(core), head_theirs)
    both = jnp.stack([after(up_proj, shard_head), after(down_proj, shard_head)], axis=1)
    theirs = partner(after(units_of(1 - core, both), shard_head))
    shard = both_cores(units_of(core, both), theirs)

    groups = [
        [(0, 0, 2 * unit)],
        [(0, 2 * unit, 4 * unit)],
        [(0, 6 * unit, unit), (1, 0, 3 * unit)],
        [(1, 3 * unit, 4 * unit)],
        [(0, quarter, half), (1, quarter, half)],
    ]
    own_rows = 4 * depth
    own_with = [
        [(0, 0, own_rows), (1, 0, own_rows), (2, 0, own_rows // 2)],
        [(2, own_rows // 2, own_rows // 2)],
        [(3, 0, own_rows // 2)],
        [(3, own_rows // 2, own_rows // 2)],
        [(4, 0, own_rows)],
    ]

    def own(group, row, n, first=0, wide=None):
        parts = []
        last = first + (wide or sum(k for _, _, k in groups[group]))
        at = 0
        for member, start, k in groups[group]:
            low, high = max(first, at), min(last, at + k)
            if low < high:
                parts.append(shard[member, row : row + n, start + low - at : start + high - at])
            at += k
        return jnp.concatenate(parts, axis=1)

    send = [shard_head[0]] + [own(group, 0, own_rows) for group in range(1, len(groups))]
    here, there, shifted, held = [], [], [], [[] for _ in groups]

    def along_z(step, *waits):
        mine = after(send[step], *shifted[-1], *waits) if step else send[0]
        shifted.append([shift_z(mine, d) for d in range(1, lines)])

    def across_y(step, *waits):
        wide = send[step].shape[1]
        parts = []

        def add(array, group, d, row, first):
            start = sum(a.shape[0] for a in parts)
            held[group].append((step, start, d, row, first, array.shape[0], wide))
            parts.append(array)

        for group, row, n in own_with[step]:
            for first in range(0, send[group].shape[1], wide):
                mine = send[0] if group == 0 else own(group, row, n, first, wide)
                add(mine, group, 0, row, first)
        for d, rows_from in enumerate(shifted[step]):
            add(rows_from, step, d + 1, 0, 0)
        here.append(jnp.concatenate(parts))
        there.append(over_y(after(here[step], *there[-1:], *waits)))

    def weights_of(*which):
        units = [(member, n) for group in which for member, _, n in groups[group]]
        used = sorted(set(source[0] for group in which for source in held[group]))
        sources = []
        at = 0
        for group in which:
            for i, start, d, row, first, n, wide in held[group]:
                sources.append((used.index(i), start, d, row, at + first, n, wide))
            at += send[group].shape[1]
        arrays = [here[i] for i in used], [there[i] for i in used]
        return units, lines, own_rows, *arrays, sources

    per_block = math.gcd(2 * rows, 4)
    per_chip = 2 * rows // per_block
    along_z(0)
    pick_own = member_pick[:, 0]
    pick_near = jnp.concatenate([pick_own, over_x(after(pick_own, send[0]))])
    x = after(tokens_in, shifted[0][0]).astype(F32)
    gain = jnp.zeros((rows, width), F32)
    for member in range(members):
        gain = jnp.where(pick_own[:, None] == member, norm_gain[member][None, :], gain)
    normed = x * (1.0 / jnp.sqrt(jnp.mean(x * x, axis=2, keepdims=True) + 1e-06))
    lifted = (normed * gain[:, None, :]).astype(BF16)
    near = jnp.stack([lifted, upstream])
    lifted_over = over_x(lifted)
    across_y(0)
    along_z(1)
    pick_far = partner(after(pick_near, shifted[0][-1]))

    perm, member_sorted = sort_rows(jnp.concatenate([pick_near[rows:], pick_far[rows:]]))
    perm_own, member_sorted_own = sort_rows(jnp.concatenate([pick_own, pick_far[:rows]]))
    scalars = (
        jnp.concatenate([member_sorted, member_sorted_own]),
        jnp.stack([y_at, rank // 4]),
        jnp.concatenate([perm + 2 * rows, perm_own]),
    )

    along_z(2, there[0], lifted_over, *scalars)
    across_y(1)
    over = jnp.stack([lifted_over, over_x(after(upstream, there[0], *shifted[1]))])
    along_z(3, there[1], over)
    across_y(2)
    far = partner(after(jnp.stack([near, over]), *shifted[2], there[1]))
    along_z(4, there[2], far)
    across_y(3)
    tokens_of = (near, over, far)
    over_blocks, own_blocks = (0, per_chip, per_block), (per_chip, per_chip, per_block)
    sums = chunk(
        (True, False), over_blocks, (1,), scalars,
        (near, after(over, *shifted[3]), far), weights_of(0, 1, 2), None,
    )
    across_y(4)
    sums = (after(sums[0], *shifted[4]), sums[1])
    *same, other_out, other_back = chunk(
        (False, True), over_blocks, (1,), scalars, tokens_of, weights_of(3), sums,
        (BF16, BF16), 0,
    )
    summed = [
        (a.astype(F32) + partner(b).astype(F32)).astype(BF16)
        for a, b in zip(same, (other_out, other_back))
    ]
    tokens_of = (after(near, *summed), over, far)
    across = [over_x(a) for a in summed]
    sums = chunk(
        (True, False), own_blocks, (0,), scalars, tokens_of, weights_of(0, 1, 2, 3), None, None, 0
    )
    out, back, packed_out, packed_back = chunk(
        (False, True), own_blocks, (0,), scalars, tokens_of, weights_of(4), sums, (F32, BF16), 0
    )
    return tuple(
        finish(
            pick_own, tokens_in, upstream, norm_gain, out, back,
            partner(packed_out), partner(packed_back), *across,
        )
    )


def solution(mesh):
    ranks = mesh.shape["row"]
    four = mesh.shape["feat"] == 1 and ranks % 4 == 0 and mesh.shape["grp"] == 2

    def on_device(tokens_in, upstream, member_pick, norm_gain, up_proj, down_proj):
        args = (tokens_in, upstream, member_pick, norm_gain, up_proj, down_proj)
        if four and member_pick.shape[1] == 1 and up_proj.shape[0] == 2:
            return on_device_shared(ranks, *args)
        return on_device_general(*args)

    in_specs = (
        P(("grp", "row"), None, "feat"),
        P(("grp", "row"), None, "feat"),
        P(("grp", "row"), None),
        P(),
        P(None, "row", "feat"),
        P(None, "row", "feat"),
    )
    out_specs = (
        P(("grp", "row"), None, "feat"),
        P(("grp", "row"), None, "feat"),
        P(("grp", "row"), None),
    )
    return jax.shard_map(
        on_device, mesh=mesh, in_specs=in_specs, out_specs=out_specs, check_vma=False
    )
```

```python
import functools
import math

import jax
import jax.numpy as jnp
from jax import lax
from jax.experimental import pallas as pl
from jax.experimental.pallas import tpu as pltpu
from jax.sharding import PartitionSpec as P

coef_c = math.sqrt(2.0 / math.pi)


def gelu_tanh(v):
    return 0.5 * v * (1.0 + jnp.tanh(coef_c * (v + 0.044715 * v * v * v)))


def gelu_slope(v):
    inner = jnp.tanh(coef_c * (v + 0.044715 * v * v * v))
    return 0.5 * (1.0 + inner) + 0.5 * v * (1.0 - inner * inner) * coef_c * (
        1.0 + 3.0 * 0.044715 * v * v
    )


def on_device_general(tokens_in, upstream, member_pick, norm_gain, up_proj, down_proj):
    rows, seq, half = tokens_in.shape
    count = rows * seq
    members = up_proj.shape[0]
    pick = member_pick.shape[1]
    whole_x, whole_g = (
        lax.all_gather(tokens_in, "feat", axis=2, tiled=True),
        lax.all_gather(upstream, "feat", axis=2, tiled=True),
    )
    width = whole_x.shape[2]
    flat_x = whole_x.reshape(count, width).astype(jnp.float32)
    flat_g = whole_g.reshape(count, width)
    inv_rms = 1.0 / jnp.sqrt(jnp.mean(flat_x * flat_x, axis=1, keepdims=True) + 1e-06)
    normed = flat_x * inv_rms
    labels = jnp.arange(members, dtype=jnp.int32)
    chosen = (
        jnp.sum((member_pick[:, :, None] == labels[None, None, :]).astype(jnp.float32), axis=1)
        / pick
    )
    chosen_tok = jnp.repeat(chosen, seq, axis=0)
    out_half = jnp.zeros((count, half), jnp.float32)
    back_half = jnp.zeros((count, half), jnp.float32)
    for member in range(members):
        lifted = (normed * norm_gain[member][None, :]).astype(jnp.bfloat16)
        up_full = lax.all_gather(up_proj[member], "row", axis=0, tiled=True)
        hidden = jnp.dot(lifted, up_full, preferred_element_type=jnp.float32)
        act = gelu_tanh(hidden).astype(jnp.bfloat16)
        piece = lax.all_gather(down_proj[member], "row", axis=0, tiled=True)
        block = lax.dot_general(
            act, piece, (((1,), (1,)), ((), ())), preferred_element_type=jnp.float32
        )
        grads = jnp.dot(flat_g, piece, preferred_element_type=jnp.float32)
        pre_grad = (grads * gelu_slope(hidden)).astype(jnp.bfloat16)
        in_grad = lax.dot_general(
            pre_grad, up_full, (((1,), (1,)), ((), ())), preferred_element_type=jnp.float32
        )
        weight_col = chosen_tok[:, member : member + 1]
        out_term = weight_col * block
        back_term = weight_col * norm_gain[member][None, :] * in_grad
        out_part, back_part = (
            lax.psum_scatter(
                out_term.astype(jnp.bfloat16), "feat", scatter_dimension=1, tiled=True
            ).astype(jnp.float32),
            lax.psum_scatter(
                back_term.astype(jnp.bfloat16), "feat", scatter_dimension=1, tiled=True
            ).astype(jnp.float32),
        )
        out_half = out_half + out_part
        back_half = back_half + back_part
    own_x = tokens_in.reshape(count, half).astype(jnp.float32)
    normed_half = own_x * inv_rms
    stat = lax.psum(jnp.sum(normed_half * back_half, axis=1, keepdims=True), "feat") / width
    coupling = stat * math.sqrt(width)
    own_g = upstream.reshape(count, half).astype(jnp.float32)
    value_out = (own_x + out_half).astype(jnp.bfloat16)
    grad_in = (own_g + (back_half - normed_half * stat) * inv_rms).astype(jnp.bfloat16)
    return (
        value_out.reshape(rows, seq, half),
        grad_in.reshape(rows, seq, half),
        coupling.reshape(rows, seq),
    )


VMEM_LIMIT = 20 * 1024 * 1024
BF16 = jnp.bfloat16
F32 = jnp.float32


def chunk_kernel(
    offset, kind, units, chips, sources, sorted_ref, place_ref, perm_ref, *refs
):
    first, last = kind
    parts = len(units)
    arrays = 1 + max(source[0] for source in sources)
    tokens_of, refs = refs[: len(chips) + 1], refs[len(chips) + 1 :]
    here_refs, there_refs, refs = refs[:arrays], refs[arrays : 2 * arrays], refs[2 * arrays :]
    if first:
        *outs, tokens_ref, weights_ref, sems, lifted_ref, g_ref, act_ref, pre_ref = refs
    elif last:
        out_in, back_in, *outs, tokens_ref, weights_ref, sems = refs[:-6]
        lifted_ref, g_ref, act_ref, pre_ref = refs[-6:-2]
        out_acc, back_acc = refs[-2:]
    else:
        out_in, back_in, *outs, tokens_ref, weights_ref, sems = refs[:-4]
        lifted_ref, g_ref, act_ref, pre_ref = refs[-4:]
    if not last:
        out_acc, back_acc = outs
    j = pl.program_id(0)
    rows, seq = tokens_ref.shape[2:4]
    per_block = lifted_ref.shape[0] // seq
    places = [(j + offset) * per_block + i for i in range(per_block)]
    lines, _, depth2, _ = weights_ref.shape
    depth = depth2 // 2
    starts = [sum(n for _, n in units[:part]) for part in range(parts)]

    @pl.when(j == 0)
    def _():
        y, z = place_ref[0], place_ref[1]
        copies = []
        for i, chip in enumerate(chips):
            for k, ref in enumerate((tokens_of[i], tokens_of[-1].at[chip])):
                copies.append(
                    pltpu.make_async_copy(ref, tokens_ref.at[2 * i + k], sems.at[len(copies)])
                )
        for i, start, d, to_row, to_unit, n, wide in sources:
            from_z = lax.rem(z + lines - d, lines)
            for to_y, ref in ((y, here_refs[i]), (1 - y, there_refs[i])):
                to = weights_ref.at[from_z, to_y, pl.ds(to_row, n), pl.ds(to_unit, wide)]
                copies.append(
                    pltpu.make_async_copy(ref.at[pl.ds(start, n)], to, sems.at[len(copies)])
                )
        for copy in copies:
            copy.start()
        for copy in copies:
            copy.wait()

    width = lifted_ref.shape[1]
    here = [sorted_ref[at] for at in places]

    def pick_up(member):
        for i, at in enumerate(places):
            row = perm_ref[at]
            source = row // rows - 2 * chips[0]
            tokens = pl.ds(i * seq, seq)

            @pl.when(here[i] == member)
            def _():
                lifted_ref[tokens, :] = tokens_ref[source, 0, lax.rem(row, rows)]
                g_ref[tokens, :] = tokens_ref[source, 1, lax.rem(row, rows)]

            @pl.when(here[i] != member)
            def _():
                lifted_ref[tokens, :] = jnp.zeros((seq, width), BF16)
                g_ref[tokens, :] = jnp.zeros((seq, width), BF16)

    def sums(member):
        pick_up(member)
        mine = [(start, n) for (m, n), start in zip(units, starts) if m == member]
        low, high = mine[0][0], mine[-1][0] + mine[-1][1]
        for s in range(low, high, 256):
            e = min(s + 256, high)
            up = weights_ref[:, :, :depth, s:e].reshape(width, e - s)
            down = weights_ref[:, :, depth:, s:e].reshape(width, e - s)
            v = jnp.dot(lifted_ref[...], up, preferred_element_type=F32)
            grads = jnp.dot(g_ref[...], down, preferred_element_type=F32)
            square = v * v
            t = jnp.tanh(v * (coef_c + (coef_c * 0.044715) * square))
            half_v = 0.5 * v
            act_ref[:, s - low : e - low] = (half_v + half_v * t).astype(BF16)
            slope = (0.5 + 0.5 * t) + (half_v * (1.0 - t * t)) * (
                coef_c + (3.0 * coef_c * 0.044715) * square
            )
            pre_ref[:, s - low : e - low] = (grads * slope).astype(BF16)
        up = weights_ref[:, :, :depth, low:high].reshape(width, high - low)
        down = weights_ref[:, :, depth:, low:high].reshape(width, high - low)
        dims = (((1,), (1,)), ((), ()))
        return (
            lax.dot_general(act_ref[:, : high - low], down, dims, preferred_element_type=F32),
            lax.dot_general(pre_ref[:, : high - low], up, dims, preferred_element_type=F32),
        )

    for at, member in enumerate(sorted(set(m for m, _ in units))):
        used = functools.reduce(jnp.logical_or, [m == member for m in here])

        @pl.when(used)
        def _():
            out_sum, back_sum = sums(member)
            if at > 0:
                out_acc[...] += out_sum
                back_acc[...] += back_sum
            elif first:
                out_acc[...] = out_sum
                back_acc[...] = back_sum
            else:
                out_acc[...] = out_in[...] + out_sum
                back_acc[...] = back_in[...] + back_sum

        if at == 0:

            @pl.when(jnp.logical_not(used))
            def _():
                out_acc[...] = jnp.zeros(out_acc.shape, F32) if first else out_in[...]
                back_acc[...] = jnp.zeros(back_acc.shape, F32) if first else back_in[...]

    if last:
        for p, at in enumerate(places):
            row = lax.rem(perm_ref[at], 2 * rows)
            tokens = pl.ds(p * seq, seq)
            low = 0
            for to_out, to_back in zip(outs[::2], outs[1::2]):
                n = to_out.shape[0]

                @pl.when(jnp.logical_and(row >= low, row < low + n))
                def _():
                    to = jnp.clip(row - low, 0, n - 1)
                    to_out[to] = out_acc[tokens, :].astype(to_out.dtype)
                    to_back[to] = back_acc[tokens, :].astype(to_back.dtype)

                low += n


def chunk(kind, blocks, chips, scalars, tokens_of, weights, sums, outs=None, weight=1):
    first, last = kind
    offset, number, per_block = blocks
    units, lines, depth2, here, there, sources = weights
    _, rows, seq, width = tokens_of[0].shape
    hidden = sum(n for _, n in units)
    size = per_block * seq

    tok = pl.BlockSpec((size, width), lambda j, *_: (j, 0))
    hbm = pl.BlockSpec(memory_space=pl.ANY)
    args = [*scalars, *(tokens_of[chip] for chip in chips), tokens_of[-1], *here, *there]
    specs = [pl.BlockSpec(memory_space=pltpu.HBM)] * (len(chips) + 1) + [hbm] * (2 * len(here))
    alias = {}
    out_specs = [tok, tok]
    out_shape = [jax.ShapeDtypeStruct((number * size, width), F32)] * 2
    scratch = [
        pltpu.VMEM((2 * len(chips), 2, rows, seq, width), BF16),
        pltpu.VMEM((lines, 2, depth2, hidden), BF16),
        pltpu.SemaphoreType.DMA((2 * len(sources) + 2 * len(chips),)),
        pltpu.VMEM((size, width), BF16),
        pltpu.VMEM((size, width), BF16),
        pltpu.VMEM((size, hidden), BF16),
        pltpu.VMEM((size, hidden), BF16),
    ]
    if not first:
        alias = {len(args): 0, len(args) + 1: 1}
        args += list(sums)
        specs += [tok, tok]
    if last:
        alias = {}
        shape = (rows, seq, width)
        out_shape = [jax.ShapeDtypeStruct(shape, dtype) for dtype in outs for _ in range(2)]
        out_specs = [pl.BlockSpec(shape, lambda *_: (0, 0, 0))] * len(out_shape)
        scratch += [pltpu.VMEM((size, width), F32)] * 2

    return pl.pallas_call(
        functools.partial(chunk_kernel, offset, kind, units, chips, sources),
        grid_spec=pltpu.PrefetchScalarGridSpec(
            num_scalar_prefetch=len(scalars),
            grid=(number,),
            in_specs=specs,
            out_specs=out_specs,
            scratch_shapes=scratch,
        ),
        out_shape=out_shape,
        input_output_aliases=alias,
        compiler_params=pltpu.CompilerParams(vmem_limit_bytes=VMEM_LIMIT),
        cost_estimate=pl.CostEstimate(
            flops=weight * 8 * number * size * width * hidden * 2 // 3,
            bytes_accessed=weight * (4 * width * hidden + 20 * number * size * width),
            transcendentals=weight * number * size * hidden,
        ),
        name="chunk",
    )(*args)


def finish_kernel(
    member_ref, x_ref, g_ref, gain_ref, out_ref, back_ref, other_out_ref, other_back_ref,
    across_out_ref, across_back_ref, value_ref, grad_ref, coupling_ref,
):
    rows, seq, width = x_ref.shape
    diagonal = lax.broadcasted_iota(jnp.int32, (seq, seq), 0) == lax.broadcasted_iota(
        jnp.int32, (seq, seq), 1
    )
    for r in range(rows):
        x = x_ref[r].astype(F32)
        inv = 1.0 / jnp.sqrt(jnp.mean(x * x, axis=1, keepdims=True) + 1e-06)
        normed = x * inv
        gain = gain_ref[pl.ds(member_ref[pl.program_id(0) * rows + r], 1), :]
        back = gain * (
            back_ref[r] + other_back_ref[r].astype(F32) + across_back_ref[r].astype(F32)
        )
        stat = jnp.sum(normed * back, axis=1, keepdims=True) / width
        out = out_ref[r] + other_out_ref[r].astype(F32) + across_out_ref[r].astype(F32)
        value_ref[r] = (x + out).astype(BF16)
        grad_ref[r] = (g_ref[r].astype(F32) + (back - normed * stat) * inv).astype(BF16)
        line = jnp.sum(jnp.where(diagonal, stat, 0.0), axis=0, keepdims=True)
        coupling_ref[pl.ds(pl.program_id(0) * rows + r, 1), :] = line * math.sqrt(width)


def finish(member_own, x, g, gain, *sums):
    rows, seq, width = x.shape
    step = math.gcd(rows, 2)
    row = pl.BlockSpec((step, seq, width), lambda r, mem: (r, 0, 0))
    return pl.pallas_call(
        finish_kernel,
        grid_spec=pltpu.PrefetchScalarGridSpec(
            num_scalar_prefetch=1,
            grid=(rows // step,),
            in_specs=[
                row, row, pl.BlockSpec(gain.shape, lambda r, mem: (0, 0)), row, row, row, row, row, row
            ],
            out_specs=[row, row, pl.BlockSpec((rows, seq), lambda r, mem: (0, 0))],
        ),
        out_shape=[
            jax.ShapeDtypeStruct((rows, seq, width), BF16),
            jax.ShapeDtypeStruct((rows, seq, width), BF16),
            jax.ShapeDtypeStruct((rows, seq), F32),
        ],
        compiler_params=pltpu.CompilerParams(vmem_limit_bytes=VMEM_LIMIT // 2),
        name="finish",
    )(member_own, x, g, gain, *sums)


def sort_rows(picks):
    index = jnp.arange(picks.shape[0], dtype=jnp.int32)
    before = (picks[None, :] < picks[:, None]) | (
        (picks[None, :] == picks[:, None]) & (index[None, :] < index[:, None])
    )
    pos = jnp.sum(before.astype(jnp.int32), axis=1)
    at = pos[None, :] == index[:, None]
    perm = jnp.sum(jnp.where(at, index[None, :], 0), axis=1)
    return perm, jnp.sum(jnp.where(at, picks[None, :], 0), axis=1)


def on_device_shared(ranks, tokens_in, upstream, member_pick, norm_gain, up_proj, down_proj):
    rows, seq, width = tokens_in.shape
    members, depth, hidden = up_proj.shape
    rank = lax.axis_index("row")
    core = lax.rem(rank, 2)
    x_at = lax.axis_index("grp")
    y_at = lax.rem(rank // 2, 2)
    lines = ranks // 4

    def partner(a):
        return lax.ppermute(a, "row", [(i, i ^ 1) for i in range(ranks)])

    def over_y(a):
        return lax.ppermute(a, "row", [(i, i ^ 2) for i in range(ranks)])

    def over_x(a):
        return lax.ppermute(a, "grp", [(0, 1), (1, 0)])

    def shift_z(a, d):
        return lax.ppermute(a, "row", [(i, (i + 4 * d) % ranks) for i in range(ranks)])

    def after(a, *others):
        return lax.optimization_barrier((a, *others))[0]

    unit = hidden // 32
    quarter, half = 7 * unit, 2 * unit

    def units_of(c, both):
        return jnp.concatenate(
            [
                lax.dynamic_slice_in_dim(both, (2 * x_at + c) * quarter, quarter, 3),
                lax.dynamic_slice_in_dim(both, 4 * quarter + c * half, half, 3),
            ],
            axis=3,
        )

    def both_cores(mine, theirs):
        even = core == 0
        whole = jnp.concatenate(
            [jnp.where(even, mine, theirs), jnp.where(even, theirs, mine)], axis=2
        )
        return whole.reshape(mine.shape[0], 4 * depth, mine.shape[3])

    def head_of(c):
        at = (2 * x_at + c) * quarter
        return jnp.stack(
            [lax.dynamic_slice(a, (0, 0, at), (1, depth, 2 * unit)) for a in (up_proj, down_proj)],
            axis=1,
        )

    head_theirs = partner(head_of(1 - core))
    shard_head = both_cores(head_of(core), head_theirs)
    both = jnp.stack([after(up_proj, shard_head), after(down_proj, shard_head)], axis=1)
    theirs = partner(after(units_of(1 - core, both), shard_head))
    shard = both_cores(units_of(core, both), theirs)

    groups = [
        [(0, 0, 2 * unit)],
        [(0, 2 * unit, 4 * unit)],
        [(0, 6 * unit, unit), (1, 0, 3 * unit)],
        [(1, 3 * unit, 4 * unit)],
        [(0, quarter, half), (1, quarter, half)],
    ]
    own_rows = 4 * depth
    own_with = [
        [(0, 0, own_rows), (1, 0, own_rows), (2, 0, own_rows // 2)],
        [(2, own_rows // 2, own_rows // 2)],
        [(3, 0, own_rows // 2)],
        [(3, own_rows // 2, own_rows // 2)],
        [(4, 0, own_rows)],
    ]

    def own(group, row, n, first=0, wide=None):
        parts = []
        last = first + (wide or sum(k for _, _, k in groups[group]))
        at = 0
        for member, start, k in groups[group]:
            low, high = max(first, at), min(last, at + k)
            if low < high:
                parts.append(shard[member, row : row + n, start + low - at : start + high - at])
            at += k
        return jnp.concatenate(parts, axis=1)

    send = [shard_head[0]] + [own(group, 0, own_rows) for group in range(1, len(groups))]
    here, there, shifted, held = [], [], [], [[] for _ in groups]

    def along_z(step, *waits):
        mine = after(send[step], *shifted[-1], *waits) if step else send[0]
        shifted.append([shift_z(mine, d) for d in range(1, lines)])

    def across_y(step, *waits):
        wide = send[step].shape[1]
        parts = []

        def add(array, group, d, row, first):
            start = sum(a.shape[0] for a in parts)
            held[group].append((step, start, d, row, first, array.shape[0], wide))
            parts.append(array)

        for group, row, n in own_with[step]:
            for first in range(0, send[group].shape[1], wide):
                mine = send[0] if group == 0 else own(group, row, n, first, wide)
                add(mine, group, 0, row, first)
        for d, rows_from in enumerate(shifted[step]):
            add(rows_from, step, d + 1, 0, 0)
        here.append(jnp.concatenate(parts))
        there.append(over_y(after(here[step], *there[-1:], *waits)))

    def weights_of(*which):
        units = [(member, n) for group in which for member, _, n in groups[group]]
        used = sorted(set(source[0] for group in which for source in held[group]))
        sources = []
        at = 0
        for group in which:
            for i, start, d, row, first, n, wide in held[group]:
                sources.append((used.index(i), start, d, row, at + first, n, wide))
            at += send[group].shape[1]
        arrays = [here[i] for i in used], [there[i] for i in used]
        return units, lines, own_rows, *arrays, sources

    per_block = math.gcd(2 * rows, 4)
    per_chip = 2 * rows // per_block
    g_over = over_x(upstream)
    along_z(0)
    pick_own = member_pick[:, 0]
    pick_near = jnp.concatenate([pick_own, over_x(after(pick_own, send[0]))])
    x = after(tokens_in, shifted[0][0]).astype(F32)
    gain = jnp.zeros((rows, width), F32)
    for member in range(members):
        gain = jnp.where(pick_own[:, None] == member, norm_gain[member][None, :], gain)
    normed = x * (1.0 / jnp.sqrt(jnp.mean(x * x, axis=2, keepdims=True) + 1e-06))
    lifted = (normed * gain[:, None, :]).astype(BF16)
    near = jnp.stack([lifted, upstream])
    lifted_over = over_x(lifted)
    across_y(0)
    along_z(1)
    pick_far = partner(after(pick_near, shifted[0][-1]))

    perm, member_sorted = sort_rows(jnp.concatenate([pick_near[rows:], pick_far[rows:]]))
    perm_own, member_sorted_own = sort_rows(jnp.concatenate([pick_own, pick_far[:rows]]))
    scalars = (
        jnp.concatenate([member_sorted, member_sorted_own]),
        jnp.stack([y_at, rank // 4]),
        jnp.concatenate([perm + 2 * rows, perm_own]),
    )

    along_z(2, there[0], lifted_over, *scalars)
    across_y(1)
    over = jnp.stack([lifted_over, g_over])
    along_z(3, there[1], over)
    across_y(2)
    far = partner(after(jnp.stack([near, over]), *shifted[2], there[1]))
    along_z(4, there[2], far)
    across_y(3)
    tokens_of = (near, over, far)
    over_blocks, own_blocks = (0, per_chip, per_block), (per_chip, per_chip, per_block)
    sums = chunk(
        (True, False), over_blocks, (1,), scalars,
        (near, after(over, *shifted[3]), far), weights_of(0, 1, 2), None,
    )
    across_y(4)
    sums = (after(sums[0], shifted[4][0]), sums[1])
    *same, other_out, other_back = chunk(
        (False, True), over_blocks, (1,), scalars, tokens_of, weights_of(3), sums,
        (BF16, BF16), 0,
    )
    summed = [
        (a.astype(F32) + partner(b).astype(F32)).astype(BF16)
        for a, b in zip(same, (other_out, other_back))
    ]
    tokens_of = (after(near, *summed), over, far)
    across = [over_x(a) for a in summed]
    sums = chunk(
        (True, False), own_blocks, (0,), scalars, tokens_of, weights_of(0, 1, 2, 3), None, None, 0
    )
    out, back, packed_out, packed_back = chunk(
        (False, True), own_blocks, (0,), scalars, tokens_of, weights_of(4), sums, (F32, BF16), 0
    )
    return tuple(
        finish(
            pick_own, tokens_in, upstream, norm_gain, out, back,
            partner(packed_out), partner(packed_back), *across,
        )
    )


def solution(mesh):
    ranks = mesh.shape["row"]
    four = mesh.shape["feat"] == 1 and ranks % 4 == 0 and mesh.shape["grp"] == 2

    def on_device(tokens_in, upstream, member_pick, norm_gain, up_proj, down_proj):
        args = (tokens_in, upstream, member_pick, norm_gain, up_proj, down_proj)
        if four and member_pick.shape[1] == 1 and up_proj.shape[0] == 2:
            return on_device_shared(ranks, *args)
        return on_device_general(*args)

    in_specs = (
        P(("grp", "row"), None, "feat"),
        P(("grp", "row"), None, "feat"),
        P(("grp", "row"), None),
        P(),
        P(None, "row", "feat"),
        P(None, "row", "feat"),
    )
    out_specs = (
        P(("grp", "row"), None, "feat"),
        P(("grp", "row"), None, "feat"),
        P(("grp", "row"), None),
    )
    return jax.shard_map(
        on_device, mesh=mesh, in_specs=in_specs, out_specs=out_specs, check_vma=False
    )
```

```python
import functools
import math

import jax
import jax.numpy as jnp
from jax import lax
from jax.experimental import pallas as pl
from jax.experimental.pallas import tpu as pltpu
from jax.sharding import PartitionSpec as P

coef_c = math.sqrt(2.0 / math.pi)


def gelu_tanh(v):
    return 0.5 * v * (1.0 + jnp.tanh(coef_c * (v + 0.044715 * v * v * v)))


def gelu_slope(v):
    inner = jnp.tanh(coef_c * (v + 0.044715 * v * v * v))
    return 0.5 * (1.0 + inner) + 0.5 * v * (1.0 - inner * inner) * coef_c * (
        1.0 + 3.0 * 0.044715 * v * v
    )


def on_device_general(tokens_in, upstream, member_pick, norm_gain, up_proj, down_proj):
    rows, seq, half = tokens_in.shape
    count = rows * seq
    members = up_proj.shape[0]
    pick = member_pick.shape[1]
    whole_x, whole_g = (
        lax.all_gather(tokens_in, "feat", axis=2, tiled=True),
        lax.all_gather(upstream, "feat", axis=2, tiled=True),
    )
    width = whole_x.shape[2]
    flat_x = whole_x.reshape(count, width).astype(jnp.float32)
    flat_g = whole_g.reshape(count, width)
    inv_rms = 1.0 / jnp.sqrt(jnp.mean(flat_x * flat_x, axis=1, keepdims=True) + 1e-06)
    normed = flat_x * inv_rms
    labels = jnp.arange(members, dtype=jnp.int32)
    chosen = (
        jnp.sum((member_pick[:, :, None] == labels[None, None, :]).astype(jnp.float32), axis=1)
        / pick
    )
    chosen_tok = jnp.repeat(chosen, seq, axis=0)
    out_half = jnp.zeros((count, half), jnp.float32)
    back_half = jnp.zeros((count, half), jnp.float32)
    for member in range(members):
        lifted = (normed * norm_gain[member][None, :]).astype(jnp.bfloat16)
        up_full = lax.all_gather(up_proj[member], "row", axis=0, tiled=True)
        hidden = jnp.dot(lifted, up_full, preferred_element_type=jnp.float32)
        act = gelu_tanh(hidden).astype(jnp.bfloat16)
        piece = lax.all_gather(down_proj[member], "row", axis=0, tiled=True)
        block = lax.dot_general(
            act, piece, (((1,), (1,)), ((), ())), preferred_element_type=jnp.float32
        )
        grads = jnp.dot(flat_g, piece, preferred_element_type=jnp.float32)
        pre_grad = (grads * gelu_slope(hidden)).astype(jnp.bfloat16)
        in_grad = lax.dot_general(
            pre_grad, up_full, (((1,), (1,)), ((), ())), preferred_element_type=jnp.float32
        )
        weight_col = chosen_tok[:, member : member + 1]
        out_term = weight_col * block
        back_term = weight_col * norm_gain[member][None, :] * in_grad
        out_part, back_part = (
            lax.psum_scatter(
                out_term.astype(jnp.bfloat16), "feat", scatter_dimension=1, tiled=True
            ).astype(jnp.float32),
            lax.psum_scatter(
                back_term.astype(jnp.bfloat16), "feat", scatter_dimension=1, tiled=True
            ).astype(jnp.float32),
        )
        out_half = out_half + out_part
        back_half = back_half + back_part
    own_x = tokens_in.reshape(count, half).astype(jnp.float32)
    normed_half = own_x * inv_rms
    stat = lax.psum(jnp.sum(normed_half * back_half, axis=1, keepdims=True), "feat") / width
    coupling = stat * math.sqrt(width)
    own_g = upstream.reshape(count, half).astype(jnp.float32)
    value_out = (own_x + out_half).astype(jnp.bfloat16)
    grad_in = (own_g + (back_half - normed_half * stat) * inv_rms).astype(jnp.bfloat16)
    return (
        value_out.reshape(rows, seq, half),
        grad_in.reshape(rows, seq, half),
        coupling.reshape(rows, seq),
    )


VMEM_LIMIT = 20 * 1024 * 1024
BF16 = jnp.bfloat16
F32 = jnp.float32


def chunk_kernel(
    offset, kind, units, chips, sources, sorted_ref, place_ref, perm_ref, *refs
):
    first, last = kind
    parts = len(units)
    arrays = 1 + max(source[0] for source in sources)
    tokens_of, refs = refs[: len(chips) + 1], refs[len(chips) + 1 :]
    here_refs, there_refs, refs = refs[:arrays], refs[arrays : 2 * arrays], refs[2 * arrays :]
    if first:
        *outs, tokens_ref, weights_ref, sems, lifted_ref, g_ref, act_ref, pre_ref = refs
    elif last:
        out_in, back_in, *outs, tokens_ref, weights_ref, sems = refs[:-6]
        lifted_ref, g_ref, act_ref, pre_ref = refs[-6:-2]
        out_acc, back_acc = refs[-2:]
    else:
        out_in, back_in, *outs, tokens_ref, weights_ref, sems = refs[:-4]
        lifted_ref, g_ref, act_ref, pre_ref = refs[-4:]
    if not last:
        out_acc, back_acc = outs
    j = pl.program_id(0)
    rows, seq = tokens_ref.shape[2:4]
    per_block = lifted_ref.shape[0] // seq
    places = [(j + offset) * per_block + i for i in range(per_block)]
    lines, _, depth2, _ = weights_ref.shape
    depth = depth2 // 2
    starts = [sum(n for _, n in units[:part]) for part in range(parts)]

    @pl.when(j == 0)
    def _():
        y, z = place_ref[0], place_ref[1]
        copies = []
        for i, chip in enumerate(chips):
            for k, ref in enumerate((tokens_of[i], tokens_of[-1].at[chip])):
                copies.append(
                    pltpu.make_async_copy(ref, tokens_ref.at[2 * i + k], sems.at[len(copies)])
                )
        for i, start, d, to_row, to_unit, n, wide in sources:
            from_z = lax.rem(z + lines - d, lines)
            for to_y, ref in ((y, here_refs[i]), (1 - y, there_refs[i])):
                to = weights_ref.at[from_z, to_y, pl.ds(to_row, n), pl.ds(to_unit, wide)]
                copies.append(
                    pltpu.make_async_copy(ref.at[pl.ds(start, n)], to, sems.at[len(copies)])
                )
        for copy in copies:
            copy.start()
        for copy in copies:
            copy.wait()

    width = lifted_ref.shape[1]
    here = [sorted_ref[at] for at in places]

    def pick_up(member):
        for i, at in enumerate(places):
            row = perm_ref[at]
            source = row // rows - 2 * chips[0]
            tokens = pl.ds(i * seq, seq)

            @pl.when(here[i] == member)
            def _():
                lifted_ref[tokens, :] = tokens_ref[source, 0, lax.rem(row, rows)]
                g_ref[tokens, :] = tokens_ref[source, 1, lax.rem(row, rows)]

            @pl.when(here[i] != member)
            def _():
                lifted_ref[tokens, :] = jnp.zeros((seq, width), BF16)
                g_ref[tokens, :] = jnp.zeros((seq, width), BF16)

    def sums(member):
        pick_up(member)
        mine = [(start, n) for (m, n), start in zip(units, starts) if m == member]
        low, high = mine[0][0], mine[-1][0] + mine[-1][1]
        for s in range(low, high, 256):
            e = min(s + 256, high)
            up = weights_ref[:, :, :depth, s:e].reshape(width, e - s)
            down = weights_ref[:, :, depth:, s:e].reshape(width, e - s)
            v = jnp.dot(lifted_ref[...], up, preferred_element_type=F32)
            grads = jnp.dot(g_ref[...], down, preferred_element_type=F32)
            square = v * v
            t = jnp.tanh(v * (coef_c + (coef_c * 0.044715) * square))
            half_v = 0.5 * v
            act_ref[:, s - low : e - low] = (half_v + half_v * t).astype(BF16)
            slope = (0.5 + 0.5 * t) + (half_v * (1.0 - t * t)) * (
                coef_c + (3.0 * coef_c * 0.044715) * square
            )
            pre_ref[:, s - low : e - low] = (grads * slope).astype(BF16)
        up = weights_ref[:, :, :depth, low:high].reshape(width, high - low)
        down = weights_ref[:, :, depth:, low:high].reshape(width, high - low)
        dims = (((1,), (1,)), ((), ()))
        return (
            lax.dot_general(act_ref[:, : high - low], down, dims, preferred_element_type=F32),
            lax.dot_general(pre_ref[:, : high - low], up, dims, preferred_element_type=F32),
        )

    for at, member in enumerate(sorted(set(m for m, _ in units))):
        used = functools.reduce(jnp.logical_or, [m == member for m in here])

        @pl.when(used)
        def _():
            out_sum, back_sum = sums(member)
            if at > 0:
                out_acc[...] += out_sum
                back_acc[...] += back_sum
            elif first:
                out_acc[...] = out_sum
                back_acc[...] = back_sum
            else:
                out_acc[...] = out_in[...] + out_sum
                back_acc[...] = back_in[...] + back_sum

        if at == 0:

            @pl.when(jnp.logical_not(used))
            def _():
                out_acc[...] = jnp.zeros(out_acc.shape, F32) if first else out_in[...]
                back_acc[...] = jnp.zeros(back_acc.shape, F32) if first else back_in[...]

    if last:
        for p, at in enumerate(places):
            row = lax.rem(perm_ref[at], 2 * rows)
            tokens = pl.ds(p * seq, seq)
            low = 0
            for to_out, to_back in zip(outs[::2], outs[1::2]):
                n = to_out.shape[0]

                @pl.when(jnp.logical_and(row >= low, row < low + n))
                def _():
                    to = jnp.clip(row - low, 0, n - 1)
                    to_out[to] = out_acc[tokens, :].astype(to_out.dtype)
                    to_back[to] = back_acc[tokens, :].astype(to_back.dtype)

                low += n


def chunk(kind, blocks, chips, scalars, tokens_of, weights, sums, outs=None, weight=1):
    first, last = kind
    offset, number, per_block = blocks
    units, lines, depth2, here, there, sources = weights
    _, rows, seq, width = tokens_of[0].shape
    hidden = sum(n for _, n in units)
    size = per_block * seq

    tok = pl.BlockSpec((size, width), lambda j, *_: (j, 0))
    hbm = pl.BlockSpec(memory_space=pl.ANY)
    args = [*scalars, *(tokens_of[chip] for chip in chips), tokens_of[-1], *here, *there]
    specs = [pl.BlockSpec(memory_space=pltpu.HBM)] * (len(chips) + 1) + [hbm] * (2 * len(here))
    alias = {}
    out_specs = [tok, tok]
    out_shape = [jax.ShapeDtypeStruct((number * size, width), F32)] * 2
    scratch = [
        pltpu.VMEM((2 * len(chips), 2, rows, seq, width), BF16),
        pltpu.VMEM((lines, 2, depth2, hidden), BF16),
        pltpu.SemaphoreType.DMA((2 * len(sources) + 2 * len(chips),)),
        pltpu.VMEM((size, width), BF16),
        pltpu.VMEM((size, width), BF16),
        pltpu.VMEM((size, hidden), BF16),
        pltpu.VMEM((size, hidden), BF16),
    ]
    if not first:
        alias = {len(args): 0, len(args) + 1: 1}
        args += list(sums)
        specs += [tok, tok]
    if last:
        alias = {}
        shape = (rows, seq, width)
        out_shape = [jax.ShapeDtypeStruct(shape, dtype) for dtype in outs for _ in range(2)]
        out_specs = [pl.BlockSpec(shape, lambda *_: (0, 0, 0))] * len(out_shape)
        scratch += [pltpu.VMEM((size, width), F32)] * 2

    return pl.pallas_call(
        functools.partial(chunk_kernel, offset, kind, units, chips, sources),
        grid_spec=pltpu.PrefetchScalarGridSpec(
            num_scalar_prefetch=len(scalars),
            grid=(number,),
            in_specs=specs,
            out_specs=out_specs,
            scratch_shapes=scratch,
        ),
        out_shape=out_shape,
        input_output_aliases=alias,
        compiler_params=pltpu.CompilerParams(vmem_limit_bytes=VMEM_LIMIT),
        cost_estimate=pl.CostEstimate(
            flops=weight * 8 * number * size * width * hidden * 2 // 3,
            bytes_accessed=weight * (4 * width * hidden + 20 * number * size * width),
            transcendentals=weight * number * size * hidden,
        ),
        name="chunk",
    )(*args)


def finish_kernel(
    member_ref, x_ref, g_ref, gain_ref, out_ref, back_ref, other_out_ref, other_back_ref,
    across_out_ref, across_back_ref, value_ref, grad_ref, coupling_ref,
):
    rows, seq, width = x_ref.shape
    diagonal = lax.broadcasted_iota(jnp.int32, (seq, seq), 0) == lax.broadcasted_iota(
        jnp.int32, (seq, seq), 1
    )
    for r in range(rows):
        x = x_ref[r].astype(F32)
        inv = 1.0 / jnp.sqrt(jnp.mean(x * x, axis=1, keepdims=True) + 1e-06)
        normed = x * inv
        gain = gain_ref[pl.ds(member_ref[pl.program_id(0) * rows + r], 1), :]
        back = gain * (
            back_ref[r] + other_back_ref[r].astype(F32) + across_back_ref[r].astype(F32)
        )
        stat = jnp.sum(normed * back, axis=1, keepdims=True) / width
        out = out_ref[r] + other_out_ref[r].astype(F32) + across_out_ref[r].astype(F32)
        value_ref[r] = (x + out).astype(BF16)
        grad_ref[r] = (g_ref[r].astype(F32) + (back - normed * stat) * inv).astype(BF16)
        line = jnp.sum(jnp.where(diagonal, stat, 0.0), axis=0, keepdims=True)
        coupling_ref[pl.ds(pl.program_id(0) * rows + r, 1), :] = line * math.sqrt(width)


def finish(member_own, x, g, gain, *sums):
    rows, seq, width = x.shape
    step = math.gcd(rows, 2)
    row = pl.BlockSpec((step, seq, width), lambda r, mem: (r, 0, 0))
    return pl.pallas_call(
        finish_kernel,
        grid_spec=pltpu.PrefetchScalarGridSpec(
            num_scalar_prefetch=1,
            grid=(rows // step,),
            in_specs=[
                row, row, pl.BlockSpec(gain.shape, lambda r, mem: (0, 0)), row, row, row, row, row, row
            ],
            out_specs=[row, row, pl.BlockSpec((rows, seq), lambda r, mem: (0, 0))],
        ),
        out_shape=[
            jax.ShapeDtypeStruct((rows, seq, width), BF16),
            jax.ShapeDtypeStruct((rows, seq, width), BF16),
            jax.ShapeDtypeStruct((rows, seq), F32),
        ],
        compiler_params=pltpu.CompilerParams(vmem_limit_bytes=VMEM_LIMIT // 2),
        name="finish",
    )(member_own, x, g, gain, *sums)


def sort_rows(picks):
    index = jnp.arange(picks.shape[0], dtype=jnp.int32)
    before = (picks[None, :] < picks[:, None]) | (
        (picks[None, :] == picks[:, None]) & (index[None, :] < index[:, None])
    )
    pos = jnp.sum(before.astype(jnp.int32), axis=1)
    at = pos[None, :] == index[:, None]
    perm = jnp.sum(jnp.where(at, index[None, :], 0), axis=1)
    return perm, jnp.sum(jnp.where(at, picks[None, :], 0), axis=1)


def on_device_shared(ranks, tokens_in, upstream, member_pick, norm_gain, up_proj, down_proj):
    rows, seq, width = tokens_in.shape
    members, depth, hidden = up_proj.shape
    rank = lax.axis_index("row")
    core = lax.rem(rank, 2)
    x_at = lax.axis_index("grp")
    y_at = lax.rem(rank // 2, 2)
    lines = ranks // 4

    def partner(a):
        return lax.ppermute(a, "row", [(i, i ^ 1) for i in range(ranks)])

    def over_y(a):
        return lax.ppermute(a, "row", [(i, i ^ 2) for i in range(ranks)])

    def over_x(a):
        return lax.ppermute(a, "grp", [(0, 1), (1, 0)])

    def shift_z(a, d):
        return lax.ppermute(a, "row", [(i, (i + 4 * d) % ranks) for i in range(ranks)])

    def after(a, *others):
        return lax.optimization_barrier((a, *others))[0]

    unit = hidden // 32
    quarter, half = 7 * unit, 2 * unit

    def units_of(c, both):
        return jnp.concatenate(
            [
                lax.dynamic_slice_in_dim(both, (2 * x_at + c) * quarter, quarter, 3),
                lax.dynamic_slice_in_dim(both, 4 * quarter + c * half, half, 3),
            ],
            axis=3,
        )

    def both_cores(mine, theirs):
        even = core == 0
        whole = jnp.concatenate(
            [jnp.where(even, mine, theirs), jnp.where(even, theirs, mine)], axis=2
        )
        return whole.reshape(mine.shape[0], 4 * depth, mine.shape[3])

    def head_of(c):
        at = (2 * x_at + c) * quarter
        return jnp.stack(
            [lax.dynamic_slice(a, (0, 0, at), (1, depth, 2 * unit)) for a in (up_proj, down_proj)],
            axis=1,
        )

    head_theirs = partner(head_of(1 - core))
    shard_head = both_cores(head_of(core), head_theirs)
    both = jnp.stack([after(up_proj, shard_head), after(down_proj, shard_head)], axis=1)
    theirs = partner(after(units_of(1 - core, both), shard_head))
    shard = both_cores(units_of(core, both), theirs)

    groups = [
        [(0, 0, 2 * unit)],
        [(0, 2 * unit, 4 * unit)],
        [(0, 6 * unit, unit), (1, 0, 3 * unit)],
        [(1, 3 * unit, 4 * unit)],
        [(0, quarter, half), (1, quarter, half)],
    ]
    own_rows = 4 * depth
    own_with = [
        [(0, 0, own_rows), (1, 0, own_rows), (2, 0, own_rows // 2)],
        [(2, own_rows // 2, own_rows // 2)],
        [(3, 0, own_rows // 2)],
        [(3, own_rows // 2, own_rows // 2)],
        [(4, 0, own_rows)],
    ]

    def own(group, row, n, first=0, wide=None):
        parts = []
        last = first + (wide or sum(k for _, _, k in groups[group]))
        at = 0
        for member, start, k in groups[group]:
            low, high = max(first, at), min(last, at + k)
            if low < high:
                parts.append(shard[member, row : row + n, start + low - at : start + high - at])
            at += k
        return jnp.concatenate(parts, axis=1)

    send = [shard_head[0]] + [own(group, 0, own_rows) for group in range(1, len(groups))]
    here, there, shifted, held = [], [], [], [[] for _ in groups]

    def along_z(step, *waits):
        mine = after(send[step], *shifted[-1], *waits) if step else send[0]
        shifted.append([shift_z(mine, d) for d in range(1, lines)])

    def across_y(step, *waits):
        wide = send[step].shape[1]
        parts = []

        def add(array, group, d, row, first):
            start = sum(a.shape[0] for a in parts)
            held[group].append((step, start, d, row, first, array.shape[0], wide))
            parts.append(array)

        for group, row, n in own_with[step]:
            for first in range(0, send[group].shape[1], wide):
                mine = send[0] if group == 0 else own(group, row, n, first, wide)
                add(mine, group, 0, row, first)
        for d, rows_from in enumerate(shifted[step]):
            add(rows_from, step, d + 1, 0, 0)
        here.append(jnp.concatenate(parts))
        there.append(over_y(after(here[step], *there[-1:], *waits)))

    def weights_of(*which):
        units = [(member, n) for group in which for member, _, n in groups[group]]
        used = sorted(set(source[0] for group in which for source in held[group]))
        sources = []
        at = 0
        for group in which:
            for i, start, d, row, first, n, wide in held[group]:
                sources.append((used.index(i), start, d, row, at + first, n, wide))
            at += send[group].shape[1]
        arrays = [here[i] for i in used], [there[i] for i in used]
        return units, lines, own_rows, *arrays, sources

    per_block = math.gcd(2 * rows, 4)
    per_chip = 2 * rows // per_block
    along_z(0)
    pick_own = member_pick[:, 0]
    pick_near = jnp.concatenate([pick_own, over_x(after(pick_own, send[0]))])
    x = after(tokens_in, shifted[0][0]).astype(F32)
    gain = jnp.zeros((rows, width), F32)
    for member in range(members):
        gain = jnp.where(pick_own[:, None] == member, norm_gain[member][None, :], gain)
    normed = x * (1.0 / jnp.sqrt(jnp.mean(x * x, axis=2, keepdims=True) + 1e-06))
    lifted = (normed * gain[:, None, :]).astype(BF16)
    near = jnp.stack([lifted, upstream])
    lifted_over = over_x(lifted)
    across_y(0)
    along_z(1)
    pick_far = partner(after(pick_near, shifted[0][-1]))

    perm, member_sorted = sort_rows(jnp.concatenate([pick_near[rows:], pick_far[rows:]]))
    perm_own, member_sorted_own = sort_rows(jnp.concatenate([pick_own, pick_far[:rows]]))
    scalars = (
        jnp.concatenate([member_sorted, member_sorted_own]),
        jnp.stack([y_at, rank // 4]),
        jnp.concatenate([perm + 2 * rows, perm_own]),
    )

    along_z(2, there[0], lifted_over, *scalars)
    across_y(1)
    over = jnp.stack([lifted_over, over_x(after(upstream, there[0], *shifted[1]))])
    along_z(3, there[1], over)
    across_y(2)
    far = partner(after(jnp.stack([near, over]), *shifted[2], there[1]))
    along_z(4, there[2], far)
    across_y(3)
    tokens_of = (near, over, far)
    over_blocks, own_blocks = (0, per_chip, per_block), (per_chip, per_chip, per_block)
    sums = chunk(
        (True, False), over_blocks, (1,), scalars,
        (near, after(over, *shifted[3]), far), weights_of(0, 1, 2), None,
    )
    across_y(4)
    sums = (after(sums[0], shifted[4][0]), sums[1])
    *same, other_out, other_back = chunk(
        (False, True), over_blocks, (1,), scalars, tokens_of, weights_of(3), sums,
        (BF16, BF16), 0,
    )
    summed = [
        (a.astype(F32) + partner(b).astype(F32)).astype(BF16)
        for a, b in zip(same, (other_out, other_back))
    ]
    tokens_of = (after(near, *summed), over, far)
    across = [over_x(a) for a in summed]
    sums = chunk(
        (True, False), own_blocks, (0,), scalars, tokens_of, weights_of(0, 1, 2, 3), None, None, 0
    )
    out, back, packed_out, packed_back = chunk(
        (False, True), own_blocks, (0,), scalars, tokens_of, weights_of(4), sums, (F32, BF16), 0
    )
    return tuple(
        finish(
            pick_own, tokens_in, upstream, norm_gain, out, back,
            partner(packed_out), partner(packed_back), *across,
        )
    )


def solution(mesh):
    ranks = mesh.shape["row"]
    four = mesh.shape["feat"] == 1 and ranks % 4 == 0 and mesh.shape["grp"] == 2

    def on_device(tokens_in, upstream, member_pick, norm_gain, up_proj, down_proj):
        args = (tokens_in, upstream, member_pick, norm_gain, up_proj, down_proj)
        if four and member_pick.shape[1] == 1 and up_proj.shape[0] == 2:
            return on_device_shared(ranks, *args)
        return on_device_general(*args)

    in_specs = (
        P(("grp", "row"), None, "feat"),
        P(("grp", "row"), None, "feat"),
        P(("grp", "row"), None),
        P(),
        P(None, "row", "feat"),
        P(None, "row", "feat"),
    )
    out_specs = (
        P(("grp", "row"), None, "feat"),
        P(("grp", "row"), None, "feat"),
        P(("grp", "row"), None),
    )
    return jax.shard_map(
        on_device, mesh=mesh, in_specs=in_specs, out_specs=out_specs, check_vma=False
    )
```

```python
import functools
import math

import jax
import jax.numpy as jnp
from jax import lax
from jax.experimental import pallas as pl
from jax.experimental.pallas import tpu as pltpu
from jax.sharding import PartitionSpec as P

coef_c = math.sqrt(2.0 / math.pi)


def gelu_tanh(v):
    return 0.5 * v * (1.0 + jnp.tanh(coef_c * (v + 0.044715 * v * v * v)))


def gelu_slope(v):
    inner = jnp.tanh(coef_c * (v + 0.044715 * v * v * v))
    return 0.5 * (1.0 + inner) + 0.5 * v * (1.0 - inner * inner) * coef_c * (
        1.0 + 3.0 * 0.044715 * v * v
    )


def on_device_general(tokens_in, upstream, member_pick, norm_gain, up_proj, down_proj):
    rows, seq, half = tokens_in.shape
    count = rows * seq
    members = up_proj.shape[0]
    pick = member_pick.shape[1]
    whole_x, whole_g = (
        lax.all_gather(tokens_in, "feat", axis=2, tiled=True),
        lax.all_gather(upstream, "feat", axis=2, tiled=True),
    )
    width = whole_x.shape[2]
    flat_x = whole_x.reshape(count, width).astype(jnp.float32)
    flat_g = whole_g.reshape(count, width)
    inv_rms = 1.0 / jnp.sqrt(jnp.mean(flat_x * flat_x, axis=1, keepdims=True) + 1e-06)
    normed = flat_x * inv_rms
    labels = jnp.arange(members, dtype=jnp.int32)
    chosen = (
        jnp.sum((member_pick[:, :, None] == labels[None, None, :]).astype(jnp.float32), axis=1)
        / pick
    )
    chosen_tok = jnp.repeat(chosen, seq, axis=0)
    out_half = jnp.zeros((count, half), jnp.float32)
    back_half = jnp.zeros((count, half), jnp.float32)
    for member in range(members):
        lifted = (normed * norm_gain[member][None, :]).astype(jnp.bfloat16)
        up_full = lax.all_gather(up_proj[member], "row", axis=0, tiled=True)
        hidden = jnp.dot(lifted, up_full, preferred_element_type=jnp.float32)
        act = gelu_tanh(hidden).astype(jnp.bfloat16)
        piece = lax.all_gather(down_proj[member], "row", axis=0, tiled=True)
        block = lax.dot_general(
            act, piece, (((1,), (1,)), ((), ())), preferred_element_type=jnp.float32
        )
        grads = jnp.dot(flat_g, piece, preferred_element_type=jnp.float32)
        pre_grad = (grads * gelu_slope(hidden)).astype(jnp.bfloat16)
        in_grad = lax.dot_general(
            pre_grad, up_full, (((1,), (1,)), ((), ())), preferred_element_type=jnp.float32
        )
        weight_col = chosen_tok[:, member : member + 1]
        out_term = weight_col * block
        back_term = weight_col * norm_gain[member][None, :] * in_grad
        out_part, back_part = (
            lax.psum_scatter(
                out_term.astype(jnp.bfloat16), "feat", scatter_dimension=1, tiled=True
            ).astype(jnp.float32),
            lax.psum_scatter(
                back_term.astype(jnp.bfloat16), "feat", scatter_dimension=1, tiled=True
            ).astype(jnp.float32),
        )
        out_half = out_half + out_part
        back_half = back_half + back_part
    own_x = tokens_in.reshape(count, half).astype(jnp.float32)
    normed_half = own_x * inv_rms
    stat = lax.psum(jnp.sum(normed_half * back_half, axis=1, keepdims=True), "feat") / width
    coupling = stat * math.sqrt(width)
    own_g = upstream.reshape(count, half).astype(jnp.float32)
    value_out = (own_x + out_half).astype(jnp.bfloat16)
    grad_in = (own_g + (back_half - normed_half * stat) * inv_rms).astype(jnp.bfloat16)
    return (
        value_out.reshape(rows, seq, half),
        grad_in.reshape(rows, seq, half),
        coupling.reshape(rows, seq),
    )


VMEM_LIMIT = 20 * 1024 * 1024
BF16 = jnp.bfloat16
F32 = jnp.float32


def along(z, d, lines):
    return z ^ d if lines & (lines - 1) == 0 else (z + lines - d) % lines


def chunk_kernel(
    offset, kind, units, chips, sources, sorted_ref, place_ref, perm_ref, *refs
):
    first, last = kind
    parts = len(units)
    arrays = 1 + max(source[0] for source in sources)
    tokens_of, refs = refs[: len(chips) + 1], refs[len(chips) + 1 :]
    here_refs, there_refs, refs = refs[:arrays], refs[arrays : 2 * arrays], refs[2 * arrays :]
    if first:
        *outs, tokens_ref, weights_ref, sems, lifted_ref, g_ref, act_ref, pre_ref = refs
    elif last:
        out_in, back_in, *outs, tokens_ref, weights_ref, sems = refs[:-6]
        lifted_ref, g_ref, act_ref, pre_ref = refs[-6:-2]
        out_acc, back_acc = refs[-2:]
    else:
        out_in, back_in, *outs, tokens_ref, weights_ref, sems = refs[:-4]
        lifted_ref, g_ref, act_ref, pre_ref = refs[-4:]
    if not last:
        out_acc, back_acc = outs
    j = pl.program_id(0)
    rows, seq = tokens_ref.shape[2:4]
    per_block = lifted_ref.shape[0] // seq
    places = [(j + offset) * per_block + i for i in range(per_block)]
    lines, _, depth2, _ = weights_ref.shape
    depth = depth2 // 2
    starts = [sum(n for _, n in units[:part]) for part in range(parts)]

    @pl.when(j == 0)
    def _():
        y, z = place_ref[0], place_ref[1]
        copies = []
        for i, chip in enumerate(chips):
            for k, ref in enumerate((tokens_of[i], tokens_of[-1].at[chip])):
                copies.append(
                    pltpu.make_async_copy(ref, tokens_ref.at[2 * i + k], sems.at[len(copies)])
                )
        for i, start, d, to_row, to_unit, n, wide in sources:
            from_z = along(z, d, lines)
            for to_y, ref in ((y, here_refs[i]), (1 - y, there_refs[i])):
                to = weights_ref.at[from_z, to_y, pl.ds(to_row, n), pl.ds(to_unit, wide)]
                copies.append(
                    pltpu.make_async_copy(ref.at[pl.ds(start, n)], to, sems.at[len(copies)])
                )
        for copy in copies:
            copy.start()
        for copy in copies:
            copy.wait()

    width = lifted_ref.shape[1]
    here = [sorted_ref[at] for at in places]

    def pick_up(member):
        for i, at in enumerate(places):
            row = perm_ref[at]
            source = row // rows - 2 * chips[0]
            tokens = pl.ds(i * seq, seq)

            @pl.when(here[i] == member)
            def _():
                lifted_ref[tokens, :] = tokens_ref[source, 0, lax.rem(row, rows)]
                g_ref[tokens, :] = tokens_ref[source, 1, lax.rem(row, rows)]

            @pl.when(here[i] != member)
            def _():
                lifted_ref[tokens, :] = jnp.zeros((seq, width), BF16)
                g_ref[tokens, :] = jnp.zeros((seq, width), BF16)

    def sums(member):
        pick_up(member)
        mine = [(start, n) for (m, n), start in zip(units, starts) if m == member]
        low, high = mine[0][0], mine[-1][0] + mine[-1][1]
        for s in range(low, high, 256):
            e = min(s + 256, high)
            up = weights_ref[:, :, :depth, s:e].reshape(width, e - s)
            down = weights_ref[:, :, depth:, s:e].reshape(width, e - s)
            v = jnp.dot(lifted_ref[...], up, preferred_element_type=F32)
            grads = jnp.dot(g_ref[...], down, preferred_element_type=F32)
            square = v * v
            t = jnp.tanh(v * (coef_c + (coef_c * 0.044715) * square))
            half_v = 0.5 * v
            act_ref[:, s - low : e - low] = (half_v + half_v * t).astype(BF16)
            slope = (0.5 + 0.5 * t) + (half_v * (1.0 - t * t)) * (
                coef_c + (3.0 * coef_c * 0.044715) * square
            )
            pre_ref[:, s - low : e - low] = (grads * slope).astype(BF16)
        up = weights_ref[:, :, :depth, low:high].reshape(width, high - low)
        down = weights_ref[:, :, depth:, low:high].reshape(width, high - low)
        dims = (((1,), (1,)), ((), ()))
        return (
            lax.dot_general(act_ref[:, : high - low], down, dims, preferred_element_type=F32),
            lax.dot_general(pre_ref[:, : high - low], up, dims, preferred_element_type=F32),
        )

    for at, member in enumerate(sorted(set(m for m, _ in units))):
        used = functools.reduce(jnp.logical_or, [m == member for m in here])

        @pl.when(used)
        def _():
            out_sum, back_sum = sums(member)
            if at > 0:
                out_acc[...] += out_sum
                back_acc[...] += back_sum
            elif first:
                out_acc[...] = out_sum
                back_acc[...] = back_sum
            else:
                out_acc[...] = out_in[...] + out_sum
                back_acc[...] = back_in[...] + back_sum

        if at == 0:

            @pl.when(jnp.logical_not(used))
            def _():
                out_acc[...] = jnp.zeros(out_acc.shape, F32) if first else out_in[...]
                back_acc[...] = jnp.zeros(back_acc.shape, F32) if first else back_in[...]

    if last:
        for p, at in enumerate(places):
            row = lax.rem(perm_ref[at], 2 * rows)
            tokens = pl.ds(p * seq, seq)
            low = 0
            for to_out, to_back in zip(outs[::2], outs[1::2]):
                n = to_out.shape[0]

                @pl.when(jnp.logical_and(row >= low, row < low + n))
                def _():
                    to = jnp.clip(row - low, 0, n - 1)
                    to_out[to] = out_acc[tokens, :].astype(to_out.dtype)
                    to_back[to] = back_acc[tokens, :].astype(to_back.dtype)

                low += n


def chunk(kind, blocks, chips, scalars, tokens_of, weights, sums, outs=None, weight=1):
    first, last = kind
    offset, number, per_block = blocks
    units, lines, depth2, here, there, sources = weights
    _, rows, seq, width = tokens_of[0].shape
    hidden = sum(n for _, n in units)
    size = per_block * seq

    tok = pl.BlockSpec((size, width), lambda j, *_: (j, 0))
    hbm = pl.BlockSpec(memory_space=pl.ANY)
    args = [*scalars, *(tokens_of[chip] for chip in chips), tokens_of[-1], *here, *there]
    specs = [pl.BlockSpec(memory_space=pltpu.HBM)] * (len(chips) + 1) + [hbm] * (2 * len(here))
    alias = {}
    out_specs = [tok, tok]
    out_shape = [jax.ShapeDtypeStruct((number * size, width), F32)] * 2
    scratch = [
        pltpu.VMEM((2 * len(chips), 2, rows, seq, width), BF16),
        pltpu.VMEM((lines, 2, depth2, hidden), BF16),
        pltpu.SemaphoreType.DMA((2 * len(sources) + 2 * len(chips),)),
        pltpu.VMEM((size, width), BF16),
        pltpu.VMEM((size, width), BF16),
        pltpu.VMEM((size, hidden), BF16),
        pltpu.VMEM((size, hidden), BF16),
    ]
    if not first:
        alias = {len(args): 0, len(args) + 1: 1}
        args += list(sums)
        specs += [tok, tok]
    if last:
        alias = {}
        shape = (rows, seq, width)
        out_shape = [jax.ShapeDtypeStruct(shape, dtype) for dtype in outs for _ in range(2)]
        out_specs = [pl.BlockSpec(shape, lambda *_: (0, 0, 0))] * len(out_shape)
        scratch += [pltpu.VMEM((size, width), F32)] * 2

    return pl.pallas_call(
        functools.partial(chunk_kernel, offset, kind, units, chips, sources),
        grid_spec=pltpu.PrefetchScalarGridSpec(
            num_scalar_prefetch=len(scalars),
            grid=(number,),
            in_specs=specs,
            out_specs=out_specs,
            scratch_shapes=scratch,
        ),
        out_shape=out_shape,
        input_output_aliases=alias,
        compiler_params=pltpu.CompilerParams(vmem_limit_bytes=VMEM_LIMIT),
        cost_estimate=pl.CostEstimate(
            flops=weight * 8 * number * size * width * hidden * 2 // 3,
            bytes_accessed=weight * (4 * width * hidden + 20 * number * size * width),
            transcendentals=weight * number * size * hidden,
        ),
        name="chunk",
    )(*args)


def finish_kernel(
    member_ref, x_ref, g_ref, gain_ref, out_ref, back_ref, other_out_ref, other_back_ref,
    across_out_ref, across_back_ref, value_ref, grad_ref, coupling_ref,
):
    rows, seq, width = x_ref.shape
    diagonal = lax.broadcasted_iota(jnp.int32, (seq, seq), 0) == lax.broadcasted_iota(
        jnp.int32, (seq, seq), 1
    )
    for r in range(rows):
        x = x_ref[r].astype(F32)
        inv = 1.0 / jnp.sqrt(jnp.mean(x * x, axis=1, keepdims=True) + 1e-06)
        normed = x * inv
        gain = gain_ref[pl.ds(member_ref[pl.program_id(0) * rows + r], 1), :]
        back = gain * (
            back_ref[r] + other_back_ref[r].astype(F32) + across_back_ref[r].astype(F32)
        )
        stat = jnp.sum(normed * back, axis=1, keepdims=True) / width
        out = out_ref[r] + other_out_ref[r].astype(F32) + across_out_ref[r].astype(F32)
        value_ref[r] = (x + out).astype(BF16)
        grad_ref[r] = (g_ref[r].astype(F32) + (back - normed * stat) * inv).astype(BF16)
        line = jnp.sum(jnp.where(diagonal, stat, 0.0), axis=0, keepdims=True)
        coupling_ref[pl.ds(pl.program_id(0) * rows + r, 1), :] = line * math.sqrt(width)


def finish(member_own, x, g, gain, *sums):
    rows, seq, width = x.shape
    step = math.gcd(rows, 2)
    row = pl.BlockSpec((step, seq, width), lambda r, mem: (r, 0, 0))
    return pl.pallas_call(
        finish_kernel,
        grid_spec=pltpu.PrefetchScalarGridSpec(
            num_scalar_prefetch=1,
            grid=(rows // step,),
            in_specs=[
                row, row, pl.BlockSpec(gain.shape, lambda r, mem: (0, 0)), row, row, row, row, row, row
            ],
            out_specs=[row, row, pl.BlockSpec((rows, seq), lambda r, mem: (0, 0))],
        ),
        out_shape=[
            jax.ShapeDtypeStruct((rows, seq, width), BF16),
            jax.ShapeDtypeStruct((rows, seq, width), BF16),
            jax.ShapeDtypeStruct((rows, seq), F32),
        ],
        compiler_params=pltpu.CompilerParams(vmem_limit_bytes=VMEM_LIMIT // 2),
        name="finish",
    )(member_own, x, g, gain, *sums)


def sort_rows(picks):
    index = jnp.arange(picks.shape[0], dtype=jnp.int32)
    before = (picks[None, :] < picks[:, None]) | (
        (picks[None, :] == picks[:, None]) & (index[None, :] < index[:, None])
    )
    pos = jnp.sum(before.astype(jnp.int32), axis=1)
    at = pos[None, :] == index[:, None]
    perm = jnp.sum(jnp.where(at, index[None, :], 0), axis=1)
    return perm, jnp.sum(jnp.where(at, picks[None, :], 0), axis=1)


def on_device_shared(ranks, tokens_in, upstream, member_pick, norm_gain, up_proj, down_proj):
    rows, seq, width = tokens_in.shape
    members, depth, hidden = up_proj.shape
    rank = lax.axis_index("row")
    core = lax.rem(rank, 2)
    x_at = lax.axis_index("grp")
    y_at = lax.rem(rank // 2, 2)
    lines = ranks // 4

    def partner(a):
        return lax.ppermute(a, "row", [(i, i ^ 1) for i in range(ranks)])

    def over_y(a):
        return lax.ppermute(a, "row", [(i, i ^ 2) for i in range(ranks)])

    def over_x(a):
        return lax.ppermute(a, "grp", [(0, 1), (1, 0)])

    def shift_z(a, d):
        pairs = [(4 * along(i // 4, d, lines) + i % 4, i) for i in range(ranks)]
        return lax.ppermute(a, "row", pairs)

    def after(a, *others):
        return lax.optimization_barrier((a, *others))[0]

    unit = hidden // 32
    quarter, half = 7 * unit, 2 * unit

    def units_of(c, both):
        return jnp.concatenate(
            [
                lax.dynamic_slice_in_dim(both, (2 * x_at + c) * quarter, quarter, 3),
                lax.dynamic_slice_in_dim(both, 4 * quarter + c * half, half, 3),
            ],
            axis=3,
        )

    def both_cores(mine, theirs):
        even = core == 0
        whole = jnp.concatenate(
            [jnp.where(even, mine, theirs), jnp.where(even, theirs, mine)], axis=2
        )
        return whole.reshape(mine.shape[0], 4 * depth, mine.shape[3])

    def head_of(c):
        at = (2 * x_at + c) * quarter
        return jnp.stack(
            [lax.dynamic_slice(a, (0, 0, at), (1, depth, 2 * unit)) for a in (up_proj, down_proj)],
            axis=1,
        )

    head_theirs = partner(head_of(1 - core))
    shard_head = both_cores(head_of(core), head_theirs)
    both = jnp.stack([after(up_proj, shard_head), after(down_proj, shard_head)], axis=1)
    theirs = partner(after(units_of(1 - core, both), shard_head))
    shard = both_cores(units_of(core, both), theirs)

    groups = [
        [(0, 0, 2 * unit)],
        [(0, 2 * unit, 4 * unit)],
        [(0, 6 * unit, unit), (1, 0, 3 * unit)],
        [(1, 3 * unit, 4 * unit)],
        [(0, quarter, half), (1, quarter, half)],
    ]
    own_rows = 4 * depth
    own_with = [
        [(0, 0, own_rows), (1, 0, own_rows), (2, 0, own_rows // 2)],
        [(2, own_rows // 2, own_rows // 2), (3, own_rows // 2, own_rows // 4)],
        [(3, 0, own_rows // 2), (3, 3 * own_rows // 4, own_rows // 4)],
        [],
        [(4, 0, own_rows)],
    ]

    def own(group, row, n, first=0, wide=None):
        parts = []
        last = first + (wide or sum(k for _, _, k in groups[group]))
        at = 0
        for member, start, k in groups[group]:
            low, high = max(first, at), min(last, at + k)
            if low < high:
                parts.append(shard[member, row : row + n, start + low - at : start + high - at])
            at += k
        return jnp.concatenate(parts, axis=1)

    send = [shard_head[0]] + [own(group, 0, own_rows) for group in range(1, len(groups))]
    here, there, shifted, held = [], [], [], [[] for _ in groups]

    def along_z(step, *waits):
        mine = after(send[step], *shifted[-1], *waits) if step else send[0]
        shifted.append([shift_z(mine, d) for d in range(1, lines)])

    def across_y(step, *waits):
        wide = send[step].shape[1]
        parts = []

        def add(array, group, d, row, first):
            start = sum(a.shape[0] for a in parts)
            held[group].append((step, start, d, row, first, array.shape[0], wide))
            parts.append(array)

        for group, row, n in own_with[step]:
            for first in range(0, send[group].shape[1], wide):
                mine = send[0] if group == 0 else own(group, row, n, first, wide)
                add(mine, group, 0, row, first)
        for d, rows_from in enumerate(shifted[step]):
            add(rows_from, step, d + 1, 0, 0)
        here.append(jnp.concatenate(parts))
        there.append(over_y(after(here[step], *there[-1:], *waits)))

    def weights_of(*which):
        units = [(member, n) for group in which for member, _, n in groups[group]]
        used = sorted(set(source[0] for group in which for source in held[group]))
        sources = []
        at = 0
        for group in which:
            for i, start, d, row, first, n, wide in held[group]:
                sources.append((used.index(i), start, d, row, at + first, n, wide))
            at += send[group].shape[1]
        arrays = [here[i] for i in used], [there[i] for i in used]
        return units, lines, own_rows, *arrays, sources

    per_block = math.gcd(2 * rows, 4)
    per_chip = 2 * rows // per_block
    along_z(0)
    pick_own = member_pick[:, 0]
    pick_near = jnp.concatenate([pick_own, over_x(after(pick_own, send[0]))])
    x = after(tokens_in, shifted[0][0]).astype(F32)
    gain = jnp.zeros((rows, width), F32)
    for member in range(members):
        gain = jnp.where(pick_own[:, None] == member, norm_gain[member][None, :], gain)
    normed = x * (1.0 / jnp.sqrt(jnp.mean(x * x, axis=2, keepdims=True) + 1e-06))
    lifted = (normed * gain[:, None, :]).astype(BF16)
    near = jnp.stack([lifted, upstream])
    lifted_over = over_x(lifted)
    across_y(0)
    along_z(1)
    pick_far = partner(after(pick_near, shifted[0][-1]))

    perm, member_sorted = sort_rows(jnp.concatenate([pick_near[rows:], pick_far[rows:]]))
    perm_own, member_sorted_own = sort_rows(jnp.concatenate([pick_own, pick_far[:rows]]))
    scalars = (
        jnp.concatenate([member_sorted, member_sorted_own]),
        jnp.stack([y_at, rank // 4]),
        jnp.concatenate([perm + 2 * rows, perm_own]),
    )

    along_z(2, there[0], lifted_over, *scalars)
    across_y(1)
    over = jnp.stack([lifted_over, over_x(after(upstream, there[0], *shifted[1]))])
    along_z(3, there[1], over)
    across_y(2)
    far = partner(after(jnp.stack([near, over]), *shifted[2], there[1]))
    along_z(4, there[2], far)
    across_y(3)
    tokens_of = (near, over, far)
    over_blocks, own_blocks = (0, per_chip, per_block), (per_chip, per_chip, per_block)
    sums = chunk(
        (True, False), over_blocks, (1,), scalars,
        (near, after(over, *shifted[3]), far), weights_of(0, 1, 2), None,
    )
    across_y(4)
    sums = (after(sums[0], shifted[4][0]), sums[1])
    *same, other_out, other_back = chunk(
        (False, True), over_blocks, (1,), scalars, tokens_of, weights_of(3), sums,
        (BF16, BF16), 0,
    )
    summed = [
        (a.astype(F32) + partner(b).astype(F32)).astype(BF16)
        for a, b in zip(same, (other_out, other_back))
    ]
    tokens_of = (after(near, *summed), over, far)
    across = [over_x(a) for a in summed]
    sums = chunk(
        (True, False), own_blocks, (0,), scalars, tokens_of, weights_of(0, 1, 2, 3), None, None, 0
    )
    out, back, packed_out, packed_back = chunk(
        (False, True), own_blocks, (0,), scalars, tokens_of, weights_of(4), sums, (F32, BF16), 0
    )
    return tuple(
        finish(
            pick_own, tokens_in, upstream, norm_gain, out, back,
            partner(packed_out), partner(packed_back), *across,
        )
    )


def solution(mesh):
    ranks = mesh.shape["row"]
    four = mesh.shape["feat"] == 1 and ranks % 4 == 0 and mesh.shape["grp"] == 2

    def on_device(tokens_in, upstream, member_pick, norm_gain, up_proj, down_proj):
        args = (tokens_in, upstream, member_pick, norm_gain, up_proj, down_proj)
        if four and member_pick.shape[1] == 1 and up_proj.shape[0] == 2:
            return on_device_shared(ranks, *args)
        return on_device_general(*args)

    in_specs = (
        P(("grp", "row"), None, "feat"),
        P(("grp", "row"), None, "feat"),
        P(("grp", "row"), None),
        P(),
        P(None, "row", "feat"),
        P(None, "row", "feat"),
    )
    out_specs = (
        P(("grp", "row"), None, "feat"),
        P(("grp", "row"), None, "feat"),
        P(("grp", "row"), None),
    )
    return jax.shard_map(
        on_device, mesh=mesh, in_specs=in_specs, out_specs=out_specs, check_vma=False
    )
```

```python
import functools
import math

import jax
import jax.numpy as jnp
from jax import lax
from jax.experimental import pallas as pl
from jax.experimental.pallas import tpu as pltpu
from jax.sharding import PartitionSpec as P

coef_c = math.sqrt(2.0 / math.pi)


def gelu_tanh(v):
    return 0.5 * v * (1.0 + jnp.tanh(coef_c * (v + 0.044715 * v * v * v)))


def gelu_slope(v):
    inner = jnp.tanh(coef_c * (v + 0.044715 * v * v * v))
    return 0.5 * (1.0 + inner) + 0.5 * v * (1.0 - inner * inner) * coef_c * (
        1.0 + 3.0 * 0.044715 * v * v
    )


def on_device_general(tokens_in, upstream, member_pick, norm_gain, up_proj, down_proj):
    rows, seq, half = tokens_in.shape
    count = rows * seq
    members = up_proj.shape[0]
    pick = member_pick.shape[1]
    whole_x, whole_g = (
        lax.all_gather(tokens_in, "feat", axis=2, tiled=True),
        lax.all_gather(upstream, "feat", axis=2, tiled=True),
    )
    width = whole_x.shape[2]
    flat_x = whole_x.reshape(count, width).astype(jnp.float32)
    flat_g = whole_g.reshape(count, width)
    inv_rms = 1.0 / jnp.sqrt(jnp.mean(flat_x * flat_x, axis=1, keepdims=True) + 1e-06)
    normed = flat_x * inv_rms
    labels = jnp.arange(members, dtype=jnp.int32)
    chosen = (
        jnp.sum((member_pick[:, :, None] == labels[None, None, :]).astype(jnp.float32), axis=1)
        / pick
    )
    chosen_tok = jnp.repeat(chosen, seq, axis=0)
    out_half = jnp.zeros((count, half), jnp.float32)
    back_half = jnp.zeros((count, half), jnp.float32)
    for member in range(members):
        lifted = (normed * norm_gain[member][None, :]).astype(jnp.bfloat16)
        up_full = lax.all_gather(up_proj[member], "row", axis=0, tiled=True)
        hidden = jnp.dot(lifted, up_full, preferred_element_type=jnp.float32)
        act = gelu_tanh(hidden).astype(jnp.bfloat16)
        piece = lax.all_gather(down_proj[member], "row", axis=0, tiled=True)
        block = lax.dot_general(
            act, piece, (((1,), (1,)), ((), ())), preferred_element_type=jnp.float32
        )
        grads = jnp.dot(flat_g, piece, preferred_element_type=jnp.float32)
        pre_grad = (grads * gelu_slope(hidden)).astype(jnp.bfloat16)
        in_grad = lax.dot_general(
            pre_grad, up_full, (((1,), (1,)), ((), ())), preferred_element_type=jnp.float32
        )
        weight_col = chosen_tok[:, member : member + 1]
        out_term = weight_col * block
        back_term = weight_col * norm_gain[member][None, :] * in_grad
        out_part, back_part = (
            lax.psum_scatter(
                out_term.astype(jnp.bfloat16), "feat", scatter_dimension=1, tiled=True
            ).astype(jnp.float32),
            lax.psum_scatter(
                back_term.astype(jnp.bfloat16), "feat", scatter_dimension=1, tiled=True
            ).astype(jnp.float32),
        )
        out_half = out_half + out_part
        back_half = back_half + back_part
    own_x = tokens_in.reshape(count, half).astype(jnp.float32)
    normed_half = own_x * inv_rms
    stat = lax.psum(jnp.sum(normed_half * back_half, axis=1, keepdims=True), "feat") / width
    coupling = stat * math.sqrt(width)
    own_g = upstream.reshape(count, half).astype(jnp.float32)
    value_out = (own_x + out_half).astype(jnp.bfloat16)
    grad_in = (own_g + (back_half - normed_half * stat) * inv_rms).astype(jnp.bfloat16)
    return (
        value_out.reshape(rows, seq, half),
        grad_in.reshape(rows, seq, half),
        coupling.reshape(rows, seq),
    )


VMEM_LIMIT = 20 * 1024 * 1024
BF16 = jnp.bfloat16
F32 = jnp.float32


def along(z, d, lines):
    return z ^ d if lines & (lines - 1) == 0 else (z + lines - d) % lines


def chunk_kernel(
    offset, kind, units, chips, sources, sorted_ref, place_ref, perm_ref, *refs
):
    first, last = kind
    parts = len(units)
    arrays = 1 + max(source[0] for source in sources)
    tokens_of, refs = refs[: len(chips) + 1], refs[len(chips) + 1 :]
    here_refs, there_refs, refs = refs[:arrays], refs[arrays : 2 * arrays], refs[2 * arrays :]
    if first:
        *outs, tokens_ref, weights_ref, sems, lifted_ref, g_ref, act_ref, pre_ref = refs
    elif last:
        out_in, back_in, *outs, tokens_ref, weights_ref, sems = refs[:-6]
        lifted_ref, g_ref, act_ref, pre_ref = refs[-6:-2]
        out_acc, back_acc = refs[-2:]
    else:
        out_in, back_in, *outs, tokens_ref, weights_ref, sems = refs[:-4]
        lifted_ref, g_ref, act_ref, pre_ref = refs[-4:]
    if not last:
        out_acc, back_acc = outs
    j = pl.program_id(0)
    rows, seq = tokens_ref.shape[2:4]
    per_block = lifted_ref.shape[0] // seq
    places = [(j + offset) * per_block + i for i in range(per_block)]
    lines, _, depth2, _ = weights_ref.shape
    depth = depth2 // 2
    starts = [sum(n for _, n in units[:part]) for part in range(parts)]

    @pl.when(j == 0)
    def _():
        y, z = place_ref[0], place_ref[1]
        copies = []
        for i, chip in enumerate(chips):
            for k, ref in enumerate((tokens_of[i], tokens_of[-1].at[chip])):
                copies.append(
                    pltpu.make_async_copy(ref, tokens_ref.at[2 * i + k], sems.at[len(copies)])
                )
        for i, start, d, to_row, to_unit, n, wide in sources:
            from_z = along(z, d, lines)
            for to_y, ref in ((y, here_refs[i]), (1 - y, there_refs[i])):
                to = weights_ref.at[from_z, to_y, pl.ds(to_row, n), pl.ds(to_unit, wide)]
                copies.append(
                    pltpu.make_async_copy(ref.at[pl.ds(start, n)], to, sems.at[len(copies)])
                )
        for copy in copies:
            copy.start()
        for copy in copies:
            copy.wait()

    width = lifted_ref.shape[1]
    here = [sorted_ref[at] for at in places]

    def pick_up(member):
        for i, at in enumerate(places):
            row = perm_ref[at]
            source = row // rows - 2 * chips[0]
            tokens = pl.ds(i * seq, seq)

            @pl.when(here[i] == member)
            def _():
                lifted_ref[tokens, :] = tokens_ref[source, 0, lax.rem(row, rows)]
                g_ref[tokens, :] = tokens_ref[source, 1, lax.rem(row, rows)]

            @pl.when(here[i] != member)
            def _():
                lifted_ref[tokens, :] = jnp.zeros((seq, width), BF16)
                g_ref[tokens, :] = jnp.zeros((seq, width), BF16)

    def sums(member):
        pick_up(member)
        mine = [(start, n) for (m, n), start in zip(units, starts) if m == member]
        low, high = mine[0][0], mine[-1][0] + mine[-1][1]
        for s in range(low, high, 256):
            e = min(s + 256, high)
            up = weights_ref[:, :, :depth, s:e].reshape(width, e - s)
            down = weights_ref[:, :, depth:, s:e].reshape(width, e - s)
            v = jnp.dot(lifted_ref[...], up, preferred_element_type=F32)
            grads = jnp.dot(g_ref[...], down, preferred_element_type=F32)
            square = v * v
            t = jnp.tanh(v * (coef_c + (coef_c * 0.044715) * square))
            half_v = 0.5 * v
            act_ref[:, s - low : e - low] = (half_v + half_v * t).astype(BF16)
            slope = (0.5 + 0.5 * t) + (half_v * (1.0 - t * t)) * (
                coef_c + (3.0 * coef_c * 0.044715) * square
            )
            pre_ref[:, s - low : e - low] = (grads * slope).astype(BF16)
        up = weights_ref[:, :, :depth, low:high].reshape(width, high - low)
        down = weights_ref[:, :, depth:, low:high].reshape(width, high - low)
        dims = (((1,), (1,)), ((), ()))
        return (
            lax.dot_general(act_ref[:, : high - low], down, dims, preferred_element_type=F32),
            lax.dot_general(pre_ref[:, : high - low], up, dims, preferred_element_type=F32),
        )

    for at, member in enumerate(sorted(set(m for m, _ in units))):
        used = functools.reduce(jnp.logical_or, [m == member for m in here])

        @pl.when(used)
        def _():
            out_sum, back_sum = sums(member)
            if at > 0:
                out_acc[...] += out_sum
                back_acc[...] += back_sum
            elif first:
                out_acc[...] = out_sum
                back_acc[...] = back_sum
            else:
                out_acc[...] = out_in[...] + out_sum
                back_acc[...] = back_in[...] + back_sum

        if at == 0:

            @pl.when(jnp.logical_not(used))
            def _():
                out_acc[...] = jnp.zeros(out_acc.shape, F32) if first else out_in[...]
                back_acc[...] = jnp.zeros(back_acc.shape, F32) if first else back_in[...]

    if last:
        for p, at in enumerate(places):
            row = lax.rem(perm_ref[at], 2 * rows)
            tokens = pl.ds(p * seq, seq)
            low = 0
            for to_out, to_back in zip(outs[::2], outs[1::2]):
                n = to_out.shape[0]

                @pl.when(jnp.logical_and(row >= low, row < low + n))
                def _():
                    to = jnp.clip(row - low, 0, n - 1)
                    to_out[to] = out_acc[tokens, :].astype(to_out.dtype)
                    to_back[to] = back_acc[tokens, :].astype(to_back.dtype)

                low += n


def chunk(kind, blocks, chips, scalars, tokens_of, weights, sums, outs=None, weight=1):
    first, last = kind
    offset, number, per_block = blocks
    units, lines, depth2, here, there, sources = weights
    _, rows, seq, width = tokens_of[0].shape
    hidden = sum(n for _, n in units)
    size = per_block * seq

    tok = pl.BlockSpec((size, width), lambda j, *_: (j, 0))
    hbm = pl.BlockSpec(memory_space=pl.ANY)
    args = [*scalars, *(tokens_of[chip] for chip in chips), tokens_of[-1], *here, *there]
    specs = [pl.BlockSpec(memory_space=pltpu.HBM)] * (len(chips) + 1) + [hbm] * (2 * len(here))
    alias = {}
    out_specs = [tok, tok]
    out_shape = [jax.ShapeDtypeStruct((number * size, width), F32)] * 2
    scratch = [
        pltpu.VMEM((2 * len(chips), 2, rows, seq, width), BF16),
        pltpu.VMEM((lines, 2, depth2, hidden), BF16),
        pltpu.SemaphoreType.DMA((2 * len(sources) + 2 * len(chips),)),
        pltpu.VMEM((size, width), BF16),
        pltpu.VMEM((size, width), BF16),
        pltpu.VMEM((size, hidden), BF16),
        pltpu.VMEM((size, hidden), BF16),
    ]
    if not first:
        alias = {len(args): 0, len(args) + 1: 1}
        args += list(sums)
        specs += [tok, tok]
    if last:
        alias = {}
        shape = (rows, seq, width)
        out_shape = [jax.ShapeDtypeStruct(shape, dtype) for dtype in outs for _ in range(2)]
        out_specs = [pl.BlockSpec(shape, lambda *_: (0, 0, 0))] * len(out_shape)
        scratch += [pltpu.VMEM((size, width), F32)] * 2

    return pl.pallas_call(
        functools.partial(chunk_kernel, offset, kind, units, chips, sources),
        grid_spec=pltpu.PrefetchScalarGridSpec(
            num_scalar_prefetch=len(scalars),
            grid=(number,),
            in_specs=specs,
            out_specs=out_specs,
            scratch_shapes=scratch,
        ),
        out_shape=out_shape,
        input_output_aliases=alias,
        compiler_params=pltpu.CompilerParams(vmem_limit_bytes=VMEM_LIMIT),
        cost_estimate=pl.CostEstimate(
            flops=weight * 8 * number * size * width * hidden * 2 // 3,
            bytes_accessed=weight * (4 * width * hidden + 20 * number * size * width),
            transcendentals=weight * number * size * hidden,
        ),
        name="chunk",
    )(*args)


def finish_kernel(
    member_ref, x_ref, g_ref, gain_ref, out_ref, back_ref, other_out_ref, other_back_ref,
    across_out_ref, across_back_ref, value_ref, grad_ref, coupling_ref,
):
    rows, seq, width = x_ref.shape
    diagonal = lax.broadcasted_iota(jnp.int32, (seq, seq), 0) == lax.broadcasted_iota(
        jnp.int32, (seq, seq), 1
    )
    for r in range(rows):
        x = x_ref[r].astype(F32)
        inv = 1.0 / jnp.sqrt(jnp.mean(x * x, axis=1, keepdims=True) + 1e-06)
        normed = x * inv
        gain = gain_ref[pl.ds(member_ref[pl.program_id(0) * rows + r], 1), :]
        back = gain * (
            back_ref[r] + other_back_ref[r].astype(F32) + across_back_ref[r].astype(F32)
        )
        stat = jnp.sum(normed * back, axis=1, keepdims=True) / width
        out = out_ref[r] + other_out_ref[r].astype(F32) + across_out_ref[r].astype(F32)
        value_ref[r] = (x + out).astype(BF16)
        grad_ref[r] = (g_ref[r].astype(F32) + (back - normed * stat) * inv).astype(BF16)
        line = jnp.sum(jnp.where(diagonal, stat, 0.0), axis=0, keepdims=True)
        coupling_ref[pl.ds(pl.program_id(0) * rows + r, 1), :] = line * math.sqrt(width)


def finish(member_own, x, g, gain, *sums):
    rows, seq, width = x.shape
    step = math.gcd(rows, 2)
    row = pl.BlockSpec((step, seq, width), lambda r, mem: (r, 0, 0))
    return pl.pallas_call(
        finish_kernel,
        grid_spec=pltpu.PrefetchScalarGridSpec(
            num_scalar_prefetch=1,
            grid=(rows // step,),
            in_specs=[
                row, row, pl.BlockSpec(gain.shape, lambda r, mem: (0, 0)), row, row, row, row, row, row
            ],
            out_specs=[row, row, pl.BlockSpec((rows, seq), lambda r, mem: (0, 0))],
        ),
        out_shape=[
            jax.ShapeDtypeStruct((rows, seq, width), BF16),
            jax.ShapeDtypeStruct((rows, seq, width), BF16),
            jax.ShapeDtypeStruct((rows, seq), F32),
        ],
        compiler_params=pltpu.CompilerParams(vmem_limit_bytes=VMEM_LIMIT // 2),
        name="finish",
    )(member_own, x, g, gain, *sums)


def sort_rows(picks):
    index = jnp.arange(picks.shape[0], dtype=jnp.int32)
    before = (picks[None, :] < picks[:, None]) | (
        (picks[None, :] == picks[:, None]) & (index[None, :] < index[:, None])
    )
    pos = jnp.sum(before.astype(jnp.int32), axis=1)
    at = pos[None, :] == index[:, None]
    perm = jnp.sum(jnp.where(at, index[None, :], 0), axis=1)
    return perm, jnp.sum(jnp.where(at, picks[None, :], 0), axis=1)


def on_device_shared(ranks, tokens_in, upstream, member_pick, norm_gain, up_proj, down_proj):
    rows, seq, width = tokens_in.shape
    members, depth, hidden = up_proj.shape
    rank = lax.axis_index("row")
    core = lax.rem(rank, 2)
    x_at = lax.axis_index("grp")
    y_at = lax.rem(rank // 2, 2)
    lines = ranks // 4

    def partner(a):
        return lax.ppermute(a, "row", [(i, i ^ 1) for i in range(ranks)])

    def over_y(a):
        return lax.ppermute(a, "row", [(i, i ^ 2) for i in range(ranks)])

    def over_x(a):
        return lax.ppermute(a, "grp", [(0, 1), (1, 0)])

    def shift_z(a, d):
        pairs = [(4 * along(i // 4, d, lines) + i % 4, i) for i in range(ranks)]
        return lax.ppermute(a, "row", pairs)

    def after(a, *others):
        return lax.optimization_barrier((a, *others))[0]

    unit = hidden // 32
    quarter, half = 7 * unit, 2 * unit

    def units_of(c, both):
        return jnp.concatenate(
            [
                lax.dynamic_slice_in_dim(both, (2 * x_at + c) * quarter, quarter, 3),
                lax.dynamic_slice_in_dim(both, 4 * quarter + c * half, half, 3),
            ],
            axis=3,
        )

    def both_cores(mine, theirs):
        even = core == 0
        whole = jnp.concatenate(
            [jnp.where(even, mine, theirs), jnp.where(even, theirs, mine)], axis=2
        )
        return whole.reshape(mine.shape[0], 4 * depth, mine.shape[3])

    def head_of(c):
        at = (2 * x_at + c) * quarter
        return jnp.stack(
            [lax.dynamic_slice(a, (0, 0, at), (1, depth, 2 * unit)) for a in (up_proj, down_proj)],
            axis=1,
        )

    head_theirs = partner(head_of(1 - core))
    shard_head = both_cores(head_of(core), head_theirs)
    both = jnp.stack([after(up_proj, shard_head), after(down_proj, shard_head)], axis=1)
    theirs = partner(after(units_of(1 - core, both), shard_head))
    shard = both_cores(units_of(core, both), theirs)

    groups = [
        [(0, 0, 2 * unit)],
        [(0, 2 * unit, 5 * unit)],
        [(1, 0, 4 * unit)],
        [(1, 4 * unit, 3 * unit)],
        [(0, quarter, half), (1, quarter, half)],
    ]
    own_rows = 4 * depth
    own_with = [
        [(0, 0, own_rows), (1, 0, own_rows), (2, 0, own_rows), (3, 0, own_rows)],
        [],
        [],
        [],
        [(4, 0, own_rows)],
    ]

    def own(group, row, n, first=0, wide=None):
        parts = []
        last = first + (wide or sum(k for _, _, k in groups[group]))
        at = 0
        for member, start, k in groups[group]:
            low, high = max(first, at), min(last, at + k)
            if low < high:
                parts.append(shard[member, row : row + n, start + low - at : start + high - at])
            at += k
        return jnp.concatenate(parts, axis=1)

    send = [shard_head[0]] + [own(group, 0, own_rows) for group in range(1, len(groups))]
    here, there, shifted, held = [], [], [], [[] for _ in groups]

    def along_z(step, *waits):
        mine = after(send[step], *shifted[-1], *waits) if step else send[0]
        shifted.append([shift_z(mine, d) for d in range(1, lines)])

    def across_y(step, *waits):
        wide = send[step].shape[1] if step else unit
        parts = []

        def add(array, group, d, row, first):
            start = sum(a.shape[0] for a in parts)
            held[group].append((step, start, d, row, first, array.shape[0], wide))
            parts.append(array)

        for group, row, n in own_with[step]:
            for first in range(0, send[group].shape[1], wide):
                mine = (
                    own(group, row, n, first, wide)
                    if group
                    else send[0][:, first : first + wide]
                )
                add(mine, group, 0, row, first)
        for d, rows_from in enumerate(shifted[step]):
            for first in range(0, rows_from.shape[1], wide):
                add(rows_from[:, first : first + wide], step, d + 1, 0, first)
        here.append(jnp.concatenate(parts))
        there.append(over_y(after(here[step], *there[-1:], *waits)))

    def weights_of(*which):
        units = [(member, n) for group in which for member, _, n in groups[group]]
        used = sorted(set(source[0] for group in which for source in held[group]))
        sources = []
        at = 0
        for group in which:
            for i, start, d, row, first, n, wide in held[group]:
                sources.append((used.index(i), start, d, row, at + first, n, wide))
            at += send[group].shape[1]
        arrays = [here[i] for i in used], [there[i] for i in used]
        return units, lines, own_rows, *arrays, sources

    per_block = math.gcd(2 * rows, 4)
    per_chip = 2 * rows // per_block
    along_z(0)
    pick_own = member_pick[:, 0]
    pick_near = jnp.concatenate([pick_own, over_x(after(pick_own, send[0]))])
    x = after(tokens_in, shifted[0][0]).astype(F32)
    gain = jnp.zeros((rows, width), F32)
    for member in range(members):
        gain = jnp.where(pick_own[:, None] == member, norm_gain[member][None, :], gain)
    normed = x * (1.0 / jnp.sqrt(jnp.mean(x * x, axis=2, keepdims=True) + 1e-06))
    lifted = (normed * gain[:, None, :]).astype(BF16)
    near = jnp.stack([lifted, upstream])
    lifted_over = over_x(lifted)
    across_y(0)
    along_z(1)
    pick_far = partner(after(pick_near, shifted[0][-1]))

    perm, member_sorted = sort_rows(jnp.concatenate([pick_near[rows:], pick_far[rows:]]))
    perm_own, member_sorted_own = sort_rows(jnp.concatenate([pick_own, pick_far[:rows]]))
    scalars = (
        jnp.concatenate([member_sorted, member_sorted_own]),
        jnp.stack([y_at, rank // 4]),
        jnp.concatenate([perm + 2 * rows, perm_own]),
    )

    along_z(2, there[0], lifted_over, *scalars)
    across_y(1)
    over = jnp.stack([lifted_over, over_x(after(upstream, there[0], *shifted[1]))])
    along_z(3, there[1], over)
    across_y(2)
    far = partner(after(jnp.stack([near, over]), *shifted[2], there[1]))
    along_z(4, there[2], far)
    across_y(3)
    tokens_of = (near, over, far)
    over_blocks, own_blocks = (0, per_chip, per_block), (per_chip, per_chip, per_block)
    sums = chunk(
        (True, False), over_blocks, (1,), scalars,
        (near, after(over, *shifted[3]), far), weights_of(0, 1, 2), None,
    )
    across_y(4)
    sums = (after(sums[0], shifted[4][0]), sums[1])
    *same, other_out, other_back = chunk(
        (False, True), over_blocks, (1,), scalars, tokens_of, weights_of(3), sums,
        (BF16, BF16), 0,
    )
    summed = [
        (a.astype(F32) + partner(b).astype(F32)).astype(BF16)
        for a, b in zip(same, (other_out, other_back))
    ]
    tokens_of = (after(near, *summed), over, far)
    across = [over_x(a) for a in summed]
    sums = chunk(
        (True, False), own_blocks, (0,), scalars, tokens_of, weights_of(0, 1, 2, 3), None, None, 0
    )
    out, back, packed_out, packed_back = chunk(
        (False, True), own_blocks, (0,), scalars, tokens_of, weights_of(4), sums, (F32, BF16), 0
    )
    return tuple(
        finish(
            pick_own, tokens_in, upstream, norm_gain, out, back,
            partner(packed_out), partner(packed_back), *across,
        )
    )


def solution(mesh):
    ranks = mesh.shape["row"]
    four = mesh.shape["feat"] == 1 and ranks % 4 == 0 and mesh.shape["grp"] == 2

    def on_device(tokens_in, upstream, member_pick, norm_gain, up_proj, down_proj):
        args = (tokens_in, upstream, member_pick, norm_gain, up_proj, down_proj)
        if four and member_pick.shape[1] == 1 and up_proj.shape[0] == 2:
            return on_device_shared(ranks, *args)
        return on_device_general(*args)

    in_specs = (
        P(("grp", "row"), None, "feat"),
        P(("grp", "row"), None, "feat"),
        P(("grp", "row"), None),
        P(),
        P(None, "row", "feat"),
        P(None, "row", "feat"),
    )
    out_specs = (
        P(("grp", "row"), None, "feat"),
        P(("grp", "row"), None, "feat"),
        P(("grp", "row"), None),
    )
    return jax.shard_map(
        on_device, mesh=mesh, in_specs=in_specs, out_specs=out_specs, check_vma=False
    )
```
